32 devices in a mesh: seq: 8 (over z, x), exp: 4 (over y, core).
Axes of the slice: x: 2, y: 2, z: 4, core: 2. Of those that a mesh axis runs over, the one named last changes fastest.
Arguments:
- queries: bfloat16 [4, 32, 1536], P(None, 'exp'), may hold values from -200 to 200
- new_key_value: bfloat16 [4, 32, 2, 512], P(None, 'exp'), may hold values from -8 to 8
- key_value_cache: bfloat16 [32, 64, 64, 2, 512], P('exp', 'seq'), may hold values from -8 to 8
- page_table: int32 [32, 64], P('exp', 'seq'), may hold values from 0 to 63, as said below
- cache_len: int32 [32], P('exp'), may hold values from 1 to 4096
- routes: int32 [4, 32, 8], P(None, 'exp'), may hold values from 0 to 39, all different within a row; in each aligned block of 8 rows (0 to 7, 8 to 15, ..., all dimensions but the last counted through in order) at most 4 rows name the same one
- residual: bfloat16 [4, 32, 1536], P(None, 'exp', 'seq'), may hold values from -8 to 8
- w_out: bfloat16 [1536, 1536], P(None, 'seq'), may hold values from -0.15625 to 0.15625
- norm_gain: float32 [1536], P('seq'), may hold values from 0.1 to 1.9
- w_router: bfloat16 [1536, 40], P('seq'), may hold values from -0.15625 to 0.15625
- w_gate_up: bfloat16 [40, 1536, 2, 512], P('exp', 'seq'), may hold values from -0.15625 to 0.15625
- w_down: bfloat16 [40, 1536, 512], P('exp', 'seq'), may hold values from -0.25 to 0.25
Outputs:
- layer_out: bfloat16 [4, 32, 1536], P(None, 'exp', 'seq')
The draws below stay inside these ranges and needn't reach their ends.
Inputs may be any that keep to these rules, and one draw needn't show every extreme that they name: `page_table`: within the block of one index of exp and one index of seq (8 rows, 8 columns) the entries are each page slot once. `routes`: in each step the 8 tokens of one index of exp name one expert at most 4 times; a row's 8 experts differ.
All inputs are finite; a program needn't handle non-finite values.
Results may differ from the reference program's by a relative error of at most 0.0053.
Values may be sent and summed in bfloat16 or wider, within the bound.
No kernel may reach another device: no remote copies, remote signals or barrier semaphores. Data moves between devices by JAX's collectives and lax.ppermute only.
A program may use at most 128 MiB of HBM per device.

```python
import math
import jax
import jax.numpy as jnp
import numpy as np
from jax import lax

D = 1536
QUERY_HEADS = 24
KEY_VALUE_HEADS = 8
HEAD_SIZE = 64
EXPERTS = 40
FF = 512
TOPK = 8
REQ_DEV = 8
SHARD_POSITIONS = 512
PAGE_POSITIONS = 64
DECODE_STEPS = 4
REQUEST_COUNT = 32
PAGES_PER_SHARD = 8
MAXLEN = 4096
CAP = 4
N_SEQ = 8


def drawn_keys(key):
    base_offset = jax.random.normal(jax.random.fold_in(key, 11), (DECODE_STEPS, REQUEST_COUNT, 2, KEY_VALUE_HEADS * HEAD_SIZE), jnp.float32) * 1.6
    base_offset = jnp.clip(base_offset, -8.0, 8.0)
    return base_offset


def draw_key_value_cache(key, part):
    page_count = MAXLEN // PAGE_POSITIONS
    shape = (REQUEST_COUNT, page_count, PAGE_POSITIONS, 2, KEY_VALUE_HEADS * HEAD_SIZE)
    base = jnp.clip(jax.random.normal(jax.random.fold_in(key, 61), shape, jnp.float32) * 1.6, -8.0, 8.0).astype(jnp.bfloat16)
    return base


def draw_new_key_value(key, part):
    base_offset = drawn_keys(jax.random.fold_in(key, 5))
    return base_offset.astype(jnp.bfloat16)


def draw_queries(key, part):
    noise_key = jax.random.fold_in(key, 21)
    drawn = jnp.clip(jax.random.normal(noise_key, (DECODE_STEPS, REQUEST_COUNT, QUERY_HEADS * HEAD_SIZE), jnp.float32) * 1.6, -8.0, 8.0)
    return drawn.astype(jnp.bfloat16)


def draw_page_table(key, part):
    exp_groups = REQUEST_COUNT // REQ_DEV
    seq_groups = MAXLEN // SHARD_POSITIONS
    block_keys = jax.random.split(key, exp_groups * seq_groups)
    orders = jax.vmap(lambda block_key: jax.random.permutation(block_key, REQ_DEV * PAGES_PER_SHARD))(block_keys)
    orders = orders.reshape(exp_groups, seq_groups, REQ_DEV, PAGES_PER_SHARD)
    orders = jnp.transpose(orders, (0, 2, 1, 3)).reshape(REQUEST_COUNT, seq_groups * PAGES_PER_SHARD)
    return orders.astype(jnp.int32)


def draw_cache_len(key, part):
    length_bits = MAXLEN.bit_length() - 1
    exponent = jax.random.randint(jax.random.fold_in(key, 41), (REQUEST_COUNT,), 4, length_bits + 1)
    ceiling = jnp.left_shift(jnp.ones((REQUEST_COUNT,), jnp.int32), exponent)
    lengths = jax.random.randint(jax.random.fold_in(key, 42), (REQUEST_COUNT,), 0, MAXLEN) % ceiling + 1
    longest = jax.random.randint(jax.random.fold_in(key, 43), (), 0, REQUEST_COUNT)
    lengths = jnp.where(jnp.arange(REQUEST_COUNT) == longest, MAXLEN, lengths)
    return lengths.astype(jnp.int32)


def draw_residual(key, part):
    column = jnp.arange(D, dtype=jnp.float32) / max(D - 1, 1)
    col_scale = 0.05 * 10.0 ** column * jnp.exp(jax.random.uniform(jax.random.fold_in(key, 31), (D,), jnp.float32, 0.0, math.log(2.0)))
    row_scale = jnp.exp(jax.random.uniform(jax.random.fold_in(key, 32), (DECODE_STEPS, REQUEST_COUNT, 1), jnp.float32, 0.0, math.log(3.0)))
    noise = jax.random.normal(jax.random.fold_in(key, 34), (DECODE_STEPS, REQUEST_COUNT, D), jnp.float32)
    return jnp.clip(noise * col_scale * row_scale, -8.0, 8.0).astype(jnp.bfloat16)


def level_of(own_key, shape, cuts, smallest, largest):
    loudness, own = 1.0, jax.random.fold_in(own_key, 6)
    for position, shards_of in cuts:
        steps = jnp.exp(jax.random.uniform(jax.random.fold_in(own, position), (shards_of,), jnp.float32, smallest / len(cuts), largest / len(cuts)))
        loudness = loudness * jnp.repeat(steps, shape[position] // shards_of).reshape([-1 if axis == position else 1 for axis in range(len(shape))])
    return loudness


def shared_out(key, own, number, rows, count, top, reach, lean):
    sequence = jax.random.permutation(key, count)
    crowded, common = shares(count, rows * top, reach, lean, True), shares(count, rows * top, reach, lean, False)
    places = jnp.arange(count)

    def named(sizes, turn):
        used = int((sizes > 0).sum())
        fixed = max(1, used // 4)
        moved = fixed + (places - fixed + turn * (used - fixed)) % max(1, count - fixed)
        return jnp.zeros((count,), jnp.int32).at[sequence[jnp.where(places < fixed, places, moved)]].set(jnp.asarray(sizes, jnp.int32))

    sizes = jnp.where(number % 4 == 0, named(crowded, number // 4), named(common, number - number // 4 - 1))
    mixed = jax.random.permutation(jax.random.fold_in(own, 3), count)
    donor, sink = mixed[0:count // 2 * 2:2], mixed[1:count // 2 * 2:2]
    room = jnp.minimum(sizes[donor] - 1, reach - sizes[sink]) // 2
    room = jnp.where((donor == sequence[0]) | (sink == sequence[0]) | (sizes[sink] == 0), 0, jnp.maximum(room, 0))
    moved = jax.random.randint(jax.random.fold_in(own, 4), (count // 2,), 0, 1 << 20) % (room + 1)
    sizes = sizes.at[donor].add(-moved).at[sink].add(moved)
    labels = jnp.searchsorted(jnp.cumsum(sizes), jnp.arange(rows * top), side="right").astype(jnp.int32)
    table = labels.reshape(top, rows).T
    table = table[jax.random.permutation(jax.random.fold_in(own, 1), rows)]
    turn = jax.random.randint(jax.random.fold_in(own, 2), (rows, 1), 0, top)
    return jnp.take_along_axis(table, (jnp.arange(top)[None, :] + turn) % top, axis=1)


def shares(number_of, total, bound, slope, full):
    weights = [(1 << 20) // math.isqrt(grade ** slope) + 1 for grade in range(1, number_of + 1)]
    largest = bound if full else min(bound, max(-(-total // number_of), total * weights[0] // sum(weights)))
    least = 1 if total - largest >= number_of - 1 else 0
    counts, spare = [largest] + [least] * (number_of - 1), total - largest - least * (number_of - 1)
    while spare > 0:
        free = [i for i in range(1, number_of) if counts[i] < largest] or [i for i in range(1, number_of) if counts[i] < bound]
        whole, budget = sum([weights[i] for i in free]), spare
        for i in free:
            more = min(bound - counts[i], max(1, budget * weights[i] // whole), spare)
            counts[i] = counts[i] + more
            spare = spare - more
    return np.array(counts)


def bell_draw(stream_key, shape, width, reach, shards=(), kind=jnp.bfloat16):
    drawn = width * jax.random.normal(stream_key, shape, jnp.float32)
    if shards:
        drawn = drawn * level_of(stream_key, shape, shards, -0.22, 0.18)
    return jnp.clip(drawn, -reach, reach).astype(kind)


def setup_inputs(seed: int = 0) -> dict:
    keys = jax.random.split(jax.random.key(seed), 13)
    queries = draw_queries(jax.random.fold_in(keys[12], 71), 0)
    new_key_value = draw_new_key_value(jax.random.fold_in(keys[12], 71), 0)
    key_value_cache = draw_key_value_cache(jax.random.fold_in(keys[12], 71), 0)
    page_table = draw_page_table(jax.random.fold_in(keys[12], 71), 0)
    cache_len = draw_cache_len(jax.random.fold_in(keys[12], 71), 0)
    routes_keys = jax.random.split(jax.random.fold_in(keys[5], 1), DECODE_STEPS * REQUEST_COUNT // REQ_DEV)
    routes_turns = jax.random.permutation(jax.random.fold_in(keys[5], 3), DECODE_STEPS * REQUEST_COUNT // REQ_DEV)
    routes = jax.vmap(lambda own, number: shared_out(jax.random.fold_in(keys[5], 2), own, number, REQ_DEV, EXPERTS, TOPK, CAP, 2))(routes_keys, routes_turns).reshape((DECODE_STEPS, REQUEST_COUNT, TOPK))
    residual = draw_residual(jax.random.fold_in(keys[12], 71), 0)
    w_out = bell_draw(keys[7], (QUERY_HEADS * HEAD_SIZE, D), (QUERY_HEADS * HEAD_SIZE) ** -0.5, 0.15625, ((1, 8),))
    norm_gain = jnp.clip(1.0 + 0.18 * jax.random.normal(keys[8], (D,), jnp.float32), 0.1, 1.9)
    w_router = bell_draw(keys[9], (D, EXPERTS), D ** -0.5, 0.15625, ((0, 8),))
    w_gate_up = bell_draw(keys[10], (EXPERTS, D, 2, FF), D ** -0.5, 0.15625, ((0, 4), (1, 8)))
    w_down = bell_draw(keys[11], (EXPERTS, D, FF), FF ** -0.5, 0.25, ((0, 4), (1, 8)))
    return dict(queries=queries, new_key_value=new_key_value, key_value_cache=key_value_cache, page_table=page_table, cache_len=cache_len, routes=routes, residual=residual, w_out=w_out, norm_gain=norm_gain, w_router=w_router, w_gate_up=w_gate_up, w_down=w_down)


NEG_FILL = -1e+30

def reference(queries, new_key_value, key_value_cache, page_table, cache_len, routes, residual, w_out, norm_gain, w_router, w_gate_up, w_down):
    query_head_group = QUERY_HEADS // KEY_VALUE_HEADS
    page_count = N_SEQ * PAGES_PER_SHARD
    step_ids = jnp.arange(DECODE_STEPS)
    causal = step_ids[None, :] <= step_ids[:, None]

    def attend(request_index):
        owner_group = request_index // REQ_DEV
        physical = page_table[request_index]
        row_ids = (owner_group * REQ_DEV + physical // PAGES_PER_SHARD).astype(jnp.int32)
        col_ids = (jnp.arange(page_count) // PAGES_PER_SHARD * PAGES_PER_SHARD + physical % PAGES_PER_SHARD).astype(jnp.int32)
        gathered_rows = key_value_cache[row_ids, col_ids]
        cached_key_rows = gathered_rows[:, :, 0].reshape(N_SEQ, SHARD_POSITIONS, KEY_VALUE_HEADS, HEAD_SIZE).astype(jnp.float32)
        cached_value_rows = gathered_rows[:, :, 1].reshape(N_SEQ, SHARD_POSITIONS, KEY_VALUE_HEADS, HEAD_SIZE).astype(jnp.float32)
        positions = jnp.arange(MAXLEN).reshape(N_SEQ, SHARD_POSITIONS)
        live_mask = (positions < cache_len[request_index])[None, None, None]
        current_query = queries[:, request_index].astype(jnp.float32).reshape(DECODE_STEPS, KEY_VALUE_HEADS, query_head_group, HEAD_SIZE)
        scores = jnp.einsum('tkgd,bskd->tkgbs', current_query, cached_key_rows) * 0.125
        scores = jnp.where(live_mask, scores, NEG_FILL)
        block_max = lax.optimization_barrier(jnp.max(scores, axis=-1))
        weights = jnp.where(live_mask, jnp.exp(scores - block_max[..., None]), 0.0)
        block_sum = lax.optimization_barrier(jnp.sum(weights, axis=-1))
        rounded = lax.optimization_barrier(weights.astype(jnp.bfloat16)).astype(jnp.float32)
        block_acc = jnp.einsum('tkgbs,bskd->tkgbd', rounded, cached_value_rows)
        new_key_rows = new_key_value[:, request_index, 0].astype(jnp.float32).reshape(DECODE_STEPS, KEY_VALUE_HEADS, HEAD_SIZE)
        new_value_rows = new_key_value[:, request_index, 1].astype(jnp.float32).reshape(DECODE_STEPS, KEY_VALUE_HEADS, HEAD_SIZE)
        fresh_scores = jnp.einsum('tkgd,ukd->tkgu', current_query, new_key_rows) * 0.125
        kept_mask = causal[:, None, None, :]
        fresh_scores = jnp.where(kept_mask, fresh_scores, NEG_FILL)
        fresh_max = lax.optimization_barrier(jnp.max(fresh_scores, axis=-1))
        fresh_weights = jnp.where(kept_mask, jnp.exp(fresh_scores - fresh_max[..., None]), 0.0)
        fresh_sum = lax.optimization_barrier(jnp.sum(fresh_weights, axis=-1))
        fresh_round = lax.optimization_barrier(fresh_weights.astype(jnp.bfloat16)).astype(jnp.float32)
        fresh_acc = jnp.einsum('tkgu,ukd->tkgd', fresh_round, new_value_rows)
        overall = jnp.maximum(lax.optimization_barrier(jnp.max(block_max, axis=-1)), fresh_max)
        block_scale = jnp.exp(block_max - overall[..., None])
        fresh_scale = jnp.exp(fresh_max - overall)
        numer = lax.optimization_barrier(jnp.sum(block_scale[..., None] * block_acc, axis=3)) + fresh_scale[..., None] * fresh_acc
        denom = lax.optimization_barrier(jnp.sum(block_scale * block_sum, axis=3)) + fresh_scale * fresh_sum
        return (numer / denom[..., None]).reshape(DECODE_STEPS, QUERY_HEADS * HEAD_SIZE)
    attention = lax.map(attend, jnp.arange(REQUEST_COUNT))
    attention = jnp.transpose(attention, (1, 0, 2)).astype(jnp.bfloat16).reshape(DECODE_STEPS * REQUEST_COUNT, QUERY_HEADS * HEAD_SIZE)
    hidden_state = residual.reshape(DECODE_STEPS * REQUEST_COUNT, D).astype(jnp.float32) + jnp.dot(attention, w_out, preferred_element_type=jnp.float32)
    inv_rms = lax.rsqrt(lax.optimization_barrier(jnp.mean(hidden_state * hidden_state, axis=-1)) + 1e-06)
    gain_f32 = norm_gain.astype(jnp.float32)
    scaled = (hidden_state * gain_f32).astype(jnp.bfloat16)
    logits = jnp.dot(scaled, w_router, preferred_element_type=jnp.float32) * inv_rms[:, None]
    normed = (hidden_state * gain_f32 * inv_rms[:, None]).astype(jnp.bfloat16)
    chosen_routes = routes.reshape(DECODE_STEPS * REQUEST_COUNT, TOPK)
    picked_logits = jnp.take_along_axis(logits, chosen_routes, axis=1)
    exp_logit = jnp.exp(picked_logits)
    gate_weights = exp_logit / lax.optimization_barrier(jnp.sum(exp_logit, axis=-1, keepdims=True))

    def one_expert(moe_total, expert):
        hit_mask = (chosen_routes == expert).astype(jnp.float32)
        weight = lax.optimization_barrier(jnp.sum(hit_mask * gate_weights, axis=-1))
        pre_act = jnp.dot(normed, w_gate_up[expert].reshape(D, 2 * FF), preferred_element_type=jnp.float32).reshape(-1, 2, FF)
        inner_act = (jax.nn.silu(pre_act[:, 0]) * pre_act[:, 1]).astype(jnp.bfloat16)
        outputs = jnp.dot(inner_act, w_down[expert].T, preferred_element_type=jnp.float32).astype(jnp.bfloat16)
        outputs = lax.optimization_barrier(outputs).astype(jnp.float32)
        return (moe_total + weight[:, None] * outputs, None)
    moe_total, unused_out = lax.scan(one_expert, jnp.zeros((DECODE_STEPS * REQUEST_COUNT, D), jnp.float32), jnp.arange(EXPERTS))
    return (hidden_state + moe_total).astype(jnp.bfloat16).reshape(DECODE_STEPS, REQUEST_COUNT, D)
```

```python
import functools

import jax
import jax.numpy as jnp
from jax import lax
from jax.experimental import pallas as pl
from jax.experimental.pallas import tpu as pltpu
from jax.sharding import PartitionSpec as P

D = 1536
QUERY_HEADS = 24
KEY_VALUE_HEADS = 8
HEAD_SIZE = 64
GROUP = QUERY_HEADS // KEY_VALUE_HEADS
KV_WIDTH = KEY_VALUE_HEADS * HEAD_SIZE
EXPERTS = 40
CAP = 4
LANES = 128
SIDE_KEYS = 2

NEG_FILL = -1e30
F32 = jnp.float32
BF16 = jnp.bfloat16
VMEM_LIMIT = 48 * 1024 * 1024


def iota(shape, dimension):
    return lax.broadcasted_iota(jnp.int32, shape, dimension)


def dot_nt(a, b):
    return lax.dot_general(a, b, (((1,), (1,)), ((), ())), preferred_element_type=F32)


def dot_tn(a, b):
    return lax.dot_general(a, b, (((0,), (0,)), ((), ())), preferred_element_type=F32)


def dot_nn(a, b):
    return lax.dot_general(a, b, (((1,), (0,)), ((), ())), preferred_element_type=F32)


def round16(x):
    return x.astype(BF16).astype(F32)


def swap_halves(x):
    return pltpu.roll(x, HEAD_SIZE, 1)


def tile_of(x, index):
    return x[:, index * LANES : (index + 1) * LANES]


def padded(width):
    return -(-width // LANES) * LANES


def params():
    return pltpu.CompilerParams(vmem_limit_bytes=VMEM_LIMIT)


def attend_kernel(steps, pages, page_rows, table_ref, len_ref, seq_ref, q_ref, fresh_ref, *refs):
    page_refs, out_ref = refs[:pages], refs[pages]
    request = pl.program_id(0)
    q = q_ref[0].astype(F32)
    low = iota((steps, LANES), 1) < HEAD_SIZE
    by_group = []
    for g in range(GROUP):
        tiles = []
        for j in range(KV_WIDTH // LANES):
            first = tile_of(q, (6 * j + g) // 2)
            second = tile_of(q, (6 * j + 3 + g) // 2)
            if g % 2 == 0:
                tiles.append(jnp.where(low, first, second))
            else:
                tiles.append(swap_halves(jnp.where(low, second, first)))
        by_group.append(jnp.concatenate(tiles, axis=1))
    rows = steps * GROUP * KEY_VALUE_HEADS
    stacked = jnp.concatenate(
        [
            jnp.broadcast_to(by_group[g][t : t + 1], (KEY_VALUE_HEADS, KV_WIDTH))
            for t in range(steps)
            for g in range(GROUP)
        ],
        axis=0,
    )
    own = iota((rows, KV_WIDTH), 1) // HEAD_SIZE == iota((rows, KV_WIDTH), 0) % KEY_VALUE_HEADS
    spread = jnp.where(own, stacked, 0.0).astype(BF16)
    keys = jnp.concatenate([ref[0, 0] for ref in page_refs], axis=0)
    values = jnp.concatenate([ref[0, 1] for ref in page_refs], axis=0)
    span = pages * page_rows
    scores = dot_nt(spread, keys) * 0.125
    live = seq_ref[0] * span + iota((rows, span), 1) < len_ref[request]
    scores = jnp.where(live, scores, NEG_FILL)
    fresh_keys, fresh_values = fresh_ref[0, 0], fresh_ref[0, 1]
    fresh_rows = fresh_keys.shape[0]
    fresh_scores = dot_nt(spread, fresh_keys) * 0.125
    row_step = iota((rows, fresh_rows), 0) // (GROUP * KEY_VALUE_HEADS)
    kept = jnp.logical_and(iota((rows, fresh_rows), 1) <= row_step, seq_ref[0] == 0)
    fresh_scores = jnp.where(kept, fresh_scores, NEG_FILL)
    largest = jnp.maximum(
        jnp.max(scores, axis=1, keepdims=True), jnp.max(fresh_scores, axis=1, keepdims=True)
    )
    weights = jnp.where(live, jnp.exp(scores - largest), 0.0)
    fresh_weights = jnp.where(kept, jnp.exp(fresh_scores - largest), 0.0)
    total = jnp.sum(weights, axis=1, keepdims=True) + jnp.sum(fresh_weights, axis=1, keepdims=True)
    acc = dot_nn(weights.astype(BF16), values) + dot_nn(fresh_weights.astype(BF16), fresh_values)
    some = total > 0.0
    safe = jnp.where(some, total, 1.0)
    acc = jnp.where(own, acc * (1.0 / safe), 0.0)
    acc = jnp.sum(acc.reshape(steps * GROUP, KEY_VALUE_HEADS, KV_WIDTH), axis=1)
    level = jnp.where(some, largest + jnp.log(safe), NEG_FILL)
    high = round16(level)
    middle = round16(level - high)
    rest = level - high - middle
    lane = iota((rows, LANES), 1)
    head = iota((rows, LANES), 0) % KEY_VALUE_HEADS
    side = jnp.where(lane == head, high, 0.0)
    side = jnp.where(lane == head + 8, middle, side)
    side = jnp.where(lane == head + 16, rest, side)
    side = jnp.sum(side.reshape(steps * GROUP, KEY_VALUE_HEADS, LANES), axis=1)
    out_ref[0, :, 0:KV_WIDTH] = acc.astype(BF16)
    out_ref[0, :, KV_WIDTH : KV_WIDTH + LANES] = side.astype(BF16)


def attend(queries, new_key_value, pool, page_table, cache_len, seq_index):
    steps, requests, width = queries.shape
    pages = page_table.shape[1]
    page_rows = pool.shape[2]
    by_request = queries.transpose(1, 0, 2)
    fresh = new_key_value.transpose(1, 2, 0, 3)
    fresh = jnp.pad(fresh, ((0, 0), (0, 0), (0, 16 - steps), (0, 0)))

    def page_map(page):
        return lambda r, table, lens, seq: (table[r * pages + page], 0, 0, 0)

    return pl.pallas_call(
        functools.partial(attend_kernel, steps, pages, page_rows),
        grid_spec=pltpu.PrefetchScalarGridSpec(
            num_scalar_prefetch=3,
            grid=(requests,),
            in_specs=[
                pl.BlockSpec((1, steps, width), lambda r, *_: (r, 0, 0)),
                pl.BlockSpec((1, 2, 16, KV_WIDTH), lambda r, *_: (r, 0, 0, 0)),
            ]
            + [pl.BlockSpec((1, 2, page_rows, KV_WIDTH), page_map(page)) for page in range(pages)],
            out_specs=pl.BlockSpec(
                (1, steps * GROUP, KV_WIDTH + LANES), lambda r, *_: (r, 0, 0)
            ),
        ),
        out_shape=jax.ShapeDtypeStruct((requests, steps * GROUP, KV_WIDTH + LANES), BF16),
        compiler_params=params(),
        name="attend",
    )(page_table.reshape(-1), cache_len, seq_index, by_request, fresh, *([pool] * pages))


def join_kernel(x_ref, out_ref):
    blocks, rows, _ = x_ref.shape
    tokens = rows // GROUP
    levels = []
    for b in range(blocks):
        side = x_ref[b, :, KV_WIDTH : KV_WIDTH + LANES].astype(F32)
        levels.append(side + pltpu.roll(side, LANES - 8, 1) + pltpu.roll(side, LANES - 16, 1))
    largest = functools.reduce(jnp.maximum, levels)
    weights = [jnp.exp(level - largest) for level in levels]
    inverse = 1.0 / functools.reduce(jnp.add, weights)
    low = iota((rows, LANES), 1) < HEAD_SIZE
    acc = [jnp.zeros((rows, LANES), F32) for _ in range(KV_WIDTH // LANES)]
    for b in range(blocks):
        share = weights[b] * inverse
        for j in range(KV_WIDTH // LANES):
            factor = jnp.where(low, share[:, 2 * j : 2 * j + 1], share[:, 2 * j + 1 : 2 * j + 2])
            acc[j] = acc[j] + factor * x_ref[b, :, j * LANES : (j + 1) * LANES].astype(F32)

    def piece(head, half):
        k, g = head // GROUP, head % GROUP
        tile = jnp.concatenate(
            [acc[k // 2][t * GROUP + g : t * GROUP + g + 1] for t in range(tokens)], axis=0
        )
        return tile if k % 2 == half else swap_halves(tile)

    low_tokens = iota((tokens, LANES), 1) < HEAD_SIZE
    for m in range(QUERY_HEADS // 2):
        tile = jnp.where(low_tokens, piece(2 * m, 0), piece(2 * m + 1, 1)).astype(BF16)
        for b in range(blocks):
            out_ref[b, :, m * LANES : (m + 1) * LANES] = tile


def join(parts):
    blocks, rows, _ = parts.shape
    return pl.pallas_call(
        join_kernel,
        out_shape=jax.ShapeDtypeStruct((blocks, rows // GROUP, QUERY_HEADS * HEAD_SIZE), BF16),
        compiler_params=params(),
        name="join",
    )(parts)


def hidden_kernel(where_ref, attn_ref, residual_ref, w_ref, gain_ref, routes_ref, hidden_ref, out_ref):
    steps, requests, features = residual_ref.shape
    tokens = steps * requests
    width = attn_ref.shape[2]
    blocks = [attn_ref[b].astype(F32) for b in range(attn_ref.shape[0])]
    attn = jnp.concatenate(blocks, axis=0).astype(BF16)
    row, column = iota((tokens, tokens), 0), iota((tokens, tokens), 1)
    reorder = jnp.logical_and(row % requests == column // steps, row // requests == column % steps)
    attn = dot_nn(reorder.astype(F32).astype(BF16), attn).astype(BF16)
    residual = residual_ref[...].astype(F32).reshape(tokens, features)
    hidden = residual + dot_nt(attn, w_ref[...])
    hidden_ref[...] = hidden
    scaled = (hidden * gain_ref[...]).astype(BF16)
    squares = jnp.sum(hidden * hidden, axis=1, keepdims=True)
    routes = routes_ref[...].reshape(tokens, routes_ref.shape[2])
    lane = iota((tokens, LANES), 1)
    chosen = jnp.zeros((tokens, LANES), F32)
    for k in range(routes.shape[1]):
        chosen = jnp.where(lane == routes[:, k : k + 1] + SIDE_KEYS, 1.0, chosen)
    earlier = jnp.logical_and(row // requests == column // requests, column < row)
    count = dot_nn(earlier.astype(F32).astype(BF16), chosen.astype(BF16))
    first = (where_ref[0] * steps + iota((tokens, LANES), 0) // requests) * CAP
    side = jnp.where(chosen > 0.0, first.astype(F32) + count, -1.0)
    high = round16(squares)
    side = jnp.where(lane == 0, high, side)
    side = jnp.where(lane == 1, squares - high, side).astype(BF16)
    wide = padded(features)
    for e in range(out_ref.shape[0]):
        if wide != features:
            out_ref[e, :, wide - LANES : wide] = jnp.zeros((tokens, LANES), BF16)
        out_ref[e, :, 0:features] = scaled
        out_ref[e, :, wide : wide + LANES] = side


def hidden_state(exp_index, attn, residual, w_out, gain, routes, exp_count):
    steps, requests, features = residual.shape
    tokens = steps * requests
    vmem = pl.BlockSpec(memory_space=pltpu.VMEM)
    return pl.pallas_call(
        hidden_kernel,
        in_specs=[pl.BlockSpec(memory_space=pltpu.SMEM)] + [vmem] * 5,
        out_shape=(
            jax.ShapeDtypeStruct((tokens, features), F32),
            jax.ShapeDtypeStruct((exp_count, tokens, padded(features) + LANES), BF16),
        ),
        compiler_params=params(),
        name="hidden",
    )(exp_index, attn, residual, w_out.T, gain.reshape(1, features), routes)


def slot_mask(side, expert, slots):
    lane = iota(side.shape, 1)
    key = jnp.sum(jnp.where(lane == expert + SIDE_KEYS, side, 0.0), axis=1, keepdims=True)
    hit = iota((side.shape[0], slots), 1) == key.astype(jnp.int32)
    return key, hit.astype(F32).astype(BF16)


def gate_up_kernel(features, local, where_ref, x_ref, w_ref, router_ref, out_ref):
    slots = out_ref.shape[0]
    expert = where_ref[0] * local + pl.program_id(0)
    wide = padded(features)
    side = x_ref[:, wide : wide + LANES].astype(F32)
    _, mask = slot_mask(side, expert, slots)
    picked = dot_tn(mask, x_ref[...])
    rows = picked[:, 0:features].astype(BF16)
    width = w_ref.shape[3]
    out_ref[:, 0:width] = dot_nn(rows, w_ref[0, 0]).astype(BF16)
    out_ref[:, width : 2 * width] = dot_nn(rows, w_ref[0, 1]).astype(BF16)
    logits = dot_nt(rows, router_ref[...])
    logit = jnp.sum(jnp.where(iota(logits.shape, 1) == expert, logits, 0.0), axis=1, keepdims=True)
    high = round16(logit)
    lane = iota((slots, LANES), 1)
    own = jnp.where(lane == 0, high, jnp.where(lane == 1, logit - high, 0.0))
    squares = pltpu.roll(picked[:, wide : wide + LANES], 2, 1)
    own = jnp.where(jnp.logical_and(lane >= 2, lane < 4), squares, own)
    out_ref[:, 2 * width : 2 * width + LANES] = own.astype(BF16)


def gate_up(exp_index, tokens, weights, w_router, slots):
    local, _, features, width = weights.shape
    total, wide = tokens.shape
    experts = w_router.shape[1]
    return pl.pallas_call(
        functools.partial(gate_up_kernel, features, local),
        grid_spec=pltpu.PrefetchScalarGridSpec(
            num_scalar_prefetch=1,
            grid=(local,),
            in_specs=[
                pl.BlockSpec((total, wide), lambda j, *_: (0, 0)),
                pl.BlockSpec((1, 2, features, width), lambda j, *_: (j, 0, 0, 0)),
                pl.BlockSpec((experts, features), lambda j, *_: (0, 0)),
            ],
            out_specs=pl.BlockSpec((slots, 2 * width + LANES), lambda j, *_: (j, 0)),
        ),
        out_shape=jax.ShapeDtypeStruct((local * slots, 2 * width + LANES), BF16),
        compiler_params=params(),
        name="gate_up",
    )(exp_index, tokens, weights, w_router.T)


def inner_kernel(x_ref, out_ref):
    blocks, rows, wide = x_ref.shape
    width = (wide - LANES) // 2
    total = x_ref[0].astype(F32)
    for b in range(1, blocks):
        total = total + x_ref[b].astype(F32)
    side = total[:, 2 * width : 2 * width + LANES]
    logit = side[:, 0:1] + side[:, 1:2]
    squares = side[:, 2:3] + side[:, 3:4]
    inverse = lax.rsqrt(squares * (1.0 / D) + 1e-6)
    gate = total[:, 0:width] * inverse
    up = total[:, width : 2 * width] * inverse
    inner = (gate / (1.0 + jnp.exp(-gate)) * up).astype(BF16)
    logit = logit * inverse
    high = round16(logit)
    middle = round16(logit - high)
    lane = iota((rows, LANES), 1)
    own = jnp.where(lane == 0, high, jnp.where(lane == 1, middle, 0.0))
    own = jnp.where(lane == 2, logit - high - middle, own).astype(BF16)
    for b in range(blocks):
        out_ref[b, :, 0:width] = inner
        out_ref[b, :, width : width + LANES] = own


def inner(parts):
    blocks, rows, wide = parts.shape
    width = (wide - LANES) // 2
    return pl.pallas_call(
        inner_kernel,
        out_shape=jax.ShapeDtypeStruct((blocks, rows, width + LANES), BF16),
        compiler_params=params(),
        name="inner",
    )(parts)


def down_kernel(features, local, where_ref, side_ref, x_ref, w_ref, out_ref, acc_ref, top_ref, sum_ref):
    slots = x_ref.shape[0]
    j = pl.program_id(0)
    width = w_ref.shape[2]

    @pl.when(j == 0)
    def _():
        acc_ref[...] = jnp.zeros_like(acc_ref)
        top_ref[...] = jnp.full_like(top_ref, NEG_FILL)
        sum_ref[...] = jnp.zeros_like(sum_ref)

    key, mask = slot_mask(side_ref[...].astype(F32), where_ref[0] * local + j, slots)
    made = dot_nt(x_ref[:, 0:width], w_ref[0]).astype(BF16)
    own = dot_nn(mask, made)
    logit = dot_nn(mask, x_ref[:, width : width + LANES])
    logit = logit[:, 0:1] + logit[:, 1:2] + logit[:, 2:3]
    here = key >= 0.0
    top = jnp.maximum(top_ref[...], jnp.where(here, logit, NEG_FILL))
    fade = jnp.exp(top_ref[...] - top)
    weight = jnp.where(here, jnp.exp(logit - top), 0.0)
    top_ref[...] = top
    sum_ref[...] = sum_ref[...] * fade + weight
    acc_ref[...] = acc_ref[...] * fade + own * weight

    @pl.when(j == local - 1)
    def _():
        count, tokens, _ = out_ref.shape
        wide = padded(features)
        lane = iota((tokens, LANES), 1)
        for e in range(count):
            at = slice(e * tokens, (e + 1) * tokens)
            if wide != features:
                out_ref[e, :, wide - LANES : wide] = jnp.zeros((tokens, LANES), F32)
            out_ref[e, :, 0:features] = acc_ref[at]
            out_ref[e, :, wide : wide + LANES] = jnp.where(lane == 0, top_ref[at], sum_ref[at])


def down(exp_index, side, rows, weights, slots, exp_count):
    local, features, width = weights.shape
    total = side.shape[0]
    last = side.shape[1] // LANES - 1
    return pl.pallas_call(
        functools.partial(down_kernel, features, local),
        grid_spec=pltpu.PrefetchScalarGridSpec(
            num_scalar_prefetch=1,
            grid=(local,),
            in_specs=[
                pl.BlockSpec((total, LANES), lambda j, *_: (0, last)),
                pl.BlockSpec((slots, width + LANES), lambda j, *_: (j, 0)),
                pl.BlockSpec((1, features, width), lambda j, *_: (j, 0, 0)),
            ],
            out_specs=pl.BlockSpec(
                (exp_count, total // exp_count, padded(features) + LANES), lambda j, *_: (0, 0, 0)
            ),
            scratch_shapes=[
                pltpu.VMEM((total, features), F32),
                pltpu.VMEM((total, 1), F32),
                pltpu.VMEM((total, 1), F32),
            ],
        ),
        out_shape=jax.ShapeDtypeStruct(
            (exp_count, total // exp_count, padded(features) + LANES), F32
        ),
        compiler_params=params(),
        name="down",
    )(exp_index, side, rows, weights)


def finish_kernel(x_ref, hidden_ref, out_ref):
    owners = x_ref.shape[0]
    features = hidden_ref.shape[1]
    wide = padded(features)
    sides = [x_ref[e, :, wide : wide + LANES] for e in range(owners)]
    tops = [side[:, 0:1] for side in sides]
    top = functools.reduce(jnp.maximum, tops)
    scales = [jnp.exp(one - top) for one in tops]
    total = functools.reduce(jnp.add, [s * side[:, 1:2] for s, side in zip(scales, sides)])
    acc = functools.reduce(
        jnp.add, [s * x_ref[e, :, 0:features] for e, s in enumerate(scales)]
    )
    out = hidden_ref[...] + acc * (1.0 / total)
    out_ref[...] = out.reshape(out_ref.shape).astype(BF16)


def finish(parts, hidden, shape):
    return pl.pallas_call(
        finish_kernel,
        out_shape=jax.ShapeDtypeStruct(shape, BF16),
        compiler_params=params(),
        name="finish",
    )(parts, hidden)


def swap(x, axis):
    return lax.all_to_all(x, axis, split_axis=0, concat_axis=0, tiled=True)


def local(
    queries,
    new_key_value,
    key_value_cache,
    page_table,
    cache_len,
    routes,
    residual,
    w_out,
    norm_gain,
    w_router,
    w_gate_up,
    w_down,
):
    exp_count = lax.axis_size("exp")
    seq_count = lax.axis_size("seq")
    exp_index = lax.axis_index("exp").astype(jnp.int32).reshape(1)
    seq_index = lax.axis_index("seq").astype(jnp.int32).reshape(1)
    steps, requests, width = queries.shape
    tokens = steps * requests
    features = w_out.shape[1]
    slots = exp_count * steps * CAP
    page_rows = key_value_cache.shape[2]
    pool = key_value_cache.reshape(-1, page_rows, 2, KV_WIDTH).transpose(0, 2, 1, 3)
    gate_up_weights = w_gate_up.transpose(0, 2, 1, 3)

    shares = attend(queries, new_key_value, pool, page_table, cache_len, seq_index)
    shares = swap(shares.reshape(seq_count, -1, KV_WIDTH + LANES), "seq")
    attn = swap(join(shares), "seq")
    hidden, outgoing = hidden_state(
        exp_index, attn, residual, w_out, norm_gain, routes, exp_count
    )
    incoming = swap(outgoing, "exp").reshape(exp_count * tokens, -1)
    partial = gate_up(exp_index, incoming, gate_up_weights, w_router, slots)
    partial = swap(partial.reshape(seq_count, -1, partial.shape[1]), "seq")
    rows = swap(inner(partial), "seq")
    made = down(
        exp_index, incoming, rows.reshape(-1, rows.shape[2]), w_down, slots, exp_count
    )
    return finish(swap(made, "exp"), hidden, (steps, requests, features))


def solution(mesh):
    in_specs = (
        P(None, "exp", None),
        P(None, "exp", None, None),
        P("exp", "seq", None, None, None),
        P("exp", "seq"),
        P("exp"),
        P(None, "exp", None),
        P(None, "exp", "seq"),
        P(None, "seq"),
        P("seq"),
        P("seq", None),
        P("exp", "seq", None, None),
        P("exp", "seq", None),
    )
    out_specs = P(None, "exp", "seq")
    return jax.shard_map(local, mesh=mesh, in_specs=in_specs, out_specs=out_specs, check_vma=False)
```

```python
import functools

import jax
import jax.numpy as jnp
from jax import lax
from jax.experimental import pallas as pl
from jax.experimental.pallas import tpu as pltpu
from jax.sharding import PartitionSpec as P

D = 1536
QUERY_HEADS = 24
KEY_VALUE_HEADS = 8
HEAD_SIZE = 64
GROUP = QUERY_HEADS // KEY_VALUE_HEADS
KV_WIDTH = KEY_VALUE_HEADS * HEAD_SIZE
EXPERTS = 40
FF = 512
CAP = 4
LANES = 128
SIDE_KEYS = 2
ROUND_ROWS = 384

NEG_FILL = -1e30
F32 = jnp.float32
BF16 = jnp.bfloat16
VMEM_LIMIT = 48 * 1024 * 1024


def iota(shape, dimension):
    return lax.broadcasted_iota(jnp.int32, shape, dimension)


def dot_nt(a, b):
    return lax.dot_general(a, b, (((1,), (1,)), ((), ())), preferred_element_type=F32)


def dot_tn(a, b):
    return lax.dot_general(a, b, (((0,), (0,)), ((), ())), preferred_element_type=F32)


def dot_nn(a, b):
    return lax.dot_general(a, b, (((1,), (0,)), ((), ())), preferred_element_type=F32)


def round16(x):
    return x.astype(BF16).astype(F32)


def swap_halves(x):
    return pltpu.roll(x, HEAD_SIZE, 1)


def tile_of(x, index):
    return x[:, index * LANES : (index + 1) * LANES]


def padded(width):
    return -(-width // LANES) * LANES


def params():
    return pltpu.CompilerParams(vmem_limit_bytes=VMEM_LIMIT)


def attend_kernel(steps, pages, page_rows, table_ref, len_ref, seq_ref, q_ref, fresh_ref, *refs):
    page_refs, out_ref = refs[:pages], refs[pages]
    request = pl.program_id(0)
    q = q_ref[0].astype(F32)
    low = iota((steps, LANES), 1) < HEAD_SIZE
    by_group = []
    for g in range(GROUP):
        tiles = []
        for j in range(KV_WIDTH // LANES):
            first = tile_of(q, (6 * j + g) // 2)
            second = tile_of(q, (6 * j + 3 + g) // 2)
            if g % 2 == 0:
                tiles.append(jnp.where(low, first, second))
            else:
                tiles.append(swap_halves(jnp.where(low, second, first)))
        by_group.append(jnp.concatenate(tiles, axis=1))
    rows = steps * GROUP * KEY_VALUE_HEADS
    stacked = jnp.concatenate(
        [
            jnp.broadcast_to(by_group[g][t : t + 1], (KEY_VALUE_HEADS, KV_WIDTH))
            for t in range(steps)
            for g in range(GROUP)
        ],
        axis=0,
    )
    own = iota((rows, KV_WIDTH), 1) // HEAD_SIZE == iota((rows, KV_WIDTH), 0) % KEY_VALUE_HEADS
    spread = jnp.where(own, stacked, 0.0).astype(BF16)
    keys = jnp.concatenate([ref[0, 0] for ref in page_refs], axis=0)
    values = jnp.concatenate([ref[0, 1] for ref in page_refs], axis=0)
    span = pages * page_rows
    scores = dot_nt(spread, keys) * 0.125
    live = seq_ref[0] * span + iota((rows, span), 1) < len_ref[request]
    scores = jnp.where(live, scores, NEG_FILL)
    fresh_keys, fresh_values = fresh_ref[0, 0], fresh_ref[0, 1]
    fresh_rows = fresh_keys.shape[0]
    fresh_scores = dot_nt(spread, fresh_keys) * 0.125
    row_step = iota((rows, fresh_rows), 0) // (GROUP * KEY_VALUE_HEADS)
    kept = jnp.logical_and(iota((rows, fresh_rows), 1) <= row_step, seq_ref[0] == 0)
    fresh_scores = jnp.where(kept, fresh_scores, NEG_FILL)
    largest = jnp.maximum(
        jnp.max(scores, axis=1, keepdims=True), jnp.max(fresh_scores, axis=1, keepdims=True)
    )
    weights = jnp.where(live, jnp.exp(scores - largest), 0.0)
    fresh_weights = jnp.where(kept, jnp.exp(fresh_scores - largest), 0.0)
    total = jnp.sum(weights, axis=1, keepdims=True) + jnp.sum(fresh_weights, axis=1, keepdims=True)
    acc = dot_nn(weights.astype(BF16), values) + dot_nn(fresh_weights.astype(BF16), fresh_values)
    some = total > 0.0
    safe = jnp.where(some, total, 1.0)
    acc = jnp.where(own, acc * (1.0 / safe), 0.0)
    acc = jnp.sum(acc.reshape(steps * GROUP, KEY_VALUE_HEADS, KV_WIDTH), axis=1)
    level = jnp.where(some, largest + jnp.log(safe), NEG_FILL)
    high = round16(level)
    middle = round16(level - high)
    rest = level - high - middle
    lane = iota((rows, LANES), 1)
    head = iota((rows, LANES), 0) % KEY_VALUE_HEADS
    side = jnp.where(lane == head, high, 0.0)
    side = jnp.where(lane == head + 8, middle, side)
    side = jnp.where(lane == head + 16, rest, side)
    side = jnp.sum(side.reshape(steps * GROUP, KEY_VALUE_HEADS, LANES), axis=1)
    out_ref[0, :, 0:KV_WIDTH] = acc.astype(BF16)
    out_ref[0, :, KV_WIDTH : KV_WIDTH + LANES] = side.astype(BF16)


def attend(queries, new_key_value, pool, page_table, cache_len, seq_index):
    steps, requests, width = queries.shape
    pages = page_table.shape[1]
    page_rows = pool.shape[2]
    by_request = queries.transpose(1, 0, 2)
    fresh = new_key_value.transpose(1, 2, 0, 3)
    fresh = jnp.pad(fresh, ((0, 0), (0, 0), (0, 16 - steps), (0, 0)))

    def page_map(page):
        return lambda r, table, lens, seq: (table[r * pages + page], 0, 0, 0)

    return pl.pallas_call(
        functools.partial(attend_kernel, steps, pages, page_rows),
        grid_spec=pltpu.PrefetchScalarGridSpec(
            num_scalar_prefetch=3,
            grid=(requests,),
            in_specs=[
                pl.BlockSpec((1, steps, width), lambda r, *_: (r, 0, 0)),
                pl.BlockSpec((1, 2, 16, KV_WIDTH), lambda r, *_: (r, 0, 0, 0)),
            ]
            + [pl.BlockSpec((1, 2, page_rows, KV_WIDTH), page_map(page)) for page in range(pages)],
            out_specs=pl.BlockSpec(
                (1, steps * GROUP, KV_WIDTH + LANES), lambda r, *_: (r, 0, 0)
            ),
        ),
        out_shape=jax.ShapeDtypeStruct((requests, steps * GROUP, KV_WIDTH + LANES), BF16),
        compiler_params=params(),
        name="attend",
    )(page_table.reshape(-1), cache_len, seq_index, by_request, fresh, *([pool] * pages))


def join_kernel(x_ref, out_ref):
    blocks, rows, _ = x_ref.shape
    tokens = rows // GROUP
    levels = []
    for b in range(blocks):
        side = x_ref[b, :, KV_WIDTH : KV_WIDTH + LANES].astype(F32)
        levels.append(side + pltpu.roll(side, LANES - 8, 1) + pltpu.roll(side, LANES - 16, 1))
    largest = functools.reduce(jnp.maximum, levels)
    weights = [jnp.exp(level - largest) for level in levels]
    inverse = 1.0 / functools.reduce(jnp.add, weights)
    low = iota((rows, LANES), 1) < HEAD_SIZE
    acc = [jnp.zeros((rows, LANES), F32) for _ in range(KV_WIDTH // LANES)]
    for b in range(blocks):
        share = weights[b] * inverse
        for j in range(KV_WIDTH // LANES):
            factor = jnp.where(low, share[:, 2 * j : 2 * j + 1], share[:, 2 * j + 1 : 2 * j + 2])
            acc[j] = acc[j] + factor * x_ref[b, :, j * LANES : (j + 1) * LANES].astype(F32)

    def piece(head, half):
        k, g = head // GROUP, head % GROUP
        tile = jnp.concatenate(
            [acc[k // 2][t * GROUP + g : t * GROUP + g + 1] for t in range(tokens)], axis=0
        )
        return tile if k % 2 == half else swap_halves(tile)

    low_tokens = iota((tokens, LANES), 1) < HEAD_SIZE
    for m in range(QUERY_HEADS // 2):
        tile = jnp.where(low_tokens, piece(2 * m, 0), piece(2 * m + 1, 1)).astype(BF16)
        for b in range(blocks):
            out_ref[b, :, m * LANES : (m + 1) * LANES] = tile


def join(parts):
    blocks, rows, _ = parts.shape
    return pl.pallas_call(
        join_kernel,
        out_shape=jax.ShapeDtypeStruct((blocks, rows // GROUP, QUERY_HEADS * HEAD_SIZE), BF16),
        compiler_params=params(),
        name="join",
    )(parts)


def side_place(features, count):
    tile, offset = features // LANES * LANES, features % LANES
    return (tile, offset) if offset and offset + count <= LANES else (padded(features), 0)


def hidden_kernel(attn_ref, residual_ref, w_ref, gain_ref, routes_ref, hidden_ref, out_ref, wide_ref):
    steps, requests, features = residual_ref.shape
    tokens = steps * requests
    blocks = [attn_ref[b].astype(F32) for b in range(attn_ref.shape[0])]
    attn = jnp.concatenate(blocks, axis=0).astype(BF16)
    row, column = iota((tokens, tokens), 0), iota((tokens, tokens), 1)
    reorder = jnp.logical_and(row % requests == column // steps, row // requests == column % steps)
    attn = dot_nn(reorder.astype(F32).astype(BF16), attn).astype(BF16)
    residual = residual_ref[...].astype(F32).reshape(tokens, features)
    hidden = residual + dot_nt(attn, w_ref[...])
    hidden_ref[...] = hidden
    squares = jnp.sum(hidden * hidden, axis=1, keepdims=True)
    tile, offset = side_place(features, SIDE_KEYS + EXPERTS)
    wide_ref[...] = jnp.zeros_like(wide_ref)
    wide_ref[:, 0:features] = hidden * gain_ref[...]
    routes = routes_ref[...].reshape(tokens, routes_ref.shape[2])
    lane = iota((tokens, LANES), 1) - offset
    side = wide_ref[:, tile : tile + LANES]
    for k in range(routes.shape[1]):
        side = jnp.where(lane == routes[:, k : k + 1] + SIDE_KEYS, 1.0, side)
    high = round16(squares)
    side = jnp.where(lane == 0, high, side)
    wide_ref[:, tile : tile + LANES] = jnp.where(lane == 1, squares - high, side)
    made = wide_ref[...].astype(BF16)
    for e in range(out_ref.shape[0]):
        out_ref[e] = made


def hidden_state(attn, residual, w_out, gain, routes, exp_count):
    steps, requests, features = residual.shape
    tokens = steps * requests
    wide = side_place(features, SIDE_KEYS + EXPERTS)[0] + LANES
    return pl.pallas_call(
        hidden_kernel,
        out_shape=(
            jax.ShapeDtypeStruct((tokens, features), F32),
            jax.ShapeDtypeStruct((exp_count, tokens, wide), BF16),
        ),
        scratch_shapes=[pltpu.VMEM((tokens, wide), F32)],
        compiler_params=params(),
        name="hidden",
    )(attn, residual, w_out.T, gain.reshape(1, features), routes)


def window_start(first, rows, window):
    return pl.multiple_of(jnp.clip(first // 16 * 16, 0, rows - window), 16)


def gate_up_kernel(
    features, local, turn, where_ref, x_ref, w_ref, router_ref,
    out_ref, pick_ref, range_ref, first_ref, most_ref, row_ref, acc_ref,
):
    total = x_ref.shape[0]
    rows = pick_ref.shape[1]
    blocks = out_ref.shape[0]
    share = rows // blocks
    width = w_ref.shape[3]
    window = total // 2 + 16
    tile, offset = side_place(features, SIDE_KEYS + EXPERTS)
    me = where_ref[0]
    own_side = x_ref[:, tile : tile + LANES].astype(F32)
    lane = iota((total, LANES), 1)
    flags = pltpu.roll(own_side, LANES - offset - SIDE_KEYS, 1)
    flags = jnp.where(lane < EXPERTS, flags, 0.0)
    owners = EXPERTS // local
    counts = jnp.sum(flags, axis=0, keepdims=True)
    most = jnp.int32(0)
    for o in range(owners):
        held = jnp.logical_and(lane[0:1] >= o * local, lane[0:1] < (o + 1) * local)
        most = jnp.maximum(most, jnp.sum(jnp.where(held, counts, 0.0)).astype(jnp.int32))
    most_ref[0] = most
    mine = pltpu.roll(flags, lax.rem(LANES - me * local, LANES), 1)
    mine = jnp.where(lane < local, mine, 0.0)
    mine16 = mine.astype(BF16)
    row, column = iota((total, total), 0), iota((total, total), 1)
    earlier = (column < row).astype(F32).astype(BF16)
    ranks = dot_nn(earlier, mine16)
    counts = jnp.sum(mine, axis=0, keepdims=True)
    before = (iota((LANES, LANES), 0) < iota((LANES, LANES), 1)).astype(F32).astype(BF16)
    first = dot_nn(jnp.broadcast_to(counts, (8, LANES)).astype(BF16), before)[0:1] - turn * rows
    place = jnp.where(mine > 0.0, first + ranks, -1.0).astype(jnp.int32)
    at = iota((total, rows), 1)
    pick = jnp.zeros((total, rows), F32)
    for j in range(local):
        pick = jnp.where(at == place[:, j : j + 1], 1.0, pick)
    pick = pick.astype(BF16)
    pick_ref[...] = pick
    ranges = jnp.where(iota((16, LANES), 0) < 8, first, first + counts)
    ranges = jnp.concatenate([ranges[0:8], ranges[8:16]] + [jnp.zeros((LANES - 16, LANES), F32)], axis=0)
    ranges = ranges.T
    range_ref[...] = ranges[0:16]
    row_ref[...] = dot_tn(pick, x_ref[...]).astype(BF16)
    acc_ref[...] = jnp.zeros_like(acc_ref)
    for j in range(local):
        start_row = jnp.sum(first[:, j : j + 1]).astype(jnp.int32)
        first_ref[j] = start_row
        start = window_start(start_row, rows, window)
        part = row_ref[pl.ds(start, window), 0:features]
        fresh = start + iota((window, width), 0) >= start_row
        for half in range(2):
            into = (pl.ds(start, window), slice(half * width, (half + 1) * width))
            made = dot_nn(part, w_ref[j, half])
            acc_ref[into] = jnp.where(fresh, made, acc_ref[into])
    for b in range(blocks):
        for piece in range(2 * width // LANES):
            out_ref[b, piece * share : (piece + 1) * share, :] = acc_ref[
                b * share : (b + 1) * share, piece * LANES : (piece + 1) * LANES
            ].astype(BF16)
    logits = dot_nt(router_ref[...], x_ref[:, 0:features])
    high = round16(logits)
    both = jnp.concatenate([high, logits - high], axis=0).astype(BF16)
    both = dot_nn(both, pick)
    turned = jnp.zeros((EXPERTS, rows), jnp.bool_)
    expert = iota((EXPERTS, rows), 0) - me * local
    where_row = iota((EXPERTS, rows), 1).astype(F32)
    for j in range(local):
        inside = jnp.logical_and(
            where_row >= first[:, j : j + 1], where_row < (first + counts)[:, j : j + 1]
        )
        turned = jnp.logical_or(turned, jnp.logical_and(inside, expert == j))
    squares = dot_tn(own_side.astype(BF16), pick)
    side = jnp.concatenate(
        [
            jnp.sum(jnp.where(turned, both[0:EXPERTS], 0.0), axis=0, keepdims=True),
            jnp.sum(jnp.where(turned, both[EXPERTS : 2 * EXPERTS], 0.0), axis=0, keepdims=True),
            squares[offset : offset + 2],
            jnp.zeros((12, rows), F32),
        ],
        axis=0,
    )
    for b in range(blocks):
        end = 2 * width // LANES * share
        out_ref[b, end : end + 16, :] = jnp.zeros((16, LANES), BF16)
        out_ref[b, end : end + 16, 0:share] = side[:, b * share : (b + 1) * share].astype(BF16)


def gate_up(exp_index, tokens, weights, w_router, rows, blocks, turn):
    local, _, features, width = weights.shape
    total, wide = tokens.shape
    smem, vmem = pl.BlockSpec(memory_space=pltpu.SMEM), pl.BlockSpec(memory_space=pltpu.VMEM)
    return pl.pallas_call(
        functools.partial(gate_up_kernel, features, local, turn),
        in_specs=[smem, vmem, vmem, vmem],
        out_specs=(vmem, vmem, vmem, smem, smem),
        out_shape=(
            jax.ShapeDtypeStruct((blocks, 2 * width // LANES * (rows // blocks) + 16, LANES), BF16),
            jax.ShapeDtypeStruct((total, rows), BF16),
            jax.ShapeDtypeStruct((16, LANES), F32),
            jax.ShapeDtypeStruct((16,), jnp.int32),
            jax.ShapeDtypeStruct((1,), jnp.int32),
        ),
        scratch_shapes=[pltpu.VMEM((rows, wide), BF16), pltpu.VMEM((rows, 2 * width), F32)],
        compiler_params=params(),
        name="gate_up",
    )(exp_index, tokens, weights, w_router.T)


def inner_kernel(x_ref, out_ref):
    blocks, height, _ = x_ref.shape
    pieces = 2 * FF // LANES
    share = (height - 16) // pieces
    half = pieces // 2

    def total(start, size):
        added = x_ref[0, start : start + size].astype(F32)
        for b in range(1, blocks):
            added = added + x_ref[b, start : start + size].astype(F32)
        return added

    side = total(pieces * share, 16)
    logit = side[0:1] + side[1:2]
    squares = side[2:3] + side[3:4]
    inverse = lax.rsqrt(squares * (1.0 / D) + 1e-6)
    down_column = jnp.broadcast_to(inverse, (LANES, LANES)).T[0:share, 0:1]
    for piece in range(half):
        gate = total(piece * share, share) * down_column
        up = total((half + piece) * share, share) * down_column
        made = (gate / (1.0 + jnp.exp(-gate)) * up).astype(BF16)
        for b in range(blocks):
            out_ref[b, piece * share : (piece + 1) * share, :] = made
    logit = logit * inverse
    high = round16(logit)
    middle = round16(logit - high)
    own = jnp.concatenate(
        [high, middle, logit - high - middle, jnp.zeros((13, LANES), F32)], axis=0
    ).astype(BF16)
    for b in range(blocks):
        out_ref[b, half * share : half * share + 16, :] = own


def inner(parts):
    blocks, height, _ = parts.shape
    return pl.pallas_call(
        inner_kernel,
        out_shape=jax.ShapeDtypeStruct((blocks, (height - 16) // 2 + 16, LANES), BF16),
        compiler_params=params(),
        name="inner",
    )(parts)


def down_kernel(features, local, first_ref, range_ref, pick_ref, x_ref, w_ref, out_ref, row_ref, made_ref):
    blocks, height, _ = x_ref.shape
    total, rows = pick_ref.shape
    width = w_ref.shape[2]
    pieces = width // LANES
    share = (height - 16) // pieces
    window = total // 2 + 16
    for b in range(blocks):
        for piece in range(pieces):
            row_ref[b * share : (b + 1) * share, piece * LANES : (piece + 1) * LANES] = x_ref[
                b, piece * share : (piece + 1) * share, :
            ]
    made_ref[...] = jnp.zeros_like(made_ref)
    for j in range(local):
        start_row = first_ref[j]
        start = window_start(start_row, rows, window)
        made = dot_nt(row_ref[pl.ds(start, window), :], w_ref[j])
        fresh = start + iota((window, features), 0) >= start_row
        into = (pl.ds(start, window), slice(0, features))
        made_ref[into] = jnp.where(fresh, made, made_ref[into])
    logit = jnp.concatenate(
        [x_ref[b, pieces * share :, 0:share].astype(F32) for b in range(blocks)], axis=1
    )
    pick = pick_ref[...]
    where_row = iota((16, rows), 1).astype(F32)
    inside = jnp.logical_and(where_row >= range_ref[:, 0:1], where_row < range_ref[:, 8:9])
    inside = jnp.logical_and(inside, iota((16, rows), 0) < local)
    spread = [jnp.where(inside, logit[k : k + 1], 0.0) for k in range(3)]
    spread.append(inside.astype(F32))
    found = dot_nt(jnp.concatenate(spread, axis=0).astype(BF16), pick)
    valid = found[48:64] > 0.5
    logits = jnp.where(valid, found[0:16] + found[16:32] + found[32:48], NEG_FILL)
    top = jnp.max(logits, axis=0, keepdims=True)
    weights = jnp.where(valid, jnp.exp(logits - top), 0.0)
    summed = jnp.sum(weights, axis=0, keepdims=True)
    high = round16(weights)
    both = dot_nn(jnp.concatenate([high, weights - high], axis=0).astype(BF16), pick)
    weight = jnp.sum(jnp.where(inside, both[0:16] + both[16:32], 0.0), axis=0, keepdims=True)
    column = jnp.broadcast_to(weight, (LANES, rows)).T[:, 0:1]
    acc = dot_nn(pick, (made_ref[...] * column).astype(BF16))
    tile, offset = side_place(features, 2)
    pair = jnp.where(iota((LANES, total), 0) == 0, top, summed).T
    count, tokens, _ = out_ref.shape
    for e in range(count):
        at = slice(e * tokens, (e + 1) * tokens)
        out_ref[e] = acc[at]
        lane = iota((tokens, LANES), 1) - offset
        side = jnp.where(lane == 0, pair[at, 0:1], acc[at, tile : tile + LANES])
        out_ref[e, :, tile : tile + LANES] = jnp.where(lane == 1, pair[at, 1:2], side)


def down(first, ranges, pick, parts, weights, exp_count):
    local, features, width = weights.shape
    total, rows = pick.shape
    wide = side_place(features, 2)[0] + LANES
    smem, vmem = pl.BlockSpec(memory_space=pltpu.SMEM), pl.BlockSpec(memory_space=pltpu.VMEM)
    return pl.pallas_call(
        functools.partial(down_kernel, features, local),
        in_specs=[smem] + [vmem] * 4,
        out_shape=jax.ShapeDtypeStruct((exp_count, total // exp_count, wide), F32),
        scratch_shapes=[pltpu.VMEM((rows, width), BF16), pltpu.VMEM((rows, wide), F32)],
        compiler_params=params(),
        name="down",
    )(first, ranges, pick, parts, weights)


def finish_kernel(x_ref, hidden_ref, out_ref):
    owners = x_ref.shape[0]
    features = hidden_ref.shape[1]
    tile, offset = side_place(features, 2)
    sides = [x_ref[e, :, tile : tile + LANES] for e in range(owners)]
    tops = [side[:, offset : offset + 1] for side in sides]
    top = functools.reduce(jnp.maximum, tops)
    scales = [jnp.exp(one - top) for one in tops]
    total = functools.reduce(
        jnp.add, [s * side[:, offset + 1 : offset + 2] for s, side in zip(scales, sides)]
    )
    acc = functools.reduce(
        jnp.add, [s * x_ref[e, :, 0:features] for e, s in enumerate(scales)]
    )
    out = hidden_ref[...] + acc * (1.0 / total)
    out_ref[...] = out.reshape(out_ref.shape).astype(BF16)


def finish(parts, hidden, shape):
    return pl.pallas_call(
        finish_kernel,
        out_shape=jax.ShapeDtypeStruct(shape, BF16),
        compiler_params=params(),
        name="finish",
    )(parts, hidden)


def join_rounds(features, one, other):
    tile, offset = side_place(features, 2)
    at = tile + offset
    top = jnp.maximum(one[..., at : at + 1], other[..., at : at + 1])
    scales = [jnp.exp(part[..., at : at + 1] - top) for part in (one, other)]
    joined = one * scales[0] + other * scales[1]
    return jnp.where(jnp.arange(one.shape[-1]) == at, top, joined)


def swap(x, axis):
    return lax.all_to_all(x, axis, split_axis=0, concat_axis=0, tiled=True)


def local(
    queries,
    new_key_value,
    key_value_cache,
    page_table,
    cache_len,
    routes,
    residual,
    w_out,
    norm_gain,
    w_router,
    w_gate_up,
    w_down,
):
    exp_count = lax.axis_size("exp")
    seq_count = lax.axis_size("seq")
    exp_index = lax.axis_index("exp").astype(jnp.int32).reshape(1)
    seq_index = lax.axis_index("seq").astype(jnp.int32).reshape(1)
    steps, requests, width = queries.shape
    tokens = steps * requests
    features = w_out.shape[1]
    page_rows = key_value_cache.shape[2]
    pool = key_value_cache.reshape(-1, page_rows, 2, KV_WIDTH).transpose(0, 2, 1, 3)

    shares = attend(queries, new_key_value, pool, page_table, cache_len, seq_index)
    shares = swap(shares.reshape(seq_count, -1, KV_WIDTH + LANES), "seq")
    attn = join(shares)
    w_gate_up, attn = lax.optimization_barrier((w_gate_up, attn))
    attn = swap(attn, "seq")
    gate_up_weights = w_gate_up.transpose(0, 2, 1, 3)
    gate_up_weights, attn = lax.optimization_barrier((gate_up_weights, attn))
    hidden, outgoing = hidden_state(attn, residual, w_out, norm_gain, routes, exp_count)
    incoming = swap(outgoing, "exp").reshape(exp_count * tokens, -1)
    rows = -(-ROUND_ROWS // (16 * seq_count)) * 16 * seq_count

    def one_round(turn):
        parts, pick, ranges, first, most = gate_up(
            exp_index, incoming, gate_up_weights, w_router, rows, seq_count, turn
        )
        made = swap(inner(swap(parts, "seq")), "seq")
        return down(first, ranges, pick, made, w_down, exp_count), most

    made, most = one_round(0)
    pairs = w_gate_up.shape[0] * exp_count * steps * CAP
    for turn in range(1, -(-pairs // rows)):
        made = lax.cond(
            most[0] > turn * rows,
            lambda made: join_rounds(features, made, one_round(turn)[0]),
            lambda made: made,
            made,
        )
    return finish(swap(made, "exp"), hidden, (steps, requests, features))


def solution(mesh):
    in_specs = (
        P(None, "exp", None),
        P(None, "exp", None, None),
        P("exp", "seq", None, None, None),
        P("exp", "seq"),
        P("exp"),
        P(None, "exp", None),
        P(None, "exp", "seq"),
        P(None, "seq"),
        P("seq"),
        P("seq", None),
        P("exp", "seq", None, None),
        P("exp", "seq", None),
    )
    out_specs = P(None, "exp", "seq")
    return jax.shard_map(local, mesh=mesh, in_specs=in_specs, out_specs=out_specs, check_vma=False)
```

```python
import functools

import jax
import jax.numpy as jnp
from jax import lax
from jax.experimental import pallas as pl
from jax.experimental.pallas import tpu as pltpu
from jax.sharding import PartitionSpec as P

D = 1536
QUERY_HEADS = 24
KEY_VALUE_HEADS = 8
HEAD_SIZE = 64
GROUP = QUERY_HEADS // KEY_VALUE_HEADS
KV_WIDTH = KEY_VALUE_HEADS * HEAD_SIZE
EXPERTS = 40
FF = 512
CAP = 4
LANES = 128
SIDE_KEYS = 2
ROUND_ROWS = 384

NEG_FILL = -1e30
F32 = jnp.float32
BF16 = jnp.bfloat16
VMEM_LIMIT = 48 * 1024 * 1024


def iota(shape, dimension):
    return lax.broadcasted_iota(jnp.int32, shape, dimension)


def dot_nt(a, b):
    return lax.dot_general(a, b, (((1,), (1,)), ((), ())), preferred_element_type=F32)


def dot_tn(a, b):
    return lax.dot_general(a, b, (((0,), (0,)), ((), ())), preferred_element_type=F32)


def dot_nn(a, b):
    return lax.dot_general(a, b, (((1,), (0,)), ((), ())), preferred_element_type=F32)


def round16(x):
    return x.astype(BF16).astype(F32)


def swap_halves(x):
    return pltpu.roll(x, HEAD_SIZE, 1)


def tile_of(x, index):
    return x[:, index * LANES : (index + 1) * LANES]


def padded(width):
    return -(-width // LANES) * LANES


def params():
    return pltpu.CompilerParams(vmem_limit_bytes=VMEM_LIMIT)


def attend_kernel(
    classes, table_ref, len_ref, seq_ref, q_ref, fresh_ref, cache_ref, out_ref,
    page_ref, split_ref, query_ref, new_ref, sems,
):
    steps, requests, _ = q_ref.shape
    page_rows = cache_ref.shape[1]
    pages = table_ref.shape[1]
    span = pages * page_rows
    first = seq_ref[0] * span

    def copy(r, page):
        at = r * pages + page
        return pltpu.make_async_copy(cache_ref.at[table_ref[r, page]], page_ref.at[at], sems.at[at])

    def needed(r, low):
        return len_ref[r] - first > low * page_rows

    bounds = list(zip((0,) + classes[:-1], classes))

    def start(r, carry):
        for low, high in bounds:

            @pl.when(needed(r, low))
            def _():
                for page in range(low, high):
                    copy(r, page).start()

        return carry

    lax.fori_loop(0, requests, start, 0)

    low = iota((requests, LANES), 1) < HEAD_SIZE
    for t in range(steps):
        q = q_ref[t].astype(F32)
        for g in range(GROUP):
            for j in range(KV_WIDTH // LANES):
                one = tile_of(q, (6 * j + g) // 2)
                two = tile_of(q, (6 * j + 3 + g) // 2)
                if g % 2 == 0:
                    tile = jnp.where(low, one, two)
                else:
                    tile = swap_halves(jnp.where(low, two, one))
                query_ref[t * GROUP + g, :, j * LANES : (j + 1) * LANES] = tile
        new_ref[t] = fresh_ref[t].reshape(2 * requests, KV_WIDTH).astype(F32)

    rows = steps * GROUP * KEY_VALUE_HEADS
    own = iota((rows, KV_WIDTH), 1) // HEAD_SIZE == iota((rows, KV_WIDTH), 0) % KEY_VALUE_HEADS
    lane = iota((rows, LANES), 1)
    head = iota((rows, LANES), 0) % KEY_VALUE_HEADS

    def fresh_rows(r, which):
        found = [new_ref[u, pl.ds(2 * r + which, 1), :] for u in range(steps)]
        return jnp.concatenate(found + [jnp.zeros((16 - steps, KV_WIDTH), F32)], axis=0).astype(BF16)

    def attend_pages(r, count):
        spread = jnp.concatenate(
            [
                jnp.broadcast_to(query_ref[i, pl.ds(r, 1), :], (KEY_VALUE_HEADS, KV_WIDTH))
                for i in range(steps * GROUP)
            ],
            axis=0,
        )
        spread = jnp.where(own, spread, 0.0).astype(BF16)
        halves = ([], [])
        for page in range(count):
            copy(r, page).wait()
            block = page_ref[r * pages + page].reshape(2 * page_rows, KV_WIDTH).astype(F32)
            for j in range(KV_WIDTH // LANES):
                split_ref[page, j] = tile_of(block, j)
            for which in range(2):
                tiles = [
                    split_ref[page, j, pl.ds(which, page_rows, 2), :] for j in range(KV_WIDTH // LANES)
                ]
                halves[which].append(jnp.concatenate(tiles, axis=1).astype(BF16))
        keys, values = jnp.concatenate(halves[0], axis=0), jnp.concatenate(halves[1], axis=0)
        scores = dot_nt(spread, keys) * 0.125
        live = first + iota((rows, count * page_rows), 1) < len_ref[r]
        scores = jnp.where(live, scores, NEG_FILL)
        fresh_scores = dot_nt(spread, fresh_rows(r, 0)) * 0.125
        row_step = iota((rows, 16), 0) // (GROUP * KEY_VALUE_HEADS)
        kept = jnp.logical_and(iota((rows, 16), 1) <= row_step, seq_ref[0] == 0)
        fresh_scores = jnp.where(kept, fresh_scores, NEG_FILL)
        largest = jnp.maximum(
            jnp.max(scores, axis=1, keepdims=True), jnp.max(fresh_scores, axis=1, keepdims=True)
        )
        weights = jnp.where(live, jnp.exp(scores - largest), 0.0)
        fresh_weights = jnp.where(kept, jnp.exp(fresh_scores - largest), 0.0)
        total = jnp.sum(weights, axis=1, keepdims=True)
        total = total + jnp.sum(fresh_weights, axis=1, keepdims=True)
        acc = dot_nn(weights.astype(BF16), values)
        acc = acc + dot_nn(fresh_weights.astype(BF16), fresh_rows(r, 1))
        acc = jnp.where(own, acc * (1.0 / total), 0.0)
        acc = jnp.sum(acc.reshape(steps * GROUP, KEY_VALUE_HEADS, KV_WIDTH), axis=1)
        level = largest + jnp.log(total)
        high = round16(level)
        middle = round16(level - high)
        side = jnp.where(lane == head, high, 0.0)
        side = jnp.where(lane == head + 8, middle, side)
        side = jnp.where(lane == head + 16, level - high - middle, side)
        side = jnp.sum(side.reshape(steps * GROUP, KEY_VALUE_HEADS, LANES), axis=1)
        out_ref[r, :, 0:KV_WIDTH] = acc.astype(BF16)
        out_ref[r, :, KV_WIDTH : KV_WIDTH + LANES] = side.astype(BF16)

    def one_request(r, carry):
        for low, high in bounds:
            enough = needed(r, low)
            if high < pages:
                enough = jnp.logical_and(enough, jnp.logical_not(needed(r, high)))

            @pl.when(enough)
            def _():
                attend_pages(r, high)

        @pl.when(jnp.logical_not(needed(r, 0)))
        def _():
            out_ref[r, :, 0:KV_WIDTH] = jnp.zeros((steps * GROUP, KV_WIDTH), BF16)
            empty = jnp.where(iota((steps * GROUP, LANES), 1) < KEY_VALUE_HEADS, NEG_FILL, 0.0)
            out_ref[r, :, KV_WIDTH : KV_WIDTH + LANES] = empty.astype(BF16)

        return carry

    lax.fori_loop(0, requests, one_request, 0)


def attend(queries, new_key_value, cache, page_table, cache_len, seq_index):
    steps, requests, _ = queries.shape
    pages = page_table.shape[1]
    page_rows = cache.shape[1]
    classes = tuple(c for c in (2, 4) if c < pages) + (pages,)
    smem, vmem = pl.BlockSpec(memory_space=pltpu.SMEM), pl.BlockSpec(memory_space=pltpu.VMEM)
    return pl.pallas_call(
        functools.partial(attend_kernel, classes),
        in_specs=[smem, smem, smem, vmem, vmem, pl.BlockSpec(memory_space=pl.ANY)],
        out_shape=jax.ShapeDtypeStruct((requests, steps * GROUP, KV_WIDTH + LANES), BF16),
        scratch_shapes=[
            pltpu.VMEM((requests * pages, page_rows, 2, KV_WIDTH), BF16),
            pltpu.VMEM((pages, KV_WIDTH // LANES, 2 * page_rows, LANES), F32),
            pltpu.VMEM((steps * GROUP, requests, KV_WIDTH), F32),
            pltpu.VMEM((steps, 2 * requests, KV_WIDTH), F32),
            pltpu.SemaphoreType.DMA((requests * pages,)),
        ],
        compiler_params=params(),
        name="attend",
    )(page_table, cache_len, seq_index, queries, new_key_value, cache)


def join_kernel(x_ref, out_ref):
    blocks, rows, _ = x_ref.shape
    tokens = rows // GROUP
    levels = []
    for b in range(blocks):
        side = x_ref[b, :, KV_WIDTH : KV_WIDTH + LANES].astype(F32)
        levels.append(side + pltpu.roll(side, LANES - 8, 1) + pltpu.roll(side, LANES - 16, 1))
    largest = functools.reduce(jnp.maximum, levels)
    weights = [jnp.exp(level - largest) for level in levels]
    inverse = 1.0 / functools.reduce(jnp.add, weights)
    low = iota((rows, LANES), 1) < HEAD_SIZE
    acc = [jnp.zeros((rows, LANES), F32) for _ in range(KV_WIDTH // LANES)]
    for b in range(blocks):
        share = weights[b] * inverse
        for j in range(KV_WIDTH // LANES):
            factor = jnp.where(low, share[:, 2 * j : 2 * j + 1], share[:, 2 * j + 1 : 2 * j + 2])
            acc[j] = acc[j] + factor * x_ref[b, :, j * LANES : (j + 1) * LANES].astype(F32)

    def piece(head, half):
        k, g = head // GROUP, head % GROUP
        tile = jnp.concatenate(
            [acc[k // 2][t * GROUP + g : t * GROUP + g + 1] for t in range(tokens)], axis=0
        )
        return tile if k % 2 == half else swap_halves(tile)

    low_tokens = iota((tokens, LANES), 1) < HEAD_SIZE
    for m in range(QUERY_HEADS // 2):
        tile = jnp.where(low_tokens, piece(2 * m, 0), piece(2 * m + 1, 1)).astype(BF16)
        for b in range(blocks):
            out_ref[b, :, m * LANES : (m + 1) * LANES] = tile


def join(parts):
    blocks, rows, _ = parts.shape
    return pl.pallas_call(
        join_kernel,
        out_shape=jax.ShapeDtypeStruct((blocks, rows // GROUP, QUERY_HEADS * HEAD_SIZE), BF16),
        compiler_params=params(),
        name="join",
    )(parts)


def side_place(features, count):
    tile, offset = features // LANES * LANES, features % LANES
    return (tile, offset) if offset and offset + count <= LANES else (padded(features), 0)


def hidden_kernel(attn_ref, residual_ref, w_ref, gain_ref, routes_ref, hidden_ref, out_ref, wide_ref):
    steps, requests, features = residual_ref.shape
    tokens = steps * requests
    blocks = [attn_ref[b].astype(F32) for b in range(attn_ref.shape[0])]
    attn = jnp.concatenate(blocks, axis=0).astype(BF16)
    row, column = iota((tokens, tokens), 0), iota((tokens, tokens), 1)
    reorder = jnp.logical_and(row % requests == column // steps, row // requests == column % steps)
    attn = dot_nn(reorder.astype(F32).astype(BF16), attn).astype(BF16)
    residual = residual_ref[...].astype(F32).reshape(tokens, features)
    hidden = residual + dot_nt(attn, w_ref[...])
    hidden_ref[...] = hidden
    squares = jnp.sum(hidden * hidden, axis=1, keepdims=True)
    tile, offset = side_place(features, SIDE_KEYS + EXPERTS)
    wide_ref[...] = jnp.zeros_like(wide_ref)
    wide_ref[:, 0:features] = hidden * gain_ref[...]
    routes = routes_ref[...].reshape(tokens, routes_ref.shape[2])
    lane = iota((tokens, LANES), 1) - offset
    side = wide_ref[:, tile : tile + LANES]
    for k in range(routes.shape[1]):
        side = jnp.where(lane == routes[:, k : k + 1] + SIDE_KEYS, 1.0, side)
    high = round16(squares)
    side = jnp.where(lane == 0, high, side)
    wide_ref[:, tile : tile + LANES] = jnp.where(lane == 1, squares - high, side)
    out_ref[...] = wide_ref[...].astype(BF16)


def hidden_state(attn, residual, w_out, gain, routes):
    steps, requests, features = residual.shape
    tokens = steps * requests
    wide = side_place(features, SIDE_KEYS + EXPERTS)[0] + LANES
    return pl.pallas_call(
        hidden_kernel,
        out_shape=(
            jax.ShapeDtypeStruct((tokens, features), F32),
            jax.ShapeDtypeStruct((tokens, wide), BF16),
        ),
        scratch_shapes=[pltpu.VMEM((tokens, wide), F32)],
        compiler_params=params(),
        name="hidden",
    )(attn, residual, w_out.T, gain.reshape(1, features), routes)


def window_start(first, rows, window):
    return pl.multiple_of(jnp.clip(first // 16 * 16, 0, rows - window), 16)


def gate_up_kernel(
    features, local, turn, sources, where_ref, w_ref, router_ref, *refs,
):
    part_refs, refs = refs[:sources], refs[sources:]
    out_ref, pick_ref, range_ref, first_ref, most_ref, x_ref, row_ref, acc_ref = refs
    total = x_ref.shape[0]
    for e, part_ref in enumerate(part_refs):
        x_ref[e * (total // sources) : (e + 1) * (total // sources)] = part_ref[...]
    rows = pick_ref.shape[1]
    blocks = out_ref.shape[0]
    share = rows // blocks
    width = w_ref.shape[3]
    window = total // 2 + 16
    tile, offset = side_place(features, SIDE_KEYS + EXPERTS)
    me = where_ref[0]
    own_side = x_ref[:, tile : tile + LANES].astype(F32)
    lane = iota((total, LANES), 1)
    flags = pltpu.roll(own_side, LANES - offset - SIDE_KEYS, 1)
    flags = jnp.where(lane < EXPERTS, flags, 0.0)
    owners = EXPERTS // local
    counts = jnp.sum(flags, axis=0, keepdims=True)
    most = jnp.int32(0)
    for o in range(owners):
        held = jnp.logical_and(lane[0:1] >= o * local, lane[0:1] < (o + 1) * local)
        most = jnp.maximum(most, jnp.sum(jnp.where(held, counts, 0.0)).astype(jnp.int32))
    most_ref[0] = most
    mine = pltpu.roll(flags, lax.rem(LANES - me * local, LANES), 1)
    mine = jnp.where(lane < local, mine, 0.0)
    mine16 = mine.astype(BF16)
    row, column = iota((total, total), 0), iota((total, total), 1)
    earlier = (column < row).astype(F32).astype(BF16)
    ranks = dot_nn(earlier, mine16)
    counts = jnp.sum(mine, axis=0, keepdims=True)
    before = (iota((LANES, LANES), 0) < iota((LANES, LANES), 1)).astype(F32).astype(BF16)
    first = dot_nn(jnp.broadcast_to(counts, (8, LANES)).astype(BF16), before)[0:1] - turn * rows
    place = jnp.where(mine > 0.0, first + ranks, -1.0).astype(jnp.int32)
    at = iota((total, rows), 1)
    pick = jnp.zeros((total, rows), F32)
    for j in range(local):
        pick = jnp.where(at == place[:, j : j + 1], 1.0, pick)
    pick = pick.astype(BF16)
    pick_ref[...] = pick
    ranges = jnp.where(iota((16, LANES), 0) < 8, first, first + counts)
    ranges = jnp.concatenate([ranges[0:8], ranges[8:16]] + [jnp.zeros((LANES - 16, LANES), F32)], axis=0)
    ranges = ranges.T
    range_ref[...] = ranges[0:16]
    row_ref[...] = dot_tn(pick, x_ref[...]).astype(BF16)
    acc_ref[...] = jnp.zeros_like(acc_ref)
    for j in range(local):
        start_row = jnp.sum(first[:, j : j + 1]).astype(jnp.int32)
        first_ref[j] = start_row
        start = window_start(start_row, rows, window)
        part = row_ref[pl.ds(start, window), 0:features]
        fresh = start + iota((window, width), 0) >= start_row
        for half in range(2):
            into = (pl.ds(start, window), slice(half * width, (half + 1) * width))
            made = dot_nn(part, w_ref[j, half])
            acc_ref[into] = jnp.where(fresh, made, acc_ref[into])
    for b in range(blocks):
        for piece in range(2 * width // LANES):
            out_ref[b, piece * share : (piece + 1) * share, :] = acc_ref[
                b * share : (b + 1) * share, piece * LANES : (piece + 1) * LANES
            ].astype(BF16)
    logits = dot_nt(router_ref[...], x_ref[:, 0:features])
    high = round16(logits)
    both = jnp.concatenate([high, logits - high], axis=0).astype(BF16)
    both = dot_nn(both, pick)
    turned = jnp.zeros((EXPERTS, rows), jnp.bool_)
    expert = iota((EXPERTS, rows), 0) - me * local
    where_row = iota((EXPERTS, rows), 1).astype(F32)
    for j in range(local):
        inside = jnp.logical_and(
            where_row >= first[:, j : j + 1], where_row < (first + counts)[:, j : j + 1]
        )
        turned = jnp.logical_or(turned, jnp.logical_and(inside, expert == j))
    squares = dot_tn(own_side.astype(BF16), pick)
    side = jnp.concatenate(
        [
            jnp.sum(jnp.where(turned, both[0:EXPERTS], 0.0), axis=0, keepdims=True),
            jnp.sum(jnp.where(turned, both[EXPERTS : 2 * EXPERTS], 0.0), axis=0, keepdims=True),
            squares[offset : offset + 2],
            jnp.zeros((12, rows), F32),
        ],
        axis=0,
    )
    for b in range(blocks):
        end = 2 * width // LANES * share
        out_ref[b, end : end + 16, :] = jnp.zeros((16, LANES), BF16)
        out_ref[b, end : end + 16, 0:share] = side[:, b * share : (b + 1) * share].astype(BF16)


def gate_up(exp_index, tokens, weights, w_router, rows, blocks, turn):
    local, _, features, width = weights.shape
    sources, wide = len(tokens), tokens[0].shape[1]
    total = sources * tokens[0].shape[0]
    smem, vmem = pl.BlockSpec(memory_space=pltpu.SMEM), pl.BlockSpec(memory_space=pltpu.VMEM)
    return pl.pallas_call(
        functools.partial(gate_up_kernel, features, local, turn, sources),
        in_specs=[smem] + [vmem] * (2 + sources),
        out_specs=(vmem, vmem, vmem, smem, smem),
        out_shape=(
            jax.ShapeDtypeStruct((blocks, 2 * width // LANES * (rows // blocks) + 16, LANES), BF16),
            jax.ShapeDtypeStruct((total, rows), BF16),
            jax.ShapeDtypeStruct((16, LANES), F32),
            jax.ShapeDtypeStruct((16,), jnp.int32),
            jax.ShapeDtypeStruct((1,), jnp.int32),
        ),
        scratch_shapes=[
            pltpu.VMEM((total, wide), BF16),
            pltpu.VMEM((rows, wide), BF16),
            pltpu.VMEM((rows, 2 * width), F32),
        ],
        compiler_params=params(),
        name="gate_up",
    )(exp_index, weights, w_router.T, *tokens)


def inner_kernel(x_ref, out_ref):
    blocks, height, _ = x_ref.shape
    pieces = 2 * FF // LANES
    share = (height - 16) // pieces
    half = pieces // 2

    def total(start, size):
        added = x_ref[0, start : start + size].astype(F32)
        for b in range(1, blocks):
            added = added + x_ref[b, start : start + size].astype(F32)
        return added

    side = total(pieces * share, 16)
    logit = side[0:1] + side[1:2]
    squares = side[2:3] + side[3:4]
    inverse = lax.rsqrt(squares * (1.0 / D) + 1e-6)
    down_column = jnp.broadcast_to(inverse, (LANES, LANES)).T[0:share, 0:1]
    for piece in range(half):
        gate = total(piece * share, share) * down_column
        up = total((half + piece) * share, share) * down_column
        made = (gate / (1.0 + jnp.exp(-gate)) * up).astype(BF16)
        for b in range(blocks):
            out_ref[b, piece * share : (piece + 1) * share, :] = made
    logit = logit * inverse
    high = round16(logit)
    middle = round16(logit - high)
    own = jnp.concatenate(
        [high, middle, logit - high - middle, jnp.zeros((13, LANES), F32)], axis=0
    ).astype(BF16)
    for b in range(blocks):
        out_ref[b, half * share : half * share + 16, :] = own


def inner(parts):
    blocks, height, _ = parts.shape
    return pl.pallas_call(
        inner_kernel,
        out_shape=jax.ShapeDtypeStruct((blocks, (height - 16) // 2 + 16, LANES), BF16),
        compiler_params=params(),
        name="inner",
    )(parts)


def down_kernel(features, local, first_ref, range_ref, pick_ref, x_ref, w_ref, *refs):
    out_refs, (row_ref, made_ref) = refs[:-2], refs[-2:]
    blocks, height, _ = x_ref.shape
    total, rows = pick_ref.shape
    width = w_ref.shape[2]
    pieces = width // LANES
    share = (height - 16) // pieces
    window = total // 2 + 16
    for b in range(blocks):
        for piece in range(pieces):
            row_ref[b * share : (b + 1) * share, piece * LANES : (piece + 1) * LANES] = x_ref[
                b, piece * share : (piece + 1) * share, :
            ]
    made_ref[...] = jnp.zeros_like(made_ref)
    for j in range(local):
        start_row = first_ref[j]
        start = window_start(start_row, rows, window)
        made = dot_nt(row_ref[pl.ds(start, window), :], w_ref[j])
        fresh = start + iota((window, features), 0) >= start_row
        into = (pl.ds(start, window), slice(0, features))
        made_ref[into] = jnp.where(fresh, made, made_ref[into])
    logit = jnp.concatenate(
        [x_ref[b, pieces * share :, 0:share].astype(F32) for b in range(blocks)], axis=1
    )
    pick = pick_ref[...]
    where_row = iota((16, rows), 1).astype(F32)
    inside = jnp.logical_and(where_row >= range_ref[:, 0:1], where_row < range_ref[:, 8:9])
    inside = jnp.logical_and(inside, iota((16, rows), 0) < local)
    spread = [jnp.where(inside, logit[k : k + 1], 0.0) for k in range(3)]
    spread.append(inside.astype(F32))
    found = dot_nt(jnp.concatenate(spread, axis=0).astype(BF16), pick)
    valid = found[48:64] > 0.5
    logits = jnp.where(valid, found[0:16] + found[16:32] + found[32:48], NEG_FILL)
    top = jnp.max(logits, axis=0, keepdims=True)
    weights = jnp.where(valid, jnp.exp(logits - top), 0.0)
    summed = jnp.sum(weights, axis=0, keepdims=True)
    high = round16(weights)
    both = dot_nn(jnp.concatenate([high, weights - high], axis=0).astype(BF16), pick)
    weight = jnp.sum(jnp.where(inside, both[0:16] + both[16:32], 0.0), axis=0, keepdims=True)
    column = jnp.broadcast_to(weight, (LANES, rows)).T[:, 0:1]
    acc = dot_nn(pick, (made_ref[...] * column).astype(BF16))
    tile, offset = side_place(features, 2)
    pair = jnp.where(iota((LANES, total), 0) == 0, top, summed).T
    tokens = total // len(out_refs)
    for e, out_ref in enumerate(out_refs):
        at = slice(e * tokens, (e + 1) * tokens)
        out_ref[...] = acc[at]
        lane = iota((tokens, LANES), 1) - offset
        side = jnp.where(lane == 0, pair[at, 0:1], acc[at, tile : tile + LANES])
        out_ref[:, tile : tile + LANES] = jnp.where(lane == 1, pair[at, 1:2], side)


def down(first, ranges, pick, parts, weights, exp_count):
    local, features, width = weights.shape
    total, rows = pick.shape
    wide = side_place(features, 2)[0] + LANES
    smem, vmem = pl.BlockSpec(memory_space=pltpu.SMEM), pl.BlockSpec(memory_space=pltpu.VMEM)
    return pl.pallas_call(
        functools.partial(down_kernel, features, local),
        in_specs=[smem] + [vmem] * 4,
        out_shape=(jax.ShapeDtypeStruct((total // exp_count, wide), F32),) * exp_count,
        scratch_shapes=[pltpu.VMEM((rows, width), BF16), pltpu.VMEM((rows, wide), F32)],
        compiler_params=params(),
        name="down",
    )(first, ranges, pick, parts, weights)


def finish_kernel(hidden_ref, *refs):
    part_refs, out_ref = refs[:-1], refs[-1]
    features = hidden_ref.shape[1]
    tile, offset = side_place(features, 2)
    sides = [x_ref[:, tile : tile + LANES] for x_ref in part_refs]
    tops = [side[:, offset : offset + 1] for side in sides]
    top = functools.reduce(jnp.maximum, tops)
    scales = [jnp.exp(one - top) for one in tops]
    total = functools.reduce(
        jnp.add, [s * side[:, offset + 1 : offset + 2] for s, side in zip(scales, sides)]
    )
    acc = functools.reduce(
        jnp.add, [s * x_ref[:, 0:features] for x_ref, s in zip(part_refs, scales)]
    )
    out = hidden_ref[...] + acc * (1.0 / total)
    out_ref[...] = out.reshape(out_ref.shape).astype(BF16)


def finish(parts, hidden, shape):
    return pl.pallas_call(
        finish_kernel,
        out_shape=jax.ShapeDtypeStruct(shape, BF16),
        compiler_params=params(),
        name="finish",
    )(hidden, *parts)


def join_rounds(features, one, other):
    tile, offset = side_place(features, 2)
    at = tile + offset
    top = jnp.maximum(one[..., at : at + 1], other[..., at : at + 1])
    scales = [jnp.exp(part[..., at : at + 1] - top) for part in (one, other)]
    joined = one * scales[0] + other * scales[1]
    return jnp.where(jnp.arange(one.shape[-1]) == at, top, joined)


def send(x, axis, distance):
    count = lax.axis_size(axis)
    return lax.ppermute(x, axis, [(i, (i + distance) % count) for i in range(count)])


def swap(x, axis):
    return lax.all_to_all(x, axis, split_axis=0, concat_axis=0, tiled=True)


def local(
    queries,
    new_key_value,
    key_value_cache,
    page_table,
    cache_len,
    routes,
    residual,
    w_out,
    norm_gain,
    w_router,
    w_gate_up,
    w_down,
):
    exp_count = lax.axis_size("exp")
    seq_count = lax.axis_size("seq")
    exp_index = lax.axis_index("exp").astype(jnp.int32).reshape(1)
    seq_index = lax.axis_index("seq").astype(jnp.int32).reshape(1)
    steps, requests, width = queries.shape
    tokens = steps * requests
    features = w_out.shape[1]
    page_rows = key_value_cache.shape[2]
    pool = key_value_cache.reshape(-1, page_rows, 2, KV_WIDTH)

    shares = attend(queries, new_key_value, pool, page_table, cache_len, seq_index)
    shares = swap(shares.reshape(seq_count, -1, KV_WIDTH + LANES), "seq")
    attn = join(shares)
    w_gate_up, attn = lax.optimization_barrier((w_gate_up, attn))
    attn = swap(attn, "seq")
    gate_up_weights = w_gate_up.transpose(0, 2, 1, 3)
    gate_up_weights, attn = lax.optimization_barrier((gate_up_weights, attn))
    hidden, outgoing = hidden_state(attn, residual, w_out, norm_gain, routes)
    incoming = [outgoing] + [send(outgoing, "exp", k) for k in range(1, exp_count)]
    rows = -(-ROUND_ROWS // (16 * seq_count)) * 16 * seq_count

    def one_round(turn):
        parts, pick, ranges, first, most = gate_up(
            exp_index, incoming, gate_up_weights, w_router, rows, seq_count, turn
        )
        made = swap(inner(swap(parts, "seq")), "seq")
        return down(first, ranges, pick, made, w_down, exp_count), most

    made, most = one_round(0)
    pairs = w_gate_up.shape[0] * exp_count * steps * CAP
    for turn in range(1, -(-pairs // rows)):
        made = lax.cond(
            most[0] > turn * rows,
            lambda made: tuple(
                join_rounds(features, *both) for both in zip(made, one_round(turn)[0])
            ),
            lambda made: made,
            made,
        )
    made = [made[0]] + [send(made[k], "exp", -k) for k in range(1, exp_count)]
    return finish(made, hidden, (steps, requests, features))


def solution(mesh):
    in_specs = (
        P(None, "exp", None),
        P(None, "exp", None, None),
        P("exp", "seq", None, None, None),
        P("exp", "seq"),
        P("exp"),
        P(None, "exp", None),
        P(None, "exp", "seq"),
        P(None, "seq"),
        P("seq"),
        P("seq", None),
        P("exp", "seq", None, None),
        P("exp", "seq", None),
    )
    out_specs = P(None, "exp", "seq")
    return jax.shard_map(local, mesh=mesh, in_specs=in_specs, out_specs=out_specs, check_vma=False)
```

```python
import functools

import jax
import jax.numpy as jnp
from jax import lax
from jax.experimental import pallas as pl
from jax.experimental.pallas import tpu as pltpu
from jax.sharding import PartitionSpec as P

D = 1536
QUERY_HEADS = 24
KEY_VALUE_HEADS = 8
HEAD_SIZE = 64
GROUP = QUERY_HEADS // KEY_VALUE_HEADS
KV_WIDTH = KEY_VALUE_HEADS * HEAD_SIZE
EXPERTS = 40
FF = 512
CAP = 4
LANES = 128
SIDE_KEYS = 2
ROUND_ROWS = 384

NEG_FILL = -1e30
F32 = jnp.float32
BF16 = jnp.bfloat16
VMEM_LIMIT = 48 * 1024 * 1024
ATTEND_VMEM = 60 * 1024 * 1024


def iota(shape, dimension):
    return lax.broadcasted_iota(jnp.int32, shape, dimension)


def dot_nt(a, b):
    return lax.dot_general(a, b, (((1,), (1,)), ((), ())), preferred_element_type=F32)


def dot_tn(a, b):
    return lax.dot_general(a, b, (((0,), (0,)), ((), ())), preferred_element_type=F32)


def dot_nn(a, b):
    return lax.dot_general(a, b, (((1,), (0,)), ((), ())), preferred_element_type=F32)


def round16(x):
    return x.astype(BF16).astype(F32)


def swap_halves(x):
    return pltpu.roll(x, HEAD_SIZE, 1)


def tile_of(x, index):
    return x[:, index * LANES : (index + 1) * LANES]


def padded(width):
    return -(-width // LANES) * LANES


def params():
    return pltpu.CompilerParams(vmem_limit_bytes=VMEM_LIMIT)


def attend_kernel(
    classes, table_ref, len_ref, seq_ref, q_hbm, fresh_hbm, cache_ref, out_ref,
    page_ref, split_ref, q_ref, fresh_ref, query_ref, new_ref, order_ref, sems, small_sems,
):
    steps, requests, _ = q_ref.shape
    page_rows = cache_ref.shape[1]
    pages = table_ref.shape[1]
    span = pages * page_rows
    first = seq_ref[0] * span
    small = [
        pltpu.make_async_copy(q_hbm, q_ref, small_sems.at[0]),
        pltpu.make_async_copy(fresh_hbm, fresh_ref, small_sems.at[1]),
    ]
    for one in small:
        one.start()

    held = [jnp.clip(len_ref[r] - first, 0, span) for r in range(requests)]
    for r in range(requests):
        ahead = jnp.int32(0)
        for other in range(requests):
            if other != r:
                longer = held[other] >= held[r] if other < r else held[other] > held[r]
                ahead = ahead + longer.astype(jnp.int32)
        order_ref[ahead] = r

    def copy(r, page):
        at = r * pages + page
        return pltpu.make_async_copy(cache_ref.at[table_ref[r, page]], page_ref.at[at], sems.at[at])

    def needed(r, low):
        return len_ref[r] - first > low * page_rows

    bounds = list(zip((0,) + classes[:-1], classes))

    def start(pair, carry):
        both = order_ref[2 * pair], order_ref[2 * pair + 1]
        for low, high in bounds:

            @pl.when(needed(both[0], low))
            def _():
                for page in range(low, high):
                    for r in both:
                        copy(r, page).start()

        return carry

    lax.fori_loop(0, requests // 2, start, 0)
    for one in small:
        one.wait()

    low = iota((requests, LANES), 1) < HEAD_SIZE
    for t in range(steps):
        q = q_ref[t].astype(F32) * 0.125
        for g in range(GROUP):
            for j in range(KV_WIDTH // LANES):
                one = tile_of(q, (6 * j + g) // 2)
                two = tile_of(q, (6 * j + 3 + g) // 2)
                if g % 2 == 0:
                    tile = jnp.where(low, one, two)
                else:
                    tile = swap_halves(jnp.where(low, two, one))
                query_ref[t * GROUP + g, :, j * LANES : (j + 1) * LANES] = tile
        new_ref[t] = fresh_ref[t].reshape(2 * requests, KV_WIDTH).astype(F32)

    rows = steps * GROUP * KEY_VALUE_HEADS
    own = iota((rows, KV_WIDTH), 1) // HEAD_SIZE == iota((rows, KV_WIDTH), 0) % KEY_VALUE_HEADS
    lane = iota((rows, LANES), 1)
    head = iota((rows, LANES), 0) % KEY_VALUE_HEADS
    row_step = iota((rows, 16), 0) // (GROUP * KEY_VALUE_HEADS)
    kept = jnp.logical_and(iota((rows, 16), 1) <= row_step, seq_ref[0] == 0)
    fresh_bias = jnp.where(kept, 0.0, NEG_FILL)

    def fresh_rows(r, which):
        found = [new_ref[u, pl.ds(2 * r + which, 1), :] for u in range(steps)]
        return jnp.concatenate(found + [jnp.zeros((16 - steps, KV_WIDTH), F32)], axis=0).astype(BF16)

    def attend_pages(r, slot, count):
        spread = jnp.concatenate(
            [
                jnp.broadcast_to(query_ref[i, pl.ds(r, 1), :], (KEY_VALUE_HEADS, KV_WIDTH))
                for i in range(steps * GROUP)
            ],
            axis=0,
        )
        spread = jnp.where(own, spread, 0.0).astype(BF16)
        halves = ([], [])
        for page in range(count):
            block = page_ref[r * pages + page].reshape(2 * page_rows, KV_WIDTH).astype(F32)
            for j in range(KV_WIDTH // LANES):
                split_ref[slot, page, j] = tile_of(block, j)
            for which in range(2):
                tiles = [
                    split_ref[slot, page, j, pl.ds(which, page_rows, 2), :]
                    for j in range(KV_WIDTH // LANES)
                ]
                halves[which].append(jnp.concatenate(tiles, axis=1).astype(BF16))
        keys, values = jnp.concatenate(halves[0], axis=0), jnp.concatenate(halves[1], axis=0)
        size = count * page_rows
        live = first + iota((1, size), 1) < len_ref[r]
        scores = dot_nt(spread, keys) + jnp.where(live, 0.0, NEG_FILL)
        fresh_scores = dot_nt(spread, fresh_rows(r, 0)) + fresh_bias
        largest = jnp.maximum(
            jnp.max(scores, axis=1, keepdims=True), jnp.max(fresh_scores, axis=1, keepdims=True)
        )
        weights = jnp.exp(scores - largest)
        fresh_weights = jnp.exp(fresh_scores - largest)
        total = jnp.sum(weights, axis=1, keepdims=True)
        total = total + jnp.sum(fresh_weights, axis=1, keepdims=True)
        acc = dot_nn(weights.astype(BF16), values)
        acc = acc + dot_nn(fresh_weights.astype(BF16), fresh_rows(r, 1))
        acc = jnp.where(own, acc * (1.0 / total), 0.0)
        acc = jnp.sum(acc.reshape(steps * GROUP, KEY_VALUE_HEADS, KV_WIDTH), axis=1)
        level = jnp.where(needed(r, 0), largest + jnp.log(total), NEG_FILL)
        high = round16(level)
        middle = round16(level - high)
        side = jnp.where(lane == head, high, 0.0)
        side = jnp.where(lane == head + 8, middle, side)
        side = jnp.where(lane == head + 16, level - high - middle, side)
        side = jnp.sum(side.reshape(steps * GROUP, KEY_VALUE_HEADS, LANES), axis=1)
        return acc.astype(BF16), side.astype(BF16)

    def one_pair(pair, carry):
        both = order_ref[2 * pair], order_ref[2 * pair + 1]
        for low, high in bounds:
            enough = needed(both[0], low)
            if high < pages:
                enough = jnp.logical_and(enough, jnp.logical_not(needed(both[0], high)))

            @pl.when(enough)
            def _():
                for page in range(high):
                    for r in both:
                        copy(r, page).wait()
                made = [attend_pages(r, slot, high) for slot, r in enumerate(both)]
                for r, (acc, side) in zip(both, made):
                    out_ref[r, :, 0:KV_WIDTH] = acc
                    out_ref[r, :, KV_WIDTH : KV_WIDTH + LANES] = side

        @pl.when(jnp.logical_not(needed(both[0], 0)))
        def _():
            empty = jnp.where(iota((steps * GROUP, LANES), 1) < KEY_VALUE_HEADS, NEG_FILL, 0.0)
            for r in both:
                out_ref[r, :, 0:KV_WIDTH] = jnp.zeros((steps * GROUP, KV_WIDTH), BF16)
                out_ref[r, :, KV_WIDTH : KV_WIDTH + LANES] = empty.astype(BF16)

        return carry

    lax.fori_loop(0, requests // 2, one_pair, 0)


def attend(queries, new_key_value, cache, page_table, cache_len, seq_index):
    steps, requests, _ = queries.shape
    pages = page_table.shape[1]
    page_rows = cache.shape[1]
    classes = tuple(c for c in (2, 4) if c < pages) + (pages,)
    smem, hbm = pl.BlockSpec(memory_space=pltpu.SMEM), pl.BlockSpec(memory_space=pl.ANY)
    return pl.pallas_call(
        functools.partial(attend_kernel, classes),
        in_specs=[smem] * 3 + [hbm] * 3,
        out_shape=jax.ShapeDtypeStruct((requests, steps * GROUP, KV_WIDTH + LANES), BF16),
        scratch_shapes=[
            pltpu.VMEM((requests * pages, page_rows, 2, KV_WIDTH), BF16),
            pltpu.VMEM((2, pages, KV_WIDTH // LANES, 2 * page_rows, LANES), F32),
            pltpu.VMEM(queries.shape, BF16),
            pltpu.VMEM(new_key_value.shape, BF16),
            pltpu.VMEM((steps * GROUP, requests, KV_WIDTH), F32),
            pltpu.VMEM((steps, 2 * requests, KV_WIDTH), F32),
            pltpu.SMEM((requests,), jnp.int32),
            pltpu.SemaphoreType.DMA((requests * pages,)),
            pltpu.SemaphoreType.DMA((2,)),
        ],
        compiler_params=pltpu.CompilerParams(vmem_limit_bytes=ATTEND_VMEM),
        name="attend",
    )(page_table, cache_len, seq_index, queries, new_key_value, cache)


def join_kernel(x_ref, out_ref):
    blocks, rows, _ = x_ref.shape
    tokens = rows // GROUP
    levels = []
    for b in range(blocks):
        side = x_ref[b, :, KV_WIDTH : KV_WIDTH + LANES].astype(F32)
        levels.append(side + pltpu.roll(side, LANES - 8, 1) + pltpu.roll(side, LANES - 16, 1))
    largest = functools.reduce(jnp.maximum, levels)
    weights = [jnp.exp(level - largest) for level in levels]
    inverse = 1.0 / functools.reduce(jnp.add, weights)
    low = iota((rows, LANES), 1) < HEAD_SIZE
    acc = [jnp.zeros((rows, LANES), F32) for _ in range(KV_WIDTH // LANES)]
    for b in range(blocks):
        share = weights[b] * inverse
        for j in range(KV_WIDTH // LANES):
            factor = jnp.where(low, share[:, 2 * j : 2 * j + 1], share[:, 2 * j + 1 : 2 * j + 2])
            acc[j] = acc[j] + factor * x_ref[b, :, j * LANES : (j + 1) * LANES].astype(F32)

    def piece(head, half):
        k, g = head // GROUP, head % GROUP
        tile = jnp.concatenate(
            [acc[k // 2][t * GROUP + g : t * GROUP + g + 1] for t in range(tokens)], axis=0
        )
        return tile if k % 2 == half else swap_halves(tile)

    low_tokens = iota((tokens, LANES), 1) < HEAD_SIZE
    for m in range(QUERY_HEADS // 2):
        tile = jnp.where(low_tokens, piece(2 * m, 0), piece(2 * m + 1, 1)).astype(BF16)
        for b in range(blocks):
            out_ref[b, :, m * LANES : (m + 1) * LANES] = tile


def join(parts):
    blocks, rows, _ = parts.shape
    return pl.pallas_call(
        join_kernel,
        out_shape=jax.ShapeDtypeStruct((blocks, rows // GROUP, QUERY_HEADS * HEAD_SIZE), BF16),
        compiler_params=params(),
        name="join",
    )(parts)


def side_place(features, count):
    tile, offset = features // LANES * LANES, features % LANES
    return (tile, offset) if offset and offset + count <= LANES else (padded(features), 0)


def hidden_kernel(attn_ref, residual_ref, w_ref, gain_ref, routes_ref, hidden_ref, out_ref, wide_ref):
    steps, requests, features = residual_ref.shape
    tokens = steps * requests
    blocks = [attn_ref[b].astype(F32) for b in range(attn_ref.shape[0])]
    attn = jnp.concatenate(blocks, axis=0).astype(BF16)
    row, column = iota((tokens, tokens), 0), iota((tokens, tokens), 1)
    reorder = jnp.logical_and(row % requests == column // steps, row // requests == column % steps)
    attn = dot_nn(reorder.astype(F32).astype(BF16), attn).astype(BF16)
    residual = residual_ref[...].astype(F32).reshape(tokens, features)
    hidden = residual + dot_nt(attn, w_ref[...])
    hidden_ref[...] = hidden
    squares = jnp.sum(hidden * hidden, axis=1, keepdims=True)
    tile, offset = side_place(features, SIDE_KEYS + EXPERTS)
    wide_ref[...] = jnp.zeros_like(wide_ref)
    wide_ref[:, 0:features] = hidden * gain_ref[...]
    routes = routes_ref[...].reshape(tokens, routes_ref.shape[2])
    lane = iota((tokens, LANES), 1) - offset
    side = wide_ref[:, tile : tile + LANES]
    for k in range(routes.shape[1]):
        side = jnp.where(lane == routes[:, k : k + 1] + SIDE_KEYS, 1.0, side)
    high = round16(squares)
    side = jnp.where(lane == 0, high, side)
    wide_ref[:, tile : tile + LANES] = jnp.where(lane == 1, squares - high, side)
    out_ref[...] = wide_ref[...].astype(BF16)


def hidden_state(attn, residual, w_out, gain, routes):
    steps, requests, features = residual.shape
    tokens = steps * requests
    wide = side_place(features, SIDE_KEYS + EXPERTS)[0] + LANES
    return pl.pallas_call(
        hidden_kernel,
        out_shape=(
            jax.ShapeDtypeStruct((tokens, features), F32),
            jax.ShapeDtypeStruct((tokens, wide), BF16),
        ),
        scratch_shapes=[pltpu.VMEM((tokens, wide), F32)],
        compiler_params=params(),
        name="hidden",
    )(attn, residual, w_out.T, gain.reshape(1, features), routes)


def window_start(first, rows, window):
    return pl.multiple_of(jnp.clip(first // 16 * 16, 0, rows - window), 16)


def gate_up_kernel(
    features, local, turn, sources, where_ref, w_ref, router_ref, *refs,
):
    part_refs, refs = refs[:sources], refs[sources:]
    out_ref, pick_ref, range_ref, first_ref, most_ref, x_ref, row_ref, acc_ref = refs
    total = x_ref.shape[0]
    for e, part_ref in enumerate(part_refs):
        x_ref[e * (total // sources) : (e + 1) * (total // sources)] = part_ref[...]
    rows = pick_ref.shape[1]
    blocks = out_ref.shape[0]
    share = rows // blocks
    width = w_ref.shape[3]
    window = total // 2 + 16
    tile, offset = side_place(features, SIDE_KEYS + EXPERTS)
    me = where_ref[0]
    own_side = x_ref[:, tile : tile + LANES].astype(F32)
    lane = iota((total, LANES), 1)
    flags = pltpu.roll(own_side, LANES - offset - SIDE_KEYS, 1)
    flags = jnp.where(lane < EXPERTS, flags, 0.0)
    owners = EXPERTS // local
    counts = jnp.sum(flags, axis=0, keepdims=True)
    most = jnp.int32(0)
    for o in range(owners):
        held = jnp.logical_and(lane[0:1] >= o * local, lane[0:1] < (o + 1) * local)
        most = jnp.maximum(most, jnp.sum(jnp.where(held, counts, 0.0)).astype(jnp.int32))
    most_ref[0] = most
    mine = pltpu.roll(flags, lax.rem(LANES - me * local, LANES), 1)
    mine = jnp.where(lane < local, mine, 0.0)
    mine16 = mine.astype(BF16)
    row, column = iota((total, total), 0), iota((total, total), 1)
    earlier = (column < row).astype(F32).astype(BF16)
    ranks = dot_nn(earlier, mine16)
    counts = jnp.sum(mine, axis=0, keepdims=True)
    before = (iota((LANES, LANES), 0) < iota((LANES, LANES), 1)).astype(F32).astype(BF16)
    first = dot_nn(jnp.broadcast_to(counts, (8, LANES)).astype(BF16), before)[0:1] - turn * rows
    place = jnp.where(mine > 0.0, first + ranks, -1.0).astype(jnp.int32)
    at = iota((total, rows), 1)
    pick = jnp.zeros((total, rows), F32)
    for j in range(local):
        pick = jnp.where(at == place[:, j : j + 1], 1.0, pick)
    pick = pick.astype(BF16)
    pick_ref[...] = pick
    ranges = jnp.where(iota((16, LANES), 0) < 8, first, first + counts)
    ranges = jnp.concatenate([ranges[0:8], ranges[8:16]] + [jnp.zeros((LANES - 16, LANES), F32)], axis=0)
    ranges = ranges.T
    range_ref[...] = ranges[0:16]
    row_ref[...] = dot_tn(pick, x_ref[...]).astype(BF16)
    acc_ref[...] = jnp.zeros_like(acc_ref)
    for j in range(local):
        start_row = jnp.sum(first[:, j : j + 1]).astype(jnp.int32)
        first_ref[j] = start_row
        start = window_start(start_row, rows, window)
        part = row_ref[pl.ds(start, window), 0:features]
        fresh = start + iota((window, width), 0) >= start_row
        for half in range(2):
            into = (pl.ds(start, window), slice(half * width, (half + 1) * width))
            made = dot_nn(part, w_ref[j, half])
            acc_ref[into] = jnp.where(fresh, made, acc_ref[into])
    for b in range(blocks):
        for piece in range(2 * width // LANES):
            out_ref[b, piece * share : (piece + 1) * share, :] = acc_ref[
                b * share : (b + 1) * share, piece * LANES : (piece + 1) * LANES
            ].astype(BF16)
    logits = dot_nt(router_ref[...], x_ref[:, 0:features])
    high = round16(logits)
    both = jnp.concatenate([high, logits - high], axis=0).astype(BF16)
    both = dot_nn(both, pick)
    turned = jnp.zeros((EXPERTS, rows), jnp.bool_)
    expert = iota((EXPERTS, rows), 0) - me * local
    where_row = iota((EXPERTS, rows), 1).astype(F32)
    for j in range(local):
        inside = jnp.logical_and(
            where_row >= first[:, j : j + 1], where_row < (first + counts)[:, j : j + 1]
        )
        turned = jnp.logical_or(turned, jnp.logical_and(inside, expert == j))
    squares = dot_tn(own_side.astype(BF16), pick)
    side = jnp.concatenate(
        [
            jnp.sum(jnp.where(turned, both[0:EXPERTS], 0.0), axis=0, keepdims=True),
            jnp.sum(jnp.where(turned, both[EXPERTS : 2 * EXPERTS], 0.0), axis=0, keepdims=True),
            squares[offset : offset + 2],
            jnp.zeros((12, rows), F32),
        ],
        axis=0,
    )
    for b in range(blocks):
        end = 2 * width // LANES * share
        out_ref[b, end : end + 16, :] = jnp.zeros((16, LANES), BF16)
        out_ref[b, end : end + 16, 0:share] = side[:, b * share : (b + 1) * share].astype(BF16)


def gate_up(exp_index, tokens, weights, w_router, rows, blocks, turn):
    local, _, features, width = weights.shape
    sources, wide = len(tokens), tokens[0].shape[1]
    total = sources * tokens[0].shape[0]
    smem, vmem = pl.BlockSpec(memory_space=pltpu.SMEM), pl.BlockSpec(memory_space=pltpu.VMEM)
    return pl.pallas_call(
        functools.partial(gate_up_kernel, features, local, turn, sources),
        in_specs=[smem] + [vmem] * (2 + sources),
        out_specs=(vmem, vmem, vmem, smem, smem),
        out_shape=(
            jax.ShapeDtypeStruct((blocks, 2 * width // LANES * (rows // blocks) + 16, LANES), BF16),
            jax.ShapeDtypeStruct((total, rows), BF16),
            jax.ShapeDtypeStruct((16, LANES), F32),
            jax.ShapeDtypeStruct((16,), jnp.int32),
            jax.ShapeDtypeStruct((1,), jnp.int32),
        ),
        scratch_shapes=[
            pltpu.VMEM((total, wide), BF16),
            pltpu.VMEM((rows, wide), BF16),
            pltpu.VMEM((rows, 2 * width), F32),
        ],
        compiler_params=params(),
        name="gate_up",
    )(exp_index, weights, w_router.T, *tokens)


def inner_kernel(x_ref, out_ref):
    blocks, height, _ = x_ref.shape
    pieces = 2 * FF // LANES
    share = (height - 16) // pieces
    half = pieces // 2

    def total(start, size):
        added = x_ref[0, start : start + size].astype(F32)
        for b in range(1, blocks):
            added = added + x_ref[b, start : start + size].astype(F32)
        return added

    side = total(pieces * share, 16)
    logit = side[0:1] + side[1:2]
    squares = side[2:3] + side[3:4]
    inverse = lax.rsqrt(squares * (1.0 / D) + 1e-6)
    down_column = jnp.broadcast_to(inverse, (LANES, LANES)).T[0:share, 0:1]
    for piece in range(half):
        gate = total(piece * share, share) * down_column
        up = total((half + piece) * share, share) * down_column
        made = (gate / (1.0 + jnp.exp(-gate)) * up).astype(BF16)
        for b in range(blocks):
            out_ref[b, piece * share : (piece + 1) * share, :] = made
    logit = logit * inverse
    high = round16(logit)
    middle = round16(logit - high)
    own = jnp.concatenate(
        [high, middle, logit - high - middle, jnp.zeros((13, LANES), F32)], axis=0
    ).astype(BF16)
    for b in range(blocks):
        out_ref[b, half * share : half * share + 16, :] = own


def inner(parts):
    blocks, height, _ = parts.shape
    return pl.pallas_call(
        inner_kernel,
        out_shape=jax.ShapeDtypeStruct((blocks, (height - 16) // 2 + 16, LANES), BF16),
        compiler_params=params(),
        name="inner",
    )(parts)


def down_kernel(features, local, first_ref, range_ref, pick_ref, x_ref, w_ref, *refs):
    out_refs, (row_ref, made_ref) = refs[:-2], refs[-2:]
    blocks, height, _ = x_ref.shape
    total, rows = pick_ref.shape
    width = w_ref.shape[2]
    pieces = width // LANES
    share = (height - 16) // pieces
    window = total // 2 + 16
    for b in range(blocks):
        for piece in range(pieces):
            row_ref[b * share : (b + 1) * share, piece * LANES : (piece + 1) * LANES] = x_ref[
                b, piece * share : (piece + 1) * share, :
            ]
    made_ref[...] = jnp.zeros_like(made_ref)
    for j in range(local):
        start_row = first_ref[j]
        start = window_start(start_row, rows, window)
        made = dot_nt(row_ref[pl.ds(start, window), :], w_ref[j])
        fresh = start + iota((window, features), 0) >= start_row
        into = (pl.ds(start, window), slice(0, features))
        made_ref[into] = jnp.where(fresh, made, made_ref[into])
    logit = jnp.concatenate(
        [x_ref[b, pieces * share :, 0:share].astype(F32) for b in range(blocks)], axis=1
    )
    pick = pick_ref[...]
    where_row = iota((16, rows), 1).astype(F32)
    inside = jnp.logical_and(where_row >= range_ref[:, 0:1], where_row < range_ref[:, 8:9])
    inside = jnp.logical_and(inside, iota((16, rows), 0) < local)
    spread = [jnp.where(inside, logit[k : k + 1], 0.0) for k in range(3)]
    spread.append(inside.astype(F32))
    found = dot_nt(jnp.concatenate(spread, axis=0).astype(BF16), pick)
    valid = found[48:64] > 0.5
    logits = jnp.where(valid, found[0:16] + found[16:32] + found[32:48], NEG_FILL)
    top = jnp.max(logits, axis=0, keepdims=True)
    weights = jnp.where(valid, jnp.exp(logits - top), 0.0)
    summed = jnp.sum(weights, axis=0, keepdims=True)
    high = round16(weights)
    both = dot_nn(jnp.concatenate([high, weights - high], axis=0).astype(BF16), pick)
    weight = jnp.sum(jnp.where(inside, both[0:16] + both[16:32], 0.0), axis=0, keepdims=True)
    column = jnp.broadcast_to(weight, (LANES, rows)).T[:, 0:1]
    acc = dot_nn(pick, (made_ref[...] * column).astype(BF16))
    tile, offset = side_place(features, 2)
    pair = jnp.where(iota((LANES, total), 0) == 0, top, summed).T
    tokens = total // len(out_refs)
    for e, out_ref in enumerate(out_refs):
        at = slice(e * tokens, (e + 1) * tokens)
        out_ref[...] = acc[at]
        lane = iota((tokens, LANES), 1) - offset
        side = jnp.where(lane == 0, pair[at, 0:1], acc[at, tile : tile + LANES])
        out_ref[:, tile : tile + LANES] = jnp.where(lane == 1, pair[at, 1:2], side)


def down(first, ranges, pick, parts, weights, exp_count):
    local, features, width = weights.shape
    total, rows = pick.shape
    wide = side_place(features, 2)[0] + LANES
    smem, vmem = pl.BlockSpec(memory_space=pltpu.SMEM), pl.BlockSpec(memory_space=pltpu.VMEM)
    return pl.pallas_call(
        functools.partial(down_kernel, features, local),
        in_specs=[smem] + [vmem] * 4,
        out_shape=(jax.ShapeDtypeStruct((total // exp_count, wide), F32),) * exp_count,
        scratch_shapes=[pltpu.VMEM((rows, width), BF16), pltpu.VMEM((rows, wide), F32)],
        compiler_params=params(),
        name="down",
    )(first, ranges, pick, parts, weights)


def finish_kernel(hidden_ref, *refs):
    part_refs, out_ref = refs[:-1], refs[-1]
    features = hidden_ref.shape[1]
    tile, offset = side_place(features, 2)
    sides = [x_ref[:, tile : tile + LANES] for x_ref in part_refs]
    tops = [side[:, offset : offset + 1] for side in sides]
    top = functools.reduce(jnp.maximum, tops)
    scales = [jnp.exp(one - top) for one in tops]
    total = functools.reduce(
        jnp.add, [s * side[:, offset + 1 : offset + 2] for s, side in zip(scales, sides)]
    )
    acc = functools.reduce(
        jnp.add, [s * x_ref[:, 0:features] for x_ref, s in zip(part_refs, scales)]
    )
    out = hidden_ref[...] + acc * (1.0 / total)
    out_ref[...] = out.reshape(out_ref.shape).astype(BF16)


def finish(parts, hidden, shape):
    return pl.pallas_call(
        finish_kernel,
        out_shape=jax.ShapeDtypeStruct(shape, BF16),
        compiler_params=params(),
        name="finish",
    )(hidden, *parts)


def join_rounds(features, one, other):
    tile, offset = side_place(features, 2)
    at = tile + offset
    top = jnp.maximum(one[..., at : at + 1], other[..., at : at + 1])
    scales = [jnp.exp(part[..., at : at + 1] - top) for part in (one, other)]
    joined = one * scales[0] + other * scales[1]
    return jnp.where(jnp.arange(one.shape[-1]) == at, top, joined)


def send(x, axis, distance):
    count = lax.axis_size(axis)
    return lax.ppermute(x, axis, [(i, (i + distance) % count) for i in range(count)])


def swap(x, axis):
    return lax.all_to_all(x, axis, split_axis=0, concat_axis=0, tiled=True)


def local(
    queries,
    new_key_value,
    key_value_cache,
    page_table,
    cache_len,
    routes,
    residual,
    w_out,
    norm_gain,
    w_router,
    w_gate_up,
    w_down,
):
    exp_count = lax.axis_size("exp")
    seq_count = lax.axis_size("seq")
    exp_index = lax.axis_index("exp").astype(jnp.int32).reshape(1)
    seq_index = lax.axis_index("seq").astype(jnp.int32).reshape(1)
    steps, requests, width = queries.shape
    tokens = steps * requests
    features = w_out.shape[1]
    page_rows = key_value_cache.shape[2]
    pool = key_value_cache.reshape(-1, page_rows, 2, KV_WIDTH)

    shares = attend(queries, new_key_value, pool, page_table, cache_len, seq_index)
    shares = swap(shares.reshape(seq_count, -1, KV_WIDTH + LANES), "seq")
    attn = join(shares)
    w_gate_up, attn = lax.optimization_barrier((w_gate_up, attn))
    attn = swap(attn, "seq")
    gate_up_weights = w_gate_up.transpose(0, 2, 1, 3)
    gate_up_weights, attn = lax.optimization_barrier((gate_up_weights, attn))
    hidden, outgoing = hidden_state(attn, residual, w_out, norm_gain, routes)
    incoming = [outgoing] + [send(outgoing, "exp", k) for k in range(1, exp_count)]
    rows = -(-ROUND_ROWS // (16 * seq_count)) * 16 * seq_count

    def one_round(turn):
        parts, pick, ranges, first, most = gate_up(
            exp_index, incoming, gate_up_weights, w_router, rows, seq_count, turn
        )
        made = swap(inner(swap(parts, "seq")), "seq")
        return down(first, ranges, pick, made, w_down, exp_count), most

    made, most = one_round(0)
    pairs = w_gate_up.shape[0] * exp_count * steps * CAP
    for turn in range(1, -(-pairs // rows)):
        made = lax.cond(
            most[0] > turn * rows,
            lambda made: tuple(
                join_rounds(features, *both) for both in zip(made, one_round(turn)[0])
            ),
            lambda made: made,
            made,
        )
    made = [made[0]] + [send(made[k], "exp", -k) for k in range(1, exp_count)]
    return finish(made, hidden, (steps, requests, features))


def solution(mesh):
    in_specs = (
        P(None, "exp", None),
        P(None, "exp", None, None),
        P("exp", "seq", None, None, None),
        P("exp", "seq"),
        P("exp"),
        P(None, "exp", None),
        P(None, "exp", "seq"),
        P(None, "seq"),
        P("seq"),
        P("seq", None),
        P("exp", "seq", None, None),
        P("exp", "seq", None),
    )
    out_specs = P(None, "exp", "seq")
    return jax.shard_map(local, mesh=mesh, in_specs=in_specs, out_specs=out_specs, check_vma=False)
```

```python
import functools

import jax
import jax.numpy as jnp
from jax import lax
from jax.experimental import pallas as pl
from jax.experimental.pallas import tpu as pltpu
from jax.sharding import PartitionSpec as P

D = 1536
QUERY_HEADS = 24
KEY_VALUE_HEADS = 8
HEAD_SIZE = 64
GROUP = QUERY_HEADS // KEY_VALUE_HEADS
KV_WIDTH = KEY_VALUE_HEADS * HEAD_SIZE
EXPERTS = 40
FF = 512
CAP = 4
LANES = 128
SIDE_KEYS = 2
ROUND_ROWS = 352
PIECES = 8
PIECE_WIDTH = FF // PIECES

NEG_FILL = -1e30
F32 = jnp.float32
BF16 = jnp.bfloat16
VMEM_LIMIT = 48 * 1024 * 1024
ATTEND_VMEM = 60 * 1024 * 1024


def iota(shape, dimension):
    return lax.broadcasted_iota(jnp.int32, shape, dimension)


def dot_nt(a, b):
    return lax.dot_general(a, b, (((1,), (1,)), ((), ())), preferred_element_type=F32)


def dot_tn(a, b):
    return lax.dot_general(a, b, (((0,), (0,)), ((), ())), preferred_element_type=F32)


def dot_nn(a, b):
    return lax.dot_general(a, b, (((1,), (0,)), ((), ())), preferred_element_type=F32)


def round16(x):
    return x.astype(BF16).astype(F32)


def swap_halves(x):
    return pltpu.roll(x, HEAD_SIZE, 1)


def tile_of(x, index):
    return x[:, index * LANES : (index + 1) * LANES]


def padded(width):
    return -(-width // LANES) * LANES


def params():
    return pltpu.CompilerParams(vmem_limit_bytes=VMEM_LIMIT)


def attend_kernel(
    classes, table_ref, len_ref, seq_ref, q_hbm, fresh_hbm, cache_ref, out_ref,
    page_ref, split_ref, q_ref, fresh_ref, query_ref, new_ref, order_ref, sems, small_sems,
):
    steps, requests, _ = q_ref.shape
    page_rows = cache_ref.shape[1]
    pages = table_ref.shape[1]
    span = pages * page_rows
    first = seq_ref[0] * span
    small = [
        pltpu.make_async_copy(q_hbm, q_ref, small_sems.at[0]),
        pltpu.make_async_copy(fresh_hbm, fresh_ref, small_sems.at[1]),
    ]
    for one in small:
        one.start()

    held = [jnp.clip(len_ref[r] - first, 0, span) for r in range(requests)]
    for r in range(requests):
        ahead = jnp.int32(0)
        for other in range(requests):
            if other != r:
                longer = held[other] >= held[r] if other < r else held[other] > held[r]
                ahead = ahead + longer.astype(jnp.int32)
        order_ref[ahead] = r

    def copy(r, page):
        at = r * pages + page
        return pltpu.make_async_copy(cache_ref.at[table_ref[r, page]], page_ref.at[at], sems.at[at])

    def needed(r, low):
        return len_ref[r] - first > low * page_rows

    bounds = list(zip((0,) + classes[:-1], classes))

    def start(pair, carry):
        both = order_ref[2 * pair], order_ref[2 * pair + 1]
        for low, high in bounds:

            @pl.when(needed(both[0], low))
            def _():
                for page in range(low, high):
                    for r in both:
                        copy(r, page).start()

        return carry

    lax.fori_loop(0, requests // 2, start, 0)
    for one in small:
        one.wait()

    low = iota((requests, LANES), 1) < HEAD_SIZE
    for t in range(steps):
        q = q_ref[t].astype(F32) * 0.125
        for g in range(GROUP):
            for j in range(KV_WIDTH // LANES):
                one = tile_of(q, (6 * j + g) // 2)
                two = tile_of(q, (6 * j + 3 + g) // 2)
                if g % 2 == 0:
                    tile = jnp.where(low, one, two)
                else:
                    tile = swap_halves(jnp.where(low, two, one))
                query_ref[t * GROUP + g, :, j * LANES : (j + 1) * LANES] = tile
        new_ref[t] = fresh_ref[t].reshape(2 * requests, KV_WIDTH).astype(F32)

    rows = steps * GROUP * KEY_VALUE_HEADS
    own = iota((rows, KV_WIDTH), 1) // HEAD_SIZE == iota((rows, KV_WIDTH), 0) % KEY_VALUE_HEADS
    lane = iota((rows, LANES), 1)
    head = iota((rows, LANES), 0) % KEY_VALUE_HEADS
    row_step = iota((rows, 16), 0) // (GROUP * KEY_VALUE_HEADS)
    kept = jnp.logical_and(iota((rows, 16), 1) <= row_step, seq_ref[0] == 0)
    fresh_bias = jnp.where(kept, 0.0, NEG_FILL)

    def fresh_rows(r, which):
        found = [new_ref[u, pl.ds(2 * r + which, 1), :] for u in range(steps)]
        return jnp.concatenate(found + [jnp.zeros((16 - steps, KV_WIDTH), F32)], axis=0).astype(BF16)

    def attend_pages(r, slot, count):
        spread = jnp.concatenate(
            [
                jnp.broadcast_to(query_ref[i, pl.ds(r, 1), :], (KEY_VALUE_HEADS, KV_WIDTH))
                for i in range(steps * GROUP)
            ],
            axis=0,
        )
        spread = jnp.where(own, spread, 0.0).astype(BF16)
        halves = ([], [])
        for page in range(count):
            block = page_ref[r * pages + page].reshape(2 * page_rows, KV_WIDTH).astype(F32)
            for j in range(KV_WIDTH // LANES):
                split_ref[slot, page, j] = tile_of(block, j)
            for which in range(2):
                tiles = [
                    split_ref[slot, page, j, pl.ds(which, page_rows, 2), :]
                    for j in range(KV_WIDTH // LANES)
                ]
                halves[which].append(jnp.concatenate(tiles, axis=1).astype(BF16))
        keys, values = jnp.concatenate(halves[0], axis=0), jnp.concatenate(halves[1], axis=0)
        size = count * page_rows
        live = first + iota((1, size), 1) < len_ref[r]
        scores = dot_nt(spread, keys) + jnp.where(live, 0.0, NEG_FILL)
        fresh_scores = dot_nt(spread, fresh_rows(r, 0)) + fresh_bias
        largest = jnp.maximum(
            jnp.max(scores, axis=1, keepdims=True), jnp.max(fresh_scores, axis=1, keepdims=True)
        )
        weights = jnp.exp(scores - largest)
        fresh_weights = jnp.exp(fresh_scores - largest)
        total = jnp.sum(weights, axis=1, keepdims=True)
        total = total + jnp.sum(fresh_weights, axis=1, keepdims=True)
        acc = dot_nn(weights.astype(BF16), values)
        acc = acc + dot_nn(fresh_weights.astype(BF16), fresh_rows(r, 1))
        acc = jnp.where(own, acc * (1.0 / total), 0.0)
        acc = jnp.sum(acc.reshape(steps * GROUP, KEY_VALUE_HEADS, KV_WIDTH), axis=1)
        level = jnp.where(needed(r, 0), largest + jnp.log(total), NEG_FILL)
        high = round16(level)
        middle = round16(level - high)
        side = jnp.where(lane == head, high, 0.0)
        side = jnp.where(lane == head + 8, middle, side)
        side = jnp.where(lane == head + 16, level - high - middle, side)
        side = jnp.sum(side.reshape(steps * GROUP, KEY_VALUE_HEADS, LANES), axis=1)
        return acc.astype(BF16), side.astype(BF16)

    def one_pair(pair, carry):
        both = order_ref[2 * pair], order_ref[2 * pair + 1]
        for low, high in bounds:
            enough = needed(both[0], low)
            if high < pages:
                enough = jnp.logical_and(enough, jnp.logical_not(needed(both[0], high)))

            @pl.when(enough)
            def _():
                for page in range(high):
                    for r in both:
                        copy(r, page).wait()
                made = [attend_pages(r, slot, high) for slot, r in enumerate(both)]
                for r, (acc, side) in zip(both, made):
                    out_ref[r, :, 0:KV_WIDTH] = acc
                    out_ref[r, :, KV_WIDTH : KV_WIDTH + LANES] = side

        @pl.when(jnp.logical_not(needed(both[0], 0)))
        def _():
            empty = jnp.where(iota((steps * GROUP, LANES), 1) < KEY_VALUE_HEADS, NEG_FILL, 0.0)
            for r in both:
                out_ref[r, :, 0:KV_WIDTH] = jnp.zeros((steps * GROUP, KV_WIDTH), BF16)
                out_ref[r, :, KV_WIDTH : KV_WIDTH + LANES] = empty.astype(BF16)

        return carry

    lax.fori_loop(0, requests // 2, one_pair, 0)


def attend(queries, new_key_value, cache, page_table, cache_len, seq_index):
    steps, requests, _ = queries.shape
    pages = page_table.shape[1]
    page_rows = cache.shape[1]
    classes = tuple(c for c in (2, 4) if c < pages) + (pages,)
    smem, hbm = pl.BlockSpec(memory_space=pltpu.SMEM), pl.BlockSpec(memory_space=pl.ANY)
    return pl.pallas_call(
        functools.partial(attend_kernel, classes),
        in_specs=[smem] * 3 + [hbm] * 3,
        out_shape=jax.ShapeDtypeStruct((requests, steps * GROUP, KV_WIDTH + LANES), BF16),
        scratch_shapes=[
            pltpu.VMEM((requests * pages, page_rows, 2, KV_WIDTH), BF16),
            pltpu.VMEM((2, pages, KV_WIDTH // LANES, 2 * page_rows, LANES), F32),
            pltpu.VMEM(queries.shape, BF16),
            pltpu.VMEM(new_key_value.shape, BF16),
            pltpu.VMEM((steps * GROUP, requests, KV_WIDTH), F32),
            pltpu.VMEM((steps, 2 * requests, KV_WIDTH), F32),
            pltpu.SMEM((requests,), jnp.int32),
            pltpu.SemaphoreType.DMA((requests * pages,)),
            pltpu.SemaphoreType.DMA((2,)),
        ],
        compiler_params=pltpu.CompilerParams(vmem_limit_bytes=ATTEND_VMEM),
        name="attend",
    )(page_table, cache_len, seq_index, queries, new_key_value, cache)


def join_kernel(x_ref, out_ref):
    blocks, rows, _ = x_ref.shape
    tokens = rows // GROUP
    levels = []
    for b in range(blocks):
        side = x_ref[b, :, KV_WIDTH : KV_WIDTH + LANES].astype(F32)
        levels.append(side + pltpu.roll(side, LANES - 8, 1) + pltpu.roll(side, LANES - 16, 1))
    largest = functools.reduce(jnp.maximum, levels)
    weights = [jnp.exp(level - largest) for level in levels]
    inverse = 1.0 / functools.reduce(jnp.add, weights)
    low = iota((rows, LANES), 1) < HEAD_SIZE
    acc = [jnp.zeros((rows, LANES), F32) for _ in range(KV_WIDTH // LANES)]
    for b in range(blocks):
        share = weights[b] * inverse
        for j in range(KV_WIDTH // LANES):
            factor = jnp.where(low, share[:, 2 * j : 2 * j + 1], share[:, 2 * j + 1 : 2 * j + 2])
            acc[j] = acc[j] + factor * x_ref[b, :, j * LANES : (j + 1) * LANES].astype(F32)

    def piece(head, half):
        k, g = head // GROUP, head % GROUP
        tile = jnp.concatenate(
            [acc[k // 2][t * GROUP + g : t * GROUP + g + 1] for t in range(tokens)], axis=0
        )
        return tile if k % 2 == half else swap_halves(tile)

    low_tokens = iota((tokens, LANES), 1) < HEAD_SIZE
    for m in range(QUERY_HEADS // 2):
        tile = jnp.where(low_tokens, piece(2 * m, 0), piece(2 * m + 1, 1)).astype(BF16)
        for b in range(blocks):
            out_ref[b, :, m * LANES : (m + 1) * LANES] = tile


def join(parts):
    blocks, rows, _ = parts.shape
    return pl.pallas_call(
        join_kernel,
        out_shape=jax.ShapeDtypeStruct((blocks, rows // GROUP, QUERY_HEADS * HEAD_SIZE), BF16),
        compiler_params=params(),
        name="join",
    )(parts)


def side_place(features, count):
    tile, offset = features // LANES * LANES, features % LANES
    return (tile, offset) if offset and offset + count <= LANES else (padded(features), 0)


def hidden_kernel(attn_ref, residual_ref, w_ref, gain_ref, routes_ref, hidden_ref, out_ref, wide_ref):
    steps, requests, features = residual_ref.shape
    tokens = steps * requests
    blocks = [attn_ref[b].astype(F32) for b in range(attn_ref.shape[0])]
    attn = jnp.concatenate(blocks, axis=0).astype(BF16)
    row, column = iota((tokens, tokens), 0), iota((tokens, tokens), 1)
    reorder = jnp.logical_and(row % requests == column // steps, row // requests == column % steps)
    attn = dot_nn(reorder.astype(F32).astype(BF16), attn).astype(BF16)
    residual = residual_ref[...].astype(F32).reshape(tokens, features)
    hidden = residual + dot_nt(attn, w_ref[...])
    hidden_ref[...] = hidden
    squares = jnp.sum(hidden * hidden, axis=1, keepdims=True)
    tile, offset = side_place(features, SIDE_KEYS + EXPERTS)
    wide_ref[...] = jnp.zeros_like(wide_ref)
    wide_ref[:, 0:features] = hidden * gain_ref[...]
    routes = routes_ref[...].reshape(tokens, routes_ref.shape[2])
    lane = iota((tokens, LANES), 1) - offset
    side = wide_ref[:, tile : tile + LANES]
    for k in range(routes.shape[1]):
        side = jnp.where(lane == routes[:, k : k + 1] + SIDE_KEYS, 1.0, side)
    high = round16(squares)
    side = jnp.where(lane == 0, high, side)
    wide_ref[:, tile : tile + LANES] = jnp.where(lane == 1, squares - high, side)
    out_ref[...] = wide_ref[...].astype(BF16)


def hidden_state(attn, residual, w_out, gain, routes):
    steps, requests, features = residual.shape
    tokens = steps * requests
    wide = side_place(features, SIDE_KEYS + EXPERTS)[0] + LANES
    return pl.pallas_call(
        hidden_kernel,
        out_shape=(
            jax.ShapeDtypeStruct((tokens, features), F32),
            jax.ShapeDtypeStruct((tokens, wide), BF16),
        ),
        scratch_shapes=[pltpu.VMEM((tokens, wide), F32)],
        compiler_params=params(),
        name="hidden",
    )(attn, residual, w_out.T, gain.reshape(1, features), routes)


def window_start(first, rows, window):
    return pl.multiple_of(jnp.clip(first // 16 * 16, 0, rows - window), 16)


def gate_up_kernel(
    features, local, turn, sources, parts, where_ref, w_ref, router_ref, *refs,
):
    part_refs, refs = refs[:sources], refs[sources:]
    out_refs, refs = refs[: len(parts)], refs[len(parts) :]
    pick_ref, range_ref, first_ref, most_ref, x_ref, row_ref, acc_ref = refs
    total = x_ref.shape[0]
    for e, part_ref in enumerate(part_refs):
        x_ref[e * (total // sources) : (e + 1) * (total // sources)] = part_ref[...]
    rows = pick_ref.shape[1]
    width = w_ref.shape[3]
    window = total // 2 + 16
    tile, offset = side_place(features, SIDE_KEYS + EXPERTS)
    me = where_ref[0]
    own_side = x_ref[:, tile : tile + LANES].astype(F32)
    lane = iota((total, LANES), 1)
    flags = pltpu.roll(own_side, LANES - offset - SIDE_KEYS, 1)
    flags = jnp.where(lane < EXPERTS, flags, 0.0)
    owners = EXPERTS // local
    counts = jnp.sum(flags, axis=0, keepdims=True)
    most = jnp.int32(0)
    for o in range(owners):
        held = jnp.logical_and(lane[0:1] >= o * local, lane[0:1] < (o + 1) * local)
        most = jnp.maximum(most, jnp.sum(jnp.where(held, counts, 0.0)).astype(jnp.int32))
    most_ref[0] = most
    mine = pltpu.roll(flags, lax.rem(LANES - me * local, LANES), 1)
    mine = jnp.where(lane < local, mine, 0.0)
    mine16 = mine.astype(BF16)
    row, column = iota((total, total), 0), iota((total, total), 1)
    earlier = (column < row).astype(F32).astype(BF16)
    ranks = dot_nn(earlier, mine16)
    counts = jnp.sum(mine, axis=0, keepdims=True)
    before = (iota((LANES, LANES), 0) < iota((LANES, LANES), 1)).astype(F32).astype(BF16)
    first = dot_nn(jnp.broadcast_to(counts, (8, LANES)).astype(BF16), before)[0:1] - turn * rows
    place = jnp.where(mine > 0.0, first + ranks, -1.0).astype(jnp.int32)
    at = iota((total, rows), 1)
    pick = jnp.zeros((total, rows), F32)
    for j in range(local):
        pick = jnp.where(at == place[:, j : j + 1], 1.0, pick)
    pick = pick.astype(BF16)
    pick_ref[...] = pick
    ranges = jnp.where(iota((16, LANES), 0) < 8, first, first + counts)
    ranges = jnp.concatenate([ranges[0:8], ranges[8:16]] + [jnp.zeros((LANES - 16, LANES), F32)], axis=0)
    ranges = ranges.T
    range_ref[...] = ranges[0:16]
    row_ref[...] = dot_tn(pick, x_ref[...]).astype(BF16)
    acc_ref[...] = jnp.zeros_like(acc_ref)
    for j in range(local):
        start_row = jnp.sum(first[:, j : j + 1]).astype(jnp.int32)
        first_ref[j] = start_row
        start = window_start(start_row, rows, window)
        part = row_ref[pl.ds(start, window), 0:features]
        fresh = start + iota((window, width), 0) >= start_row
        for half in range(2):
            into = (pl.ds(start, window), slice(half * width, (half + 1) * width))
            made = dot_nn(part, w_ref[j, half])
            acc_ref[into] = jnp.where(fresh, made, acc_ref[into])
    logits = dot_nt(router_ref[...], x_ref[:, 0:features])
    high = round16(logits)
    both = jnp.concatenate([high, logits - high], axis=0).astype(BF16)
    both = dot_nn(both, pick)
    turned = jnp.zeros((EXPERTS, rows), jnp.bool_)
    expert = iota((EXPERTS, rows), 0) - me * local
    where_row = iota((EXPERTS, rows), 1).astype(F32)
    for j in range(local):
        inside = jnp.logical_and(
            where_row >= first[:, j : j + 1], where_row < (first + counts)[:, j : j + 1]
        )
        turned = jnp.logical_or(turned, jnp.logical_and(inside, expert == j))
    squares = dot_tn(own_side.astype(BF16), pick)
    side = jnp.concatenate(
        [
            jnp.sum(jnp.where(turned, both[0:EXPERTS], 0.0), axis=0, keepdims=True),
            jnp.sum(jnp.where(turned, both[EXPERTS : 2 * EXPERTS], 0.0), axis=0, keepdims=True),
            squares[offset : offset + 2],
            jnp.zeros((12, rows), F32),
        ],
        axis=0,
    )
    begin = 0
    for part, out_ref in zip(parts, out_refs):
        blocks = out_ref.shape[0]
        share = part * PIECES // blocks
        low = iota((share, LANES), 1) < PIECE_WIDTH
        for b in range(blocks):
            piece, start = b % PIECES, begin + b // PIECES * share
            tile = piece // 2 * LANES
            gate = acc_ref[start : start + share, tile : tile + LANES]
            up = acc_ref[start : start + share, width + tile : width + tile + LANES]
            if piece % 2 == 0:
                made = jnp.where(low, gate, swap_halves(up))
            else:
                made = jnp.where(low, swap_halves(gate), up)
            out_ref[b, 0:share, :] = made.astype(BF16)
            if piece == 0:
                strips = []
                for at in range(0, share, LANES):
                    size = min(LANES, share - at)
                    strip = side[0:4, start + at : start + at + size]
                    if size < LANES:
                        strip = jnp.concatenate([strip, jnp.zeros((4, LANES - size), F32)], axis=1)
                    strips.append(strip)
                strips.append(jnp.zeros((16 - 4 * len(strips), LANES), F32))
                strips = jnp.concatenate(strips, axis=0).astype(BF16)
            out_ref[b, share : share + 16, :] = strips
        begin += part


def gate_up(exp_index, tokens, weights, w_router, parts, blocks, turn):
    local, _, features, width = weights.shape
    sources, wide = len(tokens), tokens[0].shape[1]
    total, rows = sources * tokens[0].shape[0], sum(parts)
    smem, vmem = pl.BlockSpec(memory_space=pltpu.SMEM), pl.BlockSpec(memory_space=pltpu.VMEM)
    return pl.pallas_call(
        functools.partial(gate_up_kernel, features, local, turn, sources, parts),
        in_specs=[smem] + [vmem] * (2 + sources),
        out_specs=(vmem,) * len(parts) + (vmem, vmem, smem, smem),
        out_shape=tuple(
            jax.ShapeDtypeStruct((blocks, part * PIECES // blocks + 16, LANES), BF16) for part in parts
        )
        + (
            jax.ShapeDtypeStruct((total, rows), BF16),
            jax.ShapeDtypeStruct((16, LANES), F32),
            jax.ShapeDtypeStruct((16,), jnp.int32),
            jax.ShapeDtypeStruct((1,), jnp.int32),
        ),
        scratch_shapes=[
            pltpu.VMEM((total, wide), BF16),
            pltpu.VMEM((rows, wide), BF16),
            pltpu.VMEM((rows, 2 * width), F32),
        ],
        compiler_params=params(),
        name="gate_up",
    )(exp_index, weights, w_router.T, *tokens)


def inner_kernel(x_ref, out_ref, logit_ref):
    blocks, height, _ = x_ref.shape
    share = height - 16
    half = share // 2

    def total(start, size):
        added = x_ref[0, start : start + size].astype(F32)
        for b in range(1, blocks):
            added = added + x_ref[b, start : start + size].astype(F32)
        return added

    side = total(share, 16)
    columns, logits = [], []
    for strip in range(-(-share // LANES)):
        values = side[4 * strip : 4 * strip + 4]
        inverse = lax.rsqrt((values[2:3] + values[3:4]) * (1.0 / D) + 1e-6)
        logits.append((values[0:1] + values[1:2]) * inverse)
        columns.append(jnp.broadcast_to(inverse, (LANES, LANES)).T)
    logit_ref[...] = jnp.concatenate(logits + [jnp.zeros((8 - len(logits), LANES), F32)], axis=0)
    scaled = total(0, share) * jnp.concatenate(columns, axis=0)[0:share]
    made = scaled / (1.0 + jnp.exp(-scaled)) * swap_halves(scaled)
    low = iota((half, LANES), 1) < PIECE_WIDTH
    made = jnp.where(low, made[0:half], swap_halves(made[half:share])).astype(BF16)
    for b in range(blocks):
        out_ref[b] = made


def inner(parts):
    blocks, height, _ = parts.shape
    return pl.pallas_call(
        inner_kernel,
        out_shape=(
            jax.ShapeDtypeStruct((blocks, (height - 16) // 2, LANES), BF16),
            jax.ShapeDtypeStruct((8, LANES), F32),
        ),
        compiler_params=params(),
        name="inner",
    )(parts)


def down_kernel(features, local, parts, first_ref, range_ref, pick_ref, w_ref, *refs):
    part_refs, logit_refs, refs = refs[: len(parts)], refs[len(parts) : 2 * len(parts)], refs[2 * len(parts) :]
    out_refs, (row_ref, made_ref) = refs[:-2], refs[-2:]
    total, rows = pick_ref.shape
    width = w_ref.shape[2]
    window = total // 2 + 16
    begin, logit = 0, []
    for part, x_ref, logit_ref in zip(parts, part_refs, logit_refs):
        blocks, half, _ = x_ref.shape
        share = 2 * half
        low = iota((half, LANES), 1) < PIECE_WIDTH
        for b in range(0, blocks, 2):
            start, tile = begin + b // PIECES * share, b % PIECES // 2 * LANES
            one, two = x_ref[b].astype(F32), x_ref[b + 1].astype(F32)
            above = jnp.where(low, one, swap_halves(two)).astype(BF16)
            below = jnp.where(low, swap_halves(one), two).astype(BF16)
            row_ref[start : start + half, tile : tile + LANES] = above
            row_ref[start + half : start + share, tile : tile + LANES] = below
        for piece in range(blocks // PIECES):
            for strip in range(-(-share // LANES)):
                size = min(LANES, share - strip * LANES)
                logit.append(logit_ref[piece, strip : strip + 1, 0:size])
        begin += part
    made_ref[...] = jnp.zeros_like(made_ref)
    for j in range(local):
        start_row = first_ref[j]
        start = window_start(start_row, rows, window)
        made = dot_nt(row_ref[pl.ds(start, window), :], w_ref[j])
        fresh = start + iota((window, features), 0) >= start_row
        into = (pl.ds(start, window), slice(0, features))
        made_ref[into] = jnp.where(fresh, made, made_ref[into])
    logit = jnp.concatenate(logit, axis=1)
    high = round16(logit)
    middle = round16(logit - high)
    pick = pick_ref[...]
    where_row = iota((16, rows), 1).astype(F32)
    inside = jnp.logical_and(where_row >= range_ref[:, 0:1], where_row < range_ref[:, 8:9])
    inside = jnp.logical_and(inside, iota((16, rows), 0) < local)
    spread = [jnp.where(inside, part, 0.0) for part in (high, middle, logit - high - middle)]
    spread.append(inside.astype(F32))
    found = dot_nt(jnp.concatenate(spread, axis=0).astype(BF16), pick)
    valid = found[48:64] > 0.5
    logits = jnp.where(valid, found[0:16] + found[16:32] + found[32:48], NEG_FILL)
    top = jnp.max(logits, axis=0, keepdims=True)
    weights = jnp.where(valid, jnp.exp(logits - top), 0.0)
    summed = jnp.sum(weights, axis=0, keepdims=True)
    high = round16(weights)
    both = dot_nn(jnp.concatenate([high, weights - high], axis=0).astype(BF16), pick)
    weight = jnp.sum(jnp.where(inside, both[0:16] + both[16:32], 0.0), axis=0, keepdims=True)
    column = jnp.broadcast_to(weight, (LANES, rows)).T[:, 0:1]
    acc = dot_nn(pick, (made_ref[...] * column).astype(BF16))
    tile, offset = side_place(features, 2)
    pair = jnp.where(iota((LANES, total), 0) == 0, top, summed).T
    tokens = total // len(out_refs)
    for e, out_ref in enumerate(out_refs):
        at = slice(e * tokens, (e + 1) * tokens)
        out_ref[...] = acc[at]
        lane = iota((tokens, LANES), 1) - offset
        side = jnp.where(lane == 0, pair[at, 0:1], acc[at, tile : tile + LANES])
        out_ref[:, tile : tile + LANES] = jnp.where(lane == 1, pair[at, 1:2], side)


def down(first, ranges, pick, parts, made, logits, weights, exp_count):
    local, features, width = weights.shape
    total, rows = pick.shape
    wide = side_place(features, 2)[0] + LANES
    smem, vmem = pl.BlockSpec(memory_space=pltpu.SMEM), pl.BlockSpec(memory_space=pltpu.VMEM)
    return pl.pallas_call(
        functools.partial(down_kernel, features, local, parts),
        in_specs=[smem] + [vmem] * (3 + 2 * len(parts)),
        out_shape=(jax.ShapeDtypeStruct((total // exp_count, wide), F32),) * exp_count,
        scratch_shapes=[pltpu.VMEM((rows, width), BF16), pltpu.VMEM((rows, wide), F32)],
        compiler_params=params(),
        name="down",
    )(first, ranges, pick, weights, *made, *logits)


def finish_kernel(hidden_ref, *refs):
    part_refs, out_ref = refs[:-1], refs[-1]
    features = hidden_ref.shape[1]
    tile, offset = side_place(features, 2)
    sides = [x_ref[:, tile : tile + LANES] for x_ref in part_refs]
    tops = [side[:, offset : offset + 1] for side in sides]
    top = functools.reduce(jnp.maximum, tops)
    scales = [jnp.exp(one - top) for one in tops]
    total = functools.reduce(
        jnp.add, [s * side[:, offset + 1 : offset + 2] for s, side in zip(scales, sides)]
    )
    acc = functools.reduce(
        jnp.add, [s * x_ref[:, 0:features] for x_ref, s in zip(part_refs, scales)]
    )
    out = hidden_ref[...] + acc * (1.0 / total)
    out_ref[...] = out.reshape(out_ref.shape).astype(BF16)


def finish(parts, hidden, shape):
    return pl.pallas_call(
        finish_kernel,
        out_shape=jax.ShapeDtypeStruct(shape, BF16),
        compiler_params=params(),
        name="finish",
    )(hidden, *parts)


def join_rounds(features, one, other):
    tile, offset = side_place(features, 2)
    at = tile + offset
    top = jnp.maximum(one[..., at : at + 1], other[..., at : at + 1])
    scales = [jnp.exp(part[..., at : at + 1] - top) for part in (one, other)]
    joined = one * scales[0] + other * scales[1]
    return jnp.where(jnp.arange(one.shape[-1]) == at, top, joined)


def send(x, axis, distance):
    count = lax.axis_size(axis)
    return lax.ppermute(x, axis, [(i, (i + distance) % count) for i in range(count)])


def swap(x, axis):
    return lax.all_to_all(x, axis, split_axis=0, concat_axis=0, tiled=True)


def local(
    queries,
    new_key_value,
    key_value_cache,
    page_table,
    cache_len,
    routes,
    residual,
    w_out,
    norm_gain,
    w_router,
    w_gate_up,
    w_down,
):
    exp_count = lax.axis_size("exp")
    seq_count = lax.axis_size("seq")
    exp_index = lax.axis_index("exp").astype(jnp.int32).reshape(1)
    seq_index = lax.axis_index("seq").astype(jnp.int32).reshape(1)
    steps, requests, width = queries.shape
    tokens = steps * requests
    features = w_out.shape[1]
    page_rows = key_value_cache.shape[2]
    pool = key_value_cache.reshape(-1, page_rows, 2, KV_WIDTH)

    shares = attend(queries, new_key_value, pool, page_table, cache_len, seq_index)
    shares = swap(shares.reshape(seq_count, -1, KV_WIDTH + LANES), "seq")
    attn = join(shares)
    w_gate_up, attn = lax.optimization_barrier((w_gate_up, attn))
    attn = swap(attn, "seq")
    gate_up_weights = w_gate_up.transpose(0, 2, 1, 3)
    gate_up_weights, attn = lax.optimization_barrier((gate_up_weights, attn))
    hidden, outgoing = hidden_state(attn, residual, w_out, norm_gain, routes)
    incoming = [outgoing] + [send(outgoing, "exp", k) for k in range(1, exp_count)]
    pieces = seq_count // PIECES
    units = -(-ROUND_ROWS // (32 * pieces))
    parts = tuple(32 * pieces * count for count in (-(-units // 2), units // 2))
    rows = sum(parts)

    def logits_of(row_logits):
        if pieces == 1:
            return row_logits[None]
        return lax.all_gather(row_logits, "seq")[::PIECES]

    def one_round(turn):
        *partial, pick, ranges, first, most = gate_up(
            exp_index, incoming, gate_up_weights, w_router, parts, seq_count, turn
        )
        made, logits = zip(*[inner(swap(part, "seq")) for part in partial])
        made = [swap(part, "seq") for part in made]
        logits = [logits_of(part) for part in logits]
        return down(first, ranges, pick, parts, made, logits, w_down, exp_count), most

    made, most = one_round(0)
    pairs = w_gate_up.shape[0] * exp_count * steps * CAP
    for turn in range(1, -(-pairs // rows)):
        made = lax.cond(
            most[0] > turn * rows,
            lambda made: tuple(
                join_rounds(features, *both) for both in zip(made, one_round(turn)[0])
            ),
            lambda made: made,
            made,
        )
    made = [made[0]] + [send(made[k], "exp", -k) for k in range(1, exp_count)]
    return finish(made, hidden, (steps, requests, features))


def solution(mesh):
    in_specs = (
        P(None, "exp", None),
        P(None, "exp", None, None),
        P("exp", "seq", None, None, None),
        P("exp", "seq"),
        P("exp"),
        P(None, "exp", None),
        P(None, "exp", "seq"),
        P(None, "seq"),
        P("seq"),
        P("seq", None),
        P("exp", "seq", None, None),
        P("exp", "seq", None),
    )
    out_specs = P(None, "exp", "seq")
    return jax.shard_map(local, mesh=mesh, in_specs=in_specs, out_specs=out_specs, check_vma=False)
```

```python
import functools

import jax
import jax.numpy as jnp
from jax import lax
from jax.experimental import pallas as pl
from jax.experimental.pallas import tpu as pltpu
from jax.sharding import PartitionSpec as P

D = 1536
QUERY_HEADS = 24
KEY_VALUE_HEADS = 8
HEAD_SIZE = 64
GROUP = QUERY_HEADS // KEY_VALUE_HEADS
KV_WIDTH = KEY_VALUE_HEADS * HEAD_SIZE
EXPERTS = 40
FF = 512
CAP = 4
LANES = 128
SIDE_KEYS = 2
ROUND_ROWS = 352
PIECES = 8
PIECE_WIDTH = FF // PIECES

NEG_FILL = -1e30
F32 = jnp.float32
BF16 = jnp.bfloat16
VMEM_LIMIT = 48 * 1024 * 1024
ATTEND_VMEM = 60 * 1024 * 1024


def iota(shape, dimension):
    return lax.broadcasted_iota(jnp.int32, shape, dimension)


def dot_nt(a, b):
    return lax.dot_general(a, b, (((1,), (1,)), ((), ())), preferred_element_type=F32)


def dot_tn(a, b):
    return lax.dot_general(a, b, (((0,), (0,)), ((), ())), preferred_element_type=F32)


def dot_nn(a, b):
    return lax.dot_general(a, b, (((1,), (0,)), ((), ())), preferred_element_type=F32)


def round16(x):
    return x.astype(BF16).astype(F32)


def swap_halves(x):
    return pltpu.roll(x, HEAD_SIZE, 1)


def tile_of(x, index):
    return x[:, index * LANES : (index + 1) * LANES]


def padded(width):
    return -(-width // LANES) * LANES


def params():
    return pltpu.CompilerParams(vmem_limit_bytes=VMEM_LIMIT)


def attend_kernel(
    classes, devices, table_ref, len_ref, seq_ref, q_hbm, fresh_hbm, cache_ref, *refs,
):
    out_refs, refs = refs[:devices], refs[devices:]
    share_ref, page_ref, split_ref, q_ref, fresh_ref, query_ref, new_ref, order_ref, sems, small_sems = refs
    steps, requests, _ = q_ref.shape
    page_rows = cache_ref.shape[1]
    pages = table_ref.shape[1]
    span = pages * page_rows
    first = seq_ref[0] * span
    small = [
        pltpu.make_async_copy(q_hbm, q_ref, small_sems.at[0]),
        pltpu.make_async_copy(fresh_hbm, fresh_ref, small_sems.at[1]),
    ]
    for one in small:
        one.start()

    held = [jnp.clip(len_ref[r] - first, 0, span) for r in range(requests)]
    for r in range(requests):
        ahead = jnp.int32(0)
        for other in range(requests):
            if other != r:
                longer = held[other] >= held[r] if other < r else held[other] > held[r]
                ahead = ahead + longer.astype(jnp.int32)
        order_ref[ahead] = r

    share = share_ref.shape[1]
    per_request = steps * GROUP // share

    def put(r, acc, side):
        for i in range(per_request):
            at = r * per_request + i
            share_ref[at, :, 0:KV_WIDTH] = acc[i * share : (i + 1) * share]
            share_ref[at, :, KV_WIDTH : KV_WIDTH + LANES] = side[i * share : (i + 1) * share]

    def copy(r, page):
        at = r * pages + page
        return pltpu.make_async_copy(cache_ref.at[table_ref[r, page]], page_ref.at[at], sems.at[at])

    def needed(r, low):
        return len_ref[r] - first > low * page_rows

    bounds = list(zip((0,) + classes[:-1], classes))

    def start(pair, carry):
        both = order_ref[2 * pair], order_ref[2 * pair + 1]
        for low, high in bounds:

            @pl.when(needed(both[0], low))
            def _():
                for page in range(low, high):
                    for r in both:
                        copy(r, page).start()

        return carry

    lax.fori_loop(0, requests // 2, start, 0)
    for one in small:
        one.wait()

    low = iota((requests, LANES), 1) < HEAD_SIZE
    for t in range(steps):
        q = q_ref[t].astype(F32) * 0.125
        for g in range(GROUP):
            for j in range(KV_WIDTH // LANES):
                one = tile_of(q, (6 * j + g) // 2)
                two = tile_of(q, (6 * j + 3 + g) // 2)
                if g % 2 == 0:
                    tile = jnp.where(low, one, two)
                else:
                    tile = swap_halves(jnp.where(low, two, one))
                query_ref[t * GROUP + g, :, j * LANES : (j + 1) * LANES] = tile
        new_ref[t] = fresh_ref[t].reshape(2 * requests, KV_WIDTH).astype(F32)

    rows = steps * GROUP * KEY_VALUE_HEADS
    own = iota((rows, KV_WIDTH), 1) // HEAD_SIZE == iota((rows, KV_WIDTH), 0) % KEY_VALUE_HEADS
    lane = iota((rows, LANES), 1)
    head = iota((rows, LANES), 0) % KEY_VALUE_HEADS
    row_step = iota((rows, 16), 0) // (GROUP * KEY_VALUE_HEADS)
    kept = jnp.logical_and(iota((rows, 16), 1) <= row_step, seq_ref[0] == 0)
    fresh_bias = jnp.where(kept, 0.0, NEG_FILL)

    def fresh_rows(r, which):
        found = [new_ref[u, pl.ds(2 * r + which, 1), :] for u in range(steps)]
        return jnp.concatenate(found + [jnp.zeros((16 - steps, KV_WIDTH), F32)], axis=0).astype(BF16)

    def attend_pages(r, slot, count):
        spread = jnp.concatenate(
            [
                jnp.broadcast_to(query_ref[i, pl.ds(r, 1), :], (KEY_VALUE_HEADS, KV_WIDTH))
                for i in range(steps * GROUP)
            ],
            axis=0,
        )
        spread = jnp.where(own, spread, 0.0).astype(BF16)
        halves = ([], [])
        for page in range(count):
            block = page_ref[r * pages + page].reshape(2 * page_rows, KV_WIDTH).astype(F32)
            for j in range(KV_WIDTH // LANES):
                split_ref[slot, page, j] = tile_of(block, j)
            for which in range(2):
                tiles = [
                    split_ref[slot, page, j, pl.ds(which, page_rows, 2), :]
                    for j in range(KV_WIDTH // LANES)
                ]
                halves[which].append(jnp.concatenate(tiles, axis=1).astype(BF16))
        keys, values = jnp.concatenate(halves[0], axis=0), jnp.concatenate(halves[1], axis=0)
        size = count * page_rows
        live = first + iota((1, size), 1) < len_ref[r]
        scores = dot_nt(spread, keys) + jnp.where(live, 0.0, NEG_FILL)
        fresh_scores = dot_nt(spread, fresh_rows(r, 0)) + fresh_bias
        largest = jnp.maximum(
            jnp.max(scores, axis=1, keepdims=True), jnp.max(fresh_scores, axis=1, keepdims=True)
        )
        weights = jnp.exp(scores - largest)
        fresh_weights = jnp.exp(fresh_scores - largest)
        total = jnp.sum(weights, axis=1, keepdims=True)
        total = total + jnp.sum(fresh_weights, axis=1, keepdims=True)
        acc = dot_nn(weights.astype(BF16), values)
        acc = acc + dot_nn(fresh_weights.astype(BF16), fresh_rows(r, 1))
        acc = jnp.where(own, acc * (1.0 / total), 0.0)
        acc = jnp.sum(acc.reshape(steps * GROUP, KEY_VALUE_HEADS, KV_WIDTH), axis=1)
        level = jnp.where(needed(r, 0), largest + jnp.log(total), NEG_FILL)
        high = round16(level)
        middle = round16(level - high)
        side = jnp.where(lane == head, high, 0.0)
        side = jnp.where(lane == head + 8, middle, side)
        side = jnp.where(lane == head + 16, level - high - middle, side)
        side = jnp.sum(side.reshape(steps * GROUP, KEY_VALUE_HEADS, LANES), axis=1)
        return acc.astype(BF16), side.astype(BF16)

    def one_pair(pair, carry):
        both = order_ref[2 * pair], order_ref[2 * pair + 1]
        for low, high in bounds:
            enough = needed(both[0], low)
            if high < pages:
                enough = jnp.logical_and(enough, jnp.logical_not(needed(both[0], high)))

            @pl.when(enough)
            def _():
                for page in range(high):
                    for r in both:
                        copy(r, page).wait()
                made = [attend_pages(r, slot, high) for slot, r in enumerate(both)]
                for r, (acc, side) in zip(both, made):
                    put(r, acc, side)

        @pl.when(jnp.logical_not(needed(both[0], 0)))
        def _():
            empty = jnp.where(iota((steps * GROUP, LANES), 1) < KEY_VALUE_HEADS, NEG_FILL, 0.0)
            for r in both:
                put(r, jnp.zeros((steps * GROUP, KV_WIDTH), BF16), empty.astype(BF16))

        return carry

    lax.fori_loop(0, requests // 2, one_pair, 0)
    for k, out_ref in enumerate(out_refs):
        out_ref[...] = share_ref[lax.rem(seq_ref[0] + k, devices)]


def attend(queries, new_key_value, cache, page_table, cache_len, seq_index, devices):
    steps, requests, _ = queries.shape
    pages = page_table.shape[1]
    page_rows = cache.shape[1]
    classes = tuple(c for c in (2, 4) if c < pages) + (pages,)
    share = (requests * steps * GROUP // devices, KV_WIDTH + LANES)
    smem, hbm = pl.BlockSpec(memory_space=pltpu.SMEM), pl.BlockSpec(memory_space=pl.ANY)
    return pl.pallas_call(
        functools.partial(attend_kernel, classes, devices),
        in_specs=[smem] * 3 + [hbm] * 3,
        out_shape=(jax.ShapeDtypeStruct(share, BF16),) * devices,
        scratch_shapes=[
            pltpu.VMEM((devices,) + share, BF16),
            pltpu.VMEM((requests * pages, page_rows, 2, KV_WIDTH), BF16),
            pltpu.VMEM((2, pages, KV_WIDTH // LANES, 2 * page_rows, LANES), F32),
            pltpu.VMEM(queries.shape, BF16),
            pltpu.VMEM(new_key_value.shape, BF16),
            pltpu.VMEM((steps * GROUP, requests, KV_WIDTH), F32),
            pltpu.VMEM((steps, 2 * requests, KV_WIDTH), F32),
            pltpu.SMEM((requests,), jnp.int32),
            pltpu.SemaphoreType.DMA((requests * pages,)),
            pltpu.SemaphoreType.DMA((2,)),
        ],
        compiler_params=pltpu.CompilerParams(vmem_limit_bytes=ATTEND_VMEM),
        name="attend",
    )(page_table, cache_len, seq_index, queries, new_key_value, cache)


def join_kernel(*refs):
    x_refs, out_ref = refs[:-1], refs[-1]
    rows = x_refs[0].shape[0]
    tokens = rows // GROUP
    levels = []
    for x_ref in x_refs:
        side = x_ref[:, KV_WIDTH : KV_WIDTH + LANES].astype(F32)
        levels.append(side + pltpu.roll(side, LANES - 8, 1) + pltpu.roll(side, LANES - 16, 1))
    largest = functools.reduce(jnp.maximum, levels)
    weights = [jnp.exp(level - largest) for level in levels]
    inverse = 1.0 / functools.reduce(jnp.add, weights)
    low = iota((rows, LANES), 1) < HEAD_SIZE
    acc = [jnp.zeros((rows, LANES), F32) for _ in range(KV_WIDTH // LANES)]
    for x_ref, weight in zip(x_refs, weights):
        share = weight * inverse
        for j in range(KV_WIDTH // LANES):
            factor = jnp.where(low, share[:, 2 * j : 2 * j + 1], share[:, 2 * j + 1 : 2 * j + 2])
            acc[j] = acc[j] + factor * x_ref[:, j * LANES : (j + 1) * LANES].astype(F32)

    def piece(head, half):
        k, g = head // GROUP, head % GROUP
        tile = jnp.concatenate(
            [acc[k // 2][t * GROUP + g : t * GROUP + g + 1] for t in range(tokens)], axis=0
        )
        return tile if k % 2 == half else swap_halves(tile)

    low_tokens = iota((tokens, LANES), 1) < HEAD_SIZE
    for m in range(QUERY_HEADS // 2):
        tile = jnp.where(low_tokens, piece(2 * m, 0), piece(2 * m + 1, 1)).astype(BF16)
        out_ref[:, m * LANES : (m + 1) * LANES] = tile


def join(parts):
    rows = parts[0].shape[0]
    return pl.pallas_call(
        join_kernel,
        out_shape=jax.ShapeDtypeStruct((rows // GROUP, QUERY_HEADS * HEAD_SIZE), BF16),
        compiler_params=params(),
        name="join",
    )(*parts)


def side_place(features, count):
    tile, offset = features // LANES * LANES, features % LANES
    return (tile, offset) if offset and offset + count <= LANES else (padded(features), 0)


def hidden_kernel(seq_ref, residual_ref, w_ref, gain_ref, routes_ref, *refs):
    attn_refs, (hidden_ref, out_ref, wide_ref) = refs[:-3], refs[-3:]
    steps, requests, features = residual_ref.shape
    tokens = steps * requests
    attn = jnp.concatenate([ref[...].astype(F32) for ref in attn_refs], axis=0).astype(BF16)
    row, column = iota((tokens, tokens), 0), iota((tokens, tokens), 1)
    devices, share = len(attn_refs), attn_refs[0].shape[0]
    token = seq_ref[0] + devices - column // share
    token = jnp.where(token >= devices, token - devices, token) * share + column % share
    reorder = jnp.logical_and(row % requests == token // steps, row // requests == token % steps)
    attn = dot_nn(reorder.astype(F32).astype(BF16), attn).astype(BF16)
    residual = residual_ref[...].astype(F32).reshape(tokens, features)
    hidden = residual + dot_nt(attn, w_ref[...])
    hidden_ref[...] = hidden
    squares = jnp.sum(hidden * hidden, axis=1, keepdims=True)
    tile, offset = side_place(features, SIDE_KEYS + EXPERTS)
    wide_ref[...] = jnp.zeros_like(wide_ref)
    wide_ref[:, 0:features] = hidden * gain_ref[...]
    routes = routes_ref[...].reshape(tokens, routes_ref.shape[2])
    lane = iota((tokens, LANES), 1) - offset
    side = wide_ref[:, tile : tile + LANES]
    for k in range(routes.shape[1]):
        side = jnp.where(lane == routes[:, k : k + 1] + SIDE_KEYS, 1.0, side)
    high = round16(squares)
    side = jnp.where(lane == 0, high, side)
    wide_ref[:, tile : tile + LANES] = jnp.where(lane == 1, squares - high, side)
    out_ref[...] = wide_ref[...].astype(BF16)


def hidden_state(seq_index, attn, residual, w_out, gain, routes):
    steps, requests, features = residual.shape
    tokens = steps * requests
    wide = side_place(features, SIDE_KEYS + EXPERTS)[0] + LANES
    smem, vmem = pl.BlockSpec(memory_space=pltpu.SMEM), pl.BlockSpec(memory_space=pltpu.VMEM)
    return pl.pallas_call(
        hidden_kernel,
        in_specs=[smem] + [vmem] * (4 + len(attn)),
        out_shape=(
            jax.ShapeDtypeStruct((tokens, features), F32),
            jax.ShapeDtypeStruct((tokens, wide), BF16),
        ),
        scratch_shapes=[pltpu.VMEM((tokens, wide), F32)],
        compiler_params=params(),
        name="hidden",
    )(seq_index, residual, w_out.T, gain.reshape(1, features), routes, *attn)


def window_start(first, rows, window):
    return pl.multiple_of(jnp.clip(first // 16 * 16, 0, rows - window), 16)


def gate_up_kernel(
    features, local, turn, sources, devices, where_ref, seq_ref, w_ref, router_ref, *refs,
):
    part_refs, refs = refs[:sources], refs[sources:]
    out_refs, refs = refs[:devices], refs[devices:]
    pick_ref, range_ref, first_ref, most_ref, x_ref, row_ref, acc_ref, share_ref = refs
    total = x_ref.shape[0]
    for e, part_ref in enumerate(part_refs):
        x_ref[e * (total // sources) : (e + 1) * (total // sources)] = part_ref[...]
    rows = pick_ref.shape[1]
    width = w_ref.shape[3]
    window = total // 2 + 16
    tile, offset = side_place(features, SIDE_KEYS + EXPERTS)
    me = where_ref[0]
    own_side = x_ref[:, tile : tile + LANES].astype(F32)
    lane = iota((total, LANES), 1)
    flags = pltpu.roll(own_side, LANES - offset - SIDE_KEYS, 1)
    flags = jnp.where(lane < EXPERTS, flags, 0.0)
    owners = EXPERTS // local
    counts = jnp.sum(flags, axis=0, keepdims=True)
    most = jnp.int32(0)
    for o in range(owners):
        held = jnp.logical_and(lane[0:1] >= o * local, lane[0:1] < (o + 1) * local)
        most = jnp.maximum(most, jnp.sum(jnp.where(held, counts, 0.0)).astype(jnp.int32))
    most_ref[0] = most
    mine = pltpu.roll(flags, lax.rem(LANES - me * local, LANES), 1)
    mine = jnp.where(lane < local, mine, 0.0)
    mine16 = mine.astype(BF16)
    row, column = iota((total, total), 0), iota((total, total), 1)
    earlier = (column < row).astype(F32).astype(BF16)
    ranks = dot_nn(earlier, mine16)
    counts = jnp.sum(mine, axis=0, keepdims=True)
    before = (iota((LANES, LANES), 0) < iota((LANES, LANES), 1)).astype(F32).astype(BF16)
    first = dot_nn(jnp.broadcast_to(counts, (8, LANES)).astype(BF16), before)[0:1] - turn * rows
    place = jnp.where(mine > 0.0, first + ranks, -1.0).astype(jnp.int32)
    at = iota((total, rows), 1)
    pick = jnp.zeros((total, rows), F32)
    for j in range(local):
        pick = jnp.where(at == place[:, j : j + 1], 1.0, pick)
    pick = pick.astype(BF16)
    pick_ref[...] = pick
    ranges = jnp.where(iota((16, LANES), 0) < 8, first, first + counts)
    ranges = jnp.concatenate([ranges[0:8], ranges[8:16]] + [jnp.zeros((LANES - 16, LANES), F32)], axis=0)
    ranges = ranges.T
    range_ref[...] = ranges[0:16]
    row_ref[...] = dot_tn(pick, x_ref[...]).astype(BF16)
    acc_ref[...] = jnp.zeros_like(acc_ref)
    for j in range(local):
        start_row = jnp.sum(first[:, j : j + 1]).astype(jnp.int32)
        first_ref[j] = start_row
        start = window_start(start_row, rows, window)
        part = row_ref[pl.ds(start, window), 0:features]
        fresh = start + iota((window, width), 0) >= start_row
        for half in range(2):
            into = (pl.ds(start, window), slice(half * width, (half + 1) * width))
            made = dot_nn(part, w_ref[j, half])
            acc_ref[into] = jnp.where(fresh, made, acc_ref[into])
    logits = dot_nt(router_ref[...], x_ref[:, 0:features])
    high = round16(logits)
    both = jnp.concatenate([high, logits - high], axis=0).astype(BF16)
    both = dot_nn(both, pick)
    turned = jnp.zeros((EXPERTS, rows), jnp.bool_)
    expert = iota((EXPERTS, rows), 0) - me * local
    where_row = iota((EXPERTS, rows), 1).astype(F32)
    for j in range(local):
        inside = jnp.logical_and(
            where_row >= first[:, j : j + 1], where_row < (first + counts)[:, j : j + 1]
        )
        turned = jnp.logical_or(turned, jnp.logical_and(inside, expert == j))
    squares = dot_tn(own_side.astype(BF16), pick)
    side = jnp.concatenate(
        [
            jnp.sum(jnp.where(turned, both[0:EXPERTS], 0.0), axis=0, keepdims=True),
            jnp.sum(jnp.where(turned, both[EXPERTS : 2 * EXPERTS], 0.0), axis=0, keepdims=True),
            squares[offset : offset + 2],
            jnp.zeros((12, rows), F32),
        ],
        axis=0,
    )
    share = share_ref.shape[1] - 16
    low = iota((share, LANES), 1) < PIECE_WIDTH
    for b in range(devices):
        piece, start = b % PIECES, b // PIECES * share
        tile = piece // 2 * LANES
        gate = acc_ref[start : start + share, tile : tile + LANES]
        up = acc_ref[start : start + share, width + tile : width + tile + LANES]
        if piece % 2 == 0:
            made = jnp.where(low, gate, swap_halves(up))
        else:
            made = jnp.where(low, swap_halves(gate), up)
        share_ref[b, 0:share, :] = made.astype(BF16)
        if piece == 0:
            strips = []
            for at in range(0, share, LANES):
                size = min(LANES, share - at)
                strip = side[0:4, start + at : start + at + size]
                if size < LANES:
                    strip = jnp.concatenate([strip, jnp.zeros((4, LANES - size), F32)], axis=1)
                strips.append(strip)
            strips.append(jnp.zeros((16 - 4 * len(strips), LANES), F32))
            strips = jnp.concatenate(strips, axis=0).astype(BF16)
        share_ref[b, share : share + 16, :] = strips
    for k, out_ref in enumerate(out_refs):
        out_ref[...] = share_ref[lax.rem(seq_ref[0] + k, devices)]


def gate_up(exp_index, seq_index, tokens, weights, w_router, rows, devices, turn):
    local, _, features, width = weights.shape
    sources, wide = len(tokens), tokens[0].shape[1]
    total = sources * tokens[0].shape[0]
    share = (rows * PIECES // devices + 16, LANES)
    smem, vmem = pl.BlockSpec(memory_space=pltpu.SMEM), pl.BlockSpec(memory_space=pltpu.VMEM)
    return pl.pallas_call(
        functools.partial(gate_up_kernel, features, local, turn, sources, devices),
        in_specs=[smem] * 2 + [vmem] * (2 + sources),
        out_specs=(vmem,) * devices + (vmem, vmem, smem, smem),
        out_shape=(jax.ShapeDtypeStruct(share, BF16),) * devices
        + (
            jax.ShapeDtypeStruct((total, rows), BF16),
            jax.ShapeDtypeStruct((16, LANES), F32),
            jax.ShapeDtypeStruct((16,), jnp.int32),
            jax.ShapeDtypeStruct((1,), jnp.int32),
        ),
        scratch_shapes=[
            pltpu.VMEM((total, wide), BF16),
            pltpu.VMEM((rows, wide), BF16),
            pltpu.VMEM((rows, 2 * width), F32),
            pltpu.VMEM((devices,) + share, BF16),
        ],
        compiler_params=params(),
        name="gate_up",
    )(exp_index, seq_index, weights, w_router.T, *tokens)


def inner_kernel(*refs):
    x_refs, (out_ref, logit_ref) = refs[:-2], refs[-2:]
    share = x_refs[0].shape[0] - 16
    half = share // 2

    def total(start, size):
        return functools.reduce(
            jnp.add, [x_ref[start : start + size].astype(F32) for x_ref in x_refs]
        )

    side = total(share, 16)
    columns, logits = [], []
    for strip in range(-(-share // LANES)):
        values = side[4 * strip : 4 * strip + 4]
        inverse = lax.rsqrt((values[2:3] + values[3:4]) * (1.0 / D) + 1e-6)
        logits.append((values[0:1] + values[1:2]) * inverse)
        columns.append(jnp.broadcast_to(inverse, (LANES, LANES)).T)
    logit_ref[...] = jnp.concatenate(logits + [jnp.zeros((8 - len(logits), LANES), F32)], axis=0)
    scaled = total(0, share) * jnp.concatenate(columns, axis=0)[0:share]
    made = scaled / (1.0 + jnp.exp(-scaled)) * swap_halves(scaled)
    low = iota((half, LANES), 1) < PIECE_WIDTH
    out_ref[...] = jnp.where(low, made[0:half], swap_halves(made[half:share])).astype(BF16)


def inner(parts):
    return pl.pallas_call(
        inner_kernel,
        out_shape=(
            jax.ShapeDtypeStruct(((parts[0].shape[0] - 16) // 2, LANES), BF16),
            jax.ShapeDtypeStruct((8, LANES), F32),
        ),
        compiler_params=params(),
        name="inner",
    )(*parts)


def down_kernel(features, local, devices, first_ref, seq_ref, range_ref, pick_ref, w_ref, logit_ref, *refs):
    part_refs, out_refs, (x_ref, row_ref, made_ref) = refs[:devices], refs[devices:-3], refs[-3:]
    total, rows = pick_ref.shape
    width = w_ref.shape[2]
    window = total // 2 + 16
    for k, part_ref in enumerate(part_refs):
        x_ref[lax.rem(seq_ref[0] + devices - k, devices)] = part_ref[...]
    half = x_ref.shape[1]
    share = 2 * half
    low = iota((half, LANES), 1) < PIECE_WIDTH
    for b in range(0, devices, 2):
        start, tile = b // PIECES * share, b % PIECES // 2 * LANES
        one, two = x_ref[b].astype(F32), x_ref[b + 1].astype(F32)
        above = jnp.where(low, one, swap_halves(two)).astype(BF16)
        below = jnp.where(low, swap_halves(one), two).astype(BF16)
        row_ref[start : start + half, tile : tile + LANES] = above
        row_ref[start + half : start + share, tile : tile + LANES] = below
    logit = []
    for piece in range(devices // PIECES):
        for strip in range(-(-share // LANES)):
            size = min(LANES, share - strip * LANES)
            logit.append(logit_ref[piece, strip : strip + 1, 0:size])
    made_ref[...] = jnp.zeros_like(made_ref)
    for j in range(local):
        start_row = first_ref[j]
        start = window_start(start_row, rows, window)
        made = dot_nt(row_ref[pl.ds(start, window), :], w_ref[j])
        fresh = start + iota((window, features), 0) >= start_row
        into = (pl.ds(start, window), slice(0, features))
        made_ref[into] = jnp.where(fresh, made, made_ref[into])
    logit = jnp.concatenate(logit, axis=1)
    high = round16(logit)
    middle = round16(logit - high)
    pick = pick_ref[...]
    where_row = iota((16, rows), 1).astype(F32)
    inside = jnp.logical_and(where_row >= range_ref[:, 0:1], where_row < range_ref[:, 8:9])
    inside = jnp.logical_and(inside, iota((16, rows), 0) < local)
    spread = [jnp.where(inside, part, 0.0) for part in (high, middle, logit - high - middle)]
    spread.append(inside.astype(F32))
    found = dot_nt(jnp.concatenate(spread, axis=0).astype(BF16), pick)
    valid = found[48:64] > 0.5
    logits = jnp.where(valid, found[0:16] + found[16:32] + found[32:48], NEG_FILL)
    top = jnp.max(logits, axis=0, keepdims=True)
    weights = jnp.where(valid, jnp.exp(logits - top), 0.0)
    summed = jnp.sum(weights, axis=0, keepdims=True)
    high = round16(weights)
    both = dot_nn(jnp.concatenate([high, weights - high], axis=0).astype(BF16), pick)
    weight = jnp.sum(jnp.where(inside, both[0:16] + both[16:32], 0.0), axis=0, keepdims=True)
    column = jnp.broadcast_to(weight, (LANES, rows)).T[:, 0:1]
    acc = dot_nn(pick, (made_ref[...] * column).astype(BF16))
    tile, offset = side_place(features, 2)
    pair = jnp.where(iota((LANES, total), 0) == 0, top, summed).T
    tokens = total // len(out_refs)
    for e, out_ref in enumerate(out_refs):
        at = slice(e * tokens, (e + 1) * tokens)
        out_ref[...] = acc[at]
        lane = iota((tokens, LANES), 1) - offset
        side = jnp.where(lane == 0, pair[at, 0:1], acc[at, tile : tile + LANES])
        out_ref[:, tile : tile + LANES] = jnp.where(lane == 1, pair[at, 1:2], side)


def down(first, seq_index, ranges, pick, made, logits, weights, exp_count):
    local, features, width = weights.shape
    total, rows = pick.shape
    wide = side_place(features, 2)[0] + LANES
    smem, vmem = pl.BlockSpec(memory_space=pltpu.SMEM), pl.BlockSpec(memory_space=pltpu.VMEM)
    return pl.pallas_call(
        functools.partial(down_kernel, features, local, len(made)),
        in_specs=[smem] * 2 + [vmem] * (4 + len(made)),
        out_shape=(jax.ShapeDtypeStruct((total // exp_count, wide), F32),) * exp_count,
        scratch_shapes=[
            pltpu.VMEM((len(made),) + made[0].shape, BF16),
            pltpu.VMEM((rows, width), BF16),
            pltpu.VMEM((rows, wide), F32),
        ],
        compiler_params=params(),
        name="down",
    )(first, seq_index, ranges, pick, weights, logits, *made)


def finish_kernel(hidden_ref, *refs):
    part_refs, out_ref = refs[:-1], refs[-1]
    features = hidden_ref.shape[1]
    tile, offset = side_place(features, 2)
    sides = [x_ref[:, tile : tile + LANES] for x_ref in part_refs]
    tops = [side[:, offset : offset + 1] for side in sides]
    top = functools.reduce(jnp.maximum, tops)
    scales = [jnp.exp(one - top) for one in tops]
    total = functools.reduce(
        jnp.add, [s * side[:, offset + 1 : offset + 2] for s, side in zip(scales, sides)]
    )
    acc = functools.reduce(
        jnp.add, [s * x_ref[:, 0:features] for x_ref, s in zip(part_refs, scales)]
    )
    out = hidden_ref[...] + acc * (1.0 / total)
    out_ref[...] = out.reshape(out_ref.shape).astype(BF16)


def finish(parts, hidden, shape):
    return pl.pallas_call(
        finish_kernel,
        out_shape=jax.ShapeDtypeStruct(shape, BF16),
        compiler_params=params(),
        name="finish",
    )(hidden, *parts)


def join_rounds(features, one, other):
    tile, offset = side_place(features, 2)
    at = tile + offset
    top = jnp.maximum(one[..., at : at + 1], other[..., at : at + 1])
    scales = [jnp.exp(part[..., at : at + 1] - top) for part in (one, other)]
    joined = one * scales[0] + other * scales[1]
    return jnp.where(jnp.arange(one.shape[-1]) == at, top, joined)


def send(x, axis, distance):
    count = lax.axis_size(axis)
    return lax.ppermute(x, axis, [(i, (i + distance) % count) for i in range(count)])


def exchange(parts, axis, direction):
    return [parts[0]] + [send(part, axis, direction * k) for k, part in enumerate(parts) if k]


def gather(block, axis):
    return exchange([block] * lax.axis_size(axis), axis, 1)


def local(
    queries,
    new_key_value,
    key_value_cache,
    page_table,
    cache_len,
    routes,
    residual,
    w_out,
    norm_gain,
    w_router,
    w_gate_up,
    w_down,
):
    exp_count = lax.axis_size("exp")
    seq_count = lax.axis_size("seq")
    exp_index = lax.axis_index("exp").astype(jnp.int32).reshape(1)
    seq_index = lax.axis_index("seq").astype(jnp.int32).reshape(1)
    steps, requests, width = queries.shape
    tokens = steps * requests
    features = w_out.shape[1]
    page_rows = key_value_cache.shape[2]
    pool = key_value_cache.reshape(-1, page_rows, 2, KV_WIDTH)

    shares = attend(
        queries, new_key_value, pool, page_table, cache_len, seq_index, seq_count
    )
    attn = join(exchange(shares, "seq", 1))
    w_gate_up, attn = lax.optimization_barrier((w_gate_up, attn))
    gathered = gather(attn, "seq")
    gate_up_weights = w_gate_up.transpose(0, 2, 1, 3)
    gate_up_weights, gathered = lax.optimization_barrier((gate_up_weights, gathered))
    hidden, outgoing = hidden_state(seq_index, gathered, residual, w_out, norm_gain, routes)
    incoming = gather(outgoing, "exp")
    pieces = seq_count // PIECES
    rows = -(-ROUND_ROWS // (32 * pieces)) * 32 * pieces

    def one_round(turn):
        *partial, pick, ranges, first, most = gate_up(
            exp_index, seq_index, incoming, gate_up_weights, w_router, rows, seq_count, turn
        )
        made, logits = inner(exchange(partial, "seq", 1))
        logits = logits[None] if pieces == 1 else lax.all_gather(logits, "seq")[::PIECES]
        made = gather(made, "seq")
        return down(first, seq_index, ranges, pick, made, logits, w_down, exp_count), most

    made, most = one_round(0)
    pairs = w_gate_up.shape[0] * exp_count * steps * CAP
    for turn in range(1, -(-pairs // rows)):
        made = lax.cond(
            most[0] > turn * rows,
            lambda made: tuple(
                join_rounds(features, *both) for both in zip(made, one_round(turn)[0])
            ),
            lambda made: made,
            made,
        )
    return finish(exchange(made, "exp", -1), hidden, (steps, requests, features))


def solution(mesh):
    in_specs = (
        P(None, "exp", None),
        P(None, "exp", None, None),
        P("exp", "seq", None, None, None),
        P("exp", "seq"),
        P("exp"),
        P(None, "exp", None),
        P(None, "exp", "seq"),
        P(None, "seq"),
        P("seq"),
        P("seq", None),
        P("exp", "seq", None, None),
        P("exp", "seq", None),
    )
    out_specs = P(None, "exp", "seq")
    return jax.shard_map(local, mesh=mesh, in_specs=in_specs, out_specs=out_specs, check_vma=False)
```

```python
import functools

import jax
import jax.numpy as jnp
from jax import lax
from jax.experimental import pallas as pl
from jax.experimental.pallas import tpu as pltpu
from jax.sharding import PartitionSpec as P

D = 1536
QUERY_HEADS = 24
KEY_VALUE_HEADS = 8
HEAD_SIZE = 64
GROUP = QUERY_HEADS // KEY_VALUE_HEADS
KV_WIDTH = KEY_VALUE_HEADS * HEAD_SIZE
EXPERTS = 40
FF = 512
CAP = 4
LANES = 128
SIDE_KEYS = 2
ROUND_ROWS = 352
PIECES = 8
PIECE_WIDTH = FF // PIECES

NEG_FILL = -1e30
F32 = jnp.float32
BF16 = jnp.bfloat16
VMEM_LIMIT = 48 * 1024 * 1024
ATTEND_VMEM = 60 * 1024 * 1024


def iota(shape, dimension):
    return lax.broadcasted_iota(jnp.int32, shape, dimension)


def dot_nt(a, b):
    return lax.dot_general(a, b, (((1,), (1,)), ((), ())), preferred_element_type=F32)


def dot_tn(a, b):
    return lax.dot_general(a, b, (((0,), (0,)), ((), ())), preferred_element_type=F32)


def dot_nn(a, b):
    return lax.dot_general(a, b, (((1,), (0,)), ((), ())), preferred_element_type=F32)


def round16(x):
    return x.astype(BF16).astype(F32)


def swap_halves(x):
    return pltpu.roll(x, HEAD_SIZE, 1)


def tile_of(x, index):
    return x[:, index * LANES : (index + 1) * LANES]


def padded(width):
    return -(-width // LANES) * LANES


def params():
    return pltpu.CompilerParams(vmem_limit_bytes=VMEM_LIMIT)


def attend_kernel(
    classes, seq_ref, table_hbm, len_hbm, q_hbm, fresh_hbm, cache_ref, share_ref,
    page_ref, table_ref, len_ref, q_ref, fresh_ref, query_ref, new_ref, order_ref, sems, small_sems,
):
    steps, requests, _ = q_ref.shape
    page_rows = cache_ref.shape[1]
    pages = table_ref.shape[1]
    span = pages * page_rows
    first = seq_ref[0] * span
    small = [
        pltpu.make_async_copy(source, target, small_sems.at[i])
        for i, (source, target) in enumerate(
            [(table_hbm, table_ref), (len_hbm, len_ref), (q_hbm, q_ref), (fresh_hbm, fresh_ref)]
        )
    ]
    for one in small:
        one.start()
    for one in small[:2]:
        one.wait()

    held = [jnp.clip(len_ref[r] - first, 0, span) for r in range(requests)]
    for r in range(requests):
        ahead = jnp.int32(0)
        for other in range(requests):
            if other != r:
                longer = held[other] >= held[r] if other < r else held[other] > held[r]
                ahead = ahead + longer.astype(jnp.int32)
        order_ref[ahead] = r

    share = share_ref.shape[1]
    per_request = steps * GROUP // share

    def put(r, acc, side):
        for i in range(per_request):
            at = r * per_request + i
            share_ref[at, :, 0:KV_WIDTH] = acc[i * share : (i + 1) * share]
            share_ref[at, :, KV_WIDTH : KV_WIDTH + LANES] = side[i * share : (i + 1) * share]

    def copy(r, page):
        at = r * pages + page
        return pltpu.make_async_copy(cache_ref.at[table_ref[r, page]], page_ref.at[at], sems.at[at])

    def needed(r, low):
        return len_ref[r] - first > low * page_rows

    bounds = list(zip((0,) + classes[:-1], classes))

    def start(pair, carry):
        both = order_ref[2 * pair], order_ref[2 * pair + 1]
        for low, high in bounds:

            @pl.when(needed(both[0], low))
            def _():
                for page in range(low, high):
                    for r in both:
                        copy(r, page).start()

        return carry

    lax.fori_loop(0, requests // 2, start, 0)
    for one in small[2:]:
        one.wait()

    low = iota((requests, LANES), 1) < HEAD_SIZE
    for t in range(steps):
        q = q_ref[t].astype(F32) * 0.125
        for g in range(GROUP):
            for j in range(KV_WIDTH // LANES):
                one = tile_of(q, (6 * j + g) // 2)
                two = tile_of(q, (6 * j + 3 + g) // 2)
                if g % 2 == 0:
                    tile = jnp.where(low, one, two)
                else:
                    tile = swap_halves(jnp.where(low, two, one))
                query_ref[t * GROUP + g, :, j * LANES : (j + 1) * LANES] = tile
        new_ref[t] = fresh_ref[t].reshape(2 * requests, KV_WIDTH).astype(F32)

    rows = steps * GROUP * KEY_VALUE_HEADS
    own = iota((rows, KV_WIDTH), 1) // HEAD_SIZE == iota((rows, KV_WIDTH), 0) % KEY_VALUE_HEADS
    lane = iota((rows, LANES), 1)
    head = iota((rows, LANES), 0) % KEY_VALUE_HEADS
    row_step = iota((rows, 16), 0) // (GROUP * KEY_VALUE_HEADS)
    kept = jnp.logical_and(iota((rows, 16), 1) <= row_step, seq_ref[0] == 0)
    fresh_bias = jnp.where(kept, 0.0, NEG_FILL)

    def fresh_rows(r, which):
        found = [new_ref[u, pl.ds(2 * r + which, 1), :] for u in range(steps)]
        return jnp.concatenate(found + [jnp.zeros((16 - steps, KV_WIDTH), F32)], axis=0).astype(BF16)

    def attend_pages(r, count):
        spread = jnp.concatenate(
            [
                jnp.broadcast_to(query_ref[i, pl.ds(r, 1), :], (KEY_VALUE_HEADS, KV_WIDTH))
                for i in range(steps * GROUP)
            ],
            axis=0,
        )
        spread = jnp.where(own, spread, 0.0).astype(BF16)
        both = [page_ref[r * pages + page].reshape(2 * page_rows, KV_WIDTH) for page in range(count)]
        both = jnp.concatenate(both, axis=0)
        size = 2 * count * page_rows
        place = iota((1, size), 1)
        live = jnp.logical_and(place % 2 == 0, first + place // 2 < len_ref[r])
        scores = dot_nt(spread, both) + jnp.where(live, 0.0, NEG_FILL)
        fresh_scores = dot_nt(spread, fresh_rows(r, 0)) + fresh_bias
        largest = jnp.maximum(
            jnp.max(scores, axis=1, keepdims=True), jnp.max(fresh_scores, axis=1, keepdims=True)
        )
        weights = jnp.exp(scores - largest)
        fresh_weights = jnp.exp(fresh_scores - largest)
        total = jnp.sum(weights, axis=1, keepdims=True)
        total = total + jnp.sum(fresh_weights, axis=1, keepdims=True)
        moved = [pltpu.roll(tile_of(weights, j), 1, 1) for j in range(size // LANES)]
        acc = dot_nn(jnp.concatenate(moved, axis=1).astype(BF16), both)
        acc = acc + dot_nn(fresh_weights.astype(BF16), fresh_rows(r, 1))
        acc = jnp.where(own, acc * (1.0 / total), 0.0)
        acc = jnp.sum(acc.reshape(steps * GROUP, KEY_VALUE_HEADS, KV_WIDTH), axis=1)
        level = jnp.where(needed(r, 0), largest + jnp.log(total), NEG_FILL)
        high = round16(level)
        middle = round16(level - high)
        side = jnp.where(lane == head, high, 0.0)
        side = jnp.where(lane == head + 8, middle, side)
        side = jnp.where(lane == head + 16, level - high - middle, side)
        side = jnp.sum(side.reshape(steps * GROUP, KEY_VALUE_HEADS, LANES), axis=1)
        return acc.astype(BF16), side.astype(BF16)

    def one_pair(pair, carry):
        both = order_ref[2 * pair], order_ref[2 * pair + 1]
        for low, high in bounds:
            enough = needed(both[0], low)
            if high < pages:
                enough = jnp.logical_and(enough, jnp.logical_not(needed(both[0], high)))

            @pl.when(enough)
            def _():
                for page in range(high):
                    for r in both:
                        copy(r, page).wait()
                made = [attend_pages(r, high) for r in both]
                for r, (acc, side) in zip(both, made):
                    put(r, acc, side)

        @pl.when(jnp.logical_not(needed(both[0], 0)))
        def _():
            empty = jnp.where(iota((steps * GROUP, LANES), 1) < KEY_VALUE_HEADS, NEG_FILL, 0.0)
            for r in both:
                put(r, jnp.zeros((steps * GROUP, KV_WIDTH), BF16), empty.astype(BF16))

        return carry

    lax.fori_loop(0, requests // 2, one_pair, 0)


def attend(queries, new_key_value, cache, page_table, cache_len, seq_index, devices):
    steps, requests, _ = queries.shape
    pages = page_table.shape[1]
    page_rows = cache.shape[1]
    classes = tuple(c for c in (2, 4) if c < pages) + (pages,)
    share = (requests * steps * GROUP // devices, KV_WIDTH + LANES)
    smem, hbm = pl.BlockSpec(memory_space=pltpu.SMEM), pl.BlockSpec(memory_space=pl.ANY)
    return pl.pallas_call(
        functools.partial(attend_kernel, classes),
        in_specs=[smem] + [hbm] * 5,
        out_shape=jax.ShapeDtypeStruct((devices,) + share, BF16),
        scratch_shapes=[
            pltpu.VMEM((requests * pages, page_rows, 2, KV_WIDTH), BF16),
            pltpu.SMEM(page_table.shape, jnp.int32),
            pltpu.SMEM(cache_len.shape, jnp.int32),
            pltpu.VMEM(queries.shape, BF16),
            pltpu.VMEM(new_key_value.shape, BF16),
            pltpu.VMEM((steps * GROUP, requests, KV_WIDTH), F32),
            pltpu.VMEM((steps, 2 * requests, KV_WIDTH), F32),
            pltpu.SMEM((requests,), jnp.int32),
            pltpu.SemaphoreType.DMA((requests * pages,)),
            pltpu.SemaphoreType.DMA((4,)),
        ],
        compiler_params=pltpu.CompilerParams(vmem_limit_bytes=ATTEND_VMEM),
        name="attend",
    )(seq_index, page_table, cache_len, queries, new_key_value, cache)


def join_kernel(x_ref, out_ref):
    blocks, rows, _ = x_ref.shape
    tokens = rows // GROUP
    levels = []
    for b in range(blocks):
        side = x_ref[b, :, KV_WIDTH : KV_WIDTH + LANES].astype(F32)
        levels.append(side + pltpu.roll(side, LANES - 8, 1) + pltpu.roll(side, LANES - 16, 1))
    largest = functools.reduce(jnp.maximum, levels)
    weights = [jnp.exp(level - largest) for level in levels]
    inverse = 1.0 / functools.reduce(jnp.add, weights)
    low = iota((rows, LANES), 1) < HEAD_SIZE
    acc = [jnp.zeros((rows, LANES), F32) for _ in range(KV_WIDTH // LANES)]
    for b in range(blocks):
        share = weights[b] * inverse
        for j in range(KV_WIDTH // LANES):
            factor = jnp.where(low, share[:, 2 * j : 2 * j + 1], share[:, 2 * j + 1 : 2 * j + 2])
            acc[j] = acc[j] + factor * x_ref[b, :, j * LANES : (j + 1) * LANES].astype(F32)

    def piece(head, half):
        k, g = head // GROUP, head % GROUP
        tile = jnp.concatenate(
            [acc[k // 2][t * GROUP + g : t * GROUP + g + 1] for t in range(tokens)], axis=0
        )
        return tile if k % 2 == half else swap_halves(tile)

    low_tokens = iota((tokens, LANES), 1) < HEAD_SIZE
    for m in range(QUERY_HEADS // 2):
        tile = jnp.where(low_tokens, piece(2 * m, 0), piece(2 * m + 1, 1)).astype(BF16)
        out_ref[:, m * LANES : (m + 1) * LANES] = tile


def join(parts):
    rows = parts.shape[1]
    return pl.pallas_call(
        join_kernel,
        out_shape=jax.ShapeDtypeStruct((rows // GROUP, QUERY_HEADS * HEAD_SIZE), BF16),
        compiler_params=params(),
        name="join",
    )(parts)


def side_place(features, count):
    tile, offset = features // LANES * LANES, features % LANES
    return (tile, offset) if offset and offset + count <= LANES else (padded(features), 0)


def hidden_kernel(seq_ref, residual_ref, w_ref, gain_ref, routes_ref, *refs):
    attn_refs, (hidden_ref, out_ref, wide_ref) = refs[:-3], refs[-3:]
    steps, requests, features = residual_ref.shape
    tokens = steps * requests
    blocks = [ref[i].astype(F32) for ref in attn_refs for i in range(2)]
    attn = jnp.concatenate(blocks, axis=0).astype(BF16)
    row, column = iota((tokens, tokens), 0), iota((tokens, tokens), 1)
    devices, share = len(blocks), attn_refs[0].shape[1]
    source = seq_ref[0] + devices - column // (2 * share) * 2
    source = jnp.where(source >= devices, source - devices, source)
    other = column // share % 2
    source = source + other * (1 - source % 2 * 2)
    token = source * share + column % share
    reorder = jnp.logical_and(row % requests == token // steps, row // requests == token % steps)
    attn = dot_nn(reorder.astype(F32).astype(BF16), attn).astype(BF16)
    residual = residual_ref[...].astype(F32).reshape(tokens, features)
    hidden = residual + dot_nt(attn, w_ref[...])
    hidden_ref[...] = hidden
    squares = jnp.sum(hidden * hidden, axis=1, keepdims=True)
    tile, offset = side_place(features, SIDE_KEYS + EXPERTS)
    wide_ref[...] = jnp.zeros_like(wide_ref)
    wide_ref[:, 0:features] = hidden * gain_ref[...]
    routes = routes_ref[...].reshape(tokens, routes_ref.shape[2])
    lane = iota((tokens, LANES), 1) - offset
    side = wide_ref[:, tile : tile + LANES]
    for k in range(routes.shape[1]):
        side = jnp.where(lane == routes[:, k : k + 1] + SIDE_KEYS, 1.0, side)
    high = round16(squares)
    side = jnp.where(lane == 0, high, side)
    wide_ref[:, tile : tile + LANES] = jnp.where(lane == 1, squares - high, side)
    out_ref[...] = wide_ref[...].astype(BF16)


def hidden_state(seq_index, attn, residual, w_out, gain, routes):
    steps, requests, features = residual.shape
    tokens = steps * requests
    wide = side_place(features, SIDE_KEYS + EXPERTS)[0] + LANES
    smem, vmem = pl.BlockSpec(memory_space=pltpu.SMEM), pl.BlockSpec(memory_space=pltpu.VMEM)
    return pl.pallas_call(
        hidden_kernel,
        in_specs=[smem] + [vmem] * (4 + len(attn)),
        out_shape=(
            jax.ShapeDtypeStruct((tokens, features), F32),
            jax.ShapeDtypeStruct((tokens, wide), BF16),
        ),
        scratch_shapes=[pltpu.VMEM((tokens, wide), F32)],
        compiler_params=params(),
        name="hidden",
    )(seq_index, residual, w_out.T, gain.reshape(1, features), routes, *attn)


def window_start(first, rows, window):
    return pl.multiple_of(jnp.clip(first // 16 * 16, 0, rows - window), 16)


def gate_up_kernel(
    features, local, turn, sources, devices, where_ref, seq_ref, w_ref, router_ref, *refs,
):
    part_refs, refs = refs[:sources], refs[sources:]
    out_refs, refs = refs[:devices], refs[devices:]
    pick_ref, range_ref, first_ref, most_ref, x_ref, row_ref, acc_ref, share_ref = refs
    total = x_ref.shape[0]
    for e, part_ref in enumerate(part_refs):
        x_ref[e * (total // sources) : (e + 1) * (total // sources)] = part_ref[...]
    rows = pick_ref.shape[1]
    width = w_ref.shape[3]
    window = total // 2 + 16
    tile, offset = side_place(features, SIDE_KEYS + EXPERTS)
    me = where_ref[0]
    own_side = x_ref[:, tile : tile + LANES].astype(F32)
    lane = iota((total, LANES), 1)
    flags = pltpu.roll(own_side, LANES - offset - SIDE_KEYS, 1)
    flags = jnp.where(lane < EXPERTS, flags, 0.0)
    owners = EXPERTS // local
    counts = jnp.sum(flags, axis=0, keepdims=True)
    most = jnp.int32(0)
    for o in range(owners):
        held = jnp.logical_and(lane[0:1] >= o * local, lane[0:1] < (o + 1) * local)
        most = jnp.maximum(most, jnp.sum(jnp.where(held, counts, 0.0)).astype(jnp.int32))
    most_ref[0] = most
    mine = pltpu.roll(flags, lax.rem(LANES - me * local, LANES), 1)
    mine = jnp.where(lane < local, mine, 0.0)
    mine16 = mine.astype(BF16)
    row, column = iota((total, total), 0), iota((total, total), 1)
    earlier = (column < row).astype(F32).astype(BF16)
    ranks = dot_nn(earlier, mine16)
    counts = jnp.sum(mine, axis=0, keepdims=True)
    before = (iota((LANES, LANES), 0) < iota((LANES, LANES), 1)).astype(F32).astype(BF16)
    first = dot_nn(jnp.broadcast_to(counts, (8, LANES)).astype(BF16), before)[0:1] - turn * rows
    place = jnp.where(mine > 0.0, first + ranks, -1.0).astype(jnp.int32)
    at = iota((total, rows), 1)
    pick = jnp.zeros((total, rows), F32)
    for j in range(local):
        pick = jnp.where(at == place[:, j : j + 1], 1.0, pick)
    pick = pick.astype(BF16)
    pick_ref[...] = pick
    ranges = jnp.where(iota((16, LANES), 0) < 8, first, first + counts)
    ranges = jnp.concatenate([ranges[0:8], ranges[8:16]] + [jnp.zeros((LANES - 16, LANES), F32)], axis=0)
    ranges = ranges.T
    range_ref[...] = ranges[0:16]
    row_ref[...] = dot_tn(pick, x_ref[...]).astype(BF16)
    acc_ref[...] = jnp.zeros_like(acc_ref)
    for j in range(local):
        start_row = jnp.sum(first[:, j : j + 1]).astype(jnp.int32)
        first_ref[j] = start_row
        start = window_start(start_row, rows, window)
        part = row_ref[pl.ds(start, window), 0:features]
        fresh = start + iota((window, width), 0) >= start_row
        for half in range(2):
            into = (pl.ds(start, window), slice(half * width, (half + 1) * width))
            made = dot_nn(part, w_ref[j, half])
            acc_ref[into] = jnp.where(fresh, made, acc_ref[into])
    logits = dot_nt(router_ref[...], x_ref[:, 0:features])
    high = round16(logits)
    both = jnp.concatenate([high, logits - high], axis=0).astype(BF16)
    both = dot_nn(both, pick)
    turned = jnp.zeros((EXPERTS, rows), jnp.bool_)
    expert = iota((EXPERTS, rows), 0) - me * local
    where_row = iota((EXPERTS, rows), 1).astype(F32)
    for j in range(local):
        inside = jnp.logical_and(
            where_row >= first[:, j : j + 1], where_row < (first + counts)[:, j : j + 1]
        )
        turned = jnp.logical_or(turned, jnp.logical_and(inside, expert == j))
    squares = dot_tn(own_side.astype(BF16), pick)
    side = jnp.concatenate(
        [
            jnp.sum(jnp.where(turned, both[0:EXPERTS], 0.0), axis=0, keepdims=True),
            jnp.sum(jnp.where(turned, both[EXPERTS : 2 * EXPERTS], 0.0), axis=0, keepdims=True),
            squares[offset : offset + 2],
            jnp.zeros((12, rows), F32),
        ],
        axis=0,
    )
    share = share_ref.shape[1] - 16
    low = iota((share, LANES), 1) < PIECE_WIDTH
    for b in range(devices):
        piece, start = b % PIECES, b // PIECES * share
        tile = piece // 2 * LANES
        gate = acc_ref[start : start + share, tile : tile + LANES]
        up = acc_ref[start : start + share, width + tile : width + tile + LANES]
        if piece % 2 == 0:
            made = jnp.where(low, gate, swap_halves(up))
        else:
            made = jnp.where(low, swap_halves(gate), up)
        share_ref[b, 0:share, :] = made.astype(BF16)
        if piece == 0:
            strips = []
            for at in range(0, share, LANES):
                size = min(LANES, share - at)
                strip = side[0:4, start + at : start + at + size]
                if size < LANES:
                    strip = jnp.concatenate([strip, jnp.zeros((4, LANES - size), F32)], axis=1)
                strips.append(strip)
            strips.append(jnp.zeros((16 - 4 * len(strips), LANES), F32))
            strips = jnp.concatenate(strips, axis=0).astype(BF16)
        share_ref[b, share : share + 16, :] = strips
    for k, out_ref in enumerate(out_refs):
        out_ref[...] = share_ref[lax.rem(seq_ref[0] + k, devices)]


def gate_up(exp_index, seq_index, tokens, weights, w_router, rows, devices, turn):
    local, _, features, width = weights.shape
    sources, wide = len(tokens), tokens[0].shape[1]
    total = sources * tokens[0].shape[0]
    share = (rows * PIECES // devices + 16, LANES)
    smem, vmem = pl.BlockSpec(memory_space=pltpu.SMEM), pl.BlockSpec(memory_space=pltpu.VMEM)
    return pl.pallas_call(
        functools.partial(gate_up_kernel, features, local, turn, sources, devices),
        in_specs=[smem] * 2 + [vmem] * (2 + sources),
        out_specs=(vmem,) * devices + (vmem, vmem, smem, smem),
        out_shape=(jax.ShapeDtypeStruct(share, BF16),) * devices
        + (
            jax.ShapeDtypeStruct((total, rows), BF16),
            jax.ShapeDtypeStruct((16, LANES), F32),
            jax.ShapeDtypeStruct((16,), jnp.int32),
            jax.ShapeDtypeStruct((1,), jnp.int32),
        ),
        scratch_shapes=[
            pltpu.VMEM((total, wide), BF16),
            pltpu.VMEM((rows, wide), BF16),
            pltpu.VMEM((rows, 2 * width), F32),
            pltpu.VMEM((devices,) + share, BF16),
        ],
        compiler_params=params(),
        name="gate_up",
    )(exp_index, seq_index, weights, w_router.T, *tokens)


def inner_kernel(*refs):
    x_refs, (out_ref, logit_ref) = refs[:-2], refs[-2:]
    share = x_refs[0].shape[0] - 16
    half = share // 2

    def total(start, size):
        return functools.reduce(
            jnp.add, [x_ref[start : start + size].astype(F32) for x_ref in x_refs]
        )

    side = total(share, 16)
    columns, logits = [], []
    for strip in range(-(-share // LANES)):
        values = side[4 * strip : 4 * strip + 4]
        inverse = lax.rsqrt((values[2:3] + values[3:4]) * (1.0 / D) + 1e-6)
        logits.append((values[0:1] + values[1:2]) * inverse)
        columns.append(jnp.broadcast_to(inverse, (LANES, LANES)).T)
    logit_ref[...] = jnp.concatenate(logits + [jnp.zeros((8 - len(logits), LANES), F32)], axis=0)
    scaled = total(0, share) * jnp.concatenate(columns, axis=0)[0:share]
    made = scaled / (1.0 + jnp.exp(-scaled)) * swap_halves(scaled)
    low = iota((half, LANES), 1) < PIECE_WIDTH
    made = jnp.where(low, made[0:half], swap_halves(made[half:share])).astype(BF16)
    for b in range(out_ref.shape[0]):
        out_ref[b] = made


def inner(parts):
    return pl.pallas_call(
        inner_kernel,
        out_shape=(
            jax.ShapeDtypeStruct((len(parts), (parts[0].shape[0] - 16) // 2, LANES), BF16),
            jax.ShapeDtypeStruct((8, LANES), F32),
        ),
        compiler_params=params(),
        name="inner",
    )(*parts)


def down_kernel(features, local, first_ref, range_ref, pick_ref, w_ref, logit_ref, x_ref, *refs):
    out_refs, (row_ref, made_ref) = refs[:-2], refs[-2:]
    total, rows = pick_ref.shape
    width = w_ref.shape[2]
    window = total // 2 + 16
    devices, half, _ = x_ref.shape
    share = 2 * half
    low = iota((half, LANES), 1) < PIECE_WIDTH
    for b in range(0, devices, 2):
        start, tile = b // PIECES * share, b % PIECES // 2 * LANES
        one, two = x_ref[b].astype(F32), x_ref[b + 1].astype(F32)
        above = jnp.where(low, one, swap_halves(two)).astype(BF16)
        below = jnp.where(low, swap_halves(one), two).astype(BF16)
        row_ref[start : start + half, tile : tile + LANES] = above
        row_ref[start + half : start + share, tile : tile + LANES] = below
    logit = []
    for piece in range(devices // PIECES):
        for strip in range(-(-share // LANES)):
            size = min(LANES, share - strip * LANES)
            logit.append(logit_ref[piece, strip : strip + 1, 0:size])
    made_ref[...] = jnp.zeros_like(made_ref)
    for j in range(local):
        start_row = first_ref[j]
        start = window_start(start_row, rows, window)
        made = dot_nt(row_ref[pl.ds(start, window), :], w_ref[j])
        fresh = start + iota((window, features), 0) >= start_row
        into = (pl.ds(start, window), slice(0, features))
        made_ref[into] = jnp.where(fresh, made, made_ref[into])
    logit = jnp.concatenate(logit, axis=1)
    high = round16(logit)
    middle = round16(logit - high)
    pick = pick_ref[...]
    where_row = iota((16, rows), 1).astype(F32)
    inside = jnp.logical_and(where_row >= range_ref[:, 0:1], where_row < range_ref[:, 8:9])
    inside = jnp.logical_and(inside, iota((16, rows), 0) < local)
    spread = [jnp.where(inside, part, 0.0) for part in (high, middle, logit - high - middle)]
    spread.append(inside.astype(F32))
    found = dot_nt(jnp.concatenate(spread, axis=0).astype(BF16), pick)
    valid = found[48:64] > 0.5
    logits = jnp.where(valid, found[0:16] + found[16:32] + found[32:48], NEG_FILL)
    top = jnp.max(logits, axis=0, keepdims=True)
    weights = jnp.where(valid, jnp.exp(logits - top), 0.0)
    summed = jnp.sum(weights, axis=0, keepdims=True)
    high = round16(weights)
    both = dot_nn(jnp.concatenate([high, weights - high], axis=0).astype(BF16), pick)
    weight = jnp.sum(jnp.where(inside, both[0:16] + both[16:32], 0.0), axis=0, keepdims=True)
    column = jnp.broadcast_to(weight, (LANES, rows)).T[:, 0:1]
    acc = dot_nn(pick, (made_ref[...] * column).astype(BF16))
    tile, offset = side_place(features, 2)
    pair = jnp.where(iota((LANES, total), 0) == 0, top, summed).T
    tokens = total // len(out_refs)
    for e, out_ref in enumerate(out_refs):
        at = slice(e * tokens, (e + 1) * tokens)
        out_ref[...] = acc[at]
        lane = iota((tokens, LANES), 1) - offset
        side = jnp.where(lane == 0, pair[at, 0:1], acc[at, tile : tile + LANES])
        out_ref[:, tile : tile + LANES] = jnp.where(lane == 1, pair[at, 1:2], side)


def down(first, ranges, pick, made, logits, weights, exp_count):
    local, features, width = weights.shape
    total, rows = pick.shape
    wide = side_place(features, 2)[0] + LANES
    smem, vmem = pl.BlockSpec(memory_space=pltpu.SMEM), pl.BlockSpec(memory_space=pltpu.VMEM)
    return pl.pallas_call(
        functools.partial(down_kernel, features, local),
        in_specs=[smem] + [vmem] * 5,
        out_shape=(jax.ShapeDtypeStruct((total // exp_count, wide), F32),) * exp_count,
        scratch_shapes=[
            pltpu.VMEM((rows, width), BF16),
            pltpu.VMEM((rows, wide), F32),
        ],
        compiler_params=params(),
        name="down",
    )(first, ranges, pick, weights, logits, made)


def finish_kernel(hidden_ref, *refs):
    part_refs, out_ref = refs[:-1], refs[-1]
    features = hidden_ref.shape[1]
    tile, offset = side_place(features, 2)
    sides = [x_ref[:, tile : tile + LANES] for x_ref in part_refs]
    tops = [side[:, offset : offset + 1] for side in sides]
    top = functools.reduce(jnp.maximum, tops)
    scales = [jnp.exp(one - top) for one in tops]
    total = functools.reduce(
        jnp.add, [s * side[:, offset + 1 : offset + 2] for s, side in zip(scales, sides)]
    )
    acc = functools.reduce(
        jnp.add, [s * x_ref[:, 0:features] for x_ref, s in zip(part_refs, scales)]
    )
    out = hidden_ref[...] + acc * (1.0 / total)
    out_ref[...] = out.reshape(out_ref.shape).astype(BF16)


def finish(parts, hidden, shape):
    return pl.pallas_call(
        finish_kernel,
        out_shape=jax.ShapeDtypeStruct(shape, BF16),
        compiler_params=params(),
        name="finish",
    )(hidden, *parts)


def join_rounds(features, one, other):
    tile, offset = side_place(features, 2)
    at = tile + offset
    top = jnp.maximum(one[..., at : at + 1], other[..., at : at + 1])
    scales = [jnp.exp(part[..., at : at + 1] - top) for part in (one, other)]
    joined = one * scales[0] + other * scales[1]
    return jnp.where(jnp.arange(one.shape[-1]) == at, top, joined)


def send(x, axis, distance):
    count = lax.axis_size(axis)
    return lax.ppermute(x, axis, [(i, (i + distance) % count) for i in range(count)])


def swap(x, axis):
    return lax.all_to_all(x, axis, split_axis=0, concat_axis=0, tiled=True)


def exchange(parts, axis, direction):
    return [parts[0]] + [send(part, axis, direction * k) for k, part in enumerate(parts) if k]


def gather(block, axis):
    return exchange([block] * lax.axis_size(axis), axis, 1)


def local(
    queries,
    new_key_value,
    key_value_cache,
    page_table,
    cache_len,
    routes,
    residual,
    w_out,
    norm_gain,
    w_router,
    w_gate_up,
    w_down,
):
    exp_count = lax.axis_size("exp")
    seq_count = lax.axis_size("seq")
    exp_index = lax.axis_index("exp").astype(jnp.int32).reshape(1)
    seq_index = lax.axis_index("seq").astype(jnp.int32).reshape(1)
    steps, requests, width = queries.shape
    tokens = steps * requests
    features = w_out.shape[1]
    page_rows = key_value_cache.shape[2]
    pool = key_value_cache.reshape(-1, page_rows, 2, KV_WIDTH)

    shares = attend(
        queries, new_key_value, pool, page_table, cache_len, seq_index, seq_count
    )
    w_gate_up, shares = lax.optimization_barrier((w_gate_up, shares))
    gate_up_weights = w_gate_up.transpose(0, 2, 1, 3)
    shares = swap(shares, "seq")
    gate_up_weights, shares = lax.optimization_barrier((gate_up_weights, shares))
    attn = join(shares)
    beside = lax.ppermute(attn, "seq", [(i, i ^ 1) for i in range(seq_count)])
    pair = jnp.stack([attn, beside])
    gathered = [pair] + [send(pair, "seq", k) for k in range(2, seq_count, 2)]
    hidden, outgoing = hidden_state(seq_index, gathered, residual, w_out, norm_gain, routes)
    incoming = gather(outgoing, "exp")
    pieces = seq_count // PIECES
    rows = -(-ROUND_ROWS // (32 * pieces)) * 32 * pieces

    def one_round(turn):
        *partial, pick, ranges, first, most = gate_up(
            exp_index, seq_index, incoming, gate_up_weights, w_router, rows, seq_count, turn
        )
        made, logits = inner(exchange(partial, "seq", 1))
        logits = logits[None] if pieces == 1 else lax.all_gather(logits, "seq")[::PIECES]
        return down(first, ranges, pick, swap(made, "seq"), logits, w_down, exp_count), most

    made, most = one_round(0)
    pairs = w_gate_up.shape[0] * exp_count * steps * CAP
    for turn in range(1, -(-pairs // rows)):
        made = lax.cond(
            most[0] > turn * rows,
            lambda made: tuple(
                join_rounds(features, *both) for both in zip(made, one_round(turn)[0])
            ),
            lambda made: made,
            made,
        )
    return finish(exchange(made, "exp", -1), hidden, (steps, requests, features))


def solution(mesh):
    in_specs = (
        P(None, "exp", None),
        P(None, "exp", None, None),
        P("exp", "seq", None, None, None),
        P("exp", "seq"),
        P("exp"),
        P(None, "exp", None),
        P(None, "exp", "seq"),
        P(None, "seq"),
        P("seq"),
        P("seq", None),
        P("exp", "seq", None, None),
        P("exp", "seq", None),
    )
    out_specs = P(None, "exp", "seq")
    return jax.shard_map(local, mesh=mesh, in_specs=in_specs, out_specs=out_specs, check_vma=False)
```

```python
import functools

import jax
import jax.numpy as jnp
from jax import lax
from jax.experimental import pallas as pl
from jax.experimental.pallas import tpu as pltpu
from jax.sharding import PartitionSpec as P

D = 1536
QUERY_HEADS = 24
KEY_VALUE_HEADS = 8
HEAD_SIZE = 64
GROUP = QUERY_HEADS // KEY_VALUE_HEADS
KV_WIDTH = KEY_VALUE_HEADS * HEAD_SIZE
EXPERTS = 40
FF = 512
CAP = 4
LANES = 128
SIDE_KEYS = 2
ROUND_ROWS = 352
PIECES = 8
PIECE_WIDTH = FF // PIECES

NEG_FILL = -1e30
F32 = jnp.float32
BF16 = jnp.bfloat16
VMEM_LIMIT = 48 * 1024 * 1024
ATTEND_VMEM = 60 * 1024 * 1024


def iota(shape, dimension):
    return lax.broadcasted_iota(jnp.int32, shape, dimension)


def dot_nt(a, b):
    return lax.dot_general(a, b, (((1,), (1,)), ((), ())), preferred_element_type=F32)


def dot_tn(a, b):
    return lax.dot_general(a, b, (((0,), (0,)), ((), ())), preferred_element_type=F32)


def dot_nn(a, b):
    return lax.dot_general(a, b, (((1,), (0,)), ((), ())), preferred_element_type=F32)


def round16(x):
    return x.astype(BF16).astype(F32)


def swap_halves(x):
    return pltpu.roll(x, HEAD_SIZE, 1)


def tile_of(x, index):
    return x[:, index * LANES : (index + 1) * LANES]


def padded(width):
    return -(-width // LANES) * LANES


def params():
    return pltpu.CompilerParams(vmem_limit_bytes=VMEM_LIMIT)


def attend_kernel(
    classes, seq_ref, table_hbm, len_hbm, q_hbm, fresh_hbm, cache_ref, share_ref,
    page_ref, table_ref, len_ref, q_ref, fresh_ref, query_ref, new_ref, order_ref, sems, small_sems,
):
    steps, requests, _ = q_ref.shape
    page_rows = cache_ref.shape[1]
    pages = table_ref.shape[1]
    span = pages * page_rows
    first = seq_ref[0] * span
    small = [
        pltpu.make_async_copy(source, target, small_sems.at[i])
        for i, (source, target) in enumerate(
            [(table_hbm, table_ref), (len_hbm, len_ref), (q_hbm, q_ref), (fresh_hbm, fresh_ref)]
        )
    ]
    for one in small:
        one.start()
    for one in small[:2]:
        one.wait()

    held = [jnp.clip(len_ref[r] - first, 0, span) for r in range(requests)]
    for r in range(requests):
        ahead = jnp.int32(0)
        for other in range(requests):
            if other != r:
                longer = held[other] >= held[r] if other < r else held[other] > held[r]
                ahead = ahead + longer.astype(jnp.int32)
        order_ref[ahead] = r

    share = share_ref.shape[1]
    per_request = steps * GROUP // share

    def put(r, acc, side):
        for i in range(per_request):
            at = r * per_request + i
            share_ref[at, :, 0:KV_WIDTH] = acc[i * share : (i + 1) * share]
            share_ref[at, :, KV_WIDTH : KV_WIDTH + LANES] = side[i * share : (i + 1) * share]

    def copy(r, page):
        at = r * pages + page
        return pltpu.make_async_copy(cache_ref.at[table_ref[r, page]], page_ref.at[at], sems.at[at])

    def needed(r, low):
        return len_ref[r] - first > low * page_rows

    bounds = list(zip((0,) + classes[:-1], classes))

    def start(pair, carry):
        both = order_ref[2 * pair], order_ref[2 * pair + 1]
        for low, high in bounds:

            @pl.when(needed(both[0], low))
            def _():
                for page in range(low, high):
                    for r in both:
                        copy(r, page).start()

        return carry

    lax.fori_loop(0, requests // 2, start, 0)
    for one in small[2:]:
        one.wait()

    low = iota((requests, LANES), 1) < HEAD_SIZE
    for t in range(steps):
        q = q_ref[t].astype(F32) * 0.125
        for g in range(GROUP):
            for j in range(KV_WIDTH // LANES):
                one = tile_of(q, (6 * j + g) // 2)
                two = tile_of(q, (6 * j + 3 + g) // 2)
                if g % 2 == 0:
                    tile = jnp.where(low, one, two)
                else:
                    tile = swap_halves(jnp.where(low, two, one))
                query_ref[t * GROUP + g, :, j * LANES : (j + 1) * LANES] = tile
        new_ref[t] = fresh_ref[t].reshape(2 * requests, KV_WIDTH).astype(F32)

    rows = steps * GROUP * KEY_VALUE_HEADS
    own = iota((rows, KV_WIDTH), 1) // HEAD_SIZE == iota((rows, KV_WIDTH), 0) % KEY_VALUE_HEADS
    lane = iota((rows, LANES), 1)
    head = iota((rows, LANES), 0) % KEY_VALUE_HEADS
    row_step = iota((rows, 16), 0) // (GROUP * KEY_VALUE_HEADS)
    kept = jnp.logical_and(iota((rows, 16), 1) <= row_step, seq_ref[0] == 0)
    fresh_bias = jnp.where(kept, 0.0, NEG_FILL)

    def fresh_rows(r, which):
        found = [new_ref[u, pl.ds(2 * r + which, 1), :] for u in range(steps)]
        return jnp.concatenate(found + [jnp.zeros((16 - steps, KV_WIDTH), F32)], axis=0).astype(BF16)

    def attend_pages(r, count):
        spread = jnp.concatenate(
            [
                jnp.broadcast_to(query_ref[i, pl.ds(r, 1), :], (KEY_VALUE_HEADS, KV_WIDTH))
                for i in range(steps * GROUP)
            ],
            axis=0,
        )
        spread = jnp.where(own, spread, 0.0).astype(BF16)
        both = [page_ref[r * pages + page].reshape(2 * page_rows, KV_WIDTH) for page in range(count)]
        both = jnp.concatenate(both, axis=0)
        size = 2 * count * page_rows
        place = iota((1, size), 1)
        live = jnp.logical_and(place % 2 == 0, first + place // 2 < len_ref[r])
        scores = dot_nt(spread, both) + jnp.where(live, 0.0, NEG_FILL)
        fresh_scores = dot_nt(spread, fresh_rows(r, 0)) + fresh_bias
        largest = jnp.maximum(
            jnp.max(scores, axis=1, keepdims=True), jnp.max(fresh_scores, axis=1, keepdims=True)
        )
        weights = jnp.exp(scores - largest)
        fresh_weights = jnp.exp(fresh_scores - largest)
        total = jnp.sum(weights, axis=1, keepdims=True)
        total = total + jnp.sum(fresh_weights, axis=1, keepdims=True)
        moved = [pltpu.roll(tile_of(weights, j), 1, 1) for j in range(size // LANES)]
        acc = dot_nn(jnp.concatenate(moved, axis=1).astype(BF16), both)
        acc = acc + dot_nn(fresh_weights.astype(BF16), fresh_rows(r, 1))
        acc = jnp.where(own, acc * (1.0 / total), 0.0)
        acc = jnp.sum(acc.reshape(steps * GROUP, KEY_VALUE_HEADS, KV_WIDTH), axis=1)
        level = jnp.where(needed(r, 0), largest + jnp.log(total), NEG_FILL)
        high = round16(level)
        middle = round16(level - high)
        side = jnp.where(lane == head, high, 0.0)
        side = jnp.where(lane == head + 8, middle, side)
        side = jnp.where(lane == head + 16, level - high - middle, side)
        side = jnp.sum(side.reshape(steps * GROUP, KEY_VALUE_HEADS, LANES), axis=1)
        return acc.astype(BF16), side.astype(BF16)

    def one_pair(pair, carry):
        both = order_ref[2 * pair], order_ref[2 * pair + 1]
        for low, high in bounds:
            enough = needed(both[0], low)
            if high < pages:
                enough = jnp.logical_and(enough, jnp.logical_not(needed(both[0], high)))

            @pl.when(enough)
            def _():
                for page in range(high):
                    for r in both:
                        copy(r, page).wait()
                made = [attend_pages(r, high) for r in both]
                for r, (acc, side) in zip(both, made):
                    put(r, acc, side)

        @pl.when(jnp.logical_not(needed(both[0], 0)))
        def _():
            empty = jnp.where(iota((steps * GROUP, LANES), 1) < KEY_VALUE_HEADS, NEG_FILL, 0.0)
            for r in both:
                put(r, jnp.zeros((steps * GROUP, KV_WIDTH), BF16), empty.astype(BF16))

        return carry

    lax.fori_loop(0, requests // 2, one_pair, 0)


def attend(queries, new_key_value, cache, page_table, cache_len, seq_index, devices):
    steps, requests, _ = queries.shape
    pages = page_table.shape[1]
    page_rows = cache.shape[1]
    classes = tuple(c for c in (2, 4) if c < pages) + (pages,)
    share = (requests * steps * GROUP // devices, KV_WIDTH + LANES)
    smem, hbm = pl.BlockSpec(memory_space=pltpu.SMEM), pl.BlockSpec(memory_space=pl.ANY)
    return pl.pallas_call(
        functools.partial(attend_kernel, classes),
        in_specs=[smem] + [hbm] * 5,
        out_shape=jax.ShapeDtypeStruct((devices,) + share, BF16),
        scratch_shapes=[
            pltpu.VMEM((requests * pages, page_rows, 2, KV_WIDTH), BF16),
            pltpu.SMEM(page_table.shape, jnp.int32),
            pltpu.SMEM(cache_len.shape, jnp.int32),
            pltpu.VMEM(queries.shape, BF16),
            pltpu.VMEM(new_key_value.shape, BF16),
            pltpu.VMEM((steps * GROUP, requests, KV_WIDTH), F32),
            pltpu.VMEM((steps, 2 * requests, KV_WIDTH), F32),
            pltpu.SMEM((requests,), jnp.int32),
            pltpu.SemaphoreType.DMA((requests * pages,)),
            pltpu.SemaphoreType.DMA((4,)),
        ],
        compiler_params=pltpu.CompilerParams(vmem_limit_bytes=ATTEND_VMEM),
        name="attend",
    )(seq_index, page_table, cache_len, queries, new_key_value, cache)


def levels_of(side):
    side = side.astype(F32)
    return side + pltpu.roll(side, LANES - 8, 1) + pltpu.roll(side, LANES - 16, 1)


def blend(shares, rows):
    levels = [levels_of(share[:, KV_WIDTH : KV_WIDTH + LANES]) for share in shares]
    largest = functools.reduce(jnp.maximum, levels)
    weights = [jnp.exp(level - largest) for level in levels]
    total = functools.reduce(jnp.add, weights)
    inverse = 1.0 / total
    low = iota((rows, LANES), 1) < HEAD_SIZE
    acc = [jnp.zeros((rows, LANES), F32) for _ in range(KV_WIDTH // LANES)]
    for weight, share in zip(weights, shares):
        part = weight * inverse
        for j in range(KV_WIDTH // LANES):
            factor = jnp.where(low, part[:, 2 * j : 2 * j + 1], part[:, 2 * j + 1 : 2 * j + 2])
            acc[j] = acc[j] + factor * tile_of(share, j).astype(F32)
    return acc, largest, total


def join_pair_kernel(seq_ref, own_ref, other_ref, *out_refs):
    pairs = len(out_refs)
    rows = own_ref.shape[1]
    lane = iota((rows, LANES), 1)
    for k, out_ref in enumerate(out_refs):
        pair = lax.rem(seq_ref[0] // 2 + k, pairs)
        for i in range(2):
            at = 2 * pair + i
            acc, largest, total = blend([own_ref[at], other_ref[at]], rows)
            level = jnp.where(lane < KEY_VALUE_HEADS, largest + jnp.log(total), 0.0)
            high = round16(level)
            middle = round16(level - high)
            rest = level - high - middle
            side = high + pltpu.roll(middle, 8, 1) + pltpu.roll(rest, 16, 1)
            for j, tile in enumerate(acc):
                out_ref[i, :, j * LANES : (j + 1) * LANES] = tile.astype(BF16)
            out_ref[i, :, KV_WIDTH : KV_WIDTH + LANES] = side.astype(BF16)


def join_pair(seq_index, own, other):
    devices, rows, width = own.shape
    smem, vmem = pl.BlockSpec(memory_space=pltpu.SMEM), pl.BlockSpec(memory_space=pltpu.VMEM)
    return pl.pallas_call(
        join_pair_kernel,
        in_specs=[smem, vmem, vmem],
        out_shape=(jax.ShapeDtypeStruct((2, rows, width), BF16),) * (devices // 2),
        compiler_params=params(),
        name="join_pair",
    )(seq_index, own, other)


def join_kernel(*refs):
    x_refs, out_ref = refs[:-1], refs[-1]
    _, rows, _ = x_refs[0].shape
    tokens = rows // GROUP
    low_tokens = iota((tokens, LANES), 1) < HEAD_SIZE
    for i in range(2):
        acc, _, _ = blend([x_ref[i] for x_ref in x_refs], rows)

        def piece(head, half):
            k, g = head // GROUP, head % GROUP
            tile = jnp.concatenate(
                [acc[k // 2][t * GROUP + g : t * GROUP + g + 1] for t in range(tokens)], axis=0
            )
            return tile if k % 2 == half else swap_halves(tile)

        for m in range(QUERY_HEADS // 2):
            tile = jnp.where(low_tokens, piece(2 * m, 0), piece(2 * m + 1, 1)).astype(BF16)
            out_ref[i, :, m * LANES : (m + 1) * LANES] = tile


def join(parts):
    rows = parts[0].shape[1]
    return pl.pallas_call(
        join_kernel,
        out_shape=jax.ShapeDtypeStruct((2, rows // GROUP, QUERY_HEADS * HEAD_SIZE), BF16),
        compiler_params=params(),
        name="join",
    )(*parts)


def side_place(features, count):
    tile, offset = features // LANES * LANES, features % LANES
    return (tile, offset) if offset and offset + count <= LANES else (padded(features), 0)


def hidden_kernel(seq_ref, residual_ref, w_ref, gain_ref, routes_ref, *refs):
    attn_refs, (hidden_ref, out_ref, wide_ref) = refs[:-3], refs[-3:]
    steps, requests, features = residual_ref.shape
    tokens = steps * requests
    blocks = [ref[i].astype(F32) for ref in attn_refs for i in range(2)]
    attn = jnp.concatenate(blocks, axis=0).astype(BF16)
    row, column = iota((tokens, tokens), 0), iota((tokens, tokens), 1)
    devices, share = len(blocks), attn_refs[0].shape[1]
    source = seq_ref[0] // 2 * 2 + devices - column // (2 * share) * 2
    source = jnp.where(source >= devices, source - devices, source)
    token = source * share + column % (2 * share)
    reorder = jnp.logical_and(row % requests == token // steps, row // requests == token % steps)
    attn = dot_nn(reorder.astype(F32).astype(BF16), attn).astype(BF16)
    residual = residual_ref[...].astype(F32).reshape(tokens, features)
    hidden = residual + dot_nt(attn, w_ref[...])
    hidden_ref[...] = hidden
    squares = jnp.sum(hidden * hidden, axis=1, keepdims=True)
    tile, offset = side_place(features, SIDE_KEYS + EXPERTS)
    wide_ref[...] = jnp.zeros_like(wide_ref)
    wide_ref[:, 0:features] = hidden * gain_ref[...]
    routes = routes_ref[...].reshape(tokens, routes_ref.shape[2])
    lane = iota((tokens, LANES), 1) - offset
    side = wide_ref[:, tile : tile + LANES]
    for k in range(routes.shape[1]):
        side = jnp.where(lane == routes[:, k : k + 1] + SIDE_KEYS, 1.0, side)
    high = round16(squares)
    side = jnp.where(lane == 0, high, side)
    wide_ref[:, tile : tile + LANES] = jnp.where(lane == 1, squares - high, side)
    out_ref[...] = wide_ref[...].astype(BF16)


def hidden_state(seq_index, attn, residual, w_out, gain, routes):
    steps, requests, features = residual.shape
    tokens = steps * requests
    wide = side_place(features, SIDE_KEYS + EXPERTS)[0] + LANES
    smem, vmem = pl.BlockSpec(memory_space=pltpu.SMEM), pl.BlockSpec(memory_space=pltpu.VMEM)
    return pl.pallas_call(
        hidden_kernel,
        in_specs=[smem] + [vmem] * (4 + len(attn)),
        out_shape=(
            jax.ShapeDtypeStruct((tokens, features), F32),
            jax.ShapeDtypeStruct((tokens, wide), BF16),
        ),
        scratch_shapes=[pltpu.VMEM((tokens, wide), F32)],
        compiler_params=params(),
        name="hidden",
    )(seq_index, residual, w_out.T, gain.reshape(1, features), routes, *attn)


def window_start(first, rows, window):
    return pl.multiple_of(jnp.clip(first // 16 * 16, 0, rows - window), 16)


def gate_up_kernel(
    features, local, turn, sources, devices, where_ref, seq_ref, w_ref, router_ref, *refs,
):
    part_refs, refs = refs[:sources], refs[sources:]
    out_refs, refs = refs[:devices], refs[devices:]
    pick_ref, range_ref, first_ref, most_ref, x_ref, pair_ref, acc_ref, share_ref = refs
    total = x_ref.shape[0]
    for e, part_ref in enumerate(part_refs):
        x_ref[e * (total // sources) : (e + 1) * (total // sources)] = part_ref[...]
    rows = pick_ref.shape[1]
    width = w_ref.shape[3]
    window = total // 2 + 16
    tile, offset = side_place(features, SIDE_KEYS + EXPERTS)
    me = where_ref[0]
    own_side = x_ref[:, tile : tile + LANES].astype(F32)
    lane = iota((total, LANES), 1)
    flags = pltpu.roll(own_side, LANES - offset - SIDE_KEYS, 1)
    flags = jnp.where(lane < EXPERTS, flags, 0.0)
    owners = EXPERTS // local
    counts = jnp.sum(flags, axis=0, keepdims=True)
    most = jnp.int32(0)
    for o in range(owners):
        held = jnp.logical_and(lane[0:1] >= o * local, lane[0:1] < (o + 1) * local)
        most = jnp.maximum(most, jnp.sum(jnp.where(held, counts, 0.0)).astype(jnp.int32))
    most_ref[0] = most
    mine = pltpu.roll(flags, lax.rem(LANES - me * local, LANES), 1)
    mine = jnp.where(lane < local, mine, 0.0)
    mine16 = mine.astype(BF16)
    row, column = iota((total, total), 0), iota((total, total), 1)
    earlier = (column < row).astype(F32).astype(BF16)
    ranks = dot_nn(earlier, mine16)
    counts = jnp.sum(mine, axis=0, keepdims=True)
    before = (iota((LANES, LANES), 0) < iota((LANES, LANES), 1)).astype(F32).astype(BF16)
    first = dot_nn(jnp.broadcast_to(counts, (8, LANES)).astype(BF16), before)[0:1] - turn * rows
    place = jnp.where(mine > 0.0, first + ranks, -1.0).astype(jnp.int32)
    at = iota((total, rows), 1)
    pick = jnp.zeros((total, rows), F32)
    for j in range(local):
        pick = jnp.where(at == place[:, j : j + 1], 1.0, pick)
    pick = pick.astype(BF16)
    pick_ref[...] = pick
    ranges = jnp.where(iota((16, LANES), 0) < 8, first, first + counts)
    ranges = jnp.concatenate([ranges[0:8], ranges[8:16]] + [jnp.zeros((LANES - 16, LANES), F32)], axis=0)
    ranges = ranges.T
    range_ref[...] = ranges[0:16]
    picked = dot_tn(pick, x_ref[...]).astype(BF16)
    doubled = pair_ref.shape[2]
    feature, place = iota((x_ref.shape[1], doubled), 0), iota((x_ref.shape[1], doubled), 1)
    double = jnp.logical_and(place == 2 * feature, feature < features)
    evens = dot_nn(picked, double.astype(F32).astype(BF16))
    pair_ref[0] = evens.astype(BF16)
    for j in range(doubled // LANES):
        odds = pltpu.roll(tile_of(evens, j), 1, 1)
        pair_ref[1, :, j * LANES : (j + 1) * LANES] = odds.astype(BF16)
    acc_ref[...] = jnp.zeros_like(acc_ref)
    for j in range(local):
        start_row = jnp.sum(first[:, j : j + 1]).astype(jnp.int32)
        first_ref[j] = start_row
        start = window_start(start_row, rows, window)
        part = jnp.concatenate(
            [pair_ref[half, pl.ds(start, window), 0 : 2 * features] for half in range(2)], axis=0
        )
        made = dot_nn(part, w_ref[j].reshape(2 * features, width))
        fresh = start + iota((window, width), 0) >= start_row
        for half in range(2):
            into = (pl.ds(start, window), slice(half * width, (half + 1) * width))
            acc_ref[into] = jnp.where(fresh, made[half * window : (half + 1) * window], acc_ref[into])
    logits = dot_nt(router_ref[...], x_ref[:, 0:features])
    high = round16(logits)
    both = jnp.concatenate([high, logits - high], axis=0).astype(BF16)
    both = dot_nn(both, pick)
    turned = jnp.zeros((EXPERTS, rows), jnp.bool_)
    expert = iota((EXPERTS, rows), 0) - me * local
    where_row = iota((EXPERTS, rows), 1).astype(F32)
    for j in range(local):
        inside = jnp.logical_and(
            where_row >= first[:, j : j + 1], where_row < (first + counts)[:, j : j + 1]
        )
        turned = jnp.logical_or(turned, jnp.logical_and(inside, expert == j))
    squares = dot_tn(own_side.astype(BF16), pick)
    side = jnp.concatenate(
        [
            jnp.sum(jnp.where(turned, both[0:EXPERTS], 0.0), axis=0, keepdims=True),
            jnp.sum(jnp.where(turned, both[EXPERTS : 2 * EXPERTS], 0.0), axis=0, keepdims=True),
            squares[offset : offset + 2],
            jnp.zeros((12, rows), F32),
        ],
        axis=0,
    )
    share = share_ref.shape[1] - 16
    low = iota((share, LANES), 1) < PIECE_WIDTH
    for b in range(devices):
        piece, start = b % PIECES, b // PIECES * share
        tile = piece // 2 * LANES
        gate = acc_ref[start : start + share, tile : tile + LANES]
        up = acc_ref[start : start + share, width + tile : width + tile + LANES]
        if piece % 2 == 0:
            made = jnp.where(low, gate, swap_halves(up))
        else:
            made = jnp.where(low, swap_halves(gate), up)
        share_ref[b, 0:share, :] = made.astype(BF16)
        if piece == 0:
            strips = []
            for at in range(0, share, LANES):
                size = min(LANES, share - at)
                strip = side[0:4, start + at : start + at + size]
                if size < LANES:
                    strip = jnp.concatenate([strip, jnp.zeros((4, LANES - size), F32)], axis=1)
                strips.append(strip)
            strips.append(jnp.zeros((16 - 4 * len(strips), LANES), F32))
            strips = jnp.concatenate(strips, axis=0).astype(BF16)
        share_ref[b, share : share + 16, :] = strips
    for k, out_ref in enumerate(out_refs):
        out_ref[...] = share_ref[lax.rem(seq_ref[0] + k, devices)]


def gate_up(exp_index, seq_index, tokens, weights, w_router, rows, devices, turn):
    local, features, _, width = weights.shape
    sources, wide = len(tokens), tokens[0].shape[1]
    total = sources * tokens[0].shape[0]
    share = (rows * PIECES // devices + 16, LANES)
    smem, vmem = pl.BlockSpec(memory_space=pltpu.SMEM), pl.BlockSpec(memory_space=pltpu.VMEM)
    return pl.pallas_call(
        functools.partial(gate_up_kernel, features, local, turn, sources, devices),
        in_specs=[smem] * 2 + [vmem] * (2 + sources),
        out_specs=(vmem,) * devices + (vmem, vmem, smem, smem),
        out_shape=(jax.ShapeDtypeStruct(share, BF16),) * devices
        + (
            jax.ShapeDtypeStruct((total, rows), BF16),
            jax.ShapeDtypeStruct((16, LANES), F32),
            jax.ShapeDtypeStruct((16,), jnp.int32),
            jax.ShapeDtypeStruct((1,), jnp.int32),
        ),
        scratch_shapes=[
            pltpu.VMEM((total, wide), BF16),
            pltpu.VMEM((2, rows, padded(2 * features)), BF16),
            pltpu.VMEM((rows, 2 * width), F32),
            pltpu.VMEM((devices,) + share, BF16),
        ],
        compiler_params=params(),
        name="gate_up",
    )(exp_index, seq_index, weights, w_router.T, *tokens)


def inner_kernel(*refs):
    x_refs, (out_ref, logit_ref) = refs[:-2], refs[-2:]
    share = x_refs[0].shape[0] - 16
    half = share // 2

    def total(start, size):
        return functools.reduce(
            jnp.add, [x_ref[start : start + size].astype(F32) for x_ref in x_refs]
        )

    side = total(share, 16)
    columns, logits = [], []
    for strip in range(-(-share // LANES)):
        values = side[4 * strip : 4 * strip + 4]
        inverse = lax.rsqrt((values[2:3] + values[3:4]) * (1.0 / D) + 1e-6)
        logits.append((values[0:1] + values[1:2]) * inverse)
        columns.append(jnp.broadcast_to(inverse, (LANES, LANES)).T)
    logit_ref[...] = jnp.concatenate(logits + [jnp.zeros((8 - len(logits), LANES), F32)], axis=0)
    scaled = total(0, share) * jnp.concatenate(columns, axis=0)[0:share]
    made = scaled / (1.0 + jnp.exp(-scaled)) * swap_halves(scaled)
    low = iota((half, LANES), 1) < PIECE_WIDTH
    made = jnp.where(low, made[0:half], swap_halves(made[half:share])).astype(BF16)
    out_ref[...] = made


def inner(parts):
    return pl.pallas_call(
        inner_kernel,
        out_shape=(
            jax.ShapeDtypeStruct(((parts[0].shape[0] - 16) // 2, LANES), BF16),
            jax.ShapeDtypeStruct((8, LANES), F32),
        ),
        compiler_params=params(),
        name="inner",
    )(*parts)


def down_kernel(features, local, pairs, first_ref, seq_ref, range_ref, pick_ref, w_ref, logit_ref, *refs):
    pair_refs, out_refs, (x_ref, row_ref, made_ref) = refs[:pairs], refs[pairs:-3], refs[-3:]
    total, rows = pick_ref.shape
    width = w_ref.shape[2]
    window = total // 2 + 16
    devices, half, _ = x_ref.shape
    for k, pair_ref in enumerate(pair_refs):
        source = lax.rem(seq_ref[0] + devices - 2 * k, devices)
        x_ref[source] = pair_ref[0]
        x_ref[source + 1 - lax.rem(source, 2) * 2] = pair_ref[1]
    share = 2 * half
    low = iota((half, LANES), 1) < PIECE_WIDTH
    for b in range(0, devices, 2):
        start, tile = b // PIECES * share, b % PIECES // 2 * LANES
        one, two = x_ref[b].astype(F32), x_ref[b + 1].astype(F32)
        above = jnp.where(low, one, swap_halves(two)).astype(BF16)
        below = jnp.where(low, swap_halves(one), two).astype(BF16)
        row_ref[start : start + half, tile : tile + LANES] = above
        row_ref[start + half : start + share, tile : tile + LANES] = below
    logit = []
    for piece in range(devices // PIECES):
        for strip in range(-(-share // LANES)):
            size = min(LANES, share - strip * LANES)
            logit.append(logit_ref[piece, strip : strip + 1, 0:size])
    made_ref[...] = jnp.zeros_like(made_ref)
    for j in range(local):
        start_row = first_ref[j]
        start = window_start(start_row, rows, window)
        made = dot_nt(row_ref[pl.ds(start, window), :], w_ref[j])
        fresh = start + iota((window, features), 0) >= start_row
        into = (pl.ds(start, window), slice(0, features))
        made_ref[into] = jnp.where(fresh, made, made_ref[into])
    logit = jnp.concatenate(logit, axis=1)
    high = round16(logit)
    middle = round16(logit - high)
    pick = pick_ref[...]
    where_row = iota((16, rows), 1).astype(F32)
    inside = jnp.logical_and(where_row >= range_ref[:, 0:1], where_row < range_ref[:, 8:9])
    inside = jnp.logical_and(inside, iota((16, rows), 0) < local)
    spread = [jnp.where(inside, part, 0.0) for part in (high, middle, logit - high - middle)]
    spread.append(inside.astype(F32))
    found = dot_nt(jnp.concatenate(spread, axis=0).astype(BF16), pick)
    valid = found[48:64] > 0.5
    logits = jnp.where(valid, found[0:16] + found[16:32] + found[32:48], NEG_FILL)
    top = jnp.max(logits, axis=0, keepdims=True)
    weights = jnp.where(valid, jnp.exp(logits - top), 0.0)
    summed = jnp.sum(weights, axis=0, keepdims=True)
    high = round16(weights)
    both = dot_nn(jnp.concatenate([high, weights - high], axis=0).astype(BF16), pick)
    weight = jnp.sum(jnp.where(inside, both[0:16] + both[16:32], 0.0), axis=0, keepdims=True)
    column = jnp.broadcast_to(weight, (LANES, rows)).T[:, 0:1]
    acc = dot_nn(pick, (made_ref[...] * column).astype(BF16))
    tile, offset = side_place(features, 2)
    pair = jnp.where(iota((LANES, total), 0) == 0, top, summed).T
    tokens = total // len(out_refs)
    for e, out_ref in enumerate(out_refs):
        at = slice(e * tokens, (e + 1) * tokens)
        out_ref[...] = acc[at]
        lane = iota((tokens, LANES), 1) - offset
        side = jnp.where(lane == 0, pair[at, 0:1], acc[at, tile : tile + LANES])
        out_ref[:, tile : tile + LANES] = jnp.where(lane == 1, pair[at, 1:2], side)


def down(first, seq_index, ranges, pick, made, logits, weights, exp_count):
    local, features, width = weights.shape
    total, rows = pick.shape
    wide = side_place(features, 2)[0] + LANES
    smem, vmem = pl.BlockSpec(memory_space=pltpu.SMEM), pl.BlockSpec(memory_space=pltpu.VMEM)
    return pl.pallas_call(
        functools.partial(down_kernel, features, local, len(made)),
        in_specs=[smem] * 2 + [vmem] * (4 + len(made)),
        out_shape=(jax.ShapeDtypeStruct((total // exp_count, wide), F32),) * exp_count,
        scratch_shapes=[
            pltpu.VMEM((2 * len(made),) + made[0].shape[1:], BF16),
            pltpu.VMEM((rows, width), BF16),
            pltpu.VMEM((rows, wide), F32),
        ],
        compiler_params=params(),
        name="down",
    )(first, seq_index, ranges, pick, weights, logits, *made)


def finish_kernel(hidden_ref, *refs):
    part_refs, out_ref = refs[:-1], refs[-1]
    features = hidden_ref.shape[1]
    tile, offset = side_place(features, 2)
    sides = [x_ref[:, tile : tile + LANES] for x_ref in part_refs]
    tops = [side[:, offset : offset + 1] for side in sides]
    top = functools.reduce(jnp.maximum, tops)
    scales = [jnp.exp(one - top) for one in tops]
    total = functools.reduce(
        jnp.add, [s * side[:, offset + 1 : offset + 2] for s, side in zip(scales, sides)]
    )
    acc = functools.reduce(
        jnp.add, [s * x_ref[:, 0:features] for x_ref, s in zip(part_refs, scales)]
    )
    out = hidden_ref[...] + acc * (1.0 / total)
    out_ref[...] = out.reshape(out_ref.shape).astype(BF16)


def finish(parts, hidden, shape):
    return pl.pallas_call(
        finish_kernel,
        out_shape=jax.ShapeDtypeStruct(shape, BF16),
        compiler_params=params(),
        name="finish",
    )(hidden, *parts)


def join_rounds(features, one, other):
    tile, offset = side_place(features, 2)
    at = tile + offset
    top = jnp.maximum(one[..., at : at + 1], other[..., at : at + 1])
    scales = [jnp.exp(part[..., at : at + 1] - top) for part in (one, other)]
    joined = one * scales[0] + other * scales[1]
    return jnp.where(jnp.arange(one.shape[-1]) == at, top, joined)


def send(x, axis, distance):
    count = lax.axis_size(axis)
    return lax.ppermute(x, axis, [(i, (i + distance) % count) for i in range(count)])


def neighbour(x, axis):
    return lax.ppermute(x, axis, [(i, i ^ 1) for i in range(lax.axis_size(axis))])


def exchange(parts, axis, direction):
    return [parts[0]] + [send(part, axis, direction * k) for k, part in enumerate(parts) if k]


def gather(block, axis):
    return exchange([block] * lax.axis_size(axis), axis, 1)


def local(
    queries,
    new_key_value,
    key_value_cache,
    page_table,
    cache_len,
    routes,
    residual,
    w_out,
    norm_gain,
    w_router,
    w_gate_up,
    w_down,
):
    exp_count = lax.axis_size("exp")
    seq_count = lax.axis_size("seq")
    exp_index = lax.axis_index("exp").astype(jnp.int32).reshape(1)
    seq_index = lax.axis_index("seq").astype(jnp.int32).reshape(1)
    steps, requests, width = queries.shape
    tokens = steps * requests
    features = w_out.shape[1]
    page_rows = key_value_cache.shape[2]
    pool = key_value_cache.reshape(-1, page_rows, 2, KV_WIDTH)

    shares = attend(
        queries, new_key_value, pool, page_table, cache_len, seq_index, seq_count
    )
    shares = join_pair(seq_index, shares, neighbour(shares, "seq"))
    attn = join(exchange(shares, "seq", 2))
    gathered = exchange([attn] * (seq_count // 2), "seq", 2)
    hidden, outgoing = hidden_state(seq_index, gathered, residual, w_out, norm_gain, routes)
    incoming = gather(outgoing, "exp")
    pieces = seq_count // PIECES
    rows = -(-ROUND_ROWS // (32 * pieces)) * 32 * pieces

    def one_round(turn):
        *partial, pick, ranges, first, most = gate_up(
            exp_index, seq_index, incoming, w_gate_up, w_router, rows, seq_count, turn
        )
        made, logits = inner(exchange(partial, "seq", 1))
        logits = logits[None] if pieces == 1 else lax.all_gather(logits, "seq")[::PIECES]
        made = jnp.stack([made, neighbour(made, "seq")])
        made = exchange([made] * (seq_count // 2), "seq", 2)
        return down(first, seq_index, ranges, pick, made, logits, w_down, exp_count), most

    made, most = one_round(0)
    pairs = w_gate_up.shape[0] * exp_count * steps * CAP
    for turn in range(1, -(-pairs // rows)):
        made = lax.cond(
            most[0] > turn * rows,
            lambda made: tuple(
                join_rounds(features, *both) for both in zip(made, one_round(turn)[0])
            ),
            lambda made: made,
            made,
        )
    return finish(exchange(made, "exp", -1), hidden, (steps, requests, features))


def solution(mesh):
    in_specs = (
        P(None, "exp", None),
        P(None, "exp", None, None),
        P("exp", "seq", None, None, None),
        P("exp", "seq"),
        P("exp"),
        P(None, "exp", None),
        P(None, "exp", "seq"),
        P(None, "seq"),
        P("seq"),
        P("seq", None),
        P("exp", "seq", None, None),
        P("exp", "seq", None),
    )
    out_specs = P(None, "exp", "seq")
    return jax.shard_map(local, mesh=mesh, in_specs=in_specs, out_specs=out_specs, check_vma=False)
```

```python
import functools

import jax
import jax.numpy as jnp
from jax import lax
from jax.experimental import pallas as pl
from jax.experimental.pallas import tpu as pltpu
from jax.sharding import PartitionSpec as P

D = 1536
QUERY_HEADS = 24
KEY_VALUE_HEADS = 8
HEAD_SIZE = 64
GROUP = QUERY_HEADS // KEY_VALUE_HEADS
KV_WIDTH = KEY_VALUE_HEADS * HEAD_SIZE
EXPERTS = 40
FF = 512
CAP = 4
LANES = 128
SIDE_KEYS = 2
ROUND_ROWS = 352
PIECES = 8
PIECE_WIDTH = FF // PIECES

NEG_FILL = -1e30
F32 = jnp.float32
BF16 = jnp.bfloat16
VMEM_LIMIT = 48 * 1024 * 1024
ATTEND_VMEM = 60 * 1024 * 1024


def iota(shape, dimension):
    return lax.broadcasted_iota(jnp.int32, shape, dimension)


def dot_nt(a, b):
    return lax.dot_general(a, b, (((1,), (1,)), ((), ())), preferred_element_type=F32)


def dot_tn(a, b):
    return lax.dot_general(a, b, (((0,), (0,)), ((), ())), preferred_element_type=F32)


def dot_nn(a, b):
    return lax.dot_general(a, b, (((1,), (0,)), ((), ())), preferred_element_type=F32)


def round16(x):
    return x.astype(BF16).astype(F32)


def swap_halves(x):
    return pltpu.roll(x, HEAD_SIZE, 1)


def tile_of(x, index):
    return x[:, index * LANES : (index + 1) * LANES]


def padded(width):
    return -(-width // LANES) * LANES


def params():
    return pltpu.CompilerParams(vmem_limit_bytes=VMEM_LIMIT)


def attend_kernel(
    classes, seq_ref, table_hbm, len_hbm, q_hbm, fresh_hbm, cache_ref, share_ref,
    page_ref, split_ref, table_ref, len_ref, q_ref, fresh_ref, query_ref, new_ref, sems, small_sems,
):
    steps, requests, _ = q_ref.shape
    page_rows = cache_ref.shape[1]
    pages = table_ref.shape[1]
    span = pages * page_rows
    first = seq_ref[0] * span
    small = [
        pltpu.make_async_copy(source, target, small_sems.at[i])
        for i, (source, target) in enumerate(
            [(table_hbm, table_ref), (len_hbm, len_ref), (q_hbm, q_ref), (fresh_hbm, fresh_ref)]
        )
    ]
    for one in small:
        one.start()
    for one in small[:2]:
        one.wait()

    share = share_ref.shape[1]
    per_request = steps * GROUP // share

    def put(r, acc, side):
        for i in range(per_request):
            at = r * per_request + i
            share_ref[at, :, 0:KV_WIDTH] = acc[i * share : (i + 1) * share]
            share_ref[at, :, KV_WIDTH : KV_WIDTH + LANES] = side[i * share : (i + 1) * share]

    def copy(r, page):
        at = r * pages + page
        return pltpu.make_async_copy(cache_ref.at[table_ref[r, page]], page_ref.at[at], sems.at[at])

    def needed(r, low):
        return len_ref[r] - first > low * page_rows

    bounds = list(zip((0,) + classes[:-1], classes))

    def start(r, carry):
        for low, high in bounds:

            @pl.when(needed(r, low))
            def _():
                for page in range(low, high):
                    copy(r, page).start()

        return carry

    lax.fori_loop(0, requests, start, 0)
    for one in small[2:]:
        one.wait()

    low = iota((requests, LANES), 1) < HEAD_SIZE
    for t in range(steps):
        q = q_ref[t].astype(F32) * 0.125
        for g in range(GROUP):
            for j in range(KV_WIDTH // LANES):
                one = tile_of(q, (6 * j + g) // 2)
                two = tile_of(q, (6 * j + 3 + g) // 2)
                if g % 2 == 0:
                    tile = jnp.where(low, one, two)
                else:
                    tile = swap_halves(jnp.where(low, two, one))
                query_ref[t * GROUP + g, :, j * LANES : (j + 1) * LANES] = tile
        new_ref[t] = fresh_ref[t].reshape(2 * requests, KV_WIDTH).astype(F32)

    rows = steps * GROUP * KEY_VALUE_HEADS
    own = iota((rows, KV_WIDTH), 1) // HEAD_SIZE == iota((rows, KV_WIDTH), 0) % KEY_VALUE_HEADS
    lane = iota((rows, LANES), 1)
    head = iota((rows, LANES), 0) % KEY_VALUE_HEADS
    row_step = iota((rows, 16), 0) // (GROUP * KEY_VALUE_HEADS)
    kept = jnp.logical_and(iota((rows, 16), 1) <= row_step, seq_ref[0] == 0)
    fresh_bias = jnp.where(kept, 0.0, NEG_FILL)

    def fresh_rows(r, which):
        found = [new_ref[u, pl.ds(2 * r + which, 1), :] for u in range(steps)]
        return jnp.concatenate(found + [jnp.zeros((16 - steps, KV_WIDTH), F32)], axis=0).astype(BF16)

    def attend_pages(r, count):
        spread = jnp.concatenate(
            [
                jnp.broadcast_to(query_ref[i, pl.ds(r, 1), :], (KEY_VALUE_HEADS, KV_WIDTH))
                for i in range(steps * GROUP)
            ],
            axis=0,
        )
        spread = jnp.where(own, spread, 0.0).astype(BF16)
        halves = ([], [])
        for page in range(count):
            copy(r, page).wait()
            block = page_ref[r * pages + page].reshape(2 * page_rows, KV_WIDTH).astype(F32)
            for j in range(KV_WIDTH // LANES):
                split_ref[page, j] = tile_of(block, j)
            for which in range(2):
                tiles = [
                    split_ref[page, j, pl.ds(which, page_rows, 2), :] for j in range(KV_WIDTH // LANES)
                ]
                halves[which].append(jnp.concatenate(tiles, axis=1).astype(BF16))
        keys, values = jnp.concatenate(halves[0], axis=0), jnp.concatenate(halves[1], axis=0)
        live = first + iota((1, count * page_rows), 1) < len_ref[r]
        scores = dot_nt(spread, keys) + jnp.where(live, 0.0, NEG_FILL)
        fresh_scores = dot_nt(spread, fresh_rows(r, 0)) + fresh_bias
        largest = jnp.maximum(
            jnp.max(scores, axis=1, keepdims=True), jnp.max(fresh_scores, axis=1, keepdims=True)
        )
        weights = jnp.exp(scores - largest)
        fresh_weights = jnp.exp(fresh_scores - largest)
        total = jnp.sum(weights, axis=1, keepdims=True)
        total = total + jnp.sum(fresh_weights, axis=1, keepdims=True)
        acc = dot_nn(weights.astype(BF16), values)
        acc = acc + dot_nn(fresh_weights.astype(BF16), fresh_rows(r, 1))
        acc = jnp.where(own, acc * (1.0 / total), 0.0)
        acc = jnp.sum(acc.reshape(steps * GROUP, KEY_VALUE_HEADS, KV_WIDTH), axis=1)
        level = largest + jnp.log(total)
        high = round16(level)
        middle = round16(level - high)
        side = jnp.where(lane == head, high, 0.0)
        side = jnp.where(lane == head + 8, middle, side)
        side = jnp.where(lane == head + 16, level - high - middle, side)
        side = jnp.sum(side.reshape(steps * GROUP, KEY_VALUE_HEADS, LANES), axis=1)
        return acc.astype(BF16), side.astype(BF16)

    def one_request(r, carry):
        for low, high in bounds:
            enough = needed(r, low)
            if high < pages:
                enough = jnp.logical_and(enough, jnp.logical_not(needed(r, high)))

            @pl.when(enough)
            def _():
                put(r, *attend_pages(r, high))

        @pl.when(jnp.logical_not(needed(r, 0)))
        def _():
            empty = jnp.where(iota((steps * GROUP, LANES), 1) < KEY_VALUE_HEADS, NEG_FILL, 0.0)
            put(r, jnp.zeros((steps * GROUP, KV_WIDTH), BF16), empty.astype(BF16))

        return carry

    lax.fori_loop(0, requests, one_request, 0)


def attend(queries, new_key_value, cache, page_table, cache_len, seq_index, devices):
    steps, requests, _ = queries.shape
    pages = page_table.shape[1]
    page_rows = cache.shape[1]
    classes = tuple(c for c in (2, 4, 6) if c < pages) + (pages,)
    share = (requests * steps * GROUP // devices, KV_WIDTH + LANES)
    smem, hbm = pl.BlockSpec(memory_space=pltpu.SMEM), pl.BlockSpec(memory_space=pl.ANY)
    return pl.pallas_call(
        functools.partial(attend_kernel, classes),
        in_specs=[smem] + [hbm] * 5,
        out_shape=jax.ShapeDtypeStruct((devices,) + share, BF16),
        scratch_shapes=[
            pltpu.VMEM((requests * pages, page_rows, 2, KV_WIDTH), BF16),
            pltpu.VMEM((pages, KV_WIDTH // LANES, 2 * page_rows, LANES), F32),
            pltpu.SMEM(page_table.shape, jnp.int32),
            pltpu.SMEM(cache_len.shape, jnp.int32),
            pltpu.VMEM(queries.shape, BF16),
            pltpu.VMEM(new_key_value.shape, BF16),
            pltpu.VMEM((steps * GROUP, requests, KV_WIDTH), F32),
            pltpu.VMEM((steps, 2 * requests, KV_WIDTH), F32),
            pltpu.SemaphoreType.DMA((requests * pages,)),
            pltpu.SemaphoreType.DMA((4,)),
        ],
        compiler_params=pltpu.CompilerParams(vmem_limit_bytes=ATTEND_VMEM),
        name="attend",
    )(seq_index, page_table, cache_len, queries, new_key_value, cache)


def join_kernel(x_ref, out_ref):
    blocks, rows, _ = x_ref.shape
    tokens = rows // GROUP
    levels = []
    for b in range(blocks):
        side = x_ref[b, :, KV_WIDTH : KV_WIDTH + LANES].astype(F32)
        levels.append(side + pltpu.roll(side, LANES - 8, 1) + pltpu.roll(side, LANES - 16, 1))
    largest = functools.reduce(jnp.maximum, levels)
    weights = [jnp.exp(level - largest) for level in levels]
    inverse = 1.0 / functools.reduce(jnp.add, weights)
    low = iota((rows, LANES), 1) < HEAD_SIZE
    acc = [jnp.zeros((rows, LANES), F32) for _ in range(KV_WIDTH // LANES)]
    for b in range(blocks):
        share = weights[b] * inverse
        for j in range(KV_WIDTH // LANES):
            factor = jnp.where(low, share[:, 2 * j : 2 * j + 1], share[:, 2 * j + 1 : 2 * j + 2])
            acc[j] = acc[j] + factor * x_ref[b, :, j * LANES : (j + 1) * LANES].astype(F32)

    def piece(head, half):
        k, g = head // GROUP, head % GROUP
        tile = jnp.concatenate(
            [acc[k // 2][t * GROUP + g : t * GROUP + g + 1] for t in range(tokens)], axis=0
        )
        return tile if k % 2 == half else swap_halves(tile)

    low_tokens = iota((tokens, LANES), 1) < HEAD_SIZE
    for m in range(QUERY_HEADS // 2):
        tile = jnp.where(low_tokens, piece(2 * m, 0), piece(2 * m + 1, 1)).astype(BF16)
        out_ref[:, m * LANES : (m + 1) * LANES] = tile


def join(parts):
    rows = parts.shape[1]
    return pl.pallas_call(
        join_kernel,
        out_shape=jax.ShapeDtypeStruct((rows // GROUP, QUERY_HEADS * HEAD_SIZE), BF16),
        compiler_params=params(),
        name="join",
    )(parts)


def side_place(features, count):
    tile, offset = features // LANES * LANES, features % LANES
    return (tile, offset) if offset and offset + count <= LANES else (padded(features), 0)


def hidden_kernel(seq_ref, residual_ref, w_ref, gain_ref, routes_ref, *refs):
    attn_refs, (hidden_ref, out_ref, wide_ref) = refs[:-3], refs[-3:]
    steps, requests, features = residual_ref.shape
    tokens = steps * requests
    blocks = [ref[i].astype(F32) for ref in attn_refs for i in range(2)]
    attn = jnp.concatenate(blocks, axis=0).astype(BF16)
    row, column = iota((tokens, tokens), 0), iota((tokens, tokens), 1)
    devices, share = len(blocks), attn_refs[0].shape[1]
    source = seq_ref[0] + devices - column // (2 * share) * 2
    source = jnp.where(source >= devices, source - devices, source)
    other = column // share % 2
    source = source + other * (1 - source % 2 * 2)
    token = source * share + column % share
    reorder = jnp.logical_and(row % requests == token // steps, row // requests == token % steps)
    attn = dot_nn(reorder.astype(F32).astype(BF16), attn).astype(BF16)
    residual = residual_ref[...].astype(F32).reshape(tokens, features)
    hidden = residual + dot_nt(attn, w_ref[...])
    hidden_ref[...] = hidden
    squares = jnp.sum(hidden * hidden, axis=1, keepdims=True)
    tile, offset = side_place(features, SIDE_KEYS + EXPERTS)
    wide_ref[...] = jnp.zeros_like(wide_ref)
    wide_ref[:, 0:features] = hidden * gain_ref[...]
    routes = routes_ref[...].reshape(tokens, routes_ref.shape[2])
    lane = iota((tokens, LANES), 1) - offset
    side = wide_ref[:, tile : tile + LANES]
    for k in range(routes.shape[1]):
        side = jnp.where(lane == routes[:, k : k + 1] + SIDE_KEYS, 1.0, side)
    high = round16(squares)
    side = jnp.where(lane == 0, high, side)
    wide_ref[:, tile : tile + LANES] = jnp.where(lane == 1, squares - high, side)
    out_ref[...] = wide_ref[...].astype(BF16)


def hidden_state(seq_index, attn, residual, w_out, gain, routes):
    steps, requests, features = residual.shape
    tokens = steps * requests
    wide = side_place(features, SIDE_KEYS + EXPERTS)[0] + LANES
    smem, vmem = pl.BlockSpec(memory_space=pltpu.SMEM), pl.BlockSpec(memory_space=pltpu.VMEM)
    return pl.pallas_call(
        hidden_kernel,
        in_specs=[smem] + [vmem] * (4 + len(attn)),
        out_shape=(
            jax.ShapeDtypeStruct((tokens, features), F32),
            jax.ShapeDtypeStruct((tokens, wide), BF16),
        ),
        scratch_shapes=[pltpu.VMEM((tokens, wide), F32)],
        compiler_params=params(),
        name="hidden",
    )(seq_index, residual, w_out.T, gain.reshape(1, features), routes, *attn)


def window_start(first, rows, window):
    return pl.multiple_of(jnp.clip(first // 16 * 16, 0, rows - window), 16)


def gate_up_kernel(
    features, local, turn, sources, devices, where_ref, seq_ref, w_ref, router_ref, *refs,
):
    part_refs, refs = refs[:sources], refs[sources:]
    out_refs, refs = refs[:devices], refs[devices:]
    pick_ref, range_ref, first_ref, most_ref, x_ref, row_ref, acc_ref, share_ref = refs
    total = x_ref.shape[0]
    for e, part_ref in enumerate(part_refs):
        x_ref[e * (total // sources) : (e + 1) * (total // sources)] = part_ref[...]
    rows = pick_ref.shape[1]
    width = w_ref.shape[3]
    window = total // 2 + 16
    tile, offset = side_place(features, SIDE_KEYS + EXPERTS)
    me = where_ref[0]
    own_side = x_ref[:, tile : tile + LANES].astype(F32)
    lane = iota((total, LANES), 1)
    flags = pltpu.roll(own_side, LANES - offset - SIDE_KEYS, 1)
    flags = jnp.where(lane < EXPERTS, flags, 0.0)
    owners = EXPERTS // local
    counts = jnp.sum(flags, axis=0, keepdims=True)
    most = jnp.int32(0)
    for o in range(owners):
        held = jnp.logical_and(lane[0:1] >= o * local, lane[0:1] < (o + 1) * local)
        most = jnp.maximum(most, jnp.sum(jnp.where(held, counts, 0.0)).astype(jnp.int32))
    most_ref[0] = most
    mine = pltpu.roll(flags, lax.rem(LANES - me * local, LANES), 1)
    mine = jnp.where(lane < local, mine, 0.0)
    mine16 = mine.astype(BF16)
    row, column = iota((total, total), 0), iota((total, total), 1)
    earlier = (column < row).astype(F32).astype(BF16)
    ranks = dot_nn(earlier, mine16)
    counts = jnp.sum(mine, axis=0, keepdims=True)
    before = (iota((LANES, LANES), 0) < iota((LANES, LANES), 1)).astype(F32).astype(BF16)
    first = dot_nn(jnp.broadcast_to(counts, (8, LANES)).astype(BF16), before)[0:1] - turn * rows
    place = jnp.where(mine > 0.0, first + ranks, -1.0).astype(jnp.int32)
    at = iota((total, rows), 1)
    pick = jnp.zeros((total, rows), F32)
    for j in range(local):
        pick = jnp.where(at == place[:, j : j + 1], 1.0, pick)
    pick = pick.astype(BF16)
    pick_ref[...] = pick
    ranges = jnp.where(iota((16, LANES), 0) < 8, first, first + counts)
    ranges = jnp.concatenate([ranges[0:8], ranges[8:16]] + [jnp.zeros((LANES - 16, LANES), F32)], axis=0)
    ranges = ranges.T
    range_ref[...] = ranges[0:16]
    row_ref[...] = dot_tn(pick, x_ref[...]).astype(BF16)
    acc_ref[...] = jnp.zeros_like(acc_ref)
    for j in range(local):
        start_row = jnp.sum(first[:, j : j + 1]).astype(jnp.int32)
        first_ref[j] = start_row
        start = window_start(start_row, rows, window)
        part = row_ref[pl.ds(start, window), 0:features]
        fresh = start + iota((window, width), 0) >= start_row
        for half in range(2):
            into = (pl.ds(start, window), slice(half * width, (half + 1) * width))
            made = dot_nn(part, w_ref[j, half])
            acc_ref[into] = jnp.where(fresh, made, acc_ref[into])
    logits = dot_nt(router_ref[...], x_ref[:, 0:features])
    high = round16(logits)
    both = jnp.concatenate([high, logits - high], axis=0).astype(BF16)
    both = dot_nn(both, pick)
    turned = jnp.zeros((EXPERTS, rows), jnp.bool_)
    expert = iota((EXPERTS, rows), 0) - me * local
    where_row = iota((EXPERTS, rows), 1).astype(F32)
    for j in range(local):
        inside = jnp.logical_and(
            where_row >= first[:, j : j + 1], where_row < (first + counts)[:, j : j + 1]
        )
        turned = jnp.logical_or(turned, jnp.logical_and(inside, expert == j))
    squares = dot_tn(own_side.astype(BF16), pick)
    side = jnp.concatenate(
        [
            jnp.sum(jnp.where(turned, both[0:EXPERTS], 0.0), axis=0, keepdims=True),
            jnp.sum(jnp.where(turned, both[EXPERTS : 2 * EXPERTS], 0.0), axis=0, keepdims=True),
            squares[offset : offset + 2],
            jnp.zeros((12, rows), F32),
        ],
        axis=0,
    )
    share = share_ref.shape[1] - 16
    low = iota((share, LANES), 1) < PIECE_WIDTH
    for b in range(devices):
        piece, start = b % PIECES, b // PIECES * share
        tile = piece // 2 * LANES
        gate = acc_ref[start : start + share, tile : tile + LANES]
        up = acc_ref[start : start + share, width + tile : width + tile + LANES]
        if piece % 2 == 0:
            made = jnp.where(low, gate, swap_halves(up))
        else:
            made = jnp.where(low, swap_halves(gate), up)
        share_ref[b, 0:share, :] = made.astype(BF16)
        if piece == 0:
            strips = []
            for at in range(0, share, LANES):
                size = min(LANES, share - at)
                strip = side[0:4, start + at : start + at + size]
                if size < LANES:
                    strip = jnp.concatenate([strip, jnp.zeros((4, LANES - size), F32)], axis=1)
                strips.append(strip)
            strips.append(jnp.zeros((16 - 4 * len(strips), LANES), F32))
            strips = jnp.concatenate(strips, axis=0).astype(BF16)
        share_ref[b, share : share + 16, :] = strips
    for k, out_ref in enumerate(out_refs):
        out_ref[...] = share_ref[lax.rem(seq_ref[0] + k, devices)]


def gate_up(exp_index, seq_index, tokens, weights, w_router, rows, devices, turn):
    local, _, features, width = weights.shape
    sources, wide = len(tokens), tokens[0].shape[1]
    total = sources * tokens[0].shape[0]
    share = (rows * PIECES // devices + 16, LANES)
    smem, vmem = pl.BlockSpec(memory_space=pltpu.SMEM), pl.BlockSpec(memory_space=pltpu.VMEM)
    return pl.pallas_call(
        functools.partial(gate_up_kernel, features, local, turn, sources, devices),
        in_specs=[smem] * 2 + [vmem] * (2 + sources),
        out_specs=(vmem,) * devices + (vmem, vmem, smem, smem),
        out_shape=(jax.ShapeDtypeStruct(share, BF16),) * devices
        + (
            jax.ShapeDtypeStruct((total, rows), BF16),
            jax.ShapeDtypeStruct((16, LANES), F32),
            jax.ShapeDtypeStruct((16,), jnp.int32),
            jax.ShapeDtypeStruct((1,), jnp.int32),
        ),
        scratch_shapes=[
            pltpu.VMEM((total, wide), BF16),
            pltpu.VMEM((rows, wide), BF16),
            pltpu.VMEM((rows, 2 * width), F32),
            pltpu.VMEM((devices,) + share, BF16),
        ],
        compiler_params=params(),
        name="gate_up",
    )(exp_index, seq_index, weights, w_router.T, *tokens)


def inner_kernel(*refs):
    x_refs, (out_ref, logit_ref) = refs[:-2], refs[-2:]
    share = x_refs[0].shape[0] - 16
    half = share // 2

    def total(start, size):
        return functools.reduce(
            jnp.add, [x_ref[start : start + size].astype(F32) for x_ref in x_refs]
        )

    side = total(share, 16)
    columns, logits = [], []
    for strip in range(-(-share // LANES)):
        values = side[4 * strip : 4 * strip + 4]
        inverse = lax.rsqrt((values[2:3] + values[3:4]) * (1.0 / D) + 1e-6)
        logits.append((values[0:1] + values[1:2]) * inverse)
        columns.append(jnp.broadcast_to(inverse, (LANES, LANES)).T)
    logit_ref[...] = jnp.concatenate(logits + [jnp.zeros((8 - len(logits), LANES), F32)], axis=0)
    scaled = total(0, share) * jnp.concatenate(columns, axis=0)[0:share]
    made = scaled / (1.0 + jnp.exp(-scaled)) * swap_halves(scaled)
    low = iota((half, LANES), 1) < PIECE_WIDTH
    made = jnp.where(low, made[0:half], swap_halves(made[half:share])).astype(BF16)
    out_ref[...] = made


def inner(parts):
    return pl.pallas_call(
        inner_kernel,
        out_shape=(
            jax.ShapeDtypeStruct(((parts[0].shape[0] - 16) // 2, LANES), BF16),
            jax.ShapeDtypeStruct((8, LANES), F32),
        ),
        compiler_params=params(),
        name="inner",
    )(*parts)


def down_kernel(features, local, pairs, first_ref, seq_ref, range_ref, pick_ref, w_ref, logit_ref, *refs):
    pair_refs, out_refs, (x_ref, row_ref, made_ref) = refs[:pairs], refs[pairs:-3], refs[-3:]
    total, rows = pick_ref.shape
    width = w_ref.shape[2]
    window = total // 2 + 16
    devices, half, _ = x_ref.shape
    for k, pair_ref in enumerate(pair_refs):
        source = lax.rem(seq_ref[0] + devices - 2 * k, devices)
        x_ref[source] = pair_ref[0]
        x_ref[source + 1 - lax.rem(source, 2) * 2] = pair_ref[1]
    share = 2 * half
    low = iota((half, LANES), 1) < PIECE_WIDTH
    for b in range(0, devices, 2):
        start, tile = b // PIECES * share, b % PIECES // 2 * LANES
        one, two = x_ref[b].astype(F32), x_ref[b + 1].astype(F32)
        above = jnp.where(low, one, swap_halves(two)).astype(BF16)
        below = jnp.where(low, swap_halves(one), two).astype(BF16)
        row_ref[start : start + half, tile : tile + LANES] = above
        row_ref[start + half : start + share, tile : tile + LANES] = below
    logit = []
    for piece in range(devices // PIECES):
        for strip in range(-(-share // LANES)):
            size = min(LANES, share - strip * LANES)
            logit.append(logit_ref[piece, strip : strip + 1, 0:size])
    made_ref[...] = jnp.zeros_like(made_ref)
    for j in range(local):
        start_row = first_ref[j]
        start = window_start(start_row, rows, window)
        made = dot_nt(row_ref[pl.ds(start, window), :], w_ref[j])
        fresh = start + iota((window, features), 0) >= start_row
        into = (pl.ds(start, window), slice(0, features))
        made_ref[into] = jnp.where(fresh, made, made_ref[into])
    logit = jnp.concatenate(logit, axis=1)
    high = round16(logit)
    middle = round16(logit - high)
    pick = pick_ref[...]
    where_row = iota((16, rows), 1).astype(F32)
    inside = jnp.logical_and(where_row >= range_ref[:, 0:1], where_row < range_ref[:, 8:9])
    inside = jnp.logical_and(inside, iota((16, rows), 0) < local)
    spread = [jnp.where(inside, part, 0.0) for part in (high, middle, logit - high - middle)]
    spread.append(inside.astype(F32))
    found = dot_nt(jnp.concatenate(spread, axis=0).astype(BF16), pick)
    valid = found[48:64] > 0.5
    logits = jnp.where(valid, found[0:16] + found[16:32] + found[32:48], NEG_FILL)
    top = jnp.max(logits, axis=0, keepdims=True)
    weights = jnp.where(valid, jnp.exp(logits - top), 0.0)
    summed = jnp.sum(weights, axis=0, keepdims=True)
    high = round16(weights)
    both = dot_nn(jnp.concatenate([high, weights - high], axis=0).astype(BF16), pick)
    weight = jnp.sum(jnp.where(inside, both[0:16] + both[16:32], 0.0), axis=0, keepdims=True)
    column = jnp.broadcast_to(weight, (LANES, rows)).T[:, 0:1]
    acc = dot_nn(pick, (made_ref[...] * column).astype(BF16))
    tile, offset = side_place(features, 2)
    pair = jnp.where(iota((LANES, total), 0) == 0, top, summed).T
    tokens = total // len(out_refs)
    for e, out_ref in enumerate(out_refs):
        at = slice(e * tokens, (e + 1) * tokens)
        out_ref[...] = acc[at]
        lane = iota((tokens, LANES), 1) - offset
        side = jnp.where(lane == 0, pair[at, 0:1], acc[at, tile : tile + LANES])
        out_ref[:, tile : tile + LANES] = jnp.where(lane == 1, pair[at, 1:2], side)


def down(first, seq_index, ranges, pick, made, logits, weights, exp_count):
    local, features, width = weights.shape
    total, rows = pick.shape
    wide = side_place(features, 2)[0] + LANES
    smem, vmem = pl.BlockSpec(memory_space=pltpu.SMEM), pl.BlockSpec(memory_space=pltpu.VMEM)
    return pl.pallas_call(
        functools.partial(down_kernel, features, local, len(made)),
        in_specs=[smem] * 2 + [vmem] * (4 + len(made)),
        out_shape=(jax.ShapeDtypeStruct((total // exp_count, wide), F32),) * exp_count,
        scratch_shapes=[
            pltpu.VMEM((2 * len(made),) + made[0].shape[1:], BF16),
            pltpu.VMEM((rows, width), BF16),
            pltpu.VMEM((rows, wide), F32),
        ],
        compiler_params=params(),
        name="down",
    )(first, seq_index, ranges, pick, weights, logits, *made)


def finish_kernel(hidden_ref, *refs):
    part_refs, out_ref = refs[:-1], refs[-1]
    features = hidden_ref.shape[1]
    tile, offset = side_place(features, 2)
    sides = [x_ref[:, tile : tile + LANES] for x_ref in part_refs]
    tops = [side[:, offset : offset + 1] for side in sides]
    top = functools.reduce(jnp.maximum, tops)
    scales = [jnp.exp(one - top) for one in tops]
    total = functools.reduce(
        jnp.add, [s * side[:, offset + 1 : offset + 2] for s, side in zip(scales, sides)]
    )
    acc = functools.reduce(
        jnp.add, [s * x_ref[:, 0:features] for x_ref, s in zip(part_refs, scales)]
    )
    out = hidden_ref[...] + acc * (1.0 / total)
    out_ref[...] = out.reshape(out_ref.shape).astype(BF16)


def finish(parts, hidden, shape):
    return pl.pallas_call(
        finish_kernel,
        out_shape=jax.ShapeDtypeStruct(shape, BF16),
        compiler_params=params(),
        name="finish",
    )(hidden, *parts)


def join_rounds(features, one, other):
    tile, offset = side_place(features, 2)
    at = tile + offset
    top = jnp.maximum(one[..., at : at + 1], other[..., at : at + 1])
    scales = [jnp.exp(part[..., at : at + 1] - top) for part in (one, other)]
    joined = one * scales[0] + other * scales[1]
    return jnp.where(jnp.arange(one.shape[-1]) == at, top, joined)


def send(x, axis, distance):
    count = lax.axis_size(axis)
    return lax.ppermute(x, axis, [(i, (i + distance) % count) for i in range(count)])


def swap(x, axis):
    return lax.all_to_all(x, axis, split_axis=0, concat_axis=0, tiled=True)


def exchange(parts, axis, direction):
    return [parts[0]] + [send(part, axis, direction * k) for k, part in enumerate(parts) if k]


def pair_gather(block, axis):
    count = lax.axis_size(axis)
    beside = lax.ppermute(block, axis, [(i, i ^ 1) for i in range(count)])
    pair = jnp.stack([block, beside])
    return [pair] + [send(pair, axis, k) for k in range(2, count, 2)]


def gather(block, axis):
    return exchange([block] * lax.axis_size(axis), axis, 1)


def local(
    queries,
    new_key_value,
    key_value_cache,
    page_table,
    cache_len,
    routes,
    residual,
    w_out,
    norm_gain,
    w_router,
    w_gate_up,
    w_down,
):
    exp_count = lax.axis_size("exp")
    seq_count = lax.axis_size("seq")
    exp_index = lax.axis_index("exp").astype(jnp.int32).reshape(1)
    seq_index = lax.axis_index("seq").astype(jnp.int32).reshape(1)
    steps, requests, width = queries.shape
    tokens = steps * requests
    features = w_out.shape[1]
    page_rows = key_value_cache.shape[2]
    pool = key_value_cache.reshape(-1, page_rows, 2, KV_WIDTH)

    shares = attend(
        queries, new_key_value, pool, page_table, cache_len, seq_index, seq_count
    )
    w_gate_up, shares = lax.optimization_barrier((w_gate_up, shares))
    gate_up_weights = w_gate_up.transpose(0, 2, 1, 3)
    shares = swap(shares, "seq")
    gate_up_weights, shares = lax.optimization_barrier((gate_up_weights, shares))
    attn = join(shares)
    gathered = pair_gather(attn, "seq")
    hidden, outgoing = hidden_state(seq_index, gathered, residual, w_out, norm_gain, routes)
    incoming = gather(outgoing, "exp")
    pieces = seq_count // PIECES
    rows = -(-ROUND_ROWS // (32 * pieces)) * 32 * pieces

    def one_round(turn):
        *partial, pick, ranges, first, most = gate_up(
            exp_index, seq_index, incoming, gate_up_weights, w_router, rows, seq_count, turn
        )
        made, logits = inner(exchange(partial, "seq", 1))
        logits = logits[None] if pieces == 1 else lax.all_gather(logits, "seq")[::PIECES]
        made = pair_gather(made, "seq")
        return down(first, seq_index, ranges, pick, made, logits, w_down, exp_count), most

    made, most = one_round(0)
    pairs = w_gate_up.shape[0] * exp_count * steps * CAP
    for turn in range(1, -(-pairs // rows)):
        made = lax.cond(
            most[0] > turn * rows,
            lambda made: tuple(
                join_rounds(features, *both) for both in zip(made, one_round(turn)[0])
            ),
            lambda made: made,
            made,
        )
    return finish(exchange(made, "exp", -1), hidden, (steps, requests, features))


def solution(mesh):
    in_specs = (
        P(None, "exp", None),
        P(None, "exp", None, None),
        P("exp", "seq", None, None, None),
        P("exp", "seq"),
        P("exp"),
        P(None, "exp", None),
        P(None, "exp", "seq"),
        P(None, "seq"),
        P("seq"),
        P("seq", None),
        P("exp", "seq", None, None),
        P("exp", "seq", None),
    )
    out_specs = P(None, "exp", "seq")
    return jax.shard_map(local, mesh=mesh, in_specs=in_specs, out_specs=out_specs, check_vma=False)
```

```python
import functools

import jax
import jax.numpy as jnp
from jax import lax
from jax.experimental import pallas as pl
from jax.experimental.pallas import tpu as pltpu
from jax.sharding import PartitionSpec as P

D = 1536
QUERY_HEADS = 24
KEY_VALUE_HEADS = 8
HEAD_SIZE = 64
GROUP = QUERY_HEADS // KEY_VALUE_HEADS
KV_WIDTH = KEY_VALUE_HEADS * HEAD_SIZE
EXPERTS = 40
FF = 512
CAP = 4
LANES = 128
SIDE_KEYS = 2
ROUND_ROWS = 352
PIECES = 8
PIECE_WIDTH = FF // PIECES

NEG_FILL = -1e30
F32 = jnp.float32
BF16 = jnp.bfloat16
VMEM_LIMIT = 48 * 1024 * 1024
ATTEND_VMEM = 60 * 1024 * 1024


def iota(shape, dimension):
    return lax.broadcasted_iota(jnp.int32, shape, dimension)


def dot_nt(a, b):
    return lax.dot_general(a, b, (((1,), (1,)), ((), ())), preferred_element_type=F32)


def dot_tn(a, b):
    return lax.dot_general(a, b, (((0,), (0,)), ((), ())), preferred_element_type=F32)


def dot_nn(a, b):
    return lax.dot_general(a, b, (((1,), (0,)), ((), ())), preferred_element_type=F32)


def round16(x):
    return x.astype(BF16).astype(F32)


def swap_halves(x):
    return pltpu.roll(x, HEAD_SIZE, 1)


def tile_of(x, index):
    return x[:, index * LANES : (index + 1) * LANES]


def padded(width):
    return -(-width // LANES) * LANES


def params():
    return pltpu.CompilerParams(vmem_limit_bytes=VMEM_LIMIT)


def attend_kernel(
    classes, seq_ref, table_hbm, len_hbm, q_hbm, fresh_hbm, cache_ref, share_ref,
    page_ref, table_ref, len_ref, q_ref, fresh_ref, query_ref, new_ref, order_ref, sems, small_sems,
):
    steps, requests, _ = q_ref.shape
    page_rows = cache_ref.shape[1]
    pages = table_ref.shape[1]
    span = pages * page_rows
    first = seq_ref[0] * span
    small = [
        pltpu.make_async_copy(source, target, small_sems.at[i])
        for i, (source, target) in enumerate(
            [(table_hbm, table_ref), (len_hbm, len_ref), (q_hbm, q_ref), (fresh_hbm, fresh_ref)]
        )
    ]
    for one in small:
        one.start()
    for one in small[:2]:
        one.wait()

    held = [jnp.clip(len_ref[r] - first, 0, span) for r in range(requests)]
    for r in range(requests):
        ahead = jnp.int32(0)
        for other in range(requests):
            if other != r:
                longer = held[other] >= held[r] if other < r else held[other] > held[r]
                ahead = ahead + longer.astype(jnp.int32)
        order_ref[ahead] = r

    share = share_ref.shape[1]
    per_request = steps * GROUP // share

    def put(r, acc, side):
        for i in range(per_request):
            at = r * per_request + i
            share_ref[at, :, 0:KV_WIDTH] = acc[i * share : (i + 1) * share]
            share_ref[at, :, KV_WIDTH : KV_WIDTH + LANES] = side[i * share : (i + 1) * share]

    def copy(r, page):
        at = r * pages + page
        return pltpu.make_async_copy(cache_ref.at[table_ref[r, page]], page_ref.at[at], sems.at[at])

    def needed(r, low):
        return len_ref[r] - first > low * page_rows

    bounds = list(zip((0,) + classes[:-1], classes))

    def start(pair, carry):
        both = order_ref[2 * pair], order_ref[2 * pair + 1]
        for low, high in bounds:

            @pl.when(needed(both[0], low))
            def _():
                for page in range(low, high):
                    for r in both:
                        copy(r, page).start()

        return carry

    lax.fori_loop(0, requests // 2, start, 0)
    for one in small[2:]:
        one.wait()

    low = iota((requests, LANES), 1) < HEAD_SIZE
    for t in range(steps):
        q = q_ref[t].astype(F32) * 0.125
        for g in range(GROUP):
            for j in range(KV_WIDTH // LANES):
                one = tile_of(q, (6 * j + g) // 2)
                two = tile_of(q, (6 * j + 3 + g) // 2)
                if g % 2 == 0:
                    tile = jnp.where(low, one, two)
                else:
                    tile = swap_halves(jnp.where(low, two, one))
                query_ref[t * GROUP + g, :, j * LANES : (j + 1) * LANES] = tile
        new_ref[t] = fresh_ref[t].reshape(2 * requests, KV_WIDTH).astype(F32)

    rows = steps * GROUP * KEY_VALUE_HEADS
    own = iota((rows, KV_WIDTH), 1) // HEAD_SIZE == iota((rows, KV_WIDTH), 0) % KEY_VALUE_HEADS
    lane = iota((rows, LANES), 1)
    head = iota((rows, LANES), 0) % KEY_VALUE_HEADS
    row_step = iota((rows, 16), 0) // (GROUP * KEY_VALUE_HEADS)
    kept = jnp.logical_and(iota((rows, 16), 1) <= row_step, seq_ref[0] == 0)
    fresh_bias = jnp.where(kept, 0.0, NEG_FILL)

    def fresh_rows(r, which):
        found = [new_ref[u, pl.ds(2 * r + which, 1), :] for u in range(steps)]
        return jnp.concatenate(found + [jnp.zeros((16 - steps, KV_WIDTH), F32)], axis=0).astype(BF16)

    def attend_pages(r, count):
        spread = jnp.concatenate(
            [
                jnp.broadcast_to(query_ref[i, pl.ds(r, 1), :], (KEY_VALUE_HEADS, KV_WIDTH))
                for i in range(steps * GROUP)
            ],
            axis=0,
        )
        spread = jnp.where(own, spread, 0.0).astype(BF16)
        both = [page_ref[r * pages + page].reshape(2 * page_rows, KV_WIDTH) for page in range(count)]
        both = jnp.concatenate(both, axis=0)
        size = 2 * count * page_rows
        place = iota((1, size), 1)
        live = jnp.logical_and(place % 2 == 0, first + place // 2 < len_ref[r])
        scores = dot_nt(spread, both) + jnp.where(live, 0.0, NEG_FILL)
        fresh_scores = dot_nt(spread, fresh_rows(r, 0)) + fresh_bias
        largest = jnp.maximum(
            jnp.max(scores, axis=1, keepdims=True), jnp.max(fresh_scores, axis=1, keepdims=True)
        )
        weights = jnp.exp(scores - largest)
        fresh_weights = jnp.exp(fresh_scores - largest)
        total = jnp.sum(weights, axis=1, keepdims=True)
        total = total + jnp.sum(fresh_weights, axis=1, keepdims=True)
        moved = [pltpu.roll(tile_of(weights, j), 1, 1) for j in range(size // LANES)]
        acc = dot_nn(jnp.concatenate(moved, axis=1).astype(BF16), both)
        acc = acc + dot_nn(fresh_weights.astype(BF16), fresh_rows(r, 1))
        acc = jnp.where(own, acc * (1.0 / total), 0.0)
        acc = jnp.sum(acc.reshape(steps * GROUP, KEY_VALUE_HEADS, KV_WIDTH), axis=1)
        level = jnp.where(needed(r, 0), largest + jnp.log(total), NEG_FILL)
        high = round16(level)
        middle = round16(level - high)
        side = jnp.where(lane == head, high, 0.0)
        side = jnp.where(lane == head + 8, middle, side)
        side = jnp.where(lane == head + 16, level - high - middle, side)
        side = jnp.sum(side.reshape(steps * GROUP, KEY_VALUE_HEADS, LANES), axis=1)
        return acc.astype(BF16), side.astype(BF16)

    def one_pair(pair, carry):
        both = order_ref[2 * pair], order_ref[2 * pair + 1]
        for low, high in bounds:
            enough = needed(both[0], low)
            if high < pages:
                enough = jnp.logical_and(enough, jnp.logical_not(needed(both[0], high)))

            @pl.when(enough)
            def _():
                for page in range(high):
                    for r in both:
                        copy(r, page).wait()
                made = [attend_pages(r, high) for r in both]
                for r, (acc, side) in zip(both, made):
                    put(r, acc, side)

        @pl.when(jnp.logical_not(needed(both[0], 0)))
        def _():
            empty = jnp.where(iota((steps * GROUP, LANES), 1) < KEY_VALUE_HEADS, NEG_FILL, 0.0)
            for r in both:
                put(r, jnp.zeros((steps * GROUP, KV_WIDTH), BF16), empty.astype(BF16))

        return carry

    lax.fori_loop(0, requests // 2, one_pair, 0)


def attend(queries, new_key_value, cache, page_table, cache_len, seq_index, devices):
    steps, requests, _ = queries.shape
    pages = page_table.shape[1]
    page_rows = cache.shape[1]
    classes = tuple(c for c in (2, 4, 6) if c < pages) + (pages,)
    share = (requests * steps * GROUP // devices, KV_WIDTH + LANES)
    smem, hbm = pl.BlockSpec(memory_space=pltpu.SMEM), pl.BlockSpec(memory_space=pl.ANY)
    return pl.pallas_call(
        functools.partial(attend_kernel, classes),
        in_specs=[smem] + [hbm] * 5,
        out_shape=jax.ShapeDtypeStruct((devices,) + share, BF16),
        scratch_shapes=[
            pltpu.VMEM((requests * pages, page_rows, 2, KV_WIDTH), BF16),
            pltpu.SMEM(page_table.shape, jnp.int32),
            pltpu.SMEM(cache_len.shape, jnp.int32),
            pltpu.VMEM(queries.shape, BF16),
            pltpu.VMEM(new_key_value.shape, BF16),
            pltpu.VMEM((steps * GROUP, requests, KV_WIDTH), F32),
            pltpu.VMEM((steps, 2 * requests, KV_WIDTH), F32),
            pltpu.SMEM((requests,), jnp.int32),
            pltpu.SemaphoreType.DMA((requests * pages,)),
            pltpu.SemaphoreType.DMA((4,)),
        ],
        compiler_params=pltpu.CompilerParams(vmem_limit_bytes=ATTEND_VMEM),
        name="attend",
    )(seq_index, page_table, cache_len, queries, new_key_value, cache)


def join_kernel(x_ref, out_ref):
    blocks, rows, _ = x_ref.shape
    tokens = rows // GROUP
    levels = []
    for b in range(blocks):
        side = x_ref[b, :, KV_WIDTH : KV_WIDTH + LANES].astype(F32)
        levels.append(side + pltpu.roll(side, LANES - 8, 1) + pltpu.roll(side, LANES - 16, 1))
    largest = functools.reduce(jnp.maximum, levels)
    weights = [jnp.exp(level - largest) for level in levels]
    inverse = 1.0 / functools.reduce(jnp.add, weights)
    low = iota((rows, LANES), 1) < HEAD_SIZE
    acc = [jnp.zeros((rows, LANES), F32) for _ in range(KV_WIDTH // LANES)]
    for b in range(blocks):
        share = weights[b] * inverse
        for j in range(KV_WIDTH // LANES):
            factor = jnp.where(low, share[:, 2 * j : 2 * j + 1], share[:, 2 * j + 1 : 2 * j + 2])
            acc[j] = acc[j] + factor * x_ref[b, :, j * LANES : (j + 1) * LANES].astype(F32)

    def piece(head, half):
        k, g = head // GROUP, head % GROUP
        tile = jnp.concatenate(
            [acc[k // 2][t * GROUP + g : t * GROUP + g + 1] for t in range(tokens)], axis=0
        )
        return tile if k % 2 == half else swap_halves(tile)

    low_tokens = iota((tokens, LANES), 1) < HEAD_SIZE
    for m in range(QUERY_HEADS // 2):
        tile = jnp.where(low_tokens, piece(2 * m, 0), piece(2 * m + 1, 1)).astype(BF16)
        out_ref[:, m * LANES : (m + 1) * LANES] = tile


def join(parts):
    rows = parts.shape[1]
    return pl.pallas_call(
        join_kernel,
        out_shape=jax.ShapeDtypeStruct((rows // GROUP, QUERY_HEADS * HEAD_SIZE), BF16),
        compiler_params=params(),
        name="join",
    )(parts)


def side_place(features, count):
    tile, offset = features // LANES * LANES, features % LANES
    return (tile, offset) if offset and offset + count <= LANES else (padded(features), 0)


def hidden_kernel(seq_ref, residual_ref, w_ref, gain_ref, routes_ref, *refs):
    attn_refs, (hidden_ref, out_ref, wide_ref) = refs[:-3], refs[-3:]
    steps, requests, features = residual_ref.shape
    tokens = steps * requests
    blocks = [ref[i].astype(F32) for ref in attn_refs for i in range(2)]
    attn = jnp.concatenate(blocks, axis=0).astype(BF16)
    row, column = iota((tokens, tokens), 0), iota((tokens, tokens), 1)
    devices, share = len(blocks), attn_refs[0].shape[1]
    source = seq_ref[0] + devices - column // (2 * share) * 2
    source = jnp.where(source >= devices, source - devices, source)
    other = column // share % 2
    source = source + other * (1 - source % 2 * 2)
    token = source * share + column % share
    reorder = jnp.logical_and(row % requests == token // steps, row // requests == token % steps)
    attn = dot_nn(reorder.astype(F32).astype(BF16), attn).astype(BF16)
    residual = residual_ref[...].astype(F32).reshape(tokens, features)
    hidden = residual + dot_nt(attn, w_ref[...])
    hidden_ref[...] = hidden
    squares = jnp.sum(hidden * hidden, axis=1, keepdims=True)
    tile, offset = side_place(features, SIDE_KEYS + EXPERTS)
    wide_ref[...] = jnp.zeros_like(wide_ref)
    wide_ref[:, 0:features] = hidden * gain_ref[...]
    routes = routes_ref[...].reshape(tokens, routes_ref.shape[2])
    lane = iota((tokens, LANES), 1) - offset
    side = wide_ref[:, tile : tile + LANES]
    for k in range(routes.shape[1]):
        side = jnp.where(lane == routes[:, k : k + 1] + SIDE_KEYS, 1.0, side)
    high = round16(squares)
    side = jnp.where(lane == 0, high, side)
    wide_ref[:, tile : tile + LANES] = jnp.where(lane == 1, squares - high, side)
    out_ref[...] = wide_ref[...].astype(BF16)


def hidden_state(seq_index, attn, residual, w_out, gain, routes):
    steps, requests, features = residual.shape
    tokens = steps * requests
    wide = side_place(features, SIDE_KEYS + EXPERTS)[0] + LANES
    smem, vmem = pl.BlockSpec(memory_space=pltpu.SMEM), pl.BlockSpec(memory_space=pltpu.VMEM)
    return pl.pallas_call(
        hidden_kernel,
        in_specs=[smem] + [vmem] * (4 + len(attn)),
        out_shape=(
            jax.ShapeDtypeStruct((tokens, features), F32),
            jax.ShapeDtypeStruct((tokens, wide), BF16),
        ),
        scratch_shapes=[pltpu.VMEM((tokens, wide), F32)],
        compiler_params=params(),
        name="hidden",
    )(seq_index, residual, w_out.T, gain.reshape(1, features), routes, *attn)


def window_start(first, rows, window):
    return pl.multiple_of(jnp.clip(first // 16 * 16, 0, rows - window), 16)


def gate_up_kernel(
    features, local, turn, sources, devices, where_ref, seq_ref, w_ref, router_ref, *refs,
):
    part_refs, refs = refs[:sources], refs[sources:]
    out_refs, refs = refs[:devices], refs[devices:]
    pick_ref, range_ref, first_ref, most_ref, x_ref, row_ref, acc_ref, share_ref = refs
    total = x_ref.shape[0]
    for e, part_ref in enumerate(part_refs):
        x_ref[e * (total // sources) : (e + 1) * (total // sources)] = part_ref[...]
    rows = pick_ref.shape[1]
    width = w_ref.shape[3]
    window = total // 2 + 16
    tile, offset = side_place(features, SIDE_KEYS + EXPERTS)
    me = where_ref[0]
    own_side = x_ref[:, tile : tile + LANES].astype(F32)
    lane = iota((total, LANES), 1)
    flags = pltpu.roll(own_side, LANES - offset - SIDE_KEYS, 1)
    flags = jnp.where(lane < EXPERTS, flags, 0.0)
    owners = EXPERTS // local
    counts = jnp.sum(flags, axis=0, keepdims=True)
    most = jnp.int32(0)
    for o in range(owners):
        held = jnp.logical_and(lane[0:1] >= o * local, lane[0:1] < (o + 1) * local)
        most = jnp.maximum(most, jnp.sum(jnp.where(held, counts, 0.0)).astype(jnp.int32))
    most_ref[0] = most
    mine = pltpu.roll(flags, lax.rem(LANES - me * local, LANES), 1)
    mine = jnp.where(lane < local, mine, 0.0)
    mine16 = mine.astype(BF16)
    row, column = iota((total, total), 0), iota((total, total), 1)
    earlier = (column < row).astype(F32).astype(BF16)
    ranks = dot_nn(earlier, mine16)
    counts = jnp.sum(mine, axis=0, keepdims=True)
    before = (iota((LANES, LANES), 0) < iota((LANES, LANES), 1)).astype(F32).astype(BF16)
    first = dot_nn(jnp.broadcast_to(counts, (8, LANES)).astype(BF16), before)[0:1] - turn * rows
    place = jnp.where(mine > 0.0, first + ranks, -1.0).astype(jnp.int32)
    at = iota((total, rows), 1)
    pick = jnp.zeros((total, rows), F32)
    for j in range(local):
        pick = jnp.where(at == place[:, j : j + 1], 1.0, pick)
    pick = pick.astype(BF16)
    pick_ref[...] = pick
    ranges = jnp.where(iota((16, LANES), 0) < 8, first, first + counts)
    ranges = jnp.concatenate([ranges[0:8], ranges[8:16]] + [jnp.zeros((LANES - 16, LANES), F32)], axis=0)
    ranges = ranges.T
    range_ref[...] = ranges[0:16]
    row_ref[...] = dot_tn(pick, x_ref[...]).astype(BF16)
    acc_ref[...] = jnp.zeros_like(acc_ref)
    for j in range(local):
        start_row = jnp.sum(first[:, j : j + 1]).astype(jnp.int32)
        first_ref[j] = start_row
        start = window_start(start_row, rows, window)
        part = row_ref[pl.ds(start, window), 0:features]
        fresh = start + iota((window, width), 0) >= start_row
        for half in range(2):
            into = (pl.ds(start, window), slice(half * width, (half + 1) * width))
            made = dot_nn(part, w_ref[j, half])
            acc_ref[into] = jnp.where(fresh, made, acc_ref[into])
    logits = dot_nt(router_ref[...], x_ref[:, 0:features])
    high = round16(logits)
    both = jnp.concatenate([high, logits - high], axis=0).astype(BF16)
    both = dot_nn(both, pick)
    turned = jnp.zeros((EXPERTS, rows), jnp.bool_)
    expert = iota((EXPERTS, rows), 0) - me * local
    where_row = iota((EXPERTS, rows), 1).astype(F32)
    for j in range(local):
        inside = jnp.logical_and(
            where_row >= first[:, j : j + 1], where_row < (first + counts)[:, j : j + 1]
        )
        turned = jnp.logical_or(turned, jnp.logical_and(inside, expert == j))
    squares = dot_tn(own_side.astype(BF16), pick)
    side = jnp.concatenate(
        [
            jnp.sum(jnp.where(turned, both[0:EXPERTS], 0.0), axis=0, keepdims=True),
            jnp.sum(jnp.where(turned, both[EXPERTS : 2 * EXPERTS], 0.0), axis=0, keepdims=True),
            squares[offset : offset + 2],
            jnp.zeros((12, rows), F32),
        ],
        axis=0,
    )
    share = share_ref.shape[1] - 16
    low = iota((share, LANES), 1) < PIECE_WIDTH
    for b in range(devices):
        piece, start = b % PIECES, b // PIECES * share
        tile = piece // 2 * LANES
        gate = acc_ref[start : start + share, tile : tile + LANES]
        up = acc_ref[start : start + share, width + tile : width + tile + LANES]
        if piece % 2 == 0:
            made = jnp.where(low, gate, swap_halves(up))
        else:
            made = jnp.where(low, swap_halves(gate), up)
        share_ref[b, 0:share, :] = made.astype(BF16)
        if piece == 0:
            strips = []
            for at in range(0, share, LANES):
                size = min(LANES, share - at)
                strip = side[0:4, start + at : start + at + size]
                if size < LANES:
                    strip = jnp.concatenate([strip, jnp.zeros((4, LANES - size), F32)], axis=1)
                strips.append(strip)
            strips.append(jnp.zeros((16 - 4 * len(strips), LANES), F32))
            strips = jnp.concatenate(strips, axis=0).astype(BF16)
        share_ref[b, share : share + 16, :] = strips
    for k, out_ref in enumerate(out_refs):
        out_ref[...] = share_ref[lax.rem(seq_ref[0] + k, devices)]


def gate_up(exp_index, seq_index, tokens, weights, w_router, rows, devices, turn):
    local, _, features, width = weights.shape
    sources, wide = len(tokens), tokens[0].shape[1]
    total = sources * tokens[0].shape[0]
    share = (rows * PIECES // devices + 16, LANES)
    smem, vmem = pl.BlockSpec(memory_space=pltpu.SMEM), pl.BlockSpec(memory_space=pltpu.VMEM)
    return pl.pallas_call(
        functools.partial(gate_up_kernel, features, local, turn, sources, devices),
        in_specs=[smem] * 2 + [vmem] * (2 + sources),
        out_specs=(vmem,) * devices + (vmem, vmem, smem, smem),
        out_shape=(jax.ShapeDtypeStruct(share, BF16),) * devices
        + (
            jax.ShapeDtypeStruct((total, rows), BF16),
            jax.ShapeDtypeStruct((16, LANES), F32),
            jax.ShapeDtypeStruct((16,), jnp.int32),
            jax.ShapeDtypeStruct((1,), jnp.int32),
        ),
        scratch_shapes=[
            pltpu.VMEM((total, wide), BF16),
            pltpu.VMEM((rows, wide), BF16),
            pltpu.VMEM((rows, 2 * width), F32),
            pltpu.VMEM((devices,) + share, BF16),
        ],
        compiler_params=params(),
        name="gate_up",
    )(exp_index, seq_index, weights, w_router.T, *tokens)


def inner_kernel(*refs):
    x_refs, (out_ref, logit_ref) = refs[:-2], refs[-2:]
    share = x_refs[0].shape[0] - 16
    half = share // 2

    def total(start, size):
        return functools.reduce(
            jnp.add, [x_ref[start : start + size].astype(F32) for x_ref in x_refs]
        )

    side = total(share, 16)
    columns, logits = [], []
    for strip in range(-(-share // LANES)):
        values = side[4 * strip : 4 * strip + 4]
        inverse = lax.rsqrt((values[2:3] + values[3:4]) * (1.0 / D) + 1e-6)
        logits.append((values[0:1] + values[1:2]) * inverse)
        columns.append(jnp.broadcast_to(inverse, (LANES, LANES)).T)
    logit_ref[...] = jnp.concatenate(logits + [jnp.zeros((8 - len(logits), LANES), F32)], axis=0)
    scaled = total(0, share) * jnp.concatenate(columns, axis=0)[0:share]
    made = scaled / (1.0 + jnp.exp(-scaled)) * swap_halves(scaled)
    low = iota((half, LANES), 1) < PIECE_WIDTH
    made = jnp.where(low, made[0:half], swap_halves(made[half:share])).astype(BF16)
    out_ref[...] = made


def inner(parts):
    return pl.pallas_call(
        inner_kernel,
        out_shape=(
            jax.ShapeDtypeStruct(((parts[0].shape[0] - 16) // 2, LANES), BF16),
            jax.ShapeDtypeStruct((8, LANES), F32),
        ),
        compiler_params=params(),
        name="inner",
    )(*parts)


def down_kernel(features, local, first_ref, seq_ref, range_ref, pick_ref, w_ref, logit_ref, *refs):
    (own_ref, beside_ref, behind_ref, other_ref), refs = refs[:4], refs[4:]
    out_refs, (x_ref, row_ref, made_ref) = refs[:-3], refs[-3:]
    total, rows = pick_ref.shape
    width = w_ref.shape[2]
    window = total // 2 + 16
    devices, half, _ = x_ref.shape
    for k in range(devices // 2):
        source = lax.rem(seq_ref[0] + devices - 2 * k, devices)
        x_ref[source] = behind_ref[k - 1] if k else own_ref[...]
        x_ref[source + 1 - lax.rem(source, 2) * 2] = other_ref[k - 1] if k else beside_ref[...]
    share = 2 * half
    low = iota((half, LANES), 1) < PIECE_WIDTH
    for b in range(0, devices, 2):
        start, tile = b // PIECES * share, b % PIECES // 2 * LANES
        one, two = x_ref[b].astype(F32), x_ref[b + 1].astype(F32)
        above = jnp.where(low, one, swap_halves(two)).astype(BF16)
        below = jnp.where(low, swap_halves(one), two).astype(BF16)
        row_ref[start : start + half, tile : tile + LANES] = above
        row_ref[start + half : start + share, tile : tile + LANES] = below
    logit = []
    for piece in range(devices // PIECES):
        for strip in range(-(-share // LANES)):
            size = min(LANES, share - strip * LANES)
            logit.append(logit_ref[piece, strip : strip + 1, 0:size])
    made_ref[...] = jnp.zeros_like(made_ref)
    for j in range(local):
        start_row = first_ref[j]
        start = window_start(start_row, rows, window)
        made = dot_nt(row_ref[pl.ds(start, window), :], w_ref[j])
        fresh = start + iota((window, features), 0) >= start_row
        into = (pl.ds(start, window), slice(0, features))
        made_ref[into] = jnp.where(fresh, made, made_ref[into])
    logit = jnp.concatenate(logit, axis=1)
    high = round16(logit)
    middle = round16(logit - high)
    pick = pick_ref[...]
    where_row = iota((16, rows), 1).astype(F32)
    inside = jnp.logical_and(where_row >= range_ref[:, 0:1], where_row < range_ref[:, 8:9])
    inside = jnp.logical_and(inside, iota((16, rows), 0) < local)
    spread = [jnp.where(inside, part, 0.0) for part in (high, middle, logit - high - middle)]
    spread.append(inside.astype(F32))
    found = dot_nt(jnp.concatenate(spread, axis=0).astype(BF16), pick)
    valid = found[48:64] > 0.5
    logits = jnp.where(valid, found[0:16] + found[16:32] + found[32:48], NEG_FILL)
    top = jnp.max(logits, axis=0, keepdims=True)
    weights = jnp.where(valid, jnp.exp(logits - top), 0.0)
    summed = jnp.sum(weights, axis=0, keepdims=True)
    high = round16(weights)
    both = dot_nn(jnp.concatenate([high, weights - high], axis=0).astype(BF16), pick)
    weight = jnp.sum(jnp.where(inside, both[0:16] + both[16:32], 0.0), axis=0, keepdims=True)
    column = jnp.broadcast_to(weight, (LANES, rows)).T[:, 0:1]
    acc = dot_nn(pick, (made_ref[...] * column).astype(BF16))
    tile, offset = side_place(features, 2)
    pair = jnp.where(iota((LANES, total), 0) == 0, top, summed).T
    tokens = total // len(out_refs)
    for e, out_ref in enumerate(out_refs):
        at = slice(e * tokens, (e + 1) * tokens)
        out_ref[...] = acc[at]
        lane = iota((tokens, LANES), 1) - offset
        side = jnp.where(lane == 0, pair[at, 0:1], acc[at, tile : tile + LANES])
        out_ref[:, tile : tile + LANES] = jnp.where(lane == 1, pair[at, 1:2], side)


def down(first, seq_index, ranges, pick, made, logits, weights, exp_count):
    local, features, width = weights.shape
    total, rows = pick.shape
    wide = side_place(features, 2)[0] + LANES
    smem, vmem = pl.BlockSpec(memory_space=pltpu.SMEM), pl.BlockSpec(memory_space=pltpu.VMEM)
    return pl.pallas_call(
        functools.partial(down_kernel, features, local),
        in_specs=[smem] * 2 + [vmem] * (4 + len(made)),
        out_shape=(jax.ShapeDtypeStruct((total // exp_count, wide), F32),) * exp_count,
        scratch_shapes=[
            pltpu.VMEM((2 * made[2].shape[0] + 2,) + made[0].shape, BF16),
            pltpu.VMEM((rows, width), BF16),
            pltpu.VMEM((rows, wide), F32),
        ],
        compiler_params=params(),
        name="down",
    )(first, seq_index, ranges, pick, weights, logits, *made)


def finish_kernel(hidden_ref, *refs):
    part_refs, out_ref = refs[:-1], refs[-1]
    features = hidden_ref.shape[1]
    tile, offset = side_place(features, 2)
    sides = [x_ref[:, tile : tile + LANES] for x_ref in part_refs]
    tops = [side[:, offset : offset + 1] for side in sides]
    top = functools.reduce(jnp.maximum, tops)
    scales = [jnp.exp(one - top) for one in tops]
    total = functools.reduce(
        jnp.add, [s * side[:, offset + 1 : offset + 2] for s, side in zip(scales, sides)]
    )
    acc = functools.reduce(
        jnp.add, [s * x_ref[:, 0:features] for x_ref, s in zip(part_refs, scales)]
    )
    out = hidden_ref[...] + acc * (1.0 / total)
    out_ref[...] = out.reshape(out_ref.shape).astype(BF16)


def finish(parts, hidden, shape):
    return pl.pallas_call(
        finish_kernel,
        out_shape=jax.ShapeDtypeStruct(shape, BF16),
        compiler_params=params(),
        name="finish",
    )(hidden, *parts)


def join_rounds(features, one, other):
    tile, offset = side_place(features, 2)
    at = tile + offset
    top = jnp.maximum(one[..., at : at + 1], other[..., at : at + 1])
    scales = [jnp.exp(part[..., at : at + 1] - top) for part in (one, other)]
    joined = one * scales[0] + other * scales[1]
    return jnp.where(jnp.arange(one.shape[-1]) == at, top, joined)


def send(x, axis, distance):
    count = lax.axis_size(axis)
    return lax.ppermute(x, axis, [(i, (i + distance) % count) for i in range(count)])


def swap(x, axis):
    return lax.all_to_all(x, axis, split_axis=0, concat_axis=0, tiled=True)


def exchange(parts, axis, direction):
    return [parts[0]] + [send(part, axis, direction * k) for k, part in enumerate(parts) if k]


def neighbour(x, axis):
    return lax.ppermute(x, axis, [(i, i ^ 1) for i in range(lax.axis_size(axis))])


def pair_gather(block, axis):
    pair = jnp.stack([block, neighbour(block, axis)])
    return [pair] + [send(pair, axis, k) for k in range(2, lax.axis_size(axis), 2)]


def gather(block, axis):
    return exchange([block] * lax.axis_size(axis), axis, 1)


def local(
    queries,
    new_key_value,
    key_value_cache,
    page_table,
    cache_len,
    routes,
    residual,
    w_out,
    norm_gain,
    w_router,
    w_gate_up,
    w_down,
):
    exp_count = lax.axis_size("exp")
    seq_count = lax.axis_size("seq")
    exp_index = lax.axis_index("exp").astype(jnp.int32).reshape(1)
    seq_index = lax.axis_index("seq").astype(jnp.int32).reshape(1)
    steps, requests, width = queries.shape
    tokens = steps * requests
    features = w_out.shape[1]
    page_rows = key_value_cache.shape[2]
    pool = key_value_cache.reshape(-1, page_rows, 2, KV_WIDTH)

    shares = attend(
        queries, new_key_value, pool, page_table, cache_len, seq_index, seq_count
    )
    w_gate_up, shares = lax.optimization_barrier((w_gate_up, shares))
    gate_up_weights = w_gate_up.transpose(0, 2, 1, 3)
    shares = swap(shares, "seq")
    gate_up_weights, shares = lax.optimization_barrier((gate_up_weights, shares))
    attn = join(shares)
    gathered = pair_gather(attn, "seq")
    hidden, outgoing = hidden_state(seq_index, gathered, residual, w_out, norm_gain, routes)
    incoming = gather(outgoing, "exp")
    pieces = seq_count // PIECES
    rows = -(-ROUND_ROWS // (32 * pieces)) * 32 * pieces

    def one_round(turn):
        *partial, pick, ranges, first, most = gate_up(
            exp_index, seq_index, incoming, gate_up_weights, w_router, rows, seq_count, turn
        )
        made, logits = inner(exchange(partial, "seq", 1))
        logits = logits[None] if pieces == 1 else lax.all_gather(logits, "seq")[::PIECES]
        behind = jnp.stack([send(made, "seq", k) for k in range(2, seq_count, 2)])
        made = [made, neighbour(made, "seq"), behind, neighbour(behind, "seq")]
        return down(first, seq_index, ranges, pick, made, logits, w_down, exp_count), most

    made, most = one_round(0)
    pairs = w_gate_up.shape[0] * exp_count * steps * CAP
    for turn in range(1, -(-pairs // rows)):
        made = lax.cond(
            most[0] > turn * rows,
            lambda made: tuple(
                join_rounds(features, *both) for both in zip(made, one_round(turn)[0])
            ),
            lambda made: made,
            made,
        )
    return finish(exchange(made, "exp", -1), hidden, (steps, requests, features))


def solution(mesh):
    in_specs = (
        P(None, "exp", None),
        P(None, "exp", None, None),
        P("exp", "seq", None, None, None),
        P("exp", "seq"),
        P("exp"),
        P(None, "exp", None),
        P(None, "exp", "seq"),
        P(None, "seq"),
        P("seq"),
        P("seq", None),
        P("exp", "seq", None, None),
        P("exp", "seq", None),
    )
    out_specs = P(None, "exp", "seq")
    return jax.shard_map(local, mesh=mesh, in_specs=in_specs, out_specs=out_specs, check_vma=False)
```

```python
import functools

import jax
import jax.numpy as jnp
from jax import lax
from jax.experimental import pallas as pl
from jax.experimental.pallas import tpu as pltpu
from jax.sharding import PartitionSpec as P

D = 1536
QUERY_HEADS = 24
KEY_VALUE_HEADS = 8
HEAD_SIZE = 64
GROUP = QUERY_HEADS // KEY_VALUE_HEADS
KV_WIDTH = KEY_VALUE_HEADS * HEAD_SIZE
EXPERTS = 40
FF = 512
CAP = 4
LANES = 128
SIDE_KEYS = 2
ROUND_ROWS = 352
PIECES = 8
PIECE_WIDTH = FF // PIECES

NEG_FILL = -1e30
F32 = jnp.float32
BF16 = jnp.bfloat16
VMEM_LIMIT = 48 * 1024 * 1024
ATTEND_VMEM = 60 * 1024 * 1024


def iota(shape, dimension):
    return lax.broadcasted_iota(jnp.int32, shape, dimension)


def dot_nt(a, b):
    return lax.dot_general(a, b, (((1,), (1,)), ((), ())), preferred_element_type=F32)


def dot_tn(a, b):
    return lax.dot_general(a, b, (((0,), (0,)), ((), ())), preferred_element_type=F32)


def dot_nn(a, b):
    return lax.dot_general(a, b, (((1,), (0,)), ((), ())), preferred_element_type=F32)


def round16(x):
    return x.astype(BF16).astype(F32)


def swap_halves(x):
    return pltpu.roll(x, HEAD_SIZE, 1)


def tile_of(x, index):
    return x[:, index * LANES : (index + 1) * LANES]


def padded(width):
    return -(-width // LANES) * LANES


def params():
    return pltpu.CompilerParams(vmem_limit_bytes=VMEM_LIMIT)


def attend_kernel(
    classes, seq_ref, table_hbm, len_hbm, q_hbm, fresh_hbm, cache_ref, share_ref,
    page_ref, table_ref, len_ref, q_ref, fresh_ref, query_ref, new_ref, order_ref, sems, small_sems,
):
    steps, requests, _ = q_ref.shape
    page_rows = cache_ref.shape[1]
    pages = table_ref.shape[1]
    span = pages * page_rows
    first = seq_ref[0] * span
    small = [
        pltpu.make_async_copy(source, target, small_sems.at[i])
        for i, (source, target) in enumerate(
            [(table_hbm, table_ref), (len_hbm, len_ref), (q_hbm, q_ref), (fresh_hbm, fresh_ref)]
        )
    ]
    for one in small:
        one.start()
    for one in small[:2]:
        one.wait()

    held = [jnp.clip(len_ref[r] - first, 0, span) for r in range(requests)]
    for r in range(requests):
        ahead = jnp.int32(0)
        for other in range(requests):
            if other != r:
                longer = held[other] >= held[r] if other < r else held[other] > held[r]
                ahead = ahead + longer.astype(jnp.int32)
        order_ref[ahead] = r

    share = share_ref.shape[1]
    per_request = steps * GROUP // share

    def put(r, acc, side):
        for i in range(per_request):
            at = r * per_request + i
            share_ref[at, :, 0:KV_WIDTH] = acc[i * share : (i + 1) * share]
            share_ref[at, :, KV_WIDTH : KV_WIDTH + LANES] = side[i * share : (i + 1) * share]

    def copy(r, page):
        at = r * pages + page
        return pltpu.make_async_copy(cache_ref.at[table_ref[r, page]], page_ref.at[at], sems.at[at])

    def needed(r, low):
        return len_ref[r] - first > low * page_rows

    bounds = list(zip((0,) + classes[:-1], classes))

    def start(pair, carry):
        both = order_ref[2 * pair], order_ref[2 * pair + 1]
        for low, high in bounds:

            @pl.when(needed(both[0], low))
            def _():
                for page in range(low, high):
                    for r in both:
                        copy(r, page).start()

        return carry

    lax.fori_loop(0, requests // 2, start, 0)
    for one in small[2:]:
        one.wait()

    low = iota((requests, LANES), 1) < HEAD_SIZE
    for t in range(steps):
        q = q_ref[t].astype(F32) * 0.125
        for g in range(GROUP):
            for j in range(KV_WIDTH // LANES):
                one = tile_of(q, (6 * j + g) // 2)
                two = tile_of(q, (6 * j + 3 + g) // 2)
                if g % 2 == 0:
                    tile = jnp.where(low, one, two)
                else:
                    tile = swap_halves(jnp.where(low, two, one))
                query_ref[t * GROUP + g, :, j * LANES : (j + 1) * LANES] = tile
        new_ref[t] = fresh_ref[t].reshape(2 * requests, KV_WIDTH).astype(F32)

    rows = steps * GROUP * KEY_VALUE_HEADS
    own = iota((rows, KV_WIDTH), 1) // HEAD_SIZE == iota((rows, KV_WIDTH), 0) % KEY_VALUE_HEADS
    lane = iota((rows, LANES), 1)
    head = iota((rows, LANES), 0) % KEY_VALUE_HEADS
    lane_step = iota((16, LANES), 1) // (GROUP * KEY_VALUE_HEADS)
    kept = jnp.logical_and(iota((16, LANES), 0) <= lane_step, seq_ref[0] == 0)
    fresh_bias = jnp.where(kept, 0.0, NEG_FILL)

    def fresh_rows(r, which):
        found = [new_ref[u, pl.ds(2 * r + which, 1), :] for u in range(steps)]
        return jnp.concatenate(found + [jnp.zeros((16 - steps, KV_WIDTH), F32)], axis=0).astype(BF16)

    def attend_pages(r, count):
        spread = jnp.concatenate(
            [
                jnp.broadcast_to(query_ref[i, pl.ds(r, 1), :], (KEY_VALUE_HEADS, KV_WIDTH))
                for i in range(steps * GROUP)
            ],
            axis=0,
        )
        spread = jnp.where(own, spread, 0.0)
        spread = jnp.concatenate([spread, jnp.zeros((LANES - rows, KV_WIDTH), F32)], axis=0).astype(BF16)
        both = [page_ref[r * pages + page].reshape(2 * page_rows, KV_WIDTH) for page in range(count)]
        both = jnp.concatenate(both, axis=0)
        size = 2 * count * page_rows
        place = iota((size, LANES), 0)
        live = jnp.logical_and(place % 2 == 0, place < 2 * (len_ref[r] - first))
        scores = jnp.where(live, dot_nt(both, spread), NEG_FILL)
        fresh_scores = dot_nt(fresh_rows(r, 0), spread) + fresh_bias
        largest = jnp.maximum(
            jnp.max(scores, axis=0, keepdims=True), jnp.max(fresh_scores, axis=0, keepdims=True)
        )
        weights = jnp.exp(scores - largest)
        fresh_weights = jnp.exp(fresh_scores - largest)
        total = jnp.sum(weights, axis=0, keepdims=True)
        total = total + jnp.sum(fresh_weights, axis=0, keepdims=True)
        inverse = 1.0 / total
        moved = pltpu.roll(weights * inverse, 1, 0).astype(BF16)
        acc = dot_tn(moved, both)
        acc = acc + dot_tn((fresh_weights * inverse).astype(BF16), fresh_rows(r, 1))
        acc = jnp.where(own, acc[0:rows], 0.0)
        acc = jnp.sum(acc.reshape(steps * GROUP, KEY_VALUE_HEADS, KV_WIDTH), axis=1)
        level = jnp.where(needed(r, 0), largest + jnp.log(total), NEG_FILL)
        level = jnp.broadcast_to(level, (LANES, LANES)).T[0:rows]
        high = round16(level)
        middle = round16(level - high)
        side = jnp.where(lane == head, high, 0.0)
        side = jnp.where(lane == head + 8, middle, side)
        side = jnp.where(lane == head + 16, level - high - middle, side)
        side = jnp.sum(side.reshape(steps * GROUP, KEY_VALUE_HEADS, LANES), axis=1)
        return acc.astype(BF16), side.astype(BF16)

    def one_pair(pair, carry):
        both = order_ref[2 * pair], order_ref[2 * pair + 1]
        for low, high in bounds:
            enough = needed(both[0], low)
            if high < pages:
                enough = jnp.logical_and(enough, jnp.logical_not(needed(both[0], high)))

            @pl.when(enough)
            def _():
                for page in range(high):
                    for r in both:
                        copy(r, page).wait()
                made = [attend_pages(r, high) for r in both]
                for r, (acc, side) in zip(both, made):
                    put(r, acc, side)

        @pl.when(jnp.logical_not(needed(both[0], 0)))
        def _():
            empty = jnp.where(iota((steps * GROUP, LANES), 1) < KEY_VALUE_HEADS, NEG_FILL, 0.0)
            for r in both:
                put(r, jnp.zeros((steps * GROUP, KV_WIDTH), BF16), empty.astype(BF16))

        return carry

    lax.fori_loop(0, requests // 2, one_pair, 0)


def attend(queries, new_key_value, cache, page_table, cache_len, seq_index, devices):
    steps, requests, _ = queries.shape
    pages = page_table.shape[1]
    page_rows = cache.shape[1]
    classes = tuple(c for c in (2, 4, 6) if c < pages) + (pages,)
    share = (requests * steps * GROUP // devices, KV_WIDTH + LANES)
    smem, hbm = pl.BlockSpec(memory_space=pltpu.SMEM), pl.BlockSpec(memory_space=pl.ANY)
    return pl.pallas_call(
        functools.partial(attend_kernel, classes),
        in_specs=[smem] + [hbm] * 5,
        out_shape=jax.ShapeDtypeStruct((devices,) + share, BF16),
        scratch_shapes=[
            pltpu.VMEM((requests * pages, page_rows, 2, KV_WIDTH), BF16),
            pltpu.SMEM(page_table.shape, jnp.int32),
            pltpu.SMEM(cache_len.shape, jnp.int32),
            pltpu.VMEM(queries.shape, BF16),
            pltpu.VMEM(new_key_value.shape, BF16),
            pltpu.VMEM((steps * GROUP, requests, KV_WIDTH), F32),
            pltpu.VMEM((steps, 2 * requests, KV_WIDTH), F32),
            pltpu.SMEM((requests,), jnp.int32),
            pltpu.SemaphoreType.DMA((requests * pages,)),
            pltpu.SemaphoreType.DMA((4,)),
        ],
        compiler_params=pltpu.CompilerParams(vmem_limit_bytes=ATTEND_VMEM),
        name="attend",
    )(seq_index, page_table, cache_len, queries, new_key_value, cache)


def join_kernel(x_ref, out_ref):
    blocks, rows, _ = x_ref.shape
    tokens = rows // GROUP
    levels = []
    for b in range(blocks):
        side = x_ref[b, :, KV_WIDTH : KV_WIDTH + LANES].astype(F32)
        levels.append(side + pltpu.roll(side, LANES - 8, 1) + pltpu.roll(side, LANES - 16, 1))
    largest = functools.reduce(jnp.maximum, levels)
    weights = [jnp.exp(level - largest) for level in levels]
    inverse = 1.0 / functools.reduce(jnp.add, weights)
    low = iota((rows, LANES), 1) < HEAD_SIZE
    acc = [jnp.zeros((rows, LANES), F32) for _ in range(KV_WIDTH // LANES)]
    for b in range(blocks):
        share = weights[b] * inverse
        for j in range(KV_WIDTH // LANES):
            factor = jnp.where(low, share[:, 2 * j : 2 * j + 1], share[:, 2 * j + 1 : 2 * j + 2])
            acc[j] = acc[j] + factor * x_ref[b, :, j * LANES : (j + 1) * LANES].astype(F32)

    def piece(head, half):
        k, g = head // GROUP, head % GROUP
        tile = jnp.concatenate(
            [acc[k // 2][t * GROUP + g : t * GROUP + g + 1] for t in range(tokens)], axis=0
        )
        return tile if k % 2 == half else swap_halves(tile)

    low_tokens = iota((tokens, LANES), 1) < HEAD_SIZE
    for m in range(QUERY_HEADS // 2):
        tile = jnp.where(low_tokens, piece(2 * m, 0), piece(2 * m + 1, 1)).astype(BF16)
        out_ref[:, m * LANES : (m + 1) * LANES] = tile


def join(parts):
    rows = parts.shape[1]
    return pl.pallas_call(
        join_kernel,
        out_shape=jax.ShapeDtypeStruct((rows // GROUP, QUERY_HEADS * HEAD_SIZE), BF16),
        compiler_params=params(),
        name="join",
    )(parts)


def side_place(features, count):
    tile, offset = features // LANES * LANES, features % LANES
    return (tile, offset) if offset and offset + count <= LANES else (padded(features), 0)


def hidden_kernel(seq_ref, residual_ref, w_ref, gain_ref, routes_ref, *refs):
    attn_refs, (hidden_ref, out_ref, wide_ref) = refs[:-3], refs[-3:]
    steps, requests, features = residual_ref.shape
    tokens = steps * requests
    blocks = [ref[i].astype(F32) for ref in attn_refs for i in range(2)]
    attn = jnp.concatenate(blocks, axis=0).astype(BF16)
    row, column = iota((tokens, tokens), 0), iota((tokens, tokens), 1)
    devices, share = len(blocks), attn_refs[0].shape[1]
    source = seq_ref[0] + devices - column // (2 * share) * 2
    source = jnp.where(source >= devices, source - devices, source)
    other = column // share % 2
    source = source + other * (1 - source % 2 * 2)
    token = source * share + column % share
    reorder = jnp.logical_and(row % requests == token // steps, row // requests == token % steps)
    attn = dot_nn(reorder.astype(F32).astype(BF16), attn).astype(BF16)
    residual = residual_ref[...].astype(F32).reshape(tokens, features)
    hidden = residual + dot_nt(attn, w_ref[...])
    hidden_ref[...] = hidden
    squares = jnp.sum(hidden * hidden, axis=1, keepdims=True)
    tile, offset = side_place(features, SIDE_KEYS + EXPERTS)
    wide_ref[...] = jnp.zeros_like(wide_ref)
    wide_ref[:, 0:features] = hidden * gain_ref[...]
    routes = routes_ref[...].reshape(tokens, routes_ref.shape[2])
    lane = iota((tokens, LANES), 1) - offset
    side = wide_ref[:, tile : tile + LANES]
    for k in range(routes.shape[1]):
        side = jnp.where(lane == routes[:, k : k + 1] + SIDE_KEYS, 1.0, side)
    high = round16(squares)
    side = jnp.where(lane == 0, high, side)
    wide_ref[:, tile : tile + LANES] = jnp.where(lane == 1, squares - high, side)
    out_ref[...] = wide_ref[...].astype(BF16)


def hidden_state(seq_index, attn, residual, w_out, gain, routes):
    steps, requests, features = residual.shape
    tokens = steps * requests
    wide = side_place(features, SIDE_KEYS + EXPERTS)[0] + LANES
    smem, vmem = pl.BlockSpec(memory_space=pltpu.SMEM), pl.BlockSpec(memory_space=pltpu.VMEM)
    return pl.pallas_call(
        hidden_kernel,
        in_specs=[smem] + [vmem] * (4 + len(attn)),
        out_shape=(
            jax.ShapeDtypeStruct((tokens, features), F32),
            jax.ShapeDtypeStruct((tokens, wide), BF16),
        ),
        scratch_shapes=[pltpu.VMEM((tokens, wide), F32)],
        compiler_params=params(),
        name="hidden",
    )(seq_index, residual, w_out.T, gain.reshape(1, features), routes, *attn)


def window_start(first, rows, window):
    return pl.multiple_of(jnp.clip(first // 16 * 16, 0, rows - window), 16)


def gate_up_kernel(
    features, local, turn, sources, devices, where_ref, seq_ref, w_ref, router_ref, *refs,
):
    part_refs, refs = refs[:sources], refs[sources:]
    out_refs, refs = refs[:devices], refs[devices:]
    pick_ref, range_ref, first_ref, most_ref, x_ref, row_ref, acc_ref, share_ref = refs
    total = x_ref.shape[0]
    for e, part_ref in enumerate(part_refs):
        x_ref[e * (total // sources) : (e + 1) * (total // sources)] = part_ref[...]
    rows = pick_ref.shape[1]
    width = w_ref.shape[3]
    window = total // 2 + 16
    tile, offset = side_place(features, SIDE_KEYS + EXPERTS)
    me = where_ref[0]
    own_side = x_ref[:, tile : tile + LANES].astype(F32)
    lane = iota((total, LANES), 1)
    flags = pltpu.roll(own_side, LANES - offset - SIDE_KEYS, 1)
    flags = jnp.where(lane < EXPERTS, flags, 0.0)
    owners = EXPERTS // local
    counts = jnp.sum(flags, axis=0, keepdims=True)
    most = jnp.int32(0)
    for o in range(owners):
        held = jnp.logical_and(lane[0:1] >= o * local, lane[0:1] < (o + 1) * local)
        most = jnp.maximum(most, jnp.sum(jnp.where(held, counts, 0.0)).astype(jnp.int32))
    most_ref[0] = most
    mine = pltpu.roll(flags, lax.rem(LANES - me * local, LANES), 1)
    mine = jnp.where(lane < local, mine, 0.0)
    mine16 = mine.astype(BF16)
    row, column = iota((total, total), 0), iota((total, total), 1)
    earlier = (column < row).astype(F32).astype(BF16)
    ranks = dot_nn(earlier, mine16)
    counts = jnp.sum(mine, axis=0, keepdims=True)
    before = (iota((LANES, LANES), 0) < iota((LANES, LANES), 1)).astype(F32).astype(BF16)
    first = dot_nn(jnp.broadcast_to(counts, (8, LANES)).astype(BF16), before)[0:1] - turn * rows
    place = jnp.where(mine > 0.0, first + ranks, -1.0).astype(jnp.int32)
    at = iota((total, rows), 1)
    pick = jnp.zeros((total, rows), F32)
    for j in range(local):
        pick = jnp.where(at == place[:, j : j + 1], 1.0, pick)
    pick = pick.astype(BF16)
    pick_ref[...] = pick
    ranges = jnp.where(iota((16, LANES), 0) < 8, first, first + counts)
    ranges = jnp.concatenate([ranges[0:8], ranges[8:16]] + [jnp.zeros((LANES - 16, LANES), F32)], axis=0)
    ranges = ranges.T
    range_ref[...] = ranges[0:16]
    row_ref[...] = dot_tn(pick, x_ref[...]).astype(BF16)
    acc_ref[...] = jnp.zeros_like(acc_ref)
    for j in range(local):
        start_row = jnp.sum(first[:, j : j + 1]).astype(jnp.int32)
        first_ref[j] = start_row
        start = window_start(start_row, rows, window)
        part = row_ref[pl.ds(start, window), 0:features]
        fresh = start + iota((window, width), 0) >= start_row
        for half in range(2):
            into = (pl.ds(start, window), slice(half * width, (half + 1) * width))
            made = dot_nn(part, w_ref[j, half])
            acc_ref[into] = jnp.where(fresh, made, acc_ref[into])
    logits = dot_nt(router_ref[...], x_ref[:, 0:features])
    high = round16(logits)
    both = jnp.concatenate([high, logits - high], axis=0).astype(BF16)
    both = dot_nn(both, pick)
    turned = jnp.zeros((EXPERTS, rows), jnp.bool_)
    expert = iota((EXPERTS, rows), 0) - me * local
    where_row = iota((EXPERTS, rows), 1).astype(F32)
    for j in range(local):
        inside = jnp.logical_and(
            where_row >= first[:, j : j + 1], where_row < (first + counts)[:, j : j + 1]
        )
        turned = jnp.logical_or(turned, jnp.logical_and(inside, expert == j))
    squares = dot_tn(own_side.astype(BF16), pick)
    side = jnp.concatenate(
        [
            jnp.sum(jnp.where(turned, both[0:EXPERTS], 0.0), axis=0, keepdims=True),
            jnp.sum(jnp.where(turned, both[EXPERTS : 2 * EXPERTS], 0.0), axis=0, keepdims=True),
            squares[offset : offset + 2],
            jnp.zeros((12, rows), F32),
        ],
        axis=0,
    )
    share = share_ref.shape[1] - 16
    low = iota((share, LANES), 1) < PIECE_WIDTH
    for b in range(devices):
        piece, start = b % PIECES, b // PIECES * share
        tile = piece // 2 * LANES
        gate = acc_ref[start : start + share, tile : tile + LANES]
        up = acc_ref[start : start + share, width + tile : width + tile + LANES]
        if piece % 2 == 0:
            made = jnp.where(low, gate, swap_halves(up))
        else:
            made = jnp.where(low, swap_halves(gate), up)
        share_ref[b, 0:share, :] = made.astype(BF16)
        if piece == 0:
            strips = []
            for at in range(0, share, LANES):
                size = min(LANES, share - at)
                strip = side[0:4, start + at : start + at + size]
                if size < LANES:
                    strip = jnp.concatenate([strip, jnp.zeros((4, LANES - size), F32)], axis=1)
                strips.append(strip)
            strips.append(jnp.zeros((16 - 4 * len(strips), LANES), F32))
            strips = jnp.concatenate(strips, axis=0).astype(BF16)
        share_ref[b, share : share + 16, :] = strips
    for k, out_ref in enumerate(out_refs):
        out_ref[...] = share_ref[lax.rem(seq_ref[0] + k, devices)]


def gate_up(exp_index, seq_index, tokens, weights, w_router, rows, devices, turn):
    local, _, features, width = weights.shape
    sources, wide = len(tokens), tokens[0].shape[1]
    total = sources * tokens[0].shape[0]
    share = (rows * PIECES // devices + 16, LANES)
    smem, vmem = pl.BlockSpec(memory_space=pltpu.SMEM), pl.BlockSpec(memory_space=pltpu.VMEM)
    return pl.pallas_call(
        functools.partial(gate_up_kernel, features, local, turn, sources, devices),
        in_specs=[smem] * 2 + [vmem] * (2 + sources),
        out_specs=(vmem,) * devices + (vmem, vmem, smem, smem),
        out_shape=(jax.ShapeDtypeStruct(share, BF16),) * devices
        + (
            jax.ShapeDtypeStruct((total, rows), BF16),
            jax.ShapeDtypeStruct((16, LANES), F32),
            jax.ShapeDtypeStruct((16,), jnp.int32),
            jax.ShapeDtypeStruct((1,), jnp.int32),
        ),
        scratch_shapes=[
            pltpu.VMEM((total, wide), BF16),
            pltpu.VMEM((rows, wide), BF16),
            pltpu.VMEM((rows, 2 * width), F32),
            pltpu.VMEM((devices,) + share, BF16),
        ],
        compiler_params=params(),
        name="gate_up",
    )(exp_index, seq_index, weights, w_router.T, *tokens)


def inner_kernel(*refs):
    x_refs, (out_ref, logit_ref) = refs[:-2], refs[-2:]
    share = x_refs[0].shape[0] - 16
    half = share // 2

    def total(start, size):
        return functools.reduce(
            jnp.add, [x_ref[start : start + size].astype(F32) for x_ref in x_refs]
        )

    side = total(share, 16)
    columns, logits = [], []
    for strip in range(-(-share // LANES)):
        values = side[4 * strip : 4 * strip + 4]
        inverse = lax.rsqrt((values[2:3] + values[3:4]) * (1.0 / D) + 1e-6)
        logits.append((values[0:1] + values[1:2]) * inverse)
        columns.append(jnp.broadcast_to(inverse, (LANES, LANES)).T)
    logit_ref[...] = jnp.concatenate(logits + [jnp.zeros((8 - len(logits), LANES), F32)], axis=0)
    scaled = total(0, share) * jnp.concatenate(columns, axis=0)[0:share]
    made = scaled / (1.0 + jnp.exp(-scaled)) * swap_halves(scaled)
    low = iota((half, LANES), 1) < PIECE_WIDTH
    made = jnp.where(low, made[0:half], swap_halves(made[half:share])).astype(BF16)
    out_ref[...] = made


def inner(parts):
    return pl.pallas_call(
        inner_kernel,
        out_shape=(
            jax.ShapeDtypeStruct(((parts[0].shape[0] - 16) // 2, LANES), BF16),
            jax.ShapeDtypeStruct((8, LANES), F32),
        ),
        compiler_params=params(),
        name="inner",
    )(*parts)


def down_kernel(features, local, first_ref, seq_ref, range_ref, pick_ref, w_ref, logit_ref, *refs):
    (own_ref, beside_ref, behind_ref, other_ref), refs = refs[:4], refs[4:]
    out_refs, (x_ref, row_ref, made_ref) = refs[:-3], refs[-3:]
    total, rows = pick_ref.shape
    width = w_ref.shape[2]
    window = total // 2 + 16
    devices, half, _ = x_ref.shape
    for k in range(devices // 2):
        source = lax.rem(seq_ref[0] + devices - 2 * k, devices)
        x_ref[source] = behind_ref[k - 1] if k else own_ref[...]
        x_ref[source + 1 - lax.rem(source, 2) * 2] = other_ref[k - 1] if k else beside_ref[...]
    share = 2 * half
    low = iota((half, LANES), 1) < PIECE_WIDTH
    for b in range(0, devices, 2):
        start, tile = b // PIECES * share, b % PIECES // 2 * LANES
        one, two = x_ref[b].astype(F32), x_ref[b + 1].astype(F32)
        above = jnp.where(low, one, swap_halves(two)).astype(BF16)
        below = jnp.where(low, swap_halves(one), two).astype(BF16)
        row_ref[start : start + half, tile : tile + LANES] = above
        row_ref[start + half : start + share, tile : tile + LANES] = below
    logit = []
    for piece in range(devices // PIECES):
        for strip in range(-(-share // LANES)):
            size = min(LANES, share - strip * LANES)
            logit.append(logit_ref[piece, strip : strip + 1, 0:size])
    made_ref[...] = jnp.zeros_like(made_ref)
    for j in range(local):
        start_row = first_ref[j]
        start = window_start(start_row, rows, window)
        made = dot_nt(row_ref[pl.ds(start, window), :], w_ref[j])
        fresh = start + iota((window, features), 0) >= start_row
        into = (pl.ds(start, window), slice(0, features))
        made_ref[into] = jnp.where(fresh, made, made_ref[into])
    logit = jnp.concatenate(logit, axis=1)
    high = round16(logit)
    middle = round16(logit - high)
    pick = pick_ref[...]
    where_row = iota((16, rows), 1).astype(F32)
    inside = jnp.logical_and(where_row >= range_ref[:, 0:1], where_row < range_ref[:, 8:9])
    inside = jnp.logical_and(inside, iota((16, rows), 0) < local)
    spread = [jnp.where(inside, part, 0.0) for part in (high, middle, logit - high - middle)]
    spread.append(inside.astype(F32))
    found = dot_nt(jnp.concatenate(spread, axis=0).astype(BF16), pick)
    valid = found[48:64] > 0.5
    logits = jnp.where(valid, found[0:16] + found[16:32] + found[32:48], NEG_FILL)
    top = jnp.max(logits, axis=0, keepdims=True)
    weights = jnp.where(valid, jnp.exp(logits - top), 0.0)
    summed = jnp.sum(weights, axis=0, keepdims=True)
    high = round16(weights)
    both = dot_nn(jnp.concatenate([high, weights - high], axis=0).astype(BF16), pick)
    weight = jnp.sum(jnp.where(inside, both[0:16] + both[16:32], 0.0), axis=0, keepdims=True)
    column = jnp.broadcast_to(weight, (LANES, rows)).T[:, 0:1]
    acc = dot_nn(pick, (made_ref[...] * column).astype(BF16))
    tile, offset = side_place(features, 2)
    pair = jnp.where(iota((LANES, total), 0) == 0, top, summed).T
    tokens = total // len(out_refs)
    for e, out_ref in enumerate(out_refs):
        at = slice(e * tokens, (e + 1) * tokens)
        out_ref[...] = acc[at]
        lane = iota((tokens, LANES), 1) - offset
        side = jnp.where(lane == 0, pair[at, 0:1], acc[at, tile : tile + LANES])
        out_ref[:, tile : tile + LANES] = jnp.where(lane == 1, pair[at, 1:2], side)


def down(first, seq_index, ranges, pick, made, logits, weights, exp_count):
    local, features, width = weights.shape
    total, rows = pick.shape
    wide = side_place(features, 2)[0] + LANES
    smem, vmem = pl.BlockSpec(memory_space=pltpu.SMEM), pl.BlockSpec(memory_space=pltpu.VMEM)
    return pl.pallas_call(
        functools.partial(down_kernel, features, local),
        in_specs=[smem] * 2 + [vmem] * (4 + len(made)),
        out_shape=(jax.ShapeDtypeStruct((total // exp_count, wide), F32),) * exp_count,
        scratch_shapes=[
            pltpu.VMEM((2 * made[2].shape[0] + 2,) + made[0].shape, BF16),
            pltpu.VMEM((rows, width), BF16),
            pltpu.VMEM((rows, wide), F32),
        ],
        compiler_params=params(),
        name="down",
    )(first, seq_index, ranges, pick, weights, logits, *made)


def finish_kernel(hidden_ref, *refs):
    part_refs, out_ref = refs[:-1], refs[-1]
    features = hidden_ref.shape[1]
    tile, offset = side_place(features, 2)
    sides = [x_ref[:, tile : tile + LANES] for x_ref in part_refs]
    tops = [side[:, offset : offset + 1] for side in sides]
    top = functools.reduce(jnp.maximum, tops)
    scales = [jnp.exp(one - top) for one in tops]
    total = functools.reduce(
        jnp.add, [s * side[:, offset + 1 : offset + 2] for s, side in zip(scales, sides)]
    )
    acc = functools.reduce(
        jnp.add, [s * x_ref[:, 0:features] for x_ref, s in zip(part_refs, scales)]
    )
    out = hidden_ref[...] + acc * (1.0 / total)
    out_ref[...] = out.reshape(out_ref.shape).astype(BF16)


def finish(parts, hidden, shape):
    return pl.pallas_call(
        finish_kernel,
        out_shape=jax.ShapeDtypeStruct(shape, BF16),
        compiler_params=params(),
        name="finish",
    )(hidden, *parts)


def join_rounds(features, one, other):
    tile, offset = side_place(features, 2)
    at = tile + offset
    top = jnp.maximum(one[..., at : at + 1], other[..., at : at + 1])
    scales = [jnp.exp(part[..., at : at + 1] - top) for part in (one, other)]
    joined = one * scales[0] + other * scales[1]
    return jnp.where(jnp.arange(one.shape[-1]) == at, top, joined)


def send(x, axis, distance):
    count = lax.axis_size(axis)
    return lax.ppermute(x, axis, [(i, (i + distance) % count) for i in range(count)])


def swap(x, axis):
    return lax.all_to_all(x, axis, split_axis=0, concat_axis=0, tiled=True)


def exchange(parts, axis, direction):
    return [parts[0]] + [send(part, axis, direction * k) for k, part in enumerate(parts) if k]


def neighbour(x, axis):
    return lax.ppermute(x, axis, [(i, i ^ 1) for i in range(lax.axis_size(axis))])


def pair_gather(block, axis):
    pair = jnp.stack([block, neighbour(block, axis)])
    return [pair] + [send(pair, axis, k) for k in range(2, lax.axis_size(axis), 2)]


def gather(block, axis):
    return exchange([block] * lax.axis_size(axis), axis, 1)


def local(
    queries,
    new_key_value,
    key_value_cache,
    page_table,
    cache_len,
    routes,
    residual,
    w_out,
    norm_gain,
    w_router,
    w_gate_up,
    w_down,
):
    exp_count = lax.axis_size("exp")
    seq_count = lax.axis_size("seq")
    exp_index = lax.axis_index("exp").astype(jnp.int32).reshape(1)
    seq_index = lax.axis_index("seq").astype(jnp.int32).reshape(1)
    steps, requests, width = queries.shape
    tokens = steps * requests
    features = w_out.shape[1]
    page_rows = key_value_cache.shape[2]
    pool = key_value_cache.reshape(-1, page_rows, 2, KV_WIDTH)

    shares = attend(
        queries, new_key_value, pool, page_table, cache_len, seq_index, seq_count
    )
    w_gate_up, shares = lax.optimization_barrier((w_gate_up, shares))
    gate_up_weights = w_gate_up.transpose(0, 2, 1, 3)
    shares = swap(shares, "seq")
    gate_up_weights, shares = lax.optimization_barrier((gate_up_weights, shares))
    attn = join(shares)
    gathered = pair_gather(attn, "seq")
    hidden, outgoing = hidden_state(seq_index, gathered, residual, w_out, norm_gain, routes)
    incoming = gather(outgoing, "exp")
    pieces = seq_count // PIECES
    rows = -(-ROUND_ROWS // (32 * pieces)) * 32 * pieces

    def one_round(turn):
        *partial, pick, ranges, first, most = gate_up(
            exp_index, seq_index, incoming, gate_up_weights, w_router, rows, seq_count, turn
        )
        made, logits = inner(exchange(partial, "seq", 1))
        logits = logits[None] if pieces == 1 else lax.all_gather(logits, "seq")[::PIECES]
        behind = jnp.stack([send(made, "seq", k) for k in range(2, seq_count, 2)])
        made = [made, neighbour(made, "seq"), behind, neighbour(behind, "seq")]
        return down(first, seq_index, ranges, pick, made, logits, w_down, exp_count), most

    made, most = one_round(0)
    pairs = w_gate_up.shape[0] * exp_count * steps * CAP
    for turn in range(1, -(-pairs // rows)):
        made = lax.cond(
            most[0] > turn * rows,
            lambda made: tuple(
                join_rounds(features, *both) for both in zip(made, one_round(turn)[0])
            ),
            lambda made: made,
            made,
        )
    return finish(exchange(made, "exp", -1), hidden, (steps, requests, features))


def solution(mesh):
    in_specs = (
        P(None, "exp", None),
        P(None, "exp", None, None),
        P("exp", "seq", None, None, None),
        P("exp", "seq"),
        P("exp"),
        P(None, "exp", None),
        P(None, "exp", "seq"),
        P(None, "seq"),
        P("seq"),
        P("seq", None),
        P("exp", "seq", None, None),
        P("exp", "seq", None),
    )
    out_specs = P(None, "exp", "seq")
    return jax.shard_map(local, mesh=mesh, in_specs=in_specs, out_specs=out_specs, check_vma=False)
```

```python
import functools

import jax
import jax.numpy as jnp
from jax import lax
from jax.experimental import pallas as pl
from jax.experimental.pallas import tpu as pltpu
from jax.sharding import PartitionSpec as P

D = 1536
QUERY_HEADS = 24
KEY_VALUE_HEADS = 8
HEAD_SIZE = 64
GROUP = QUERY_HEADS // KEY_VALUE_HEADS
KV_WIDTH = KEY_VALUE_HEADS * HEAD_SIZE
EXPERTS = 40
FF = 512
CAP = 4
LANES = 128
SIDE_KEYS = 2
ROUND_ROWS = 352
PIECES = 8
PIECE_WIDTH = FF // PIECES

NEG_FILL = -1e30
F32 = jnp.float32
BF16 = jnp.bfloat16
VMEM_LIMIT = 48 * 1024 * 1024
ATTEND_VMEM = 60 * 1024 * 1024


def iota(shape, dimension):
    return lax.broadcasted_iota(jnp.int32, shape, dimension)


def dot_nt(a, b):
    return lax.dot_general(a, b, (((1,), (1,)), ((), ())), preferred_element_type=F32)


def dot_tn(a, b):
    return lax.dot_general(a, b, (((0,), (0,)), ((), ())), preferred_element_type=F32)


def dot_nn(a, b):
    return lax.dot_general(a, b, (((1,), (0,)), ((), ())), preferred_element_type=F32)


def round16(x):
    return x.astype(BF16).astype(F32)


def swap_halves(x):
    return pltpu.roll(x, HEAD_SIZE, 1)


def tile_of(x, index):
    return x[:, index * LANES : (index + 1) * LANES]


def padded(width):
    return -(-width // LANES) * LANES


def params():
    return pltpu.CompilerParams(vmem_limit_bytes=VMEM_LIMIT)


def attend_kernel(
    classes, seq_ref, table_hbm, len_hbm, q_hbm, fresh_hbm, cache_ref, share_ref,
    page_ref, table_ref, len_ref, q_ref, fresh_ref, query_ref, new_ref, order_ref, sems, small_sems,
):
    steps, requests, _ = q_ref.shape
    page_rows = cache_ref.shape[1]
    pages = table_ref.shape[1]
    span = pages * page_rows
    first = seq_ref[0] * span
    small = [
        pltpu.make_async_copy(source, target, small_sems.at[i])
        for i, (source, target) in enumerate(
            [(table_hbm, table_ref), (len_hbm, len_ref), (q_hbm, q_ref), (fresh_hbm, fresh_ref)]
        )
    ]
    for one in small:
        one.start()
    for one in small[:2]:
        one.wait()

    held = [jnp.clip(len_ref[r] - first, 0, span) for r in range(requests)]
    for r in range(requests):
        ahead = jnp.int32(0)
        for other in range(requests):
            if other != r:
                longer = held[other] >= held[r] if other < r else held[other] > held[r]
                ahead = ahead + longer.astype(jnp.int32)
        order_ref[ahead] = r

    share = share_ref.shape[1]
    per_request = steps * GROUP // share

    def put(r, acc, side):
        for i in range(per_request):
            at = r * per_request + i
            share_ref[at, :, 0:KV_WIDTH] = acc[i * share : (i + 1) * share]
            share_ref[at, :, KV_WIDTH : KV_WIDTH + LANES] = side[i * share : (i + 1) * share]

    def copy(r, page):
        at = r * pages + page
        return pltpu.make_async_copy(cache_ref.at[table_ref[r, page]], page_ref.at[at], sems.at[at])

    def needed(r, low):
        return len_ref[r] - first > low * page_rows

    bounds = list(zip((0,) + classes[:-1], classes))

    def start(pair, carry):
        both = order_ref[2 * pair], order_ref[2 * pair + 1]
        for low, high in bounds:

            @pl.when(needed(both[0], low))
            def _():
                for page in range(low, high):
                    for r in both:
                        copy(r, page).start()

        return carry

    lax.fori_loop(0, requests // 2, start, 0)
    for one in small[2:]:
        one.wait()

    low = iota((requests, LANES), 1) < HEAD_SIZE
    for t in range(steps):
        q = q_ref[t].astype(F32) * 0.125
        for g in range(GROUP):
            for j in range(KV_WIDTH // LANES):
                one = tile_of(q, (6 * j + g) // 2)
                two = tile_of(q, (6 * j + 3 + g) // 2)
                if g % 2 == 0:
                    tile = jnp.where(low, one, two)
                else:
                    tile = swap_halves(jnp.where(low, two, one))
                query_ref[t * GROUP + g, :, j * LANES : (j + 1) * LANES] = tile
        new_ref[t] = fresh_ref[t].reshape(2 * requests, KV_WIDTH).astype(F32)

    rows = steps * GROUP * KEY_VALUE_HEADS
    own = iota((rows, KV_WIDTH), 1) // HEAD_SIZE == iota((rows, KV_WIDTH), 0) % KEY_VALUE_HEADS
    lane = iota((rows, LANES), 1)
    head = iota((rows, LANES), 0) % KEY_VALUE_HEADS
    row_step = iota((rows, 16), 0) // (GROUP * KEY_VALUE_HEADS)
    kept = jnp.logical_and(iota((rows, 16), 1) <= row_step, seq_ref[0] == 0)
    fresh_bias = jnp.where(kept, 0.0, NEG_FILL)

    def fresh_rows(r, which):
        found = [new_ref[u, pl.ds(2 * r + which, 1), :] for u in range(steps)]
        return jnp.concatenate(found + [jnp.zeros((16 - steps, KV_WIDTH), F32)], axis=0).astype(BF16)

    def attend_pages(r, count):
        spread = jnp.concatenate(
            [
                jnp.broadcast_to(query_ref[i, pl.ds(r, 1), :], (KEY_VALUE_HEADS, KV_WIDTH))
                for i in range(steps * GROUP)
            ],
            axis=0,
        )
        spread = jnp.where(own, spread, 0.0).astype(BF16)
        both = [page_ref[r * pages + page].reshape(2 * page_rows, KV_WIDTH) for page in range(count)]
        both = jnp.concatenate(both, axis=0)
        size = 2 * count * page_rows
        place = iota((1, size), 1)
        live = jnp.logical_and(place % 2 == 0, first + place // 2 < len_ref[r])
        scores = dot_nt(spread, both) + jnp.where(live, 0.0, NEG_FILL)
        fresh_scores = dot_nt(spread, fresh_rows(r, 0)) + fresh_bias
        largest = jnp.maximum(
            jnp.max(scores, axis=1, keepdims=True), jnp.max(fresh_scores, axis=1, keepdims=True)
        )
        weights = jnp.exp(scores - largest)
        fresh_weights = jnp.exp(fresh_scores - largest)
        total = jnp.sum(weights, axis=1, keepdims=True)
        total = total + jnp.sum(fresh_weights, axis=1, keepdims=True)
        moved = [pltpu.roll(tile_of(weights, j), 1, 1) for j in range(size // LANES)]
        acc = dot_nn(jnp.concatenate(moved, axis=1).astype(BF16), both)
        acc = acc + dot_nn(fresh_weights.astype(BF16), fresh_rows(r, 1))
        acc = jnp.where(own, acc * (1.0 / total), 0.0)
        acc = jnp.sum(acc.reshape(steps * GROUP, KEY_VALUE_HEADS, KV_WIDTH), axis=1)
        level = jnp.where(needed(r, 0), largest + jnp.log(total), NEG_FILL)
        high = round16(level)
        middle = round16(level - high)
        side = jnp.where(lane == head, high, 0.0)
        side = jnp.where(lane == head + 8, middle, side)
        side = jnp.where(lane == head + 16, level - high - middle, side)
        side = jnp.sum(side.reshape(steps * GROUP, KEY_VALUE_HEADS, LANES), axis=1)
        return acc.astype(BF16), side.astype(BF16)

    def one_pair(pair, carry):
        both = order_ref[2 * pair], order_ref[2 * pair + 1]
        for low, high in bounds:
            enough = needed(both[0], low)
            if high < pages:
                enough = jnp.logical_and(enough, jnp.logical_not(needed(both[0], high)))

            @pl.when(enough)
            def _():
                for page in range(high):
                    for r in both:
                        copy(r, page).wait()
                made = [attend_pages(r, high) for r in both]
                for r, (acc, side) in zip(both, made):
                    put(r, acc, side)

        @pl.when(jnp.logical_not(needed(both[0], 0)))
        def _():
            empty = jnp.where(iota((steps * GROUP, LANES), 1) < KEY_VALUE_HEADS, NEG_FILL, 0.0)
            for r in both:
                put(r, jnp.zeros((steps * GROUP, KV_WIDTH), BF16), empty.astype(BF16))

        return carry

    lax.fori_loop(0, requests // 2, one_pair, 0)


def attend(queries, new_key_value, cache, page_table, cache_len, seq_index, devices):
    steps, requests, _ = queries.shape
    pages = page_table.shape[1]
    page_rows = cache.shape[1]
    classes = tuple(c for c in (2, 4, 6) if c < pages) + (pages,)
    share = (requests * steps * GROUP // devices, KV_WIDTH + LANES)
    smem, hbm = pl.BlockSpec(memory_space=pltpu.SMEM), pl.BlockSpec(memory_space=pl.ANY)
    return pl.pallas_call(
        functools.partial(attend_kernel, classes),
        in_specs=[smem] + [hbm] * 5,
        out_shape=jax.ShapeDtypeStruct((devices,) + share, BF16),
        scratch_shapes=[
            pltpu.VMEM((requests * pages, page_rows, 2, KV_WIDTH), BF16),
            pltpu.SMEM(page_table.shape, jnp.int32),
            pltpu.SMEM(cache_len.shape, jnp.int32),
            pltpu.VMEM(queries.shape, BF16),
            pltpu.VMEM(new_key_value.shape, BF16),
            pltpu.VMEM((steps * GROUP, requests, KV_WIDTH), F32),
            pltpu.VMEM((steps, 2 * requests, KV_WIDTH), F32),
            pltpu.SMEM((requests,), jnp.int32),
            pltpu.SemaphoreType.DMA((requests * pages,)),
            pltpu.SemaphoreType.DMA((4,)),
        ],
        compiler_params=pltpu.CompilerParams(vmem_limit_bytes=ATTEND_VMEM),
        name="attend",
    )(seq_index, page_table, cache_len, queries, new_key_value, cache)


def join_kernel(x_ref, out_ref):
    blocks, rows, _ = x_ref.shape
    tokens = rows // GROUP
    levels = []
    for b in range(blocks):
        side = x_ref[b, :, KV_WIDTH : KV_WIDTH + LANES].astype(F32)
        levels.append(side + pltpu.roll(side, LANES - 8, 1) + pltpu.roll(side, LANES - 16, 1))
    largest = functools.reduce(jnp.maximum, levels)
    weights = [jnp.exp(level - largest) for level in levels]
    inverse = 1.0 / functools.reduce(jnp.add, weights)
    low = iota((rows, LANES), 1) < HEAD_SIZE
    acc = [jnp.zeros((rows, LANES), F32) for _ in range(KV_WIDTH // LANES)]
    for b in range(blocks):
        share = weights[b] * inverse
        for j in range(KV_WIDTH // LANES):
            factor = jnp.where(low, share[:, 2 * j : 2 * j + 1], share[:, 2 * j + 1 : 2 * j + 2])
            acc[j] = acc[j] + factor * x_ref[b, :, j * LANES : (j + 1) * LANES].astype(F32)

    def piece(head, half):
        k, g = head // GROUP, head % GROUP
        tile = jnp.concatenate(
            [acc[k // 2][t * GROUP + g : t * GROUP + g + 1] for t in range(tokens)], axis=0
        )
        return tile if k % 2 == half else swap_halves(tile)

    low_tokens = iota((tokens, LANES), 1) < HEAD_SIZE
    for m in range(QUERY_HEADS // 2):
        tile = jnp.where(low_tokens, piece(2 * m, 0), piece(2 * m + 1, 1)).astype(BF16)
        out_ref[:, m * LANES : (m + 1) * LANES] = tile


def join(parts):
    rows = parts.shape[1]
    return pl.pallas_call(
        join_kernel,
        out_shape=jax.ShapeDtypeStruct((rows // GROUP, QUERY_HEADS * HEAD_SIZE), BF16),
        compiler_params=params(),
        name="join",
    )(parts)


def side_place(features, count):
    tile, offset = features // LANES * LANES, features % LANES
    return (tile, offset) if offset and offset + count <= LANES else (padded(features), 0)


def hidden_kernel(seq_ref, residual_ref, w_ref, gain_ref, routes_ref, *refs):
    attn_refs, (hidden_ref, out_ref, wide_ref) = refs[:-3], refs[-3:]
    steps, requests, features = residual_ref.shape
    tokens = steps * requests
    blocks = [ref[i].astype(F32) for ref in attn_refs for i in range(2)]
    attn = jnp.concatenate(blocks, axis=0).astype(BF16)
    row, column = iota((tokens, tokens), 0), iota((tokens, tokens), 1)
    devices, share = len(blocks), attn_refs[0].shape[1]
    source = seq_ref[0] + devices - column // (2 * share) * 2
    source = jnp.where(source >= devices, source - devices, source)
    other = column // share % 2
    source = source + other * (1 - source % 2 * 2)
    token = source * share + column % share
    reorder = jnp.logical_and(row % requests == token // steps, row // requests == token % steps)
    attn = dot_nn(reorder.astype(F32).astype(BF16), attn).astype(BF16)
    residual = residual_ref[...].astype(F32).reshape(tokens, features)
    hidden = residual + dot_nt(attn, w_ref[...])
    hidden_ref[...] = hidden
    squares = jnp.sum(hidden * hidden, axis=1, keepdims=True)
    tile, offset = side_place(features, SIDE_KEYS + EXPERTS)
    wide_ref[...] = jnp.zeros_like(wide_ref)
    wide_ref[:, 0:features] = hidden * gain_ref[...]
    routes = routes_ref[...].reshape(tokens, routes_ref.shape[2])
    lane = iota((tokens, LANES), 1) - offset
    side = wide_ref[:, tile : tile + LANES]
    for k in range(routes.shape[1]):
        side = jnp.where(lane == routes[:, k : k + 1] + SIDE_KEYS, 1.0, side)
    high = round16(squares)
    side = jnp.where(lane == 0, high, side)
    wide_ref[:, tile : tile + LANES] = jnp.where(lane == 1, squares - high, side)
    out_ref[...] = wide_ref[...].astype(BF16)


def hidden_state(seq_index, attn, residual, w_out, gain, routes):
    steps, requests, features = residual.shape
    tokens = steps * requests
    wide = side_place(features, SIDE_KEYS + EXPERTS)[0] + LANES
    smem, vmem = pl.BlockSpec(memory_space=pltpu.SMEM), pl.BlockSpec(memory_space=pltpu.VMEM)
    return pl.pallas_call(
        hidden_kernel,
        in_specs=[smem] + [vmem] * (4 + len(attn)),
        out_shape=(
            jax.ShapeDtypeStruct((tokens, features), F32),
            jax.ShapeDtypeStruct((tokens, wide), BF16),
        ),
        scratch_shapes=[pltpu.VMEM((tokens, wide), F32)],
        compiler_params=params(),
        name="hidden",
    )(seq_index, residual, w_out.T, gain.reshape(1, features), routes, *attn)


def window_start(first, rows, window):
    return pl.multiple_of(jnp.clip(first // 16 * 16, 0, rows - window), 16)


def gate_up_kernel(
    features, local, turn, sources, devices, where_ref, seq_ref, w_ref, router_ref, *refs,
):
    part_refs, refs = refs[:sources], refs[sources:]
    out_refs, refs = refs[:devices], refs[devices:]
    pick_ref, range_ref, first_ref, most_ref, x_ref, row_ref, acc_ref, share_ref = refs
    total = x_ref.shape[0]
    for e, part_ref in enumerate(part_refs):
        x_ref[e * (total // sources) : (e + 1) * (total // sources)] = part_ref[...]
    rows = pick_ref.shape[1]
    width = w_ref.shape[3]
    window = total // 2 + 16
    tile, offset = side_place(features, SIDE_KEYS + EXPERTS)
    me = where_ref[0]
    own_side = x_ref[:, tile : tile + LANES].astype(F32)
    lane = iota((total, LANES), 1)
    flags = pltpu.roll(own_side, LANES - offset - SIDE_KEYS, 1)
    flags = jnp.where(lane < EXPERTS, flags, 0.0)
    owners = EXPERTS // local
    counts = jnp.sum(flags, axis=0, keepdims=True)
    most = jnp.int32(0)
    for o in range(owners):
        held = jnp.logical_and(lane[0:1] >= o * local, lane[0:1] < (o + 1) * local)
        most = jnp.maximum(most, jnp.sum(jnp.where(held, counts, 0.0)).astype(jnp.int32))
    most_ref[0] = most
    mine = pltpu.roll(flags, lax.rem(LANES - me * local, LANES), 1)
    mine = jnp.where(lane < local, mine, 0.0)
    mine16 = mine.astype(BF16)
    row, column = iota((total, total), 0), iota((total, total), 1)
    earlier = (column < row).astype(F32).astype(BF16)
    ranks = dot_nn(earlier, mine16)
    counts = jnp.sum(mine, axis=0, keepdims=True)
    before = (iota((LANES, LANES), 0) < iota((LANES, LANES), 1)).astype(F32).astype(BF16)
    first = dot_nn(jnp.broadcast_to(counts, (8, LANES)).astype(BF16), before)[0:1] - turn * rows
    place = jnp.where(mine > 0.0, first + ranks, -1.0).astype(jnp.int32)
    at = iota((total, rows), 1)
    pick = jnp.zeros((total, rows), F32)
    for j in range(local):
        pick = jnp.where(at == place[:, j : j + 1], 1.0, pick)
    pick = pick.astype(BF16)
    pick_ref[...] = pick
    ranges = jnp.where(iota((16, LANES), 0) < 8, first, first + counts)
    ranges = jnp.concatenate([ranges[0:8], ranges[8:16]] + [jnp.zeros((LANES - 16, LANES), F32)], axis=0)
    ranges = ranges.T
    range_ref[...] = ranges[0:16]
    row_ref[...] = dot_tn(pick, x_ref[...]).astype(BF16)
    acc_ref[...] = jnp.zeros_like(acc_ref)
    for j in range(local):
        start_row = jnp.sum(first[:, j : j + 1]).astype(jnp.int32)
        first_ref[j] = start_row
        start = window_start(start_row, rows, window)
        part = row_ref[pl.ds(start, window), 0:features]
        fresh = start + iota((window, width), 0) >= start_row
        for half in range(2):
            into = (pl.ds(start, window), slice(half * width, (half + 1) * width))
            made = dot_nn(part, w_ref[j, half])
            acc_ref[into] = jnp.where(fresh, made, acc_ref[into])
    logits = dot_nt(router_ref[...], x_ref[:, 0:features])
    high = round16(logits)
    both = jnp.concatenate([high, logits - high], axis=0).astype(BF16)
    both = dot_nn(both, pick)
    turned = jnp.zeros((EXPERTS, rows), jnp.bool_)
    expert = iota((EXPERTS, rows), 0) - me * local
    where_row = iota((EXPERTS, rows), 1).astype(F32)
    for j in range(local):
        inside = jnp.logical_and(
            where_row >= first[:, j : j + 1], where_row < (first + counts)[:, j : j + 1]
        )
        turned = jnp.logical_or(turned, jnp.logical_and(inside, expert == j))
    squares = dot_tn(own_side.astype(BF16), pick)
    side = jnp.concatenate(
        [
            jnp.sum(jnp.where(turned, both[0:EXPERTS], 0.0), axis=0, keepdims=True),
            jnp.sum(jnp.where(turned, both[EXPERTS : 2 * EXPERTS], 0.0), axis=0, keepdims=True),
            squares[offset : offset + 2],
            jnp.zeros((12, rows), F32),
        ],
        axis=0,
    )
    share = share_ref.shape[1] - 16
    low = iota((share, LANES), 1) < PIECE_WIDTH
    for b in range(devices):
        piece, start = b % PIECES, b // PIECES * share
        tile = piece // 2 * LANES
        gate = acc_ref[start : start + share, tile : tile + LANES]
        up = acc_ref[start : start + share, width + tile : width + tile + LANES]
        if piece % 2 == 0:
            made = jnp.where(low, gate, swap_halves(up))
        else:
            made = jnp.where(low, swap_halves(gate), up)
        share_ref[b, 0:share, :] = made.astype(BF16)
        if piece == 0:
            strips = []
            for at in range(0, share, LANES):
                size = min(LANES, share - at)
                strip = side[0:4, start + at : start + at + size]
                if size < LANES:
                    strip = jnp.concatenate([strip, jnp.zeros((4, LANES - size), F32)], axis=1)
                strips.append(strip)
            strips.append(jnp.zeros((16 - 4 * len(strips), LANES), F32))
            strips = jnp.concatenate(strips, axis=0).astype(BF16)
        share_ref[b, share : share + 16, :] = strips
    for k, out_ref in enumerate(out_refs):
        out_ref[...] = share_ref[lax.rem(seq_ref[0] + k, devices)]


def gate_up(exp_index, seq_index, tokens, weights, w_router, rows, devices, turn):
    local, _, features, width = weights.shape
    sources, wide = len(tokens), tokens[0].shape[1]
    total = sources * tokens[0].shape[0]
    share = (rows * PIECES // devices + 16, LANES)
    smem, vmem = pl.BlockSpec(memory_space=pltpu.SMEM), pl.BlockSpec(memory_space=pltpu.VMEM)
    return pl.pallas_call(
        functools.partial(gate_up_kernel, features, local, turn, sources, devices),
        in_specs=[smem] * 2 + [vmem] * (2 + sources),
        out_specs=(vmem,) * devices + (vmem, vmem, smem, smem),
        out_shape=(jax.ShapeDtypeStruct(share, BF16),) * devices
        + (
            jax.ShapeDtypeStruct((total, rows), BF16),
            jax.ShapeDtypeStruct((16, LANES), F32),
            jax.ShapeDtypeStruct((16,), jnp.int32),
            jax.ShapeDtypeStruct((1,), jnp.int32),
        ),
        scratch_shapes=[
            pltpu.VMEM((total, wide), BF16),
            pltpu.VMEM((rows, wide), BF16),
            pltpu.VMEM((rows, 2 * width), F32),
            pltpu.VMEM((devices,) + share, BF16),
        ],
        compiler_params=params(),
        name="gate_up",
    )(exp_index, seq_index, weights, w_router.T, *tokens)


def inner_kernel(*refs):
    x_refs, (out_ref, logit_ref) = refs[:-2], refs[-2:]
    share = x_refs[0].shape[0] - 16
    half = share // 2

    def total(start, size):
        return functools.reduce(
            jnp.add, [x_ref[start : start + size].astype(F32) for x_ref in x_refs]
        )

    side = total(share, 16)
    columns, logits = [], []
    for strip in range(-(-share // LANES)):
        values = side[4 * strip : 4 * strip + 4]
        inverse = lax.rsqrt((values[2:3] + values[3:4]) * (1.0 / D) + 1e-6)
        logits.append((values[0:1] + values[1:2]) * inverse)
        columns.append(jnp.broadcast_to(inverse, (LANES, LANES)).T)
    logit_ref[...] = jnp.concatenate(logits + [jnp.zeros((8 - len(logits), LANES), F32)], axis=0)
    scaled = total(0, share) * jnp.concatenate(columns, axis=0)[0:share]
    made = scaled / (1.0 + jnp.exp(-scaled)) * swap_halves(scaled)
    low = iota((half, LANES), 1) < PIECE_WIDTH
    made = jnp.where(low, made[0:half], swap_halves(made[half:share])).astype(BF16)
    out_ref[...] = made


def inner(parts):
    return pl.pallas_call(
        inner_kernel,
        out_shape=(
            jax.ShapeDtypeStruct(((parts[0].shape[0] - 16) // 2, LANES), BF16),
            jax.ShapeDtypeStruct((8, LANES), F32),
        ),
        compiler_params=params(),
        name="inner",
    )(*parts)


def down_kernel(features, local, pairs, first_ref, seq_ref, range_ref, pick_ref, w_ref, logit_ref, *refs):
    pair_refs, out_refs, (x_ref, row_ref, made_ref) = refs[:pairs], refs[pairs:-3], refs[-3:]
    total, rows = pick_ref.shape
    width = w_ref.shape[2]
    window = total // 2 + 16
    devices, half, _ = x_ref.shape
    for k, pair_ref in enumerate(pair_refs):
        source = lax.rem(seq_ref[0] + devices - 2 * k, devices)
        x_ref[source] = pair_ref[0]
        x_ref[source + 1 - lax.rem(source, 2) * 2] = pair_ref[1]
    share = 2 * half
    low = iota((half, LANES), 1) < PIECE_WIDTH
    for b in range(0, devices, 2):
        start, tile = b // PIECES * share, b % PIECES // 2 * LANES
        one, two = x_ref[b].astype(F32), x_ref[b + 1].astype(F32)
        above = jnp.where(low, one, swap_halves(two)).astype(BF16)
        below = jnp.where(low, swap_halves(one), two).astype(BF16)
        row_ref[start : start + half, tile : tile + LANES] = above
        row_ref[start + half : start + share, tile : tile + LANES] = below
    logit = []
    for piece in range(devices // PIECES):
        for strip in range(-(-share // LANES)):
            size = min(LANES, share - strip * LANES)
            logit.append(logit_ref[piece, strip : strip + 1, 0:size])
    made_ref[...] = jnp.zeros_like(made_ref)
    for j in range(local):
        start_row = first_ref[j]
        start = window_start(start_row, rows, window)
        made = dot_nt(row_ref[pl.ds(start, window), :], w_ref[j])
        fresh = start + iota((window, features), 0) >= start_row
        into = (pl.ds(start, window), slice(0, features))
        made_ref[into] = jnp.where(fresh, made, made_ref[into])
    logit = jnp.concatenate(logit, axis=1)
    high = round16(logit)
    middle = round16(logit - high)
    pick = pick_ref[...]
    where_row = iota((16, rows), 1).astype(F32)
    inside = jnp.logical_and(where_row >= range_ref[:, 0:1], where_row < range_ref[:, 8:9])
    inside = jnp.logical_and(inside, iota((16, rows), 0) < local)
    spread = [jnp.where(inside, part, 0.0) for part in (high, middle, logit - high - middle)]
    spread.append(inside.astype(F32))
    found = dot_nt(jnp.concatenate(spread, axis=0).astype(BF16), pick)
    valid = found[48:64] > 0.5
    logits = jnp.where(valid, found[0:16] + found[16:32] + found[32:48], NEG_FILL)
    top = jnp.max(logits, axis=0, keepdims=True)
    weights = jnp.where(valid, jnp.exp(logits - top), 0.0)
    summed = jnp.sum(weights, axis=0, keepdims=True)
    high = round16(weights)
    both = dot_nn(jnp.concatenate([high, weights - high], axis=0).astype(BF16), pick)
    weight = jnp.sum(jnp.where(inside, both[0:16] + both[16:32], 0.0), axis=0, keepdims=True)
    column = jnp.broadcast_to(weight, (LANES, rows)).T[:, 0:1]
    acc = dot_nn(pick, (made_ref[...] * column).astype(BF16))
    tile, offset = side_place(features, 2)
    pair = jnp.where(iota((LANES, total), 0) == 0, top, summed).T
    tokens = total // len(out_refs)
    for e, out_ref in enumerate(out_refs):
        at = slice(e * tokens, (e + 1) * tokens)
        out_ref[...] = acc[at]
        lane = iota((tokens, LANES), 1) - offset
        side = jnp.where(lane == 0, pair[at, 0:1], acc[at, tile : tile + LANES])
        out_ref[:, tile : tile + LANES] = jnp.where(lane == 1, pair[at, 1:2], side)


def down(first, seq_index, ranges, pick, made, logits, weights, exp_count):
    local, features, width = weights.shape
    total, rows = pick.shape
    wide = side_place(features, 2)[0] + LANES
    smem, vmem = pl.BlockSpec(memory_space=pltpu.SMEM), pl.BlockSpec(memory_space=pltpu.VMEM)
    return pl.pallas_call(
        functools.partial(down_kernel, features, local, len(made)),
        in_specs=[smem] * 2 + [vmem] * (4 + len(made)),
        out_shape=(jax.ShapeDtypeStruct((total // exp_count, wide), F32),) * exp_count,
        scratch_shapes=[
            pltpu.VMEM((2 * len(made),) + made[0].shape[1:], BF16),
            pltpu.VMEM((rows, width), BF16),
            pltpu.VMEM((rows, wide), F32),
        ],
        compiler_params=params(),
        name="down",
    )(first, seq_index, ranges, pick, weights, logits, *made)


def finish_kernel(hidden_ref, *refs):
    part_refs, out_ref = refs[:-1], refs[-1]
    features = hidden_ref.shape[1]
    tile, offset = side_place(features, 2)
    sides = [x_ref[:, tile : tile + LANES] for x_ref in part_refs]
    tops = [side[:, offset : offset + 1] for side in sides]
    top = functools.reduce(jnp.maximum, tops)
    scales = [jnp.exp(one - top) for one in tops]
    total = functools.reduce(
        jnp.add, [s * side[:, offset + 1 : offset + 2] for s, side in zip(scales, sides)]
    )
    acc = functools.reduce(
        jnp.add, [s * x_ref[:, 0:features] for x_ref, s in zip(part_refs, scales)]
    )
    out = hidden_ref[...] + acc * (1.0 / total)
    out_ref[...] = out.reshape(out_ref.shape).astype(BF16)


def finish(parts, hidden, shape):
    return pl.pallas_call(
        finish_kernel,
        out_shape=jax.ShapeDtypeStruct(shape, BF16),
        compiler_params=params(),
        name="finish",
    )(hidden, *parts)


def join_rounds(features, one, other):
    tile, offset = side_place(features, 2)
    at = tile + offset
    top = jnp.maximum(one[..., at : at + 1], other[..., at : at + 1])
    scales = [jnp.exp(part[..., at : at + 1] - top) for part in (one, other)]
    joined = one * scales[0] + other * scales[1]
    return jnp.where(jnp.arange(one.shape[-1]) == at, top, joined)


def send(x, axis, distance):
    count = lax.axis_size(axis)
    return lax.ppermute(x, axis, [(i, (i + distance) % count) for i in range(count)])


def swap(x, axis):
    return lax.all_to_all(x, axis, split_axis=0, concat_axis=0, tiled=True)


def exchange(parts, axis, direction):
    return [parts[0]] + [send(part, axis, direction * k) for k, part in enumerate(parts) if k]


def pair_gather(block, axis):
    count = lax.axis_size(axis)
    beside = lax.ppermute(block, axis, [(i, i ^ 1) for i in range(count)])
    pair = jnp.stack([block, beside])
    return [pair] + [send(pair, axis, k) for k in range(2, count, 2)]


def gather(block, axis):
    return exchange([block] * lax.axis_size(axis), axis, 1)


def local(
    queries,
    new_key_value,
    key_value_cache,
    page_table,
    cache_len,
    routes,
    residual,
    w_out,
    norm_gain,
    w_router,
    w_gate_up,
    w_down,
):
    exp_count = lax.axis_size("exp")
    seq_count = lax.axis_size("seq")
    exp_index = lax.axis_index("exp").astype(jnp.int32).reshape(1)
    seq_index = lax.axis_index("seq").astype(jnp.int32).reshape(1)
    steps, requests, width = queries.shape
    tokens = steps * requests
    features = w_out.shape[1]
    page_rows = key_value_cache.shape[2]
    pool = key_value_cache.reshape(-1, page_rows, 2, KV_WIDTH)

    shares = attend(
        queries, new_key_value, pool, page_table, cache_len, seq_index, seq_count
    )
    w_gate_up, shares = lax.optimization_barrier((w_gate_up, shares))
    gate_up_weights = w_gate_up.transpose(0, 2, 1, 3)
    shares = swap(shares, "seq")
    gate_up_weights, shares = lax.optimization_barrier((gate_up_weights, shares))
    attn = join(shares)
    gathered = pair_gather(attn, "seq")
    hidden, outgoing = hidden_state(seq_index, gathered, residual, w_out, norm_gain, routes)
    incoming = gather(outgoing, "exp")
    pieces = seq_count // PIECES
    rows = -(-ROUND_ROWS // (32 * pieces)) * 32 * pieces

    def one_round(turn):
        *partial, pick, ranges, first, most = gate_up(
            exp_index, seq_index, incoming, gate_up_weights, w_router, rows, seq_count, turn
        )
        made, logits = inner(exchange(partial, "seq", 1))
        logits = logits[None] if pieces == 1 else lax.all_gather(logits, "seq")[::PIECES]
        made = pair_gather(made, "seq")
        return down(first, seq_index, ranges, pick, made, logits, w_down, exp_count), most

    made, most = one_round(0)
    pairs = w_gate_up.shape[0] * exp_count * steps * CAP
    for turn in range(1, -(-pairs // rows)):
        made = lax.cond(
            most[0] > turn * rows,
            lambda made: tuple(
                join_rounds(features, *both) for both in zip(made, one_round(turn)[0])
            ),
            lambda made: made,
            made,
        )
    return finish(exchange(made, "exp", -1), hidden, (steps, requests, features))


def solution(mesh):
    in_specs = (
        P(None, "exp", None),
        P(None, "exp", None, None),
        P("exp", "seq", None, None, None),
        P("exp", "seq"),
        P("exp"),
        P(None, "exp", None),
        P(None, "exp", "seq"),
        P(None, "seq"),
        P("seq"),
        P("seq", None),
        P("exp", "seq", None, None),
        P("exp", "seq", None),
    )
    out_specs = P(None, "exp", "seq")
    return jax.shard_map(local, mesh=mesh, in_specs=in_specs, out_specs=out_specs, check_vma=False)
```

```python
import functools

import jax
import jax.numpy as jnp
from jax import lax
from jax.experimental import pallas as pl
from jax.experimental.pallas import tpu as pltpu
from jax.sharding import PartitionSpec as P

D = 1536
QUERY_HEADS = 24
KEY_VALUE_HEADS = 8
HEAD_SIZE = 64
GROUP = QUERY_HEADS // KEY_VALUE_HEADS
KV_WIDTH = KEY_VALUE_HEADS * HEAD_SIZE
EXPERTS = 40
FF = 512
CAP = 4
LANES = 128
SIDE_KEYS = 2
ROUND_ROWS = 352
PIECES = 8
PIECE_WIDTH = FF // PIECES

NEG_FILL = -1e30
F32 = jnp.float32
BF16 = jnp.bfloat16
VMEM_LIMIT = 48 * 1024 * 1024
ATTEND_VMEM = 60 * 1024 * 1024


def iota(shape, dimension):
    return lax.broadcasted_iota(jnp.int32, shape, dimension)


def dot_nt(a, b):
    return lax.dot_general(a, b, (((1,), (1,)), ((), ())), preferred_element_type=F32)


def dot_tn(a, b):
    return lax.dot_general(a, b, (((0,), (0,)), ((), ())), preferred_element_type=F32)


def dot_nn(a, b):
    return lax.dot_general(a, b, (((1,), (0,)), ((), ())), preferred_element_type=F32)


def round16(x):
    return x.astype(BF16).astype(F32)


def swap_halves(x):
    return pltpu.roll(x, HEAD_SIZE, 1)


def tile_of(x, index):
    return x[:, index * LANES : (index + 1) * LANES]


def padded(width):
    return -(-width // LANES) * LANES


def params():
    return pltpu.CompilerParams(vmem_limit_bytes=VMEM_LIMIT)


def attend_kernel(
    classes, seq_ref, table_hbm, len_hbm, q_hbm, fresh_hbm, cache_ref, share_ref,
    page_ref, table_ref, len_ref, q_ref, fresh_ref, query_ref, new_ref, order_ref, sems, small_sems,
):
    steps, requests, _ = q_ref.shape
    page_rows = cache_ref.shape[1]
    pages = table_ref.shape[1]
    span = pages * page_rows
    first = seq_ref[0] * span
    small = [
        pltpu.make_async_copy(source, target, small_sems.at[i])
        for i, (source, target) in enumerate(
            [(table_hbm, table_ref), (len_hbm, len_ref), (q_hbm, q_ref), (fresh_hbm, fresh_ref)]
        )
    ]
    for one in small:
        one.start()
    for one in small[:2]:
        one.wait()

    held = [jnp.clip(len_ref[r] - first, 0, span) for r in range(requests)]
    for r in range(requests):
        ahead = jnp.int32(0)
        for other in range(requests):
            if other != r:
                longer = held[other] >= held[r] if other < r else held[other] > held[r]
                ahead = ahead + longer.astype(jnp.int32)
        order_ref[ahead] = r

    share = share_ref.shape[1]
    per_request = steps * GROUP // share

    def put(r, acc, side):
        for i in range(per_request):
            at = r * per_request + i
            share_ref[at, :, 0:KV_WIDTH] = acc[i * share : (i + 1) * share]
            share_ref[at, :, KV_WIDTH : KV_WIDTH + LANES] = side[i * share : (i + 1) * share]

    def copy(r, page):
        at = r * pages + page
        return pltpu.make_async_copy(cache_ref.at[table_ref[r, page]], page_ref.at[at], sems.at[at])

    def needed(r, low):
        return len_ref[r] - first > low * page_rows

    bounds = list(zip((0,) + classes[:-1], classes))

    def start(pair, carry):
        both = order_ref[2 * pair], order_ref[2 * pair + 1]
        for low, high in bounds:

            @pl.when(needed(both[0], low))
            def _():
                for page in range(low, high):
                    for r in both:
                        copy(r, page).start()

        return carry

    lax.fori_loop(0, requests // 2, start, 0)
    for one in small[2:]:
        one.wait()

    low = iota((requests, LANES), 1) < HEAD_SIZE
    for t in range(steps):
        q = q_ref[t].astype(F32) * 0.125
        for g in range(GROUP):
            for j in range(KV_WIDTH // LANES):
                one = tile_of(q, (6 * j + g) // 2)
                two = tile_of(q, (6 * j + 3 + g) // 2)
                if g % 2 == 0:
                    tile = jnp.where(low, one, two)
                else:
                    tile = swap_halves(jnp.where(low, two, one))
                query_ref[t * GROUP + g, :, j * LANES : (j + 1) * LANES] = tile
        new_ref[t] = fresh_ref[t].reshape(2 * requests, KV_WIDTH).astype(F32)

    rows = steps * GROUP * KEY_VALUE_HEADS
    own = iota((rows, KV_WIDTH), 1) // HEAD_SIZE == iota((rows, KV_WIDTH), 0) % KEY_VALUE_HEADS
    lane = iota((rows, LANES), 1)
    head = iota((rows, LANES), 0) % KEY_VALUE_HEADS
    row_step = iota((rows, 16), 0) // (GROUP * KEY_VALUE_HEADS)
    kept = jnp.logical_and(iota((rows, 16), 1) <= row_step, seq_ref[0] == 0)
    fresh_bias = jnp.where(kept, 0.0, NEG_FILL)

    def fresh_rows(r, which):
        found = [new_ref[u, pl.ds(2 * r + which, 1), :] for u in range(steps)]
        return jnp.concatenate(found + [jnp.zeros((16 - steps, KV_WIDTH), F32)], axis=0).astype(BF16)

    def attend_pages(r, count):
        spread = jnp.concatenate(
            [
                jnp.broadcast_to(query_ref[i, pl.ds(r, 1), :], (KEY_VALUE_HEADS, KV_WIDTH))
                for i in range(steps * GROUP)
            ],
            axis=0,
        )
        spread = jnp.where(own, spread, 0.0).astype(BF16)
        both = [page_ref[r * pages + page].reshape(2 * page_rows, KV_WIDTH) for page in range(count)]
        both = jnp.concatenate(both, axis=0)
        size = 2 * count * page_rows
        place = iota((1, size), 1)
        live = jnp.logical_and(place % 2 == 0, first + place // 2 < len_ref[r])
        scores = dot_nt(spread, both) + jnp.where(live, 0.0, NEG_FILL)
        fresh_scores = dot_nt(spread, fresh_rows(r, 0)) + fresh_bias
        largest = jnp.maximum(
            jnp.max(scores, axis=1, keepdims=True), jnp.max(fresh_scores, axis=1, keepdims=True)
        )
        weights = jnp.exp(scores - largest)
        fresh_weights = jnp.exp(fresh_scores - largest)
        total = jnp.sum(weights, axis=1, keepdims=True)
        total = total + jnp.sum(fresh_weights, axis=1, keepdims=True)
        moved = [pltpu.roll(tile_of(weights, j), 1, 1) for j in range(size // LANES)]
        acc = dot_nn(jnp.concatenate(moved, axis=1).astype(BF16), both)
        acc = acc + dot_nn(fresh_weights.astype(BF16), fresh_rows(r, 1))
        acc = jnp.where(own, acc * (1.0 / total), 0.0)
        acc = jnp.sum(acc.reshape(steps * GROUP, KEY_VALUE_HEADS, KV_WIDTH), axis=1)
        level = jnp.where(needed(r, 0), largest + jnp.log(total), NEG_FILL)
        high = round16(level)
        middle = round16(level - high)
        side = jnp.where(lane == head, high, 0.0)
        side = jnp.where(lane == head + 8, middle, side)
        side = jnp.where(lane == head + 16, level - high - middle, side)
        side = jnp.sum(side.reshape(steps * GROUP, KEY_VALUE_HEADS, LANES), axis=1)
        return acc.astype(BF16), side.astype(BF16)

    def one_pair(pair, carry):
        both = order_ref[2 * pair], order_ref[2 * pair + 1]
        for low, high in bounds:
            enough = needed(both[0], low)
            if high < pages:
                enough = jnp.logical_and(enough, jnp.logical_not(needed(both[0], high)))

            @pl.when(enough)
            def _():
                for page in range(high):
                    for r in both:
                        copy(r, page).wait()
                made = [attend_pages(r, high) for r in both]
                for r, (acc, side) in zip(both, made):
                    put(r, acc, side)

        @pl.when(jnp.logical_not(needed(both[0], 0)))
        def _():
            empty = jnp.where(iota((steps * GROUP, LANES), 1) < KEY_VALUE_HEADS, NEG_FILL, 0.0)
            for r in both:
                put(r, jnp.zeros((steps * GROUP, KV_WIDTH), BF16), empty.astype(BF16))

        return carry

    lax.fori_loop(0, requests // 2, one_pair, 0)


def attend(queries, new_key_value, cache, page_table, cache_len, seq_index, devices):
    steps, requests, _ = queries.shape
    pages = page_table.shape[1]
    page_rows = cache.shape[1]
    classes = tuple(c for c in (1, 2, 4, 6) if c < pages) + (pages,)
    share = (requests * steps * GROUP // devices, KV_WIDTH + LANES)
    smem, hbm = pl.BlockSpec(memory_space=pltpu.SMEM), pl.BlockSpec(memory_space=pl.ANY)
    return pl.pallas_call(
        functools.partial(attend_kernel, classes),
        in_specs=[smem] + [hbm] * 5,
        out_shape=jax.ShapeDtypeStruct((devices,) + share, BF16),
        scratch_shapes=[
            pltpu.VMEM((requests * pages, page_rows, 2, KV_WIDTH), BF16),
            pltpu.SMEM(page_table.shape, jnp.int32),
            pltpu.SMEM(cache_len.shape, jnp.int32),
            pltpu.VMEM(queries.shape, BF16),
            pltpu.VMEM(new_key_value.shape, BF16),
            pltpu.VMEM((steps * GROUP, requests, KV_WIDTH), F32),
            pltpu.VMEM((steps, 2 * requests, KV_WIDTH), F32),
            pltpu.SMEM((requests,), jnp.int32),
            pltpu.SemaphoreType.DMA((requests * pages,)),
            pltpu.SemaphoreType.DMA((4,)),
        ],
        compiler_params=pltpu.CompilerParams(vmem_limit_bytes=ATTEND_VMEM),
        name="attend",
    )(seq_index, page_table, cache_len, queries, new_key_value, cache)


def join_kernel(x_ref, out_ref):
    blocks, rows, _ = x_ref.shape
    tokens = rows // GROUP
    levels = []
    for b in range(blocks):
        side = x_ref[b, :, KV_WIDTH : KV_WIDTH + LANES].astype(F32)
        levels.append(side + pltpu.roll(side, LANES - 8, 1) + pltpu.roll(side, LANES - 16, 1))
    largest = functools.reduce(jnp.maximum, levels)
    weights = [jnp.exp(level - largest) for level in levels]
    inverse = 1.0 / functools.reduce(jnp.add, weights)
    low = iota((rows, LANES), 1) < HEAD_SIZE
    acc = [jnp.zeros((rows, LANES), F32) for _ in range(KV_WIDTH // LANES)]
    for b in range(blocks):
        share = weights[b] * inverse
        for j in range(KV_WIDTH // LANES):
            factor = jnp.where(low, share[:, 2 * j : 2 * j + 1], share[:, 2 * j + 1 : 2 * j + 2])
            acc[j] = acc[j] + factor * x_ref[b, :, j * LANES : (j + 1) * LANES].astype(F32)

    def piece(head, half):
        k, g = head // GROUP, head % GROUP
        tile = jnp.concatenate(
            [acc[k // 2][t * GROUP + g : t * GROUP + g + 1] for t in range(tokens)], axis=0
        )
        return tile if k % 2 == half else swap_halves(tile)

    low_tokens = iota((tokens, LANES), 1) < HEAD_SIZE
    for m in range(QUERY_HEADS // 2):
        tile = jnp.where(low_tokens, piece(2 * m, 0), piece(2 * m + 1, 1)).astype(BF16)
        out_ref[:, m * LANES : (m + 1) * LANES] = tile


def join(parts):
    rows = parts.shape[1]
    return pl.pallas_call(
        join_kernel,
        out_shape=jax.ShapeDtypeStruct((rows // GROUP, QUERY_HEADS * HEAD_SIZE), BF16),
        compiler_params=params(),
        name="join",
    )(parts)


def side_place(features, count):
    tile, offset = features // LANES * LANES, features % LANES
    return (tile, offset) if offset and offset + count <= LANES else (padded(features), 0)


def hidden_kernel(seq_ref, residual_ref, w_ref, gain_ref, routes_ref, *refs):
    attn_refs, (hidden_ref, out_ref, wide_ref) = refs[:-3], refs[-3:]
    steps, requests, features = residual_ref.shape
    tokens = steps * requests
    blocks = [ref[i].astype(F32) for ref in attn_refs for i in range(2)]
    attn = jnp.concatenate(blocks, axis=0).astype(BF16)
    row, column = iota((tokens, tokens), 0), iota((tokens, tokens), 1)
    devices, share = len(blocks), attn_refs[0].shape[1]
    source = seq_ref[0] + devices - column // (2 * share) * 2
    source = jnp.where(source >= devices, source - devices, source)
    other = column // share % 2
    source = source + other * (1 - source % 2 * 2)
    token = source * share + column % share
    reorder = jnp.logical_and(row % requests == token // steps, row // requests == token % steps)
    attn = dot_nn(reorder.astype(F32).astype(BF16), attn).astype(BF16)
    residual = residual_ref[...].astype(F32).reshape(tokens, features)
    hidden = residual + dot_nt(attn, w_ref[...])
    hidden_ref[...] = hidden
    squares = jnp.sum(hidden * hidden, axis=1, keepdims=True)
    tile, offset = side_place(features, SIDE_KEYS + EXPERTS)
    wide_ref[...] = jnp.zeros_like(wide_ref)
    wide_ref[:, 0:features] = hidden * gain_ref[...]
    routes = routes_ref[...].reshape(tokens, routes_ref.shape[2])
    lane = iota((tokens, LANES), 1) - offset
    side = wide_ref[:, tile : tile + LANES]
    for k in range(routes.shape[1]):
        side = jnp.where(lane == routes[:, k : k + 1] + SIDE_KEYS, 1.0, side)
    high = round16(squares)
    side = jnp.where(lane == 0, high, side)
    wide_ref[:, tile : tile + LANES] = jnp.where(lane == 1, squares - high, side)
    out_ref[...] = wide_ref[...].astype(BF16)


def hidden_state(seq_index, attn, residual, w_out, gain, routes):
    steps, requests, features = residual.shape
    tokens = steps * requests
    wide = side_place(features, SIDE_KEYS + EXPERTS)[0] + LANES
    smem, vmem = pl.BlockSpec(memory_space=pltpu.SMEM), pl.BlockSpec(memory_space=pltpu.VMEM)
    return pl.pallas_call(
        hidden_kernel,
        in_specs=[smem] + [vmem] * (4 + len(attn)),
        out_shape=(
            jax.ShapeDtypeStruct((tokens, features), F32),
            jax.ShapeDtypeStruct((tokens, wide), BF16),
        ),
        scratch_shapes=[pltpu.VMEM((tokens, wide), F32)],
        compiler_params=params(),
        name="hidden",
    )(seq_index, residual, w_out.T, gain.reshape(1, features), routes, *attn)


def window_start(first, rows, window):
    return pl.multiple_of(jnp.clip(first // 16 * 16, 0, rows - window), 16)


def gate_up_kernel(
    features, local, turn, sources, devices, where_ref, seq_ref, w_ref, router_ref, *refs,
):
    part_refs, refs = refs[:sources], refs[sources:]
    out_refs, refs = refs[:devices], refs[devices:]
    pick_ref, range_ref, first_ref, most_ref, x_ref, row_ref, acc_ref, share_ref = refs
    total = x_ref.shape[0]
    for e, part_ref in enumerate(part_refs):
        x_ref[e * (total // sources) : (e + 1) * (total // sources)] = part_ref[...]
    rows = pick_ref.shape[1]
    width = w_ref.shape[3]
    window = total // 2 + 16
    tile, offset = side_place(features, SIDE_KEYS + EXPERTS)
    me = where_ref[0]
    own_side = x_ref[:, tile : tile + LANES].astype(F32)
    lane = iota((total, LANES), 1)
    flags = pltpu.roll(own_side, LANES - offset - SIDE_KEYS, 1)
    flags = jnp.where(lane < EXPERTS, flags, 0.0)
    owners = EXPERTS // local
    counts = jnp.sum(flags, axis=0, keepdims=True)
    most = jnp.int32(0)
    for o in range(owners):
        held = jnp.logical_and(lane[0:1] >= o * local, lane[0:1] < (o + 1) * local)
        most = jnp.maximum(most, jnp.sum(jnp.where(held, counts, 0.0)).astype(jnp.int32))
    most_ref[0] = most
    mine = pltpu.roll(flags, lax.rem(LANES - me * local, LANES), 1)
    mine = jnp.where(lane < local, mine, 0.0)
    mine16 = mine.astype(BF16)
    row, column = iota((total, total), 0), iota((total, total), 1)
    earlier = (column < row).astype(F32).astype(BF16)
    ranks = dot_nn(earlier, mine16)
    counts = jnp.sum(mine, axis=0, keepdims=True)
    before = (iota((LANES, LANES), 0) < iota((LANES, LANES), 1)).astype(F32).astype(BF16)
    first = dot_nn(jnp.broadcast_to(counts, (8, LANES)).astype(BF16), before)[0:1] - turn * rows
    place = jnp.where(mine > 0.0, first + ranks, -1.0).astype(jnp.int32)
    at = iota((total, rows), 1)
    pick = jnp.zeros((total, rows), F32)
    for j in range(local):
        pick = jnp.where(at == place[:, j : j + 1], 1.0, pick)
    pick = pick.astype(BF16)
    pick_ref[...] = pick
    ranges = jnp.where(iota((16, LANES), 0) < 8, first, first + counts)
    ranges = jnp.concatenate([ranges[0:8], ranges[8:16]] + [jnp.zeros((LANES - 16, LANES), F32)], axis=0)
    ranges = ranges.T
    range_ref[...] = ranges[0:16]
    row_ref[...] = dot_tn(pick, x_ref[...]).astype(BF16)
    acc_ref[...] = jnp.zeros_like(acc_ref)
    for j in range(local):
        start_row = jnp.sum(first[:, j : j + 1]).astype(jnp.int32)
        first_ref[j] = start_row
        start = window_start(start_row, rows, window)
        part = row_ref[pl.ds(start, window), 0:features]
        fresh = start + iota((window, width), 0) >= start_row
        for half in range(2):
            into = (pl.ds(start, window), slice(half * width, (half + 1) * width))
            made = dot_nn(part, w_ref[j, half])
            acc_ref[into] = jnp.where(fresh, made, acc_ref[into])
    logits = dot_nt(router_ref[...], x_ref[:, 0:features])
    high = round16(logits)
    both = jnp.concatenate([high, logits - high], axis=0).astype(BF16)
    both = dot_nn(both, pick)
    turned = jnp.zeros((EXPERTS, rows), jnp.bool_)
    expert = iota((EXPERTS, rows), 0) - me * local
    where_row = iota((EXPERTS, rows), 1).astype(F32)
    for j in range(local):
        inside = jnp.logical_and(
            where_row >= first[:, j : j + 1], where_row < (first + counts)[:, j : j + 1]
        )
        turned = jnp.logical_or(turned, jnp.logical_and(inside, expert == j))
    squares = dot_tn(own_side.astype(BF16), pick)
    side = jnp.concatenate(
        [
            jnp.sum(jnp.where(turned, both[0:EXPERTS], 0.0), axis=0, keepdims=True),
            jnp.sum(jnp.where(turned, both[EXPERTS : 2 * EXPERTS], 0.0), axis=0, keepdims=True),
            squares[offset : offset + 2],
            jnp.zeros((12, rows), F32),
        ],
        axis=0,
    )
    share = share_ref.shape[1] - 16
    low = iota((share, LANES), 1) < PIECE_WIDTH
    for b in range(devices):
        piece, start = b % PIECES, b // PIECES * share
        tile = piece // 2 * LANES
        gate = acc_ref[start : start + share, tile : tile + LANES]
        up = acc_ref[start : start + share, width + tile : width + tile + LANES]
        if piece % 2 == 0:
            made = jnp.where(low, gate, swap_halves(up))
        else:
            made = jnp.where(low, swap_halves(gate), up)
        share_ref[b, 0:share, :] = made.astype(BF16)
        if piece == 0:
            strips = []
            for at in range(0, share, LANES):
                size = min(LANES, share - at)
                strip = side[0:4, start + at : start + at + size]
                if size < LANES:
                    strip = jnp.concatenate([strip, jnp.zeros((4, LANES - size), F32)], axis=1)
                strips.append(strip)
            strips.append(jnp.zeros((16 - 4 * len(strips), LANES), F32))
            strips = jnp.concatenate(strips, axis=0).astype(BF16)
        share_ref[b, share : share + 16, :] = strips
    for k, out_ref in enumerate(out_refs):
        out_ref[...] = share_ref[lax.rem(seq_ref[0] + k, devices)]


def gate_up(exp_index, seq_index, tokens, weights, w_router, rows, devices, turn):
    local, _, features, width = weights.shape
    sources, wide = len(tokens), tokens[0].shape[1]
    total = sources * tokens[0].shape[0]
    share = (rows * PIECES // devices + 16, LANES)
    smem, vmem = pl.BlockSpec(memory_space=pltpu.SMEM), pl.BlockSpec(memory_space=pltpu.VMEM)
    return pl.pallas_call(
        functools.partial(gate_up_kernel, features, local, turn, sources, devices),
        in_specs=[smem] * 2 + [vmem] * (2 + sources),
        out_specs=(vmem,) * devices + (vmem, vmem, smem, smem),
        out_shape=(jax.ShapeDtypeStruct(share, BF16),) * devices
        + (
            jax.ShapeDtypeStruct((total, rows), BF16),
            jax.ShapeDtypeStruct((16, LANES), F32),
            jax.ShapeDtypeStruct((16,), jnp.int32),
            jax.ShapeDtypeStruct((1,), jnp.int32),
        ),
        scratch_shapes=[
            pltpu.VMEM((total, wide), BF16),
            pltpu.VMEM((rows, wide), BF16),
            pltpu.VMEM((rows, 2 * width), F32),
            pltpu.VMEM((devices,) + share, BF16),
        ],
        compiler_params=params(),
        name="gate_up",
    )(exp_index, seq_index, weights, w_router.T, *tokens)


def inner_kernel(*refs):
    x_refs, (out_ref, logit_ref) = refs[:-2], refs[-2:]
    share = x_refs[0].shape[0] - 16
    half = share // 2

    def total(start, size):
        return functools.reduce(
            jnp.add, [x_ref[start : start + size].astype(F32) for x_ref in x_refs]
        )

    side = total(share, 16)
    columns, logits = [], []
    for strip in range(-(-share // LANES)):
        values = side[4 * strip : 4 * strip + 4]
        inverse = lax.rsqrt((values[2:3] + values[3:4]) * (1.0 / D) + 1e-6)
        logits.append((values[0:1] + values[1:2]) * inverse)
        columns.append(jnp.broadcast_to(inverse, (LANES, LANES)).T)
    logit_ref[...] = jnp.concatenate(logits + [jnp.zeros((8 - len(logits), LANES), F32)], axis=0)
    scaled = total(0, share) * jnp.concatenate(columns, axis=0)[0:share]
    made = scaled / (1.0 + jnp.exp(-scaled)) * swap_halves(scaled)
    low = iota((half, LANES), 1) < PIECE_WIDTH
    made = jnp.where(low, made[0:half], swap_halves(made[half:share])).astype(BF16)
    out_ref[...] = made


def inner(parts):
    return pl.pallas_call(
        inner_kernel,
        out_shape=(
            jax.ShapeDtypeStruct(((parts[0].shape[0] - 16) // 2, LANES), BF16),
            jax.ShapeDtypeStruct((8, LANES), F32),
        ),
        compiler_params=params(),
        name="inner",
    )(*parts)


def down_kernel(features, local, pairs, first_ref, seq_ref, range_ref, pick_ref, w_ref, logit_ref, *refs):
    pair_refs, out_refs, (x_ref, row_ref, made_ref) = refs[:pairs], refs[pairs:-3], refs[-3:]
    total, rows = pick_ref.shape
    width = w_ref.shape[2]
    window = total // 2 + 16
    devices, half, _ = x_ref.shape
    for k, pair_ref in enumerate(pair_refs):
        source = lax.rem(seq_ref[0] + devices - 2 * k, devices)
        x_ref[source] = pair_ref[0]
        x_ref[source + 1 - lax.rem(source, 2) * 2] = pair_ref[1]
    share = 2 * half
    low = iota((half, LANES), 1) < PIECE_WIDTH
    for b in range(0, devices, 2):
        start, tile = b // PIECES * share, b % PIECES // 2 * LANES
        one, two = x_ref[b].astype(F32), x_ref[b + 1].astype(F32)
        above = jnp.where(low, one, swap_halves(two)).astype(BF16)
        below = jnp.where(low, swap_halves(one), two).astype(BF16)
        row_ref[start : start + half, tile : tile + LANES] = above
        row_ref[start + half : start + share, tile : tile + LANES] = below
    logit = []
    for piece in range(devices // PIECES):
        for strip in range(-(-share // LANES)):
            size = min(LANES, share - strip * LANES)
            logit.append(logit_ref[piece, strip : strip + 1, 0:size])
    made_ref[...] = jnp.zeros_like(made_ref)
    for j in range(local):
        start_row = first_ref[j]
        start = window_start(start_row, rows, window)
        made = dot_nt(row_ref[pl.ds(start, window), :], w_ref[j])
        fresh = start + iota((window, features), 0) >= start_row
        into = (pl.ds(start, window), slice(0, features))
        made_ref[into] = jnp.where(fresh, made, made_ref[into])
    logit = jnp.concatenate(logit, axis=1)
    high = round16(logit)
    middle = round16(logit - high)
    pick = pick_ref[...]
    where_row = iota((16, rows), 1).astype(F32)
    inside = jnp.logical_and(where_row >= range_ref[:, 0:1], where_row < range_ref[:, 8:9])
    inside = jnp.logical_and(inside, iota((16, rows), 0) < local)
    spread = [jnp.where(inside, part, 0.0) for part in (high, middle, logit - high - middle)]
    spread.append(inside.astype(F32))
    found = dot_nt(jnp.concatenate(spread, axis=0).astype(BF16), pick)
    valid = found[48:64] > 0.5
    logits = jnp.where(valid, found[0:16] + found[16:32] + found[32:48], NEG_FILL)
    top = jnp.max(logits, axis=0, keepdims=True)
    weights = jnp.where(valid, jnp.exp(logits - top), 0.0)
    summed = jnp.sum(weights, axis=0, keepdims=True)
    high = round16(weights)
    both = dot_nn(jnp.concatenate([high, weights - high], axis=0).astype(BF16), pick)
    weight = jnp.sum(jnp.where(inside, both[0:16] + both[16:32], 0.0), axis=0, keepdims=True)
    column = jnp.broadcast_to(weight, (LANES, rows)).T[:, 0:1]
    acc = dot_nn(pick, (made_ref[...] * column).astype(BF16))
    tile, offset = side_place(features, 2)
    pair = jnp.where(iota((LANES, total), 0) == 0, top, summed).T
    tokens = total // len(out_refs)
    for e, out_ref in enumerate(out_refs):
        at = slice(e * tokens, (e + 1) * tokens)
        out_ref[...] = acc[at]
        lane = iota((tokens, LANES), 1) - offset
        side = jnp.where(lane == 0, pair[at, 0:1], acc[at, tile : tile + LANES])
        out_ref[:, tile : tile + LANES] = jnp.where(lane == 1, pair[at, 1:2], side)


def down(first, seq_index, ranges, pick, made, logits, weights, exp_count):
    local, features, width = weights.shape
    total, rows = pick.shape
    wide = side_place(features, 2)[0] + LANES
    smem, vmem = pl.BlockSpec(memory_space=pltpu.SMEM), pl.BlockSpec(memory_space=pltpu.VMEM)
    return pl.pallas_call(
        functools.partial(down_kernel, features, local, len(made)),
        in_specs=[smem] * 2 + [vmem] * (4 + len(made)),
        out_shape=(jax.ShapeDtypeStruct((total // exp_count, wide), F32),) * exp_count,
        scratch_shapes=[
            pltpu.VMEM((2 * len(made),) + made[0].shape[1:], BF16),
            pltpu.VMEM((rows, width), BF16),
            pltpu.VMEM((rows, wide), F32),
        ],
        compiler_params=params(),
        name="down",
    )(first, seq_index, ranges, pick, weights, logits, *made)


def finish_kernel(hidden_ref, *refs):
    part_refs, out_ref = refs[:-1], refs[-1]
    features = hidden_ref.shape[1]
    tile, offset = side_place(features, 2)
    sides = [x_ref[:, tile : tile + LANES] for x_ref in part_refs]
    tops = [side[:, offset : offset + 1] for side in sides]
    top = functools.reduce(jnp.maximum, tops)
    scales = [jnp.exp(one - top) for one in tops]
    total = functools.reduce(
        jnp.add, [s * side[:, offset + 1 : offset + 2] for s, side in zip(scales, sides)]
    )
    acc = functools.reduce(
        jnp.add, [s * x_ref[:, 0:features] for x_ref, s in zip(part_refs, scales)]
    )
    out = hidden_ref[...] + acc * (1.0 / total)
    out_ref[...] = out.reshape(out_ref.shape).astype(BF16)


def finish(parts, hidden, shape):
    return pl.pallas_call(
        finish_kernel,
        out_shape=jax.ShapeDtypeStruct(shape, BF16),
        compiler_params=params(),
        name="finish",
    )(hidden, *parts)


def join_rounds(features, one, other):
    tile, offset = side_place(features, 2)
    at = tile + offset
    top = jnp.maximum(one[..., at : at + 1], other[..., at : at + 1])
    scales = [jnp.exp(part[..., at : at + 1] - top) for part in (one, other)]
    joined = one * scales[0] + other * scales[1]
    return jnp.where(jnp.arange(one.shape[-1]) == at, top, joined)


def send(x, axis, distance):
    count = lax.axis_size(axis)
    return lax.ppermute(x, axis, [(i, (i + distance) % count) for i in range(count)])


def swap(x, axis):
    return lax.all_to_all(x, axis, split_axis=0, concat_axis=0, tiled=True)


def exchange(parts, axis, direction):
    return [parts[0]] + [send(part, axis, direction * k) for k, part in enumerate(parts) if k]


def pair_gather(block, axis):
    count = lax.axis_size(axis)
    beside = lax.ppermute(block, axis, [(i, i ^ 1) for i in range(count)])
    pair = jnp.stack([block, beside])
    return [pair] + [send(pair, axis, k) for k in range(2, count, 2)]


def gather(block, axis):
    return exchange([block] * lax.axis_size(axis), axis, 1)


def local(
    queries,
    new_key_value,
    key_value_cache,
    page_table,
    cache_len,
    routes,
    residual,
    w_out,
    norm_gain,
    w_router,
    w_gate_up,
    w_down,
):
    exp_count = lax.axis_size("exp")
    seq_count = lax.axis_size("seq")
    exp_index = lax.axis_index("exp").astype(jnp.int32).reshape(1)
    seq_index = lax.axis_index("seq").astype(jnp.int32).reshape(1)
    steps, requests, width = queries.shape
    tokens = steps * requests
    features = w_out.shape[1]
    page_rows = key_value_cache.shape[2]
    pool = key_value_cache.reshape(-1, page_rows, 2, KV_WIDTH)

    shares = attend(
        queries, new_key_value, pool, page_table, cache_len, seq_index, seq_count
    )
    w_gate_up, shares = lax.optimization_barrier((w_gate_up, shares))
    gate_up_weights = w_gate_up.transpose(0, 2, 1, 3)
    shares = swap(shares, "seq")
    gate_up_weights, shares = lax.optimization_barrier((gate_up_weights, shares))
    attn = join(shares)
    gathered = pair_gather(attn, "seq")
    hidden, outgoing = hidden_state(seq_index, gathered, residual, w_out, norm_gain, routes)
    incoming = gather(outgoing, "exp")
    pieces = seq_count // PIECES
    rows = -(-ROUND_ROWS // (32 * pieces)) * 32 * pieces

    def one_round(turn):
        *partial, pick, ranges, first, most = gate_up(
            exp_index, seq_index, incoming, gate_up_weights, w_router, rows, seq_count, turn
        )
        made, logits = inner(exchange(partial, "seq", 1))
        logits = logits[None] if pieces == 1 else lax.all_gather(logits, "seq")[::PIECES]
        made = pair_gather(made, "seq")
        return down(first, seq_index, ranges, pick, made, logits, w_down, exp_count), most

    made, most = one_round(0)
    pairs = w_gate_up.shape[0] * exp_count * steps * CAP
    for turn in range(1, -(-pairs // rows)):
        made = lax.cond(
            most[0] > turn * rows,
            lambda made: tuple(
                join_rounds(features, *both) for both in zip(made, one_round(turn)[0])
            ),
            lambda made: made,
            made,
        )
    return finish(exchange(made, "exp", -1), hidden, (steps, requests, features))


def solution(mesh):
    in_specs = (
        P(None, "exp", None),
        P(None, "exp", None, None),
        P("exp", "seq", None, None, None),
        P("exp", "seq"),
        P("exp"),
        P(None, "exp", None),
        P(None, "exp", "seq"),
        P(None, "seq"),
        P("seq"),
        P("seq", None),
        P("exp", "seq", None, None),
        P("exp", "seq", None),
    )
    out_specs = P(None, "exp", "seq")
    return jax.shard_map(local, mesh=mesh, in_specs=in_specs, out_specs=out_specs, check_vma=False)
```
